32 devices in a mesh: groups: 1, tensor: 32 (over z, y, x, core).
Axes of the slice: x: 2, y: 2, z: 4, core: 2. Of those that a mesh axis runs over, the one named last changes fastest.
Arguments:
- tokens: bfloat16 [32, 6, 4096], P(('groups', 'tensor')), may hold values from -6 to 6
- w_gate: bfloat16 [32, 4096, 1792], P('tensor'), may hold values from -0.0625 to 0.0625
- w_up: bfloat16 [32, 4096, 1792], P('tensor'), may hold values from -0.0625 to 0.0625
- w_down: bfloat16 [32, 1792, 4096], P('tensor'), may hold values from -0.03125 to 0.03125
- shrink_factors: bfloat16 [2, 8192, 512], P('groups', 'tensor'), may hold values from -0.0625 to 0.0625
- expand_factors: bfloat16 [2, 512, 28672], P('groups', 'tensor'), may hold values from -1.5 to 1.5
- rank_blocks: int32 [8], P('groups'), may hold values from 1 to 8, 32 in all
- row_counts: int32 [8], P('groups'), may hold values from 1 to 24, 96 in all
Outputs:
- mixed: bfloat16 [32, 6, 4096], P(('groups', 'tensor'))
The draws below stay inside these ranges and needn't reach their ends.
Inputs may be any that keep to these rules, and one draw needn't show every extreme that they name: `rank_blocks`: sums to 32; some adapter has 8 blocks. `row_counts`: sums to 96; some adapter has 24 rows.
All inputs are finite; a program needn't handle non-finite values.
Results may differ from the reference program's by a relative error of at most 0.0055.
Values may be sent and summed in bfloat16 or wider, within the bound.
No kernel may reach another device: no remote copies, remote signals or barrier semaphores. Data moves between devices by JAX's collectives and lax.ppermute only.
A program may use at most 192 MiB of HBM per device.

```python
import math
import jax
import jax.numpy as jnp
import numpy as np

D = 8192
FF = 28672
FGROUPS = 2
ROWS = 96
RBLK = 32
RANKCOLS = 512
ADAPTERS = 8
ROWMOST = 24
N_TENSOR = 32


def shard_levels(stream_key, extent, cuts, smallest, high):
    loudness, own = 1.0, jax.random.fold_in(stream_key, 6)
    for axis_at, parts in cuts:
        heights = jnp.exp(jax.random.uniform(jax.random.fold_in(own, axis_at), (parts,), jnp.float32, smallest / len(cuts), high / len(cuts)))
        loudness = loudness * jnp.repeat(heights, extent[axis_at] // parts).reshape([-1 if axis == axis_at else 1 for axis in range(len(extent))])
    return loudness


def length_profile(number_of, total, most, skew):
    weights = [(1 << 20) // math.isqrt(standing ** skew) + 1 for standing in range(2, number_of + 1)]
    rest, given = total - most - (number_of - 1), [1] * (number_of - 1)
    while rest > 0:
        candidates = [i for i in range(number_of - 1) if given[i] < most]
        pool, remaining = sum([weights[i] for i in candidates]), rest
        for i in candidates:
            extra = min(most - given[i], max(1, remaining * weights[i] // pool), rest)
            given[i] = given[i] + extra
            rest = rest - extra
    return np.array([most] + given)


def ragged_sizes(key, number_of, total, limit, skew):
    if number_of == 2:
        one = jax.random.randint(key, (), max(1, total - limit), min(limit, total - 1) + 1)
        return jnp.stack([one, total - one])
    sizes = jnp.asarray(length_profile(number_of, total, limit, skew), jnp.int32)
    twos = (number_of - 1) // 2
    source_of, receiver = sizes[1:1 + 2 * twos:2], sizes[2:2 + 2 * twos:2]
    room = jnp.minimum(source_of - 1, limit - receiver)
    shifted = jax.random.randint(jax.random.fold_in(key, 1), (twos,), 0, 1 << 20) % (room + 1)
    sizes = sizes.at[1:1 + 2 * twos:2].set(source_of - shifted).at[2:2 + 2 * twos:2].set(receiver + shifted)
    return sizes[jax.random.permutation(jax.random.fold_in(key, 2), number_of)]


def noise(rng, dims, scale, most, shards=(), kind=jnp.bfloat16):
    result = scale * jax.random.normal(rng, dims, jnp.float32)
    if shards:
        result = result * shard_levels(rng, dims, shards, -0.22, 0.18)
    return jnp.clip(result, -most, most).astype(kind)


def setup_inputs(seed: int = 0, part: int = 0) -> dict:
    key_list = jax.random.split(jax.random.key(seed), 9)
    part_keys = jax.random.split(jax.random.fold_in(key_list[8], part), 9)
    tokens = noise(part_keys[0], (N_TENSOR, ROWS // 16, D // FGROUPS), 1.0, 6.0, ((0, 32),))
    w_gate = noise(key_list[1], (N_TENSOR, D // FGROUPS, FF // 16), D ** -0.5, 0.0625, ((0, 32),))
    w_up = noise(key_list[2], (N_TENSOR, D // FGROUPS, FF // 16), D ** -0.5, 0.0625, ((0, 32),))
    w_down = noise(key_list[3], (N_TENSOR, FF // 16, D // FGROUPS), FF ** -0.5, 0.03125, ((0, 32),))
    shrink_factors = noise(part_keys[4], (2, D, RANKCOLS), D ** -0.5, 0.0625, ((1, 32),))
    expand_factors = noise(part_keys[5], (2, RANKCOLS, FF), 16 ** -0.5, 1.5, ((1, 32),))
    rank_blocks = ragged_sizes(part_keys[6], ADAPTERS, RBLK, 8, 2).astype(jnp.int32)
    row_counts = ragged_sizes(part_keys[7], ADAPTERS, ROWS, ROWMOST, 2).astype(jnp.int32)
    return dict(tokens=tokens, w_gate=w_gate, w_up=w_up, w_down=w_down, shrink_factors=shrink_factors, expand_factors=expand_factors, rank_blocks=rank_blocks, row_counts=row_counts)


def owners(rank_blocks, row_counts, total_blocks, total_rows):
    block_end = jnp.cumsum(rank_blocks).astype(jnp.int32)
    block_ids = jnp.arange(total_blocks, dtype=jnp.int32)
    block_owner = jnp.sum((block_end[None, :] <= block_ids[:, None]).astype(jnp.int32), axis=1).astype(jnp.int32)
    column_owner = jnp.repeat(block_owner, 16, total_repeat_length=total_blocks * 16)
    row_end = jnp.cumsum(row_counts).astype(jnp.int32)
    row_ids = jnp.arange(total_rows, dtype=jnp.int32)
    row_owner = jnp.sum((row_end[None, :] <= row_ids[:, None]).astype(jnp.int32), axis=1).astype(jnp.int32)
    adapter_ids = jnp.arange(rank_blocks.shape[0], dtype=jnp.int32)
    row_blocks = jnp.sum(jnp.where(row_owner[:, None] == adapter_ids[None, :], rank_blocks[None, :], 0), axis=1)
    row_scale = 1.0 / row_blocks.astype(jnp.float32)
    return (row_owner[:, None] == column_owner[None, :]).astype(jnp.float32) * row_scale[:, None]


def reference(tokens, w_gate, w_up, w_down, shrink_factors, expand_factors, rank_blocks, row_counts):
    fgroups = N_TENSOR // 16
    count, row_block, group_width = tokens.shape
    slab = group_width // 16
    natural = tokens.reshape(16, fgroups, row_block, 16, slab).transpose(0, 2, 3, 1, 4).reshape(16 * row_block, 16 * fgroups * slab)
    grouped = tokens.reshape(16, fgroups, row_block, group_width).transpose(0, 2, 1, 3).reshape(16 * row_block, fgroups * group_width)
    keep = owners(rank_blocks, row_counts, RBLK, ROWS)
    shrink_gate = (jnp.dot(natural, shrink_factors[0], preferred_element_type=jnp.float32) * keep).astype(jnp.bfloat16)
    shrink_upper = (jnp.dot(natural, shrink_factors[1], preferred_element_type=jnp.float32) * keep).astype(jnp.bfloat16)
    gate_blocks = w_gate.reshape(16, fgroups * group_width, w_gate.shape[2])
    up_blocks = w_up.reshape(16, fgroups * group_width, w_up.shape[2])
    gate = jnp.concatenate([jnp.dot(grouped, gate_blocks[b], preferred_element_type=jnp.float32) for b in range(16)], axis=1)
    upward = jnp.concatenate([jnp.dot(grouped, up_blocks[b], preferred_element_type=jnp.float32) for b in range(16)], axis=1)
    gate = gate + jnp.dot(shrink_gate, expand_factors[0], preferred_element_type=jnp.float32)
    upward = upward + jnp.dot(shrink_upper, expand_factors[1], preferred_element_type=jnp.float32)
    hidden = (jax.nn.silu(gate) * upward).astype(jnp.bfloat16)
    unit_width = w_down.shape[1]
    down_blocks = w_down.reshape(16, fgroups, unit_width, group_width)
    outputs = []
    for a in range(fgroups):
        total = jnp.zeros((hidden.shape[0], group_width), jnp.float32)
        for b in range(16):
            total = total + jnp.dot(hidden[:, b * unit_width:(b + 1) * unit_width], down_blocks[b, a], preferred_element_type=jnp.float32)
        outputs.append(total.astype(jnp.bfloat16).reshape(16, row_block, group_width))
    return jnp.stack(outputs, axis=1).reshape(16 * fgroups, row_block, group_width)
```

```python
import jax
import jax.numpy as jnp
from jax import lax
from jax.experimental import pallas as pl
from jax.experimental.pallas import tpu as pltpu
from jax.sharding import PartitionSpec as P

HIDDEN_BITS = 4
FOLD = 128


def swapped(block, axis, apart):
    count = lax.axis_size(axis)
    return lax.ppermute(block, axis, [(i, i ^ (1 << apart)) for i in range(count)])


def split_kernel(count, strip, source, target, sem):
    copies = [
        pltpu.make_async_copy(
            source.at[:, :, pl.ds(j * strip, strip)], target.at[j], sem.at[j]
        )
        for j in range(count)
    ]
    for copy in copies:
        copy.start()
    for copy in copies:
        copy.wait()


def by_target(expand, count):
    kinds, depth, width = expand.shape
    strip = width // count
    if strip % 128 or depth % 16:
        return expand.reshape(kinds, depth, count, strip).transpose(2, 0, 1, 3)
    return pl.pallas_call(
        lambda *refs: split_kernel(count, strip, *refs),
        out_shape=jax.ShapeDtypeStruct((count, kinds, depth, strip), expand.dtype),
        in_specs=[pl.BlockSpec(memory_space=pl.ANY)],
        out_specs=pl.BlockSpec(memory_space=pl.ANY),
        scratch_shapes=[pltpu.SemaphoreType.DMA((count,))],
        cost_estimate=pl.CostEstimate(
            flops=0, bytes_accessed=4 * expand.size, transcendentals=0
        ),
    )(expand)


def owner_of(ends, ids):
    return jnp.sum((ends[None, :] <= ids[:, None]).astype(jnp.int32), axis=1)


def keep_mask(rank_blocks, row_counts, columns, rows):
    adapters = rank_blocks.shape[0]
    earlier = jnp.arange(adapters)[:, None] >= jnp.arange(adapters)[None, :]
    block_end = jnp.sum(jnp.where(earlier, rank_blocks[None, :], 0), axis=1)
    row_end = jnp.sum(jnp.where(earlier, row_counts[None, :], 0), axis=1)
    column_owner = owner_of(block_end, jnp.arange(columns, dtype=jnp.int32) // 16)
    row_owner = owner_of(row_end, jnp.arange(rows, dtype=jnp.int32))
    ids = jnp.arange(adapters, dtype=jnp.int32)
    row_blocks = jnp.sum(
        jnp.where(row_owner[:, None] == ids[None, :], rank_blocks[None, :], 0), axis=1
    )
    same = (row_owner[:, None] == column_owner[None, :]).astype(jnp.float32)
    return same, 1.0 / row_blocks.astype(jnp.float32)


def shards(tokens, w_gate, w_up, w_down, shrink_factors, expand_factors, rank_blocks, row_counts):
    count = lax.axis_size("tensor")
    low_bits = count.bit_length() - 1 - HIDDEN_BITS
    fgroups = 1 << low_bits
    place = lax.axis_index("tensor")
    feature_group = place % fgroups
    hidden_group = place // fgroups
    block_rows = tokens.shape[1]
    rows = block_rows << HIDDEN_BITS
    units = w_gate.shape[2]
    strip = units // fgroups

    expand = lax.all_to_all(
        by_target(expand_factors, count), "tensor", split_axis=0, concat_axis=0, tiled=True
    )

    gathered = tokens[0]
    for bit in reversed(range(HIDDEN_BITS)):
        other = swapped(gathered, "tensor", low_bits + bit)
        gathered = jnp.concatenate([gathered, other], 0)
    spots = jnp.arange(1 << HIDDEN_BITS, dtype=jnp.int32)
    moved = sum(((spots >> i) & 1) << (HIDDEN_BITS - 1 - i) for i in range(HIDDEN_BITS))
    natural = (
        (moved ^ hidden_group)[:, None] * block_rows + jnp.arange(block_rows, dtype=jnp.int32)[None, :]
    ).reshape(rows)
    to_own = (natural[:, None] == jnp.arange(rows, dtype=jnp.int32)[None, :]).astype(jnp.bfloat16)

    columns = shrink_factors.shape[2]
    same, scale = keep_mask(rank_blocks, row_counts, columns, rows)
    slab = shrink_factors.shape[1]
    features = lax.dynamic_slice_in_dim(gathered, hidden_group * slab, slab, 1)
    features = jnp.dot(to_own.T, features, preferred_element_type=jnp.float32).astype(jnp.bfloat16)
    partial_value = jnp.einsum(
        "rd,kdc->krc", features, shrink_factors, preferred_element_type=jnp.float32
    )
    folded = jnp.sum((partial_value * same).reshape(2, rows, columns // FOLD, FOLD), axis=2)
    for bit in range(low_bits + HIDDEN_BITS):
        folded = folded + swapped(folded, "tensor", bit)
    shrunk = jnp.tile(folded, (1, 1, columns // FOLD)) * (same * scale[:, None])[None]
    shrunk = shrunk.astype(jnp.bfloat16)
    shrunk = jnp.einsum("or,krc->koc", to_own, shrunk, preferred_element_type=jnp.float32)
    shrunk = shrunk.astype(jnp.bfloat16)

    gate_part = jnp.dot(gathered, w_gate[0], preferred_element_type=jnp.float32)
    up_part = jnp.dot(gathered, w_up[0], preferred_element_type=jnp.float32)
    partials = jnp.stack([gate_part, up_part])
    for step in range(low_bits):
        bit = low_bits - 1 - step
        half = partials.shape[2] // 2
        high = feature_group // (1 << bit) % 2
        outgoing = lax.dynamic_slice_in_dim(partials, (1 - high) * half, half, 2)
        staying = lax.dynamic_slice_in_dim(partials, high * half, half, 2)
        partials = staying + swapped(outgoing, "tensor", bit)
    depth = expand.shape[2]
    low_rank = jnp.einsum(
        "krsd,skdc->krc",
        shrunk.reshape(2, rows, count, depth),
        expand,
        preferred_element_type=jnp.float32,
    )
    partials = partials + low_rank
    hidden = (jax.nn.silu(partials[0]) * partials[1]).astype(jnp.bfloat16)
    for step in range(low_bits):
        other = swapped(hidden, "tensor", step)
        high = feature_group // (1 << step) % 2 == 1
        hidden = jnp.where(
            high, jnp.concatenate([other, hidden], 1), jnp.concatenate([hidden, other], 1)
        )
    terms = jnp.dot(hidden, w_down[0], preferred_element_type=jnp.float32)
    for bit in range(HIDDEN_BITS):
        half = terms.shape[0] // 2
        outgoing = terms[half:].astype(jnp.bfloat16)
        terms = terms[:half] + swapped(outgoing, "tensor", low_bits + bit).astype(jnp.float32)
    return terms.astype(jnp.bfloat16)[None]


def solution(mesh):
    placed = (
        P(("groups", "tensor"), None, None),
        P("tensor", None, None),
        P("tensor", None, None),
        P("tensor", None, None),
        P("groups", "tensor", None),
        P("groups", "tensor", None),
        P("groups"),
        P("groups"),
    )
    return jax.shard_map(
        shards,
        mesh=mesh,
        in_specs=placed,
        out_specs=P(("groups", "tensor"), None, None),
        check_vma=False,
    )
```

```python
import functools

import jax
import jax.numpy as jnp
from jax import lax
from jax.experimental import pallas as pl
from jax.experimental.pallas import tpu as pltpu
from jax.sharding import PartitionSpec as P

HIDDEN_BITS = 4
FOLD = 128


def swapped(block, axis, apart):
    count = lax.axis_size(axis)
    return lax.ppermute(block, axis, [(i, i ^ (1 << apart)) for i in range(count)])


def by_target(expand, count):
    kinds, depth, width = expand.shape
    return expand.reshape(kinds, depth, count, width // count).transpose(2, 0, 1, 3)


def owner_of(ends, ids):
    return jnp.sum((ends[None, :] <= ids[:, None]).astype(jnp.int32), axis=1)


def keep_mask(rank_blocks, row_counts, columns, rows):
    adapters = rank_blocks.shape[0]
    earlier = jnp.arange(adapters)[:, None] >= jnp.arange(adapters)[None, :]
    block_end = jnp.sum(jnp.where(earlier, rank_blocks[None, :], 0), axis=1)
    row_end = jnp.sum(jnp.where(earlier, row_counts[None, :], 0), axis=1)
    column_owner = owner_of(block_end, jnp.arange(columns, dtype=jnp.int32) // 16)
    row_owner = owner_of(row_end, jnp.arange(rows, dtype=jnp.int32))
    ids = jnp.arange(adapters, dtype=jnp.int32)
    row_blocks = jnp.sum(
        jnp.where(row_owner[:, None] == ids[None, :], rank_blocks[None, :], 0), axis=1
    )
    same = (row_owner[:, None] == column_owner[None, :]).astype(jnp.float32)
    return same, 1.0 / row_blocks.astype(jnp.float32)


def general_shards(tokens, w_gate, w_up, w_down, shrink_factors, expand_factors, rank_blocks, row_counts):
    count = lax.axis_size("tensor")
    low_bits = count.bit_length() - 1 - HIDDEN_BITS
    fgroups = 1 << low_bits
    place = lax.axis_index("tensor")
    feature_group = place % fgroups
    hidden_group = place // fgroups
    block_rows = tokens.shape[1]
    rows = block_rows << HIDDEN_BITS
    units = w_gate.shape[2]
    strip = units // fgroups

    expand = lax.all_to_all(
        by_target(expand_factors, count), "tensor", split_axis=0, concat_axis=0, tiled=True
    )

    gathered = tokens[0]
    for bit in reversed(range(HIDDEN_BITS)):
        other = swapped(gathered, "tensor", low_bits + bit)
        gathered = jnp.concatenate([gathered, other], 0)
    spots = jnp.arange(1 << HIDDEN_BITS, dtype=jnp.int32)
    moved = sum(((spots >> i) & 1) << (HIDDEN_BITS - 1 - i) for i in range(HIDDEN_BITS))
    natural = (
        (moved ^ hidden_group)[:, None] * block_rows + jnp.arange(block_rows, dtype=jnp.int32)[None, :]
    ).reshape(rows)
    to_own = (natural[:, None] == jnp.arange(rows, dtype=jnp.int32)[None, :]).astype(jnp.bfloat16)

    columns = shrink_factors.shape[2]
    same, scale = keep_mask(rank_blocks, row_counts, columns, rows)
    slab = shrink_factors.shape[1]
    features = lax.dynamic_slice_in_dim(gathered, hidden_group * slab, slab, 1)
    features = jnp.dot(to_own.T, features, preferred_element_type=jnp.float32).astype(jnp.bfloat16)
    partial_value = jnp.einsum(
        "rd,kdc->krc", features, shrink_factors, preferred_element_type=jnp.float32
    )
    folded = jnp.sum((partial_value * same).reshape(2, rows, columns // FOLD, FOLD), axis=2)
    for bit in range(low_bits + HIDDEN_BITS):
        folded = folded + swapped(folded, "tensor", bit)
    shrunk = jnp.tile(folded, (1, 1, columns // FOLD)) * (same * scale[:, None])[None]
    shrunk = shrunk.astype(jnp.bfloat16)
    shrunk = jnp.einsum("or,krc->koc", to_own, shrunk, preferred_element_type=jnp.float32)
    shrunk = shrunk.astype(jnp.bfloat16)

    gate_part = jnp.dot(gathered, w_gate[0], preferred_element_type=jnp.float32)
    up_part = jnp.dot(gathered, w_up[0], preferred_element_type=jnp.float32)
    partials = jnp.stack([gate_part, up_part])
    for step in range(low_bits):
        bit = low_bits - 1 - step
        half = partials.shape[2] // 2
        high = feature_group // (1 << bit) % 2
        outgoing = lax.dynamic_slice_in_dim(partials, (1 - high) * half, half, 2)
        staying = lax.dynamic_slice_in_dim(partials, high * half, half, 2)
        partials = staying + swapped(outgoing, "tensor", bit)
    depth = expand.shape[2]
    low_rank = jnp.einsum(
        "krsd,skdc->krc",
        shrunk.reshape(2, rows, count, depth),
        expand,
        preferred_element_type=jnp.float32,
    )
    partials = partials + low_rank
    hidden = (jax.nn.silu(partials[0]) * partials[1]).astype(jnp.bfloat16)
    for step in range(low_bits):
        other = swapped(hidden, "tensor", step)
        high = feature_group // (1 << step) % 2 == 1
        hidden = jnp.where(
            high, jnp.concatenate([other, hidden], 1), jnp.concatenate([hidden, other], 1)
        )
    terms = jnp.dot(hidden, w_down[0], preferred_element_type=jnp.float32)
    for bit in range(HIDDEN_BITS):
        half = terms.shape[0] // 2
        outgoing = terms[half:].astype(jnp.bfloat16)
        terms = terms[:half] + swapped(outgoing, "tensor", low_bits + bit).astype(jnp.float32)
    return terms.astype(jnp.bfloat16)[None]


def owners(rank_blocks, row_counts, columns, rows):
    adapters = rank_blocks.shape[0]
    ids = jnp.arange(adapters, dtype=jnp.int32)
    earlier = ids[:, None] >= ids[None, :]
    block_end = jnp.sum(jnp.where(earlier, rank_blocks[None, :], 0), axis=1)
    row_end = jnp.sum(jnp.where(earlier, row_counts[None, :], 0), axis=1)
    column_owner = owner_of(block_end, jnp.arange(columns, dtype=jnp.int32) // 16)
    row_owner = owner_of(row_end, jnp.arange(rows, dtype=jnp.int32))
    row_blocks = jnp.sum(
        jnp.where(row_owner[:, None] == ids[None, :], rank_blocks[None, :], 0), axis=1
    )
    scale = 1.0 / row_blocks.astype(jnp.float32)
    return column_owner[None, :], row_owner[:, None], scale[:, None]


VMEM = pl.BlockSpec(memory_space=pltpu.VMEM)
SMEM = pl.BlockSpec(memory_space=pltpu.SMEM)
XY = (1, 2, 3)
ZZ = (4, 8, 12)


def to_chips(block, apart):
    count = lax.axis_size("tensor")
    return lax.ppermute(block, "tensor", [(i, i ^ (apart << 1)) for i in range(count)])


def cost(flops, read):
    return pl.CostEstimate(flops=flops, bytes_accessed=read, transcendentals=0)


def blocks_kernel(count, strip, source, target):
    for j in range(count):
        target[j] = source[:, :, j * strip : (j + 1) * strip]


def blocks_of(expand, count):
    kinds, depth, width = expand.shape
    strip = width // count
    return pl.pallas_call(
        functools.partial(blocks_kernel, count, strip),
        out_shape=jax.ShapeDtypeStruct((count, kinds, depth, strip), expand.dtype),
        in_specs=[VMEM],
        out_specs=VMEM,
        cost_estimate=cost(0, 4 * expand.size),
        compiler_params=pltpu.CompilerParams(vmem_limit_bytes=16 << 20),
    )(expand)


def shrink_kernel(features, factors, row_owner, column_owner, folded):
    same = row_owner[...] == column_owner[...]
    for k in range(2):
        value = jnp.dot(features[...], factors[k], preferred_element_type=jnp.float32)
        value = jnp.where(same, value, 0.0)
        total = value[:, :FOLD]
        for start in range(FOLD, value.shape[1], FOLD):
            total = total + value[:, start : start + FOLD]
        folded[k] = total


def shrink_sums(features, factors, row_owner, column_owner):
    rows = features.shape[0]
    return pl.pallas_call(
        shrink_kernel,
        out_shape=jax.ShapeDtypeStruct((2, rows, FOLD), jnp.float32),
        in_specs=[VMEM] * 4,
        out_specs=VMEM,
        cost_estimate=cost(2 * rows * factors.size, 2 * factors.size),
        compiler_params=pltpu.CompilerParams(vmem_limit_bytes=16 << 20),
    )(features, factors, row_owner, column_owner)


def hidden_kernel(
    place, mine, other, row_owner, column_owner, scale, natural, expand, gate, gate_in, up, up_in, hidden
):
    rows, columns = row_owner.shape[0], column_owner.shape[1]
    keep = jnp.where(row_owner[...] == column_owner[...], scale[...], 0.0)
    first = place[0] == 0
    folded = (
        jnp.where(first, mine[...], other[...]),
        jnp.where(first, other[...], mine[...]),
    )
    order = (natural[...] == lax.broadcasted_iota(jnp.int32, (rows, rows), 1)).astype(jnp.bfloat16)
    sums = []
    for k in range(2):
        shrunk = jnp.concatenate([folded[k]] * (columns // FOLD), axis=1) * keep
        shrunk = jnp.dot(
            order, shrunk.astype(jnp.bfloat16), preferred_element_type=jnp.float32
        ).astype(jnp.bfloat16)
        factors = expand[:, k].reshape(columns, expand.shape[3])
        sums.append(jnp.dot(shrunk, factors, preferred_element_type=jnp.float32))
    gate_sum = gate[...] + gate_in[...] + sums[0]
    up_sum = up[...] + up_in[...] + sums[1]
    hidden[...] = (gate_sum / (1.0 + jnp.exp(-gate_sum)) * up_sum).astype(hidden.dtype)


def hidden_strip(*operands):
    expand, gate = operands[7], operands[8]
    return pl.pallas_call(
        hidden_kernel,
        out_shape=jax.ShapeDtypeStruct(gate.shape, jnp.bfloat16),
        in_specs=[SMEM] + [VMEM] * 11,
        out_specs=VMEM,
        cost_estimate=cost(2 * gate.shape[0] * expand.size, 2 * expand.size),
        compiler_params=pltpu.CompilerParams(vmem_limit_bytes=32 << 20),
    )(*operands)


def down_kernel(transposed, place, mine, other, weights, own, *rest):
    sends, hidden = rest[:-1], rest[-1]
    strip = mine.shape[1]

    @pl.when(pl.program_id(0) == 0)
    def _():
        first = place[0] == 0
        left = jnp.where(first, mine[...], other[...])
        right = jnp.where(first, other[...], mine[...])
        if transposed:
            rows = mine.shape[0]
            block = rows // 16
            to = lax.broadcasted_iota(jnp.int32, (rows, rows), 0)
            source = lax.broadcasted_iota(jnp.int32, (rows, rows), 1)
            to_block, source_block = to // block, source // block
            order = (
                (to_block // 4 == source_block % 4)
                & (to_block % 4 == source_block // 4)
                & (to - to_block * block == source - source_block * block)
            ).astype(jnp.bfloat16)
            left = jnp.dot(order, left, preferred_element_type=jnp.float32).astype(jnp.bfloat16)
            right = jnp.dot(order, right, preferred_element_type=jnp.float32).astype(jnp.bfloat16)
        hidden[:, :strip] = left
        hidden[:, strip:] = right

    terms = jnp.dot(hidden[...], weights[0], preferred_element_type=jnp.float32)
    quarter = terms.shape[0] // 4
    own[...] = terms[:quarter]
    for i, send in enumerate(sends):
        send[...] = terms[(i + 1) * quarter : (i + 2) * quarter].astype(jnp.bfloat16)


def down(place, mine, other, weights, start, width, tile, transposed):
    rows, strip = mine.shape
    units = weights.shape[1]
    quarter = rows // 4
    out = pl.BlockSpec((quarter, tile), lambda i: (0, i))
    return pl.pallas_call(
        functools.partial(down_kernel, transposed),
        grid=(width // tile,),
        out_shape=[jax.ShapeDtypeStruct((quarter, width), jnp.float32)]
        + [jax.ShapeDtypeStruct((quarter, width), jnp.bfloat16)] * 3,
        in_specs=[
            SMEM,
            pl.BlockSpec((rows, strip), lambda i: (0, 0)),
            pl.BlockSpec((rows, strip), lambda i: (0, 0)),
            pl.BlockSpec((1, units, tile), lambda i: (0, 0, start // tile + i)),
        ],
        out_specs=[out] * 4,
        scratch_shapes=[pltpu.VMEM((rows, 2 * strip), jnp.bfloat16)],
        cost_estimate=cost(2 * rows * units * width, 2 * units * width),
        compiler_params=pltpu.CompilerParams(vmem_limit_bytes=32 << 20),
    )(place, mine, other, weights)


def shards(tokens, w_gate, w_up, w_down, shrink_factors, expand_factors, rank_blocks, row_counts):
    count = lax.axis_size("tensor")
    units = w_gate.shape[2]
    if count != 32 or units % 256:
        return general_shards(
            tokens, w_gate, w_up, w_down, shrink_factors, expand_factors, rank_blocks, row_counts
        )
    place = lax.axis_index("tensor")
    core, chip = place % 2, place // 2
    core_ref = core.reshape(1)
    block_rows, width = tokens.shape[1], tokens.shape[2]
    rows = 16 * block_rows
    strip = units // 2
    slab = width // 16
    columns = shrink_factors.shape[2]

    slabs = tokens[0].reshape(block_rows, 16, slab).transpose(1, 0, 2)
    same_core = [[2 * i + a for i in range(16)] for a in range(2)]
    slabs = lax.all_to_all(
        slabs, "tensor", split_axis=0, concat_axis=0, axis_index_groups=same_core, tiled=True
    )
    column_owner, row_owner, scale = owners(rank_blocks, row_counts, columns, rows)
    folded = shrink_sums(slabs.reshape(rows, slab), shrink_factors, row_owner, column_owner)
    outgoing = lax.dynamic_index_in_dim(folded, 1 - core, 0, False)
    staying = lax.dynamic_index_in_dim(folded, core, 0, False)
    folded = staying + swapped(outgoing, "tensor", 0)
    for hop in (XY, ZZ):
        received = [to_chips(folded, apart) for apart in hop]
        folded = (folded + received[0]) + (received[1] + received[2])

    gathered = tokens[0]
    for hop in (ZZ, XY):
        gathered = jnp.concatenate([gathered] + [to_chips(gathered, apart) for apart in hop], 0)
    spots = jnp.arange(16, dtype=jnp.int32)
    far = spots // 4 + spots % 4 * 4
    natural = (
        (far ^ chip)[:, None] * block_rows + jnp.arange(block_rows, dtype=jnp.int32)[None, :]
    ).reshape(rows, 1)

    blocks, folded = lax.optimization_barrier((blocks_of(expand_factors, count), folded))
    expand = lax.all_to_all(blocks, "tensor", split_axis=0, concat_axis=0, tiled=True)

    gate = jnp.dot(gathered, w_gate[0], preferred_element_type=jnp.float32)
    up = jnp.dot(gathered, w_up[0], preferred_element_type=jnp.float32)
    here, there = core * strip, (1 - core) * strip
    gate_in = swapped(lax.dynamic_slice_in_dim(gate, there, strip, 1), "tensor", 0)
    up_in = swapped(lax.dynamic_slice_in_dim(up, there, strip, 1), "tensor", 0)
    hidden = hidden_strip(
        core_ref,
        folded,
        swapped(folded, "tensor", 0),
        row_owner,
        column_owner,
        scale,
        natural,
        expand,
        lax.dynamic_slice_in_dim(gate, here, strip, 1),
        gate_in,
        lax.dynamic_slice_in_dim(up, here, strip, 1),
        up_in,
    )
    other = swapped(hidden, "tensor", 0)
    split = width // 3 // 256 * 256
    results = []
    for start, size, transposed in ((0, split, True), (split, width - split, False)):
        terms, *sends = down(core_ref, hidden, other, w_down, start, size, 256, transposed)
        hops = (ZZ, XY) if transposed else (XY, ZZ)
        received = [to_chips(send, apart) for send, apart in zip(sends, hops[0])]
        terms = (terms + received[0]) + (received[1].astype(jnp.float32) + received[2])
        sends = [terms[(i + 1) * block_rows : (i + 2) * block_rows].astype(jnp.bfloat16) for i in range(3)]
        received = [to_chips(send, apart) for send, apart in zip(sends, hops[1])]
        terms = terms[:block_rows]
        terms = (terms + received[0]) + (received[1].astype(jnp.float32) + received[2])
        results.append(terms.astype(jnp.bfloat16))
    return jnp.concatenate(results, 1)[None]


def solution(mesh):
    placed = (
        P(("groups", "tensor"), None, None),
        P("tensor", None, None),
        P("tensor", None, None),
        P("tensor", None, None),
        P("groups", "tensor", None),
        P("groups", "tensor", None),
        P("groups"),
        P("groups"),
    )
    return jax.shard_map(
        shards,
        mesh=mesh,
        in_specs=placed,
        out_specs=P(("groups", "tensor"), None, None),
        check_vma=False,
    )
```

```python
import functools

import jax
import jax.numpy as jnp
from jax import lax
from jax.experimental import pallas as pl
from jax.experimental.pallas import tpu as pltpu
from jax.sharding import PartitionSpec as P

HIDDEN_BITS = 4
FOLD = 128


def swapped(block, axis, apart):
    count = lax.axis_size(axis)
    return lax.ppermute(block, axis, [(i, i ^ (1 << apart)) for i in range(count)])


def by_target(expand, count):
    kinds, depth, width = expand.shape
    return expand.reshape(kinds, depth, count, width // count).transpose(2, 0, 1, 3)


def owner_of(ends, ids):
    return jnp.sum((ends[None, :] <= ids[:, None]).astype(jnp.int32), axis=1)


def keep_mask(rank_blocks, row_counts, columns, rows):
    adapters = rank_blocks.shape[0]
    earlier = jnp.arange(adapters)[:, None] >= jnp.arange(adapters)[None, :]
    block_end = jnp.sum(jnp.where(earlier, rank_blocks[None, :], 0), axis=1)
    row_end = jnp.sum(jnp.where(earlier, row_counts[None, :], 0), axis=1)
    column_owner = owner_of(block_end, jnp.arange(columns, dtype=jnp.int32) // 16)
    row_owner = owner_of(row_end, jnp.arange(rows, dtype=jnp.int32))
    ids = jnp.arange(adapters, dtype=jnp.int32)
    row_blocks = jnp.sum(
        jnp.where(row_owner[:, None] == ids[None, :], rank_blocks[None, :], 0), axis=1
    )
    same = (row_owner[:, None] == column_owner[None, :]).astype(jnp.float32)
    return same, 1.0 / row_blocks.astype(jnp.float32)


def general_shards(tokens, w_gate, w_up, w_down, shrink_factors, expand_factors, rank_blocks, row_counts):
    count = lax.axis_size("tensor")
    low_bits = count.bit_length() - 1 - HIDDEN_BITS
    fgroups = 1 << low_bits
    place = lax.axis_index("tensor")
    feature_group = place % fgroups
    hidden_group = place // fgroups
    block_rows = tokens.shape[1]
    rows = block_rows << HIDDEN_BITS
    units = w_gate.shape[2]
    strip = units // fgroups

    expand = lax.all_to_all(
        by_target(expand_factors, count), "tensor", split_axis=0, concat_axis=0, tiled=True
    )

    gathered = tokens[0]
    for bit in reversed(range(HIDDEN_BITS)):
        other = swapped(gathered, "tensor", low_bits + bit)
        gathered = jnp.concatenate([gathered, other], 0)
    spots = jnp.arange(1 << HIDDEN_BITS, dtype=jnp.int32)
    moved = sum(((spots >> i) & 1) << (HIDDEN_BITS - 1 - i) for i in range(HIDDEN_BITS))
    natural = (
        (moved ^ hidden_group)[:, None] * block_rows + jnp.arange(block_rows, dtype=jnp.int32)[None, :]
    ).reshape(rows)
    to_own = (natural[:, None] == jnp.arange(rows, dtype=jnp.int32)[None, :]).astype(jnp.bfloat16)

    columns = shrink_factors.shape[2]
    same, scale = keep_mask(rank_blocks, row_counts, columns, rows)
    slab = shrink_factors.shape[1]
    features = lax.dynamic_slice_in_dim(gathered, hidden_group * slab, slab, 1)
    features = jnp.dot(to_own.T, features, preferred_element_type=jnp.float32).astype(jnp.bfloat16)
    partial_value = jnp.einsum(
        "rd,kdc->krc", features, shrink_factors, preferred_element_type=jnp.float32
    )
    folded = jnp.sum((partial_value * same).reshape(2, rows, columns // FOLD, FOLD), axis=2)
    for bit in range(low_bits + HIDDEN_BITS):
        folded = folded + swapped(folded, "tensor", bit)
    shrunk = jnp.tile(folded, (1, 1, columns // FOLD)) * (same * scale[:, None])[None]
    shrunk = shrunk.astype(jnp.bfloat16)
    shrunk = jnp.einsum("or,krc->koc", to_own, shrunk, preferred_element_type=jnp.float32)
    shrunk = shrunk.astype(jnp.bfloat16)

    gate_part = jnp.dot(gathered, w_gate[0], preferred_element_type=jnp.float32)
    up_part = jnp.dot(gathered, w_up[0], preferred_element_type=jnp.float32)
    partials = jnp.stack([gate_part, up_part])
    for step in range(low_bits):
        bit = low_bits - 1 - step
        half = partials.shape[2] // 2
        high = feature_group // (1 << bit) % 2
        outgoing = lax.dynamic_slice_in_dim(partials, (1 - high) * half, half, 2)
        staying = lax.dynamic_slice_in_dim(partials, high * half, half, 2)
        partials = staying + swapped(outgoing, "tensor", bit)
    depth = expand.shape[2]
    low_rank = jnp.einsum(
        "krsd,skdc->krc",
        shrunk.reshape(2, rows, count, depth),
        expand,
        preferred_element_type=jnp.float32,
    )
    partials = partials + low_rank
    hidden = (jax.nn.silu(partials[0]) * partials[1]).astype(jnp.bfloat16)
    for step in range(low_bits):
        other = swapped(hidden, "tensor", step)
        high = feature_group // (1 << step) % 2 == 1
        hidden = jnp.where(
            high, jnp.concatenate([other, hidden], 1), jnp.concatenate([hidden, other], 1)
        )
    terms = jnp.dot(hidden, w_down[0], preferred_element_type=jnp.float32)
    for bit in range(HIDDEN_BITS):
        half = terms.shape[0] // 2
        outgoing = terms[half:].astype(jnp.bfloat16)
        terms = terms[:half] + swapped(outgoing, "tensor", low_bits + bit).astype(jnp.float32)
    return terms.astype(jnp.bfloat16)[None]


def owners(rank_blocks, row_counts, columns, rows):
    adapters = rank_blocks.shape[0]
    ids = jnp.arange(adapters, dtype=jnp.int32)
    earlier = ids[:, None] >= ids[None, :]
    block_end = jnp.sum(jnp.where(earlier, rank_blocks[None, :], 0), axis=1)
    row_end = jnp.sum(jnp.where(earlier, row_counts[None, :], 0), axis=1)
    column_owner = owner_of(block_end, jnp.arange(columns, dtype=jnp.int32) // 16)
    natural = jnp.arange(rows, dtype=jnp.int32).reshape(4, 4, rows // 16).transpose(1, 0, 2).reshape(rows)
    row_owner = owner_of(row_end, natural)
    row_blocks = jnp.sum(
        jnp.where(row_owner[:, None] == ids[None, :], rank_blocks[None, :], 0), axis=1
    )
    scale = 1.0 / row_blocks.astype(jnp.float32)
    return column_owner[None, :], row_owner[:, None], scale[:, None]


VMEM = pl.BlockSpec(memory_space=pltpu.VMEM)
SMEM = pl.BlockSpec(memory_space=pltpu.SMEM)
PLANE = [[8 * z + 2 * xy + core for xy in range(4)] for z in range(4) for core in range(2)]
LINE = [[8 * z + 2 * xy + core for z in range(4)] for xy in range(4) for core in range(2)]


def spread(blocks, groups=None):
    return lax.all_to_all(
        blocks, "tensor", split_axis=0, concat_axis=0, axis_index_groups=groups, tiled=True
    )


def to_all(block, groups=None):
    peers = len(groups[0]) if groups else lax.axis_size("tensor")
    return spread(jnp.broadcast_to(block[None], (peers, *block.shape)), groups)


def block_order(rows, to, source):
    block = rows // 16
    to_block, source_block = to // block, source // block
    return (
        (to_block // 4 == source_block % 4)
        & (to_block % 4 == source_block // 4)
        & (to - to_block * block == source - source_block * block)
    )


def cost(flops, read):
    return pl.CostEstimate(flops=flops, bytes_accessed=read, transcendentals=0)


def blocks_kernel(count, strip, source, *rest):
    target = rest[-1]
    for j in range(count):
        target[j] = source[:, :, j * strip : (j + 1) * strip]


def blocks_of(expand, count, *after):
    kinds, depth, width = expand.shape
    strip = width // count
    return pl.pallas_call(
        functools.partial(blocks_kernel, count, strip),
        out_shape=jax.ShapeDtypeStruct((count, kinds, depth, strip), expand.dtype),
        in_specs=[VMEM] + [pl.BlockSpec(memory_space=pl.ANY)] * len(after),
        out_specs=VMEM,
        cost_estimate=cost(0, 4 * expand.size),
        compiler_params=pltpu.CompilerParams(vmem_limit_bytes=16 << 20),
    )(expand, *after)


def shrink_kernel(features, factors, row_owner, column_owner, folded):
    same = row_owner[...] == column_owner[...]
    rows = features.shape[0]
    ids = [lax.broadcasted_iota(jnp.int32, (rows, rows), axis) for axis in range(2)]
    order = block_order(rows, *ids).astype(jnp.bfloat16)
    ordered = jnp.dot(order, features[...], preferred_element_type=jnp.float32).astype(jnp.bfloat16)
    for k in range(2):
        value = jnp.dot(ordered, factors[k], preferred_element_type=jnp.float32)
        value = jnp.where(same, value, 0.0)
        total = value[:, :FOLD]
        for start in range(FOLD, value.shape[1], FOLD):
            total = total + value[:, start : start + FOLD]
        folded[k] = total


def shrink_sums(features, factors, row_owner, column_owner):
    rows = features.shape[0]
    return pl.pallas_call(
        shrink_kernel,
        out_shape=jax.ShapeDtypeStruct((2, rows, FOLD), jnp.float32),
        in_specs=[VMEM] * 4,
        out_specs=VMEM,
        cost_estimate=cost(2 * rows * factors.size, 2 * factors.size),
        compiler_params=pltpu.CompilerParams(vmem_limit_bytes=16 << 20),
    )(features, factors, row_owner, column_owner)


def hidden_kernel(folded, row_owner, column_owner, scale, expand, gate, gate_in, up, up_in, hidden):
    columns = column_owner.shape[1]
    keep = jnp.where(row_owner[...] == column_owner[...], scale[...], 0.0)
    sums = []
    for k in range(2):
        shrunk = jnp.concatenate([folded[k]] * (columns // FOLD), axis=1) * keep
        factors = expand[:, k].reshape(columns, expand.shape[3])
        sums.append(
            jnp.dot(shrunk.astype(jnp.bfloat16), factors, preferred_element_type=jnp.float32)
        )
    gate_sum = gate[...] + gate_in[...] + sums[0]
    up_sum = up[...] + up_in[...] + sums[1]
    hidden[...] = (gate_sum / (1.0 + jnp.exp(-gate_sum)) * up_sum).astype(hidden.dtype)


def hidden_strip(*operands):
    expand, gate = operands[4], operands[5]
    return pl.pallas_call(
        hidden_kernel,
        out_shape=jax.ShapeDtypeStruct(gate.shape, jnp.bfloat16),
        in_specs=[VMEM] * 9,
        out_specs=VMEM,
        cost_estimate=cost(2 * gate.shape[0] * expand.size, 2 * expand.size),
        compiler_params=pltpu.CompilerParams(vmem_limit_bytes=32 << 20),
    )(*operands)


def down_kernel(tile, place, mine, other, weights, *parts):
    rows = mine.shape[0]
    first = place[0] == 0
    hidden = jnp.concatenate(
        [jnp.where(first, mine[...], other[...]), jnp.where(first, other[...], mine[...])], axis=1
    )
    ids = [lax.broadcasted_iota(jnp.int32, (rows, rows), axis) for axis in range(2)]
    order = block_order(rows, *ids).astype(jnp.bfloat16)
    ordered = jnp.dot(order, hidden, preferred_element_type=jnp.float32).astype(jnp.bfloat16)
    start = 0
    for part, value in zip(parts, (ordered, hidden)):
        for at in range(0, part.shape[2], tile):
            terms = jnp.dot(
                value, weights[0, :, start + at : start + at + tile], preferred_element_type=jnp.float32
            )
            part[:, :, at : at + tile] = terms.reshape(4, rows // 4, tile).astype(jnp.bfloat16)
        start += part.shape[2]


def down(place, mine, other, weights, widths, tile):
    rows = mine.shape[0]
    return pl.pallas_call(
        functools.partial(down_kernel, tile),
        out_shape=[jax.ShapeDtypeStruct((4, rows // 4, width), jnp.bfloat16) for width in widths],
        in_specs=[SMEM, VMEM, VMEM, VMEM],
        out_specs=[VMEM] * 2,
        cost_estimate=cost(2 * rows * weights.size, 2 * weights.size),
        compiler_params=pltpu.CompilerParams(vmem_limit_bytes=24 << 20),
    )(place, mine, other, pltpu.with_memory_space_constraint(weights, pltpu.VMEM))


def shards(tokens, w_gate, w_up, w_down, shrink_factors, expand_factors, rank_blocks, row_counts):
    count = lax.axis_size("tensor")
    units = w_gate.shape[2]
    if count != 32 or units % 256:
        return general_shards(
            tokens, w_gate, w_up, w_down, shrink_factors, expand_factors, rank_blocks, row_counts
        )
    core = lax.axis_index("tensor") % 2
    core_ref = core.reshape(1)
    block_rows, width = tokens.shape[1], tokens.shape[2]
    rows = 16 * block_rows
    strip = units // 2
    slab = width // 16
    columns = shrink_factors.shape[2]

    gathered = to_all(tokens[0], LINE).reshape(4 * block_rows, width)
    gathered = to_all(gathered, PLANE).reshape(rows, width)

    slabs = tokens[0].reshape(block_rows, 16, slab).transpose(1, 0, 2)
    slabs = spread(slabs, [[2 * i + a for i in range(16)] for a in range(2)])
    column_owner, row_owner, scale = owners(rank_blocks, row_counts, columns, rows)
    folded = shrink_sums(slabs.reshape(rows, slab), shrink_factors, row_owner, column_owner)
    share = 2 * rows // count
    folded = spread(folded.reshape(count, share, FOLD))
    folded = jnp.sum(folded, axis=0)
    blocks = blocks_of(expand_factors, count, gathered, folded)
    folded = to_all(folded).reshape(2, rows, FOLD)

    expand = spread(blocks)

    gate = jnp.dot(gathered, w_gate[0], preferred_element_type=jnp.float32)
    up = jnp.dot(gathered, w_up[0], preferred_element_type=jnp.float32)
    here, there = core * strip, (1 - core) * strip
    gate_in = swapped(lax.dynamic_slice_in_dim(gate, there, strip, 1), "tensor", 0)
    up_in = swapped(lax.dynamic_slice_in_dim(up, there, strip, 1), "tensor", 0)
    hidden = hidden_strip(
        folded,
        row_owner,
        column_owner,
        scale,
        expand,
        lax.dynamic_slice_in_dim(gate, here, strip, 1),
        gate_in,
        lax.dynamic_slice_in_dim(up, here, strip, 1),
        up_in,
    )
    other = swapped(hidden, "tensor", 0)
    split = width // 3 // 256 * 256
    results = []
    parts = down(core_ref, hidden, other, w_down, (split, width - split), 256)
    for terms, hops in zip(parts, ((LINE, PLANE), (PLANE, LINE))):
        terms = jnp.sum(spread(terms, hops[0]).astype(jnp.float32), axis=0).astype(jnp.bfloat16)
        terms = terms.reshape(4, block_rows, terms.shape[1])
        results.append(jnp.sum(spread(terms, hops[1]).astype(jnp.float32), axis=0).astype(jnp.bfloat16))
    return jnp.concatenate(results, 1)[None]


def solution(mesh):
    placed = (
        P(("groups", "tensor"), None, None),
        P("tensor", None, None),
        P("tensor", None, None),
        P("tensor", None, None),
        P("groups", "tensor", None),
        P("groups", "tensor", None),
        P("groups"),
        P("groups"),
    )
    return jax.shard_map(
        shards,
        mesh=mesh,
        in_specs=placed,
        out_specs=P(("groups", "tensor"), None, None),
        check_vma=False,
    )
```

```python
import functools

import jax
import jax.numpy as jnp
from jax import lax
from jax.experimental import pallas as pl
from jax.experimental.pallas import tpu as pltpu
from jax.sharding import PartitionSpec as P

HIDDEN_BITS = 4
FOLD = 128


def swapped(block, axis, apart):
    count = lax.axis_size(axis)
    return lax.ppermute(block, axis, [(i, i ^ (1 << apart)) for i in range(count)])


def by_target(expand, count):
    kinds, depth, width = expand.shape
    return expand.reshape(kinds, depth, count, width // count).transpose(2, 0, 1, 3)


def owner_of(ends, ids):
    return jnp.sum((ends[None, :] <= ids[:, None]).astype(jnp.int32), axis=1)


def keep_mask(rank_blocks, row_counts, columns, rows):
    adapters = rank_blocks.shape[0]
    earlier = jnp.arange(adapters)[:, None] >= jnp.arange(adapters)[None, :]
    block_end = jnp.sum(jnp.where(earlier, rank_blocks[None, :], 0), axis=1)
    row_end = jnp.sum(jnp.where(earlier, row_counts[None, :], 0), axis=1)
    column_owner = owner_of(block_end, jnp.arange(columns, dtype=jnp.int32) // 16)
    row_owner = owner_of(row_end, jnp.arange(rows, dtype=jnp.int32))
    ids = jnp.arange(adapters, dtype=jnp.int32)
    row_blocks = jnp.sum(
        jnp.where(row_owner[:, None] == ids[None, :], rank_blocks[None, :], 0), axis=1
    )
    same = (row_owner[:, None] == column_owner[None, :]).astype(jnp.float32)
    return same, 1.0 / row_blocks.astype(jnp.float32)


def general_shards(tokens, w_gate, w_up, w_down, shrink_factors, expand_factors, rank_blocks, row_counts):
    count = lax.axis_size("tensor")
    low_bits = count.bit_length() - 1 - HIDDEN_BITS
    fgroups = 1 << low_bits
    place = lax.axis_index("tensor")
    feature_group = place % fgroups
    hidden_group = place // fgroups
    block_rows = tokens.shape[1]
    rows = block_rows << HIDDEN_BITS
    units = w_gate.shape[2]
    strip = units // fgroups

    expand = lax.all_to_all(
        by_target(expand_factors, count), "tensor", split_axis=0, concat_axis=0, tiled=True
    )

    gathered = tokens[0]
    for bit in reversed(range(HIDDEN_BITS)):
        other = swapped(gathered, "tensor", low_bits + bit)
        gathered = jnp.concatenate([gathered, other], 0)
    spots = jnp.arange(1 << HIDDEN_BITS, dtype=jnp.int32)
    moved = sum(((spots >> i) & 1) << (HIDDEN_BITS - 1 - i) for i in range(HIDDEN_BITS))
    natural = (
        (moved ^ hidden_group)[:, None] * block_rows + jnp.arange(block_rows, dtype=jnp.int32)[None, :]
    ).reshape(rows)
    to_own = (natural[:, None] == jnp.arange(rows, dtype=jnp.int32)[None, :]).astype(jnp.bfloat16)

    columns = shrink_factors.shape[2]
    same, scale = keep_mask(rank_blocks, row_counts, columns, rows)
    slab = shrink_factors.shape[1]
    features = lax.dynamic_slice_in_dim(gathered, hidden_group * slab, slab, 1)
    features = jnp.dot(to_own.T, features, preferred_element_type=jnp.float32).astype(jnp.bfloat16)
    partial_value = jnp.einsum(
        "rd,kdc->krc", features, shrink_factors, preferred_element_type=jnp.float32
    )
    folded = jnp.sum((partial_value * same).reshape(2, rows, columns // FOLD, FOLD), axis=2)
    for bit in range(low_bits + HIDDEN_BITS):
        folded = folded + swapped(folded, "tensor", bit)
    shrunk = jnp.tile(folded, (1, 1, columns // FOLD)) * (same * scale[:, None])[None]
    shrunk = shrunk.astype(jnp.bfloat16)
    shrunk = jnp.einsum("or,krc->koc", to_own, shrunk, preferred_element_type=jnp.float32)
    shrunk = shrunk.astype(jnp.bfloat16)

    gate_part = jnp.dot(gathered, w_gate[0], preferred_element_type=jnp.float32)
    up_part = jnp.dot(gathered, w_up[0], preferred_element_type=jnp.float32)
    partials = jnp.stack([gate_part, up_part])
    for step in range(low_bits):
        bit = low_bits - 1 - step
        half = partials.shape[2] // 2
        high = feature_group // (1 << bit) % 2
        outgoing = lax.dynamic_slice_in_dim(partials, (1 - high) * half, half, 2)
        staying = lax.dynamic_slice_in_dim(partials, high * half, half, 2)
        partials = staying + swapped(outgoing, "tensor", bit)
    depth = expand.shape[2]
    low_rank = jnp.einsum(
        "krsd,skdc->krc",
        shrunk.reshape(2, rows, count, depth),
        expand,
        preferred_element_type=jnp.float32,
    )
    partials = partials + low_rank
    hidden = (jax.nn.silu(partials[0]) * partials[1]).astype(jnp.bfloat16)
    for step in range(low_bits):
        other = swapped(hidden, "tensor", step)
        high = feature_group // (1 << step) % 2 == 1
        hidden = jnp.where(
            high, jnp.concatenate([other, hidden], 1), jnp.concatenate([hidden, other], 1)
        )
    terms = jnp.dot(hidden, w_down[0], preferred_element_type=jnp.float32)
    for bit in range(HIDDEN_BITS):
        half = terms.shape[0] // 2
        outgoing = terms[half:].astype(jnp.bfloat16)
        terms = terms[:half] + swapped(outgoing, "tensor", low_bits + bit).astype(jnp.float32)
    return terms.astype(jnp.bfloat16)[None]


def owners(rank_blocks, row_counts, columns, rows):
    adapters = rank_blocks.shape[0]
    ids = jnp.arange(adapters, dtype=jnp.int32)
    earlier = ids[:, None] >= ids[None, :]
    block_end = jnp.sum(jnp.where(earlier, rank_blocks[None, :], 0), axis=1)
    row_end = jnp.sum(jnp.where(earlier, row_counts[None, :], 0), axis=1)
    column_owner = owner_of(block_end, jnp.arange(columns, dtype=jnp.int32) // 16)
    row_owner = owner_of(row_end, jnp.arange(rows, dtype=jnp.int32))
    row_blocks = jnp.sum(
        jnp.where(row_owner[:, None] == ids[None, :], rank_blocks[None, :], 0), axis=1
    )
    scale = 1.0 / row_blocks.astype(jnp.float32)
    return column_owner[None, :], row_owner[:, None], scale[:, None]


VMEM = pl.BlockSpec(memory_space=pltpu.VMEM)
SMEM = pl.BlockSpec(memory_space=pltpu.SMEM)
ANY = pl.BlockSpec(memory_space=pl.ANY)
X, Y, Z1, Z2 = 1, 2, 4, 8


def to_chip(block, apart):
    count = lax.axis_size("tensor")
    return lax.ppermute(block, "tensor", [(i, i ^ (apart << 1)) for i in range(count)])


def cost(flops, read):
    return pl.CostEstimate(flops=flops, bytes_accessed=read, transcendentals=0)


def in_hbm(array):
    return pltpu.with_memory_space_constraint(array, pltpu.HBM)


def blocks_kernel(count, strip, source, *rest):
    target = rest[-1]
    for j in range(count):
        target[j] = source[:, :, j * strip : (j + 1) * strip]


def blocks_of(expand, count, *after):
    kinds, depth, width = expand.shape
    strip = width // count
    return pl.pallas_call(
        functools.partial(blocks_kernel, count, strip),
        out_shape=jax.ShapeDtypeStruct((count, kinds, depth, strip), expand.dtype),
        in_specs=[VMEM] + [ANY] * len(after),
        out_specs=VMEM,
        cost_estimate=cost(0, 4 * expand.size),
        compiler_params=pltpu.CompilerParams(vmem_limit_bytes=16 << 20),
    )(expand, *after)


def shrink_kernel(features, factors, row_owner, column_owner, folded):
    same = row_owner[...] == column_owner[...]
    for k in range(2):
        value = jnp.dot(features[...], factors[k], preferred_element_type=jnp.float32)
        value = jnp.where(same, value, 0.0)
        total = value[:, :FOLD]
        for start in range(FOLD, value.shape[1], FOLD):
            total = total + value[:, start : start + FOLD]
        folded[k] = total


def shrink_sums(features, factors, row_owner, column_owner):
    rows = features.shape[0]
    return pl.pallas_call(
        shrink_kernel,
        out_shape=jax.ShapeDtypeStruct((2, rows, FOLD), jnp.float32),
        in_specs=[VMEM] * 4,
        out_specs=VMEM,
        cost_estimate=cost(2 * rows * factors.size, 2 * factors.size),
        compiler_params=pltpu.CompilerParams(vmem_limit_bytes=16 << 20),
    )(features, factors, row_owner, column_owner)


def inner_kernel(place, near, far, gate, up, *refs):
    outs, (rows, gate_sum, up_sum) = refs[:4], refs[4:]
    step = pl.program_id(0)
    half = near.shape[0]
    rows[:half] = near[...]
    rows[half:] = far[...]
    for weights, total in ((gate, gate_sum), (up, up_sum)):
        term = jnp.dot(rows[...], weights[0], preferred_element_type=jnp.float32)

        @pl.when(step == 0)
        def _():
            total[...] = term

        @pl.when(step > 0)
        def _():
            total[...] += term

    @pl.when(step == pl.num_programs(0) - 1)
    def _():
        strip = outs[0].shape[1]
        first = place[0] % 2 == 0
        for total, here, there in ((gate_sum, *outs[:2]), (up_sum, *outs[2:])):
            left, right = total[:, :strip], total[:, strip:]
            here[...] = jnp.where(first, left, right)
            there[...] = jnp.where(first, right, left)


def inner(place, near, far, gate, up, depth):
    half, width = near.shape
    units = gate.shape[2]
    rows = pl.BlockSpec((half, depth), lambda i: (0, i))
    weights = pl.BlockSpec((1, depth, units), lambda i: (0, i, 0))
    strip = jax.ShapeDtypeStruct((2 * half, units // 2), jnp.float32)
    return pl.pallas_call(
        inner_kernel,
        grid=(width // depth,),
        out_shape=[strip] * 4,
        in_specs=[SMEM, rows, rows, weights, weights],
        out_specs=[pl.BlockSpec(strip.shape, lambda i: (0, 0))] * 4,
        scratch_shapes=[pltpu.VMEM((2 * half, depth), near.dtype)]
        + [pltpu.VMEM((2 * half, units), jnp.float32)] * 2,
        cost_estimate=cost(4 * half * (gate.size + up.size), 2 * (gate.size + up.size)),
        compiler_params=pltpu.CompilerParams(vmem_limit_bytes=32 << 20),
    )(place, near, far, in_hbm(gate), in_hbm(up))


def hidden_kernel(
    place, folded, row_owner, column_owner, scale, expand, gate, gate_in, up, up_in, hidden
):
    rows, columns = row_owner.shape[0], column_owner.shape[1]
    keep = jnp.where(row_owner[...] == column_owner[...], scale[...], 0.0)
    block = rows // 16
    to, source = [lax.broadcasted_iota(jnp.int32, (rows, rows), axis) for axis in range(2)]
    spot = to // block
    far = spot // 8 + spot // 4 % 2 * 2 + spot // 2 % 2 * 4 + spot % 2 * 8
    natural = (far ^ (place[0] // 2)) * block + (to - spot * block)
    order = (natural == source).astype(jnp.bfloat16)
    sums = []
    for k in range(2):
        shrunk = jnp.concatenate([folded[k]] * (columns // FOLD), axis=1) * keep
        shrunk = jnp.dot(
            order, shrunk.astype(jnp.bfloat16), preferred_element_type=jnp.float32
        ).astype(jnp.bfloat16)
        factors = expand[:, k].reshape(columns, expand.shape[3])
        sums.append(jnp.dot(shrunk, factors, preferred_element_type=jnp.float32))
    gate_sum = gate[...] + gate_in[...] + sums[0]
    up_sum = up[...] + up_in[...] + sums[1]
    hidden[...] = (gate_sum / (1.0 + jnp.exp(-gate_sum)) * up_sum).astype(hidden.dtype)


def hidden_strip(*operands):
    expand, gate = operands[5], operands[6]
    return pl.pallas_call(
        hidden_kernel,
        out_shape=jax.ShapeDtypeStruct(gate.shape, jnp.bfloat16),
        in_specs=[SMEM] + [VMEM] * 9,
        out_specs=VMEM,
        cost_estimate=cost(2 * gate.shape[0] * expand.size, 2 * expand.size),
        compiler_params=pltpu.CompilerParams(vmem_limit_bytes=32 << 20),
    )(*operands)


def down_kernel(x_first, place, mine, other, weights, stays, sends, hidden):
    @pl.when(pl.program_id(0) == 0)
    def _():
        strip = mine.shape[1]
        first = place[0] % 2 == 0
        hidden[:, :strip] = jnp.where(first, mine[...], other[...])
        hidden[:, strip:] = jnp.where(first, other[...], mine[...])

    terms = jnp.dot(hidden[...], weights[0], preferred_element_type=jnp.float32)
    part = terms.shape[0] // 4
    low_y, high_y = terms[:part], terms[part : 2 * part]
    far_low, far_high = terms[2 * part : 3 * part], terms[3 * part :]
    if x_first:
        stay, send = (low_y, high_y), (far_low, far_high)
    else:
        stay, send = (low_y, far_low), (high_y, far_high)
    stays[:part], stays[part:] = stay
    sends[...] = jnp.concatenate(send, axis=0).astype(sends.dtype)


def down(x_first, place, mine, other, weights, start, width, tile):
    rows, strip = mine.shape
    units = weights.shape[1]
    whole = pl.BlockSpec((rows, strip), lambda i: (0, 0))
    out = pl.BlockSpec((rows // 2, tile), lambda i: (0, i))
    return pl.pallas_call(
        functools.partial(down_kernel, x_first),
        grid=(width // tile,),
        out_shape=[
            jax.ShapeDtypeStruct((rows // 2, width), dtype) for dtype in (jnp.float32, jnp.bfloat16)
        ],
        in_specs=[
            SMEM,
            whole,
            whole,
            pl.BlockSpec((1, units, tile), lambda i: (0, 0, start // tile + i)),
        ],
        out_specs=[out] * 2,
        scratch_shapes=[pltpu.VMEM((rows, 2 * strip), jnp.bfloat16)],
        cost_estimate=cost(2 * rows * units * width, 2 * units * width),
        compiler_params=pltpu.CompilerParams(vmem_limit_bytes=32 << 20),
    )(place, mine, other, in_hbm(weights))


def halved(terms, apart):
    half = terms.shape[0] // 2
    return terms[:half] + to_chip(terms[half:].astype(jnp.bfloat16), apart)


def shards(tokens, w_gate, w_up, w_down, shrink_factors, expand_factors, rank_blocks, row_counts):
    count = lax.axis_size("tensor")
    units = w_gate.shape[2]
    if count != 32 or units % 256:
        return general_shards(
            tokens, w_gate, w_up, w_down, shrink_factors, expand_factors, rank_blocks, row_counts
        )
    place = lax.axis_index("tensor").reshape(1)
    block_rows, width = tokens.shape[1], tokens.shape[2]
    rows = 16 * block_rows
    slab = width // 16
    columns = shrink_factors.shape[2]

    slabs = tokens[0].reshape(block_rows, 16, slab).transpose(1, 0, 2)
    slabs = lax.all_to_all(
        slabs,
        "tensor",
        split_axis=0,
        concat_axis=0,
        axis_index_groups=[[2 * i + a for i in range(16)] for a in range(2)],
        tiled=True,
    )
    column_owner, row_owner, scale = owners(rank_blocks, row_counts, columns, rows)
    folded = shrink_sums(slabs.reshape(rows, slab), shrink_factors, row_owner, column_owner)
    folded = folded + to_chip(folded, Z2)
    folded = folded + to_chip(folded, Z1)

    gathered = tokens[0]
    for apart in (Z2, Z1):
        gathered = jnp.concatenate([gathered, to_chip(gathered, apart)], 0)
    blocks = blocks_of(expand_factors, count, gathered, folded)
    expand = lax.all_to_all(blocks, "tensor", split_axis=0, concat_axis=0, tiled=True)
    gathered = jnp.concatenate([gathered, to_chip(gathered, Y)], 0)
    far = to_chip(gathered, X)

    for apart in (Y, X):
        folded = folded + to_chip(folded, apart)
    folded = folded + swapped(folded, "tensor", 0)

    gate, gate_out, up, up_out = inner(place, gathered, far, w_gate, w_up, 512)
    gate_in = swapped(gate_out, "tensor", 0)
    up_in = swapped(up_out, "tensor", 0)
    hidden = hidden_strip(
        place, folded, row_owner, column_owner, scale, expand, gate, gate_in, up, up_in
    )
    other = swapped(hidden, "tensor", 0)
    split = width // 2
    sums = []
    for x_first in (True, False):
        first, second = (X, Y) if x_first else (Y, X)
        start = 0 if x_first else split
        stays, sends = down(x_first, place, hidden, other, w_down, start, split, 512)
        sums.append((stays + to_chip(sends, first), second))
    terms = jnp.concatenate([halved(*pair) for pair in sums], 1)
    for apart in (Z1, Z2):
        terms = halved(terms, apart)
    return terms.astype(jnp.bfloat16)[None]


def solution(mesh):
    placed = (
        P(("groups", "tensor"), None, None),
        P("tensor", None, None),
        P("tensor", None, None),
        P("tensor", None, None),
        P("groups", "tensor", None),
        P("groups", "tensor", None),
        P("groups"),
        P("groups"),
    )
    return jax.shard_map(
        shards,
        mesh=mesh,
        in_specs=placed,
        out_specs=P(("groups", "tensor"), None, None),
        check_vma=False,
    )
```

```python
import functools

import jax
import jax.numpy as jnp
from jax import lax
from jax.experimental import pallas as pl
from jax.experimental.pallas import tpu as pltpu
from jax.sharding import PartitionSpec as P

HIDDEN_BITS = 4
FOLD = 128


def swapped(block, axis, apart):
    count = lax.axis_size(axis)
    return lax.ppermute(block, axis, [(i, i ^ (1 << apart)) for i in range(count)])


def by_target(expand, count):
    kinds, depth, width = expand.shape
    return expand.reshape(kinds, depth, count, width // count).transpose(2, 0, 1, 3)


def owner_of(ends, ids):
    return jnp.sum((ends[None, :] <= ids[:, None]).astype(jnp.int32), axis=1)


def keep_mask(rank_blocks, row_counts, columns, rows):
    adapters = rank_blocks.shape[0]
    earlier = jnp.arange(adapters)[:, None] >= jnp.arange(adapters)[None, :]
    block_end = jnp.sum(jnp.where(earlier, rank_blocks[None, :], 0), axis=1)
    row_end = jnp.sum(jnp.where(earlier, row_counts[None, :], 0), axis=1)
    column_owner = owner_of(block_end, jnp.arange(columns, dtype=jnp.int32) // 16)
    row_owner = owner_of(row_end, jnp.arange(rows, dtype=jnp.int32))
    ids = jnp.arange(adapters, dtype=jnp.int32)
    row_blocks = jnp.sum(
        jnp.where(row_owner[:, None] == ids[None, :], rank_blocks[None, :], 0), axis=1
    )
    same = (row_owner[:, None] == column_owner[None, :]).astype(jnp.float32)
    return same, 1.0 / row_blocks.astype(jnp.float32)


def general_shards(tokens, w_gate, w_up, w_down, shrink_factors, expand_factors, rank_blocks, row_counts):
    count = lax.axis_size("tensor")
    low_bits = count.bit_length() - 1 - HIDDEN_BITS
    fgroups = 1 << low_bits
    place = lax.axis_index("tensor")
    feature_group = place % fgroups
    hidden_group = place // fgroups
    block_rows = tokens.shape[1]
    rows = block_rows << HIDDEN_BITS
    units = w_gate.shape[2]
    strip = units // fgroups

    expand = lax.all_to_all(
        by_target(expand_factors, count), "tensor", split_axis=0, concat_axis=0, tiled=True
    )

    gathered = tokens[0]
    for bit in reversed(range(HIDDEN_BITS)):
        other = swapped(gathered, "tensor", low_bits + bit)
        gathered = jnp.concatenate([gathered, other], 0)
    spots = jnp.arange(1 << HIDDEN_BITS, dtype=jnp.int32)
    moved = sum(((spots >> i) & 1) << (HIDDEN_BITS - 1 - i) for i in range(HIDDEN_BITS))
    natural = (
        (moved ^ hidden_group)[:, None] * block_rows + jnp.arange(block_rows, dtype=jnp.int32)[None, :]
    ).reshape(rows)
    to_own = (natural[:, None] == jnp.arange(rows, dtype=jnp.int32)[None, :]).astype(jnp.bfloat16)

    columns = shrink_factors.shape[2]
    same, scale = keep_mask(rank_blocks, row_counts, columns, rows)
    slab = shrink_factors.shape[1]
    features = lax.dynamic_slice_in_dim(gathered, hidden_group * slab, slab, 1)
    features = jnp.dot(to_own.T, features, preferred_element_type=jnp.float32).astype(jnp.bfloat16)
    partial_value = jnp.einsum(
        "rd,kdc->krc", features, shrink_factors, preferred_element_type=jnp.float32
    )
    folded = jnp.sum((partial_value * same).reshape(2, rows, columns // FOLD, FOLD), axis=2)
    for bit in range(low_bits + HIDDEN_BITS):
        folded = folded + swapped(folded, "tensor", bit)
    shrunk = jnp.tile(folded, (1, 1, columns // FOLD)) * (same * scale[:, None])[None]
    shrunk = shrunk.astype(jnp.bfloat16)
    shrunk = jnp.einsum("or,krc->koc", to_own, shrunk, preferred_element_type=jnp.float32)
    shrunk = shrunk.astype(jnp.bfloat16)

    gate_part = jnp.dot(gathered, w_gate[0], preferred_element_type=jnp.float32)
    up_part = jnp.dot(gathered, w_up[0], preferred_element_type=jnp.float32)
    partials = jnp.stack([gate_part, up_part])
    for step in range(low_bits):
        bit = low_bits - 1 - step
        half = partials.shape[2] // 2
        high = feature_group // (1 << bit) % 2
        outgoing = lax.dynamic_slice_in_dim(partials, (1 - high) * half, half, 2)
        staying = lax.dynamic_slice_in_dim(partials, high * half, half, 2)
        partials = staying + swapped(outgoing, "tensor", bit)
    depth = expand.shape[2]
    low_rank = jnp.einsum(
        "krsd,skdc->krc",
        shrunk.reshape(2, rows, count, depth),
        expand,
        preferred_element_type=jnp.float32,
    )
    partials = partials + low_rank
    hidden = (jax.nn.silu(partials[0]) * partials[1]).astype(jnp.bfloat16)
    for step in range(low_bits):
        other = swapped(hidden, "tensor", step)
        high = feature_group // (1 << step) % 2 == 1
        hidden = jnp.where(
            high, jnp.concatenate([other, hidden], 1), jnp.concatenate([hidden, other], 1)
        )
    terms = jnp.dot(hidden, w_down[0], preferred_element_type=jnp.float32)
    for bit in range(HIDDEN_BITS):
        half = terms.shape[0] // 2
        outgoing = terms[half:].astype(jnp.bfloat16)
        terms = terms[:half] + swapped(outgoing, "tensor", low_bits + bit).astype(jnp.float32)
    return terms.astype(jnp.bfloat16)[None]


def owners(rank_blocks, row_counts, columns, rows):
    adapters = rank_blocks.shape[0]
    ids = jnp.arange(adapters, dtype=jnp.int32)
    earlier = ids[:, None] >= ids[None, :]
    block_end = jnp.sum(jnp.where(earlier, rank_blocks[None, :], 0), axis=1)
    row_end = jnp.sum(jnp.where(earlier, row_counts[None, :], 0), axis=1)
    column_owner = owner_of(block_end, jnp.arange(columns, dtype=jnp.int32) // 16)
    row_owner = owner_of(row_end, jnp.arange(rows, dtype=jnp.int32))
    row_blocks = jnp.sum(
        jnp.where(row_owner[:, None] == ids[None, :], rank_blocks[None, :], 0), axis=1
    )
    scale = 1.0 / row_blocks.astype(jnp.float32)
    return column_owner[None, :], row_owner[:, None], scale[:, None]


VMEM = pl.BlockSpec(memory_space=pltpu.VMEM)
SMEM = pl.BlockSpec(memory_space=pltpu.SMEM)
ANY = pl.BlockSpec(memory_space=pl.ANY)
X, Y, Z1, Z2 = 1, 2, 4, 8


def to_chip(block, apart):
    count = lax.axis_size("tensor")
    return lax.ppermute(block, "tensor", [(i, i ^ (apart << 1)) for i in range(count)])


def cost(flops, read):
    return pl.CostEstimate(flops=flops, bytes_accessed=read, transcendentals=0)


def in_hbm(array):
    return pltpu.with_memory_space_constraint(array, pltpu.HBM)


def blocks_kernel(count, strip, source, target):
    for j in range(count):
        target[j] = source[:, :, j * strip : (j + 1) * strip]


def blocks_of(expand, count):
    kinds, depth, width = expand.shape
    strip = width // count
    return pl.pallas_call(
        functools.partial(blocks_kernel, count, strip),
        out_shape=jax.ShapeDtypeStruct((count, kinds, depth, strip), expand.dtype),
        in_specs=[VMEM],
        out_specs=VMEM,
        cost_estimate=cost(0, 4 * expand.size),
        compiler_params=pltpu.CompilerParams(vmem_limit_bytes=16 << 20),
    )(expand)


def own_order(place, rows, own_axis):
    block = rows // 16
    own, natural = [lax.broadcasted_iota(jnp.int32, (rows, rows), axis) for axis in (own_axis, 1 - own_axis)]
    spot = own // block
    far = spot // 8 + spot // 4 % 2 * 2 + spot // 2 % 2 * 4 + spot % 2 * 8
    return ((far ^ (place // 2)) * block + (own - spot * block) == natural).astype(jnp.bfloat16)


def shrink_kernel(place, near, far, factors, row_owner, column_owner, folded):
    same = row_owner[...] == column_owner[...]
    rows = row_owner.shape[0]
    features = jnp.concatenate([near[...], far[...]], axis=0)
    features = jnp.dot(
        own_order(place[0], rows, 1), features, preferred_element_type=jnp.float32
    ).astype(jnp.bfloat16)
    for k in range(2):
        value = jnp.dot(features, factors[k], preferred_element_type=jnp.float32)
        value = jnp.where(same, value, 0.0)
        total = value[:, :FOLD]
        for start in range(FOLD, value.shape[1], FOLD):
            total = total + value[:, start : start + FOLD]
        folded[k] = total


def shrink_sums(place, near, far, factors, row_owner, column_owner):
    rows = row_owner.shape[0]
    return pl.pallas_call(
        shrink_kernel,
        out_shape=jax.ShapeDtypeStruct((2, rows, FOLD), jnp.float32),
        in_specs=[SMEM] + [VMEM] * 5,
        out_specs=VMEM,
        cost_estimate=cost(2 * rows * factors.size, 2 * factors.size),
        compiler_params=pltpu.CompilerParams(vmem_limit_bytes=16 << 20),
    )(place, near, far, factors, row_owner, column_owner)


def inner_kernel(place, own, left_y, left_x, right_x, right_y, gate, up, later, *refs):
    outs, kept, (rows, gate_sum, up_sum, sem) = refs[:4], refs[4], refs[5:]
    step, steps = pl.program_id(0), pl.num_programs(0)
    part = own.shape[0]
    copy = pltpu.make_async_copy(later, kept, sem)

    @pl.when(step == 0)
    def _():
        copy.start()

    def load(pieces):
        wide = [piece.astype(jnp.float32) for piece in pieces]
        rows[...] = jnp.concatenate(wide, axis=0).astype(rows.dtype)

    @pl.when(step < steps // 2)
    def _():
        load([own[...], left_y[...], left_x[...]])

    @pl.when(step >= steps // 2)
    def _():
        corner = right_y[...].astype(jnp.float32)
        load([own[...], corner[:part], right_x[...], corner[part:]])

    for weights, total in ((gate, gate_sum), (up, up_sum)):
        term = jnp.dot(rows[...], weights[0], preferred_element_type=jnp.float32)

        @pl.when(step == 0)
        def _():
            total[...] = term

        @pl.when(step > 0)
        def _():
            total[...] += term

    @pl.when(step == steps - 1)
    def _():
        copy.wait()
        strip = outs[0].shape[1]
        first = place[0] % 2 == 0
        for total, here, there in ((gate_sum, *outs[:2]), (up_sum, *outs[2:])):
            left, right = total[:, :strip], total[:, strip:]
            here[...] = jnp.where(first, left, right)
            there[...] = jnp.where(first, right, left)


def inner(place, own, left, right, gate, up, later, depth):
    part, width = own.shape
    rows, units = 4 * part, gate.shape[2]
    steps = width // depth
    weights = pl.BlockSpec((1, depth, units), lambda i: (0, i, 0))
    lefts = [pl.BlockSpec((n * part, depth), lambda i: (0, jnp.minimum(i, steps // 2 - 1))) for n in (1, 2)]
    rights = [pl.BlockSpec((n * part, depth), lambda i: (0, jnp.maximum(i - steps // 2, 0))) for n in (1, 2)]
    strip = jax.ShapeDtypeStruct((rows, units // 2), jnp.float32)
    return pl.pallas_call(
        inner_kernel,
        grid=(steps,),
        out_shape=[strip] * 4 + [pltpu.VMEM(later.shape, later.dtype)],
        in_specs=[SMEM, pl.BlockSpec((part, depth), lambda i: (0, i)), *lefts, *rights, weights, weights, ANY],
        out_specs=[pl.BlockSpec(strip.shape, lambda i: (0, 0))] * 4 + [VMEM],
        scratch_shapes=[pltpu.VMEM((rows, depth), own.dtype)]
        + [pltpu.VMEM((rows, units), jnp.float32)] * 2
        + [pltpu.SemaphoreType.DMA(())],
        cost_estimate=cost(2 * rows * (gate.size + up.size), 2 * (gate.size + up.size)),
        compiler_params=pltpu.CompilerParams(vmem_limit_bytes=32 << 20),
    )(place, own, *left, *right, in_hbm(gate), in_hbm(up), in_hbm(later))


def hidden_kernel(
    place, folded, row_owner, column_owner, scale, expand, gate, gate_in, up, up_in, hidden
):
    rows, columns = row_owner.shape[0], column_owner.shape[1]
    keep = jnp.where(row_owner[...] == column_owner[...], scale[...], 0.0)
    order = own_order(place[0], rows, 0)
    sums = []
    for k in range(2):
        shrunk = jnp.concatenate([folded[k]] * (columns // FOLD), axis=1) * keep
        shrunk = jnp.dot(
            order, shrunk.astype(jnp.bfloat16), preferred_element_type=jnp.float32
        ).astype(jnp.bfloat16)
        factors = expand[:, k].reshape(columns, expand.shape[3])
        sums.append(jnp.dot(shrunk, factors, preferred_element_type=jnp.float32))
    gate_sum = gate[...] + gate_in[...] + sums[0]
    up_sum = up[...] + up_in[...] + sums[1]
    hidden[...] = (gate_sum / (1.0 + jnp.exp(-gate_sum)) * up_sum).astype(hidden.dtype)


def hidden_strip(*operands):
    expand, gate = operands[5], operands[6]
    return pl.pallas_call(
        hidden_kernel,
        out_shape=jax.ShapeDtypeStruct(gate.shape, jnp.bfloat16),
        in_specs=[SMEM] + [VMEM] * 9,
        out_specs=VMEM,
        cost_estimate=cost(2 * gate.shape[0] * expand.size, 2 * expand.size),
        compiler_params=pltpu.CompilerParams(vmem_limit_bytes=32 << 20),
    )(*operands)


def down_kernel(tile, place, mine, other, weights, *outs):
    first = place[0] % 2 == 0
    hidden = jnp.concatenate(
        [jnp.where(first, mine[...], other[...]), jnp.where(first, other[...], mine[...])], axis=1
    )
    part = hidden.shape[0] // 4
    start = 0
    for x_first, stays, sends in ((True, *outs[:2]), (False, *outs[2:])):
        for at in range(0, stays.shape[1], tile):
            terms = jnp.dot(
                hidden, weights[0, :, start + at : start + at + tile], preferred_element_type=jnp.float32
            )
            low_y, high_y, far_low, far_high = [terms[i * part : (i + 1) * part] for i in range(4)]
            if x_first:
                stay, send = (low_y, high_y), (far_low, far_high)
            else:
                stay, send = (low_y, far_low), (high_y, far_high)
            stays[:, at : at + tile] = jnp.concatenate(stay, axis=0)
            sends[:, at : at + tile] = jnp.concatenate(send, axis=0).astype(sends.dtype)
        start += stays.shape[1]


def down(place, mine, other, weights, widths, tile):
    rows = mine.shape[0]
    return pl.pallas_call(
        functools.partial(down_kernel, tile),
        out_shape=[
            jax.ShapeDtypeStruct((rows // 2, width), dtype)
            for width in widths
            for dtype in (jnp.float32, jnp.bfloat16)
        ],
        in_specs=[SMEM] + [VMEM] * 3,
        out_specs=[VMEM] * 4,
        cost_estimate=cost(2 * rows * weights.size, 2 * weights.size),
        compiler_params=pltpu.CompilerParams(vmem_limit_bytes=24 << 20),
    )(place, mine, other, weights)


def halved(terms, apart):
    half = terms.shape[0] // 2
    return terms[:half] + to_chip(terms[half:].astype(jnp.bfloat16), apart)


def shards(tokens, w_gate, w_up, w_down, shrink_factors, expand_factors, rank_blocks, row_counts):
    count = lax.axis_size("tensor")
    units = w_gate.shape[2]
    if count != 32 or units % 256:
        return general_shards(
            tokens, w_gate, w_up, w_down, shrink_factors, expand_factors, rank_blocks, row_counts
        )
    device = lax.axis_index("tensor")
    place = device.reshape(1)
    x, y, z = device // 2 % 2, device // 4 % 2, device // 8
    block_rows, width = tokens.shape[1], tokens.shape[2]
    rows = 16 * block_rows
    slab, half = width // 16, width // 2
    columns = shrink_factors.shape[2]
    blocks = blocks_of(expand_factors, count)

    own = tokens[0]
    for apart in (Z2, Z1):
        own = jnp.concatenate([own, to_chip(own, apart)], 0)

    near = lax.dynamic_slice_in_dim(own, z * 4 * slab, 4 * slab, 1)
    for apart, bit, size in ((Y, y, 2 * slab), (X, x, slab)):
        other = to_chip(lax.dynamic_slice_in_dim(near, (1 - bit) * size, size, 1), apart)
        near = lax.dynamic_slice_in_dim(near, bit * size, size, 1)
        if apart == Y:
            near = jnp.concatenate([near, other], 0)
    column_owner, row_owner, scale = owners(rank_blocks, row_counts, columns, rows)
    folded = shrink_sums(place, near, other, shrink_factors, row_owner, column_owner)
    for apart in (Z2, Z1):
        folded = folded + to_chip(folded.astype(jnp.bfloat16), apart)

    left, right = own[:, :half], own[:, half:]
    left_y, right_x = to_chip(left, Y), to_chip(right, X)
    left_x = to_chip(jnp.concatenate([left, left_y], 0), X)
    right_y = to_chip(jnp.concatenate([right, right_x], 0), Y)

    blocks, folded, left_x, right_y = lax.optimization_barrier((blocks, folded, left_x, right_y))
    expand = lax.all_to_all(blocks, "tensor", split_axis=0, concat_axis=0, tiled=True)
    for apart in (Y, X):
        folded = folded + to_chip(folded.astype(jnp.bfloat16), apart)
    folded = folded + swapped(folded, "tensor", 0)

    gate, gate_out, up, up_out, kept = inner(
        place, own, (left_y, left_x), (right_x, right_y), w_gate, w_up, w_down, 512
    )
    gate_in = swapped(gate_out, "tensor", 0)
    up_in = swapped(up_out, "tensor", 0)
    hidden = hidden_strip(
        place, folded, row_owner, column_owner, scale, expand, gate, gate_in, up, up_in
    )
    other = swapped(hidden, "tensor", 0)
    split = width // 2
    outs = down(place, hidden, other, kept, (split, width - split), 256)
    sums = []
    for (stays, sends), (first, second) in zip((outs[:2], outs[2:]), ((X, Y), (Y, X))):
        sums.append((stays + to_chip(sends, first), second))
    terms = jnp.concatenate([halved(*pair) for pair in sums], 1)
    for apart in (Z1, Z2):
        terms = halved(terms, apart)
    return terms.astype(jnp.bfloat16)[None]


def solution(mesh):
    placed = (
        P(("groups", "tensor"), None, None),
        P("tensor", None, None),
        P("tensor", None, None),
        P("tensor", None, None),
        P("groups", "tensor", None),
        P("groups", "tensor", None),
        P("groups"),
        P("groups"),
    )
    return jax.shard_map(
        shards,
        mesh=mesh,
        in_specs=placed,
        out_specs=P(("groups", "tensor"), None, None),
        check_vma=False,
    )
```

```python
import functools

import jax
import jax.numpy as jnp
from jax import lax
from jax.experimental import pallas as pl
from jax.experimental.pallas import tpu as pltpu
from jax.sharding import PartitionSpec as P

HIDDEN_BITS = 4
FOLD = 128


def swapped(block, axis, apart):
    count = lax.axis_size(axis)
    return lax.ppermute(block, axis, [(i, i ^ (1 << apart)) for i in range(count)])


def by_target(expand, count):
    kinds, depth, width = expand.shape
    return expand.reshape(kinds, depth, count, width // count).transpose(2, 0, 1, 3)


def owner_of(ends, ids):
    return jnp.sum((ends[None, :] <= ids[:, None]).astype(jnp.int32), axis=1)


def keep_mask(rank_blocks, row_counts, columns, rows):
    adapters = rank_blocks.shape[0]
    earlier = jnp.arange(adapters)[:, None] >= jnp.arange(adapters)[None, :]
    block_end = jnp.sum(jnp.where(earlier, rank_blocks[None, :], 0), axis=1)
    row_end = jnp.sum(jnp.where(earlier, row_counts[None, :], 0), axis=1)
    column_owner = owner_of(block_end, jnp.arange(columns, dtype=jnp.int32) // 16)
    row_owner = owner_of(row_end, jnp.arange(rows, dtype=jnp.int32))
    ids = jnp.arange(adapters, dtype=jnp.int32)
    row_blocks = jnp.sum(
        jnp.where(row_owner[:, None] == ids[None, :], rank_blocks[None, :], 0), axis=1
    )
    same = (row_owner[:, None] == column_owner[None, :]).astype(jnp.float32)
    return same, 1.0 / row_blocks.astype(jnp.float32)


def general_shards(tokens, w_gate, w_up, w_down, shrink_factors, expand_factors, rank_blocks, row_counts):
    count = lax.axis_size("tensor")
    low_bits = count.bit_length() - 1 - HIDDEN_BITS
    fgroups = 1 << low_bits
    place = lax.axis_index("tensor")
    feature_group = place % fgroups
    hidden_group = place // fgroups
    block_rows = tokens.shape[1]
    rows = block_rows << HIDDEN_BITS
    units = w_gate.shape[2]
    strip = units // fgroups

    expand = lax.all_to_all(
        by_target(expand_factors, count), "tensor", split_axis=0, concat_axis=0, tiled=True
    )

    gathered = tokens[0]
    for bit in reversed(range(HIDDEN_BITS)):
        other = swapped(gathered, "tensor", low_bits + bit)
        gathered = jnp.concatenate([gathered, other], 0)
    spots = jnp.arange(1 << HIDDEN_BITS, dtype=jnp.int32)
    moved = sum(((spots >> i) & 1) << (HIDDEN_BITS - 1 - i) for i in range(HIDDEN_BITS))
    natural = (
        (moved ^ hidden_group)[:, None] * block_rows + jnp.arange(block_rows, dtype=jnp.int32)[None, :]
    ).reshape(rows)
    to_own = (natural[:, None] == jnp.arange(rows, dtype=jnp.int32)[None, :]).astype(jnp.bfloat16)

    columns = shrink_factors.shape[2]
    same, scale = keep_mask(rank_blocks, row_counts, columns, rows)
    slab = shrink_factors.shape[1]
    features = lax.dynamic_slice_in_dim(gathered, hidden_group * slab, slab, 1)
    features = jnp.dot(to_own.T, features, preferred_element_type=jnp.float32).astype(jnp.bfloat16)
    partial_value = jnp.einsum(
        "rd,kdc->krc", features, shrink_factors, preferred_element_type=jnp.float32
    )
    folded = jnp.sum((partial_value * same).reshape(2, rows, columns // FOLD, FOLD), axis=2)
    for bit in range(low_bits + HIDDEN_BITS):
        folded = folded + swapped(folded, "tensor", bit)
    shrunk = jnp.tile(folded, (1, 1, columns // FOLD)) * (same * scale[:, None])[None]
    shrunk = shrunk.astype(jnp.bfloat16)
    shrunk = jnp.einsum("or,krc->koc", to_own, shrunk, preferred_element_type=jnp.float32)
    shrunk = shrunk.astype(jnp.bfloat16)

    gate_part = jnp.dot(gathered, w_gate[0], preferred_element_type=jnp.float32)
    up_part = jnp.dot(gathered, w_up[0], preferred_element_type=jnp.float32)
    partials = jnp.stack([gate_part, up_part])
    for step in range(low_bits):
        bit = low_bits - 1 - step
        half = partials.shape[2] // 2
        high = feature_group // (1 << bit) % 2
        outgoing = lax.dynamic_slice_in_dim(partials, (1 - high) * half, half, 2)
        staying = lax.dynamic_slice_in_dim(partials, high * half, half, 2)
        partials = staying + swapped(outgoing, "tensor", bit)
    depth = expand.shape[2]
    low_rank = jnp.einsum(
        "krsd,skdc->krc",
        shrunk.reshape(2, rows, count, depth),
        expand,
        preferred_element_type=jnp.float32,
    )
    partials = partials + low_rank
    hidden = (jax.nn.silu(partials[0]) * partials[1]).astype(jnp.bfloat16)
    for step in range(low_bits):
        other = swapped(hidden, "tensor", step)
        high = feature_group // (1 << step) % 2 == 1
        hidden = jnp.where(
            high, jnp.concatenate([other, hidden], 1), jnp.concatenate([hidden, other], 1)
        )
    terms = jnp.dot(hidden, w_down[0], preferred_element_type=jnp.float32)
    for bit in range(HIDDEN_BITS):
        half = terms.shape[0] // 2
        outgoing = terms[half:].astype(jnp.bfloat16)
        terms = terms[:half] + swapped(outgoing, "tensor", low_bits + bit).astype(jnp.float32)
    return terms.astype(jnp.bfloat16)[None]


def owners(rank_blocks, row_counts, columns, rows):
    adapters = rank_blocks.shape[0]
    ids = jnp.arange(adapters, dtype=jnp.int32)
    earlier = ids[:, None] >= ids[None, :]
    block_end = jnp.sum(jnp.where(earlier, rank_blocks[None, :], 0), axis=1)
    row_end = jnp.sum(jnp.where(earlier, row_counts[None, :], 0), axis=1)
    column_owner = owner_of(block_end, jnp.arange(columns, dtype=jnp.int32) // 16)
    row_owner = owner_of(row_end, jnp.arange(rows, dtype=jnp.int32))
    row_blocks = jnp.sum(
        jnp.where(row_owner[:, None] == ids[None, :], rank_blocks[None, :], 0), axis=1
    )
    scale = 1.0 / row_blocks.astype(jnp.float32)
    return column_owner[None, :], row_owner[:, None], scale[:, None]


VMEM = pl.BlockSpec(memory_space=pltpu.VMEM)
SMEM = pl.BlockSpec(memory_space=pltpu.SMEM)
ANY = pl.BlockSpec(memory_space=pl.ANY)
X, Y, Z1, Z2 = 1, 2, 4, 8


def to_chip(block, apart):
    count = lax.axis_size("tensor")
    return lax.ppermute(block, "tensor", [(i, i ^ (apart << 1)) for i in range(count)])


def cost(flops, read):
    return pl.CostEstimate(flops=flops, bytes_accessed=read, transcendentals=0)


def in_hbm(array):
    return pltpu.with_memory_space_constraint(array, pltpu.HBM)


def blocks_kernel(count, strip, source, target):
    for j in range(count):
        target[j] = source[:, :, j * strip : (j + 1) * strip]


def blocks_of(expand, count):
    kinds, depth, width = expand.shape
    strip = width // count
    return pl.pallas_call(
        functools.partial(blocks_kernel, count, strip),
        out_shape=jax.ShapeDtypeStruct((count, kinds, depth, strip), expand.dtype),
        in_specs=[VMEM],
        out_specs=VMEM,
        cost_estimate=cost(0, 4 * expand.size),
        compiler_params=pltpu.CompilerParams(vmem_limit_bytes=10 << 20),
    )(expand)


def own_order(place, rows, own_axis):
    block = rows // 16
    own, natural = [lax.broadcasted_iota(jnp.int32, (rows, rows), axis) for axis in (own_axis, 1 - own_axis)]
    spot = own // block
    far = spot // 8 + spot // 4 % 2 * 2 + spot // 2 % 2 * 4 + spot % 2 * 8
    return ((far ^ (place // 2)) * block + (own - spot * block) == natural).astype(jnp.bfloat16)


def shrink_kernel(place, near, far, factors, row_owner, column_owner, folded):
    same = row_owner[...] == column_owner[...]
    rows = row_owner.shape[0]
    features = jnp.concatenate([near[...], far[...]], axis=0)
    features = jnp.dot(
        own_order(place[0], rows, 1), features, preferred_element_type=jnp.float32
    ).astype(jnp.bfloat16)
    for k in range(2):
        value = jnp.dot(features, factors[k], preferred_element_type=jnp.float32)
        value = jnp.where(same, value, 0.0)
        total = value[:, :FOLD]
        for start in range(FOLD, value.shape[1], FOLD):
            total = total + value[:, start : start + FOLD]
        folded[k] = total


def shrink_sums(place, near, far, factors, row_owner, column_owner):
    rows = row_owner.shape[0]
    return pl.pallas_call(
        shrink_kernel,
        out_shape=jax.ShapeDtypeStruct((2, rows, FOLD), jnp.float32),
        in_specs=[SMEM] + [VMEM] * 5,
        out_specs=VMEM,
        cost_estimate=cost(2 * rows * factors.size, 2 * factors.size),
        compiler_params=pltpu.CompilerParams(vmem_limit_bytes=10 << 20),
    )(place, near, far, factors, row_owner, column_owner)


def fetch_kernel(pieces, source, after, target, sems):
    size = source.shape[1] // pieces
    copies = [
        pltpu.make_async_copy(
            source.at[:, pl.ds(i * size, size)], target.at[:, pl.ds(i * size, size)], sems.at[i]
        )
        for i in range(pieces)
    ]
    for copy in copies:
        copy.start()
    for copy in copies:
        copy.wait()


def fetch(weights, after, pieces):
    return pl.pallas_call(
        functools.partial(fetch_kernel, pieces),
        out_shape=pltpu.VMEM(weights.shape, weights.dtype),
        in_specs=[ANY, ANY],
        out_specs=VMEM,
        scratch_shapes=[pltpu.SemaphoreType.DMA((pieces,))],
        cost_estimate=cost(0, 2 * weights.size),
        compiler_params=pltpu.CompilerParams(vmem_limit_bytes=1 << 20),
    )(in_hbm(weights), after)


def inner_kernel(streams, place, own, left_y, left_x, right_x, right_y, *refs):
    gates, ups = refs[:streams], refs[streams : 2 * streams]
    outs, (rows, gate_sum, up_sum) = refs[2 * streams : -3], refs[-3:]
    step, steps = pl.program_id(0), pl.num_programs(0)
    part = own.shape[0]

    def load(pieces):
        wide = [piece.astype(jnp.float32) for piece in pieces]
        rows[...] = jnp.concatenate(wide, axis=0).astype(rows.dtype)

    @pl.when(step < steps // 2)
    def _():
        load([own[...], left_y[...], left_x[...]])

    @pl.when(step >= steps // 2)
    def _():
        corner = right_y[...].astype(jnp.float32)
        load([own[...], corner[:part], right_x[...], corner[part:]])

    for weights, total in ((gates, gate_sum), (ups, up_sum)):
        depth = weights[0].shape[1]
        term = sum(
            jnp.dot(
                rows[:, i * depth : (i + 1) * depth], block[0], preferred_element_type=jnp.float32
            )
            for i, block in enumerate(weights)
        )

        @pl.when(step == 0)
        def _():
            total[...] = term

        @pl.when(step > 0)
        def _():
            total[...] += term

    @pl.when(step == steps - 1)
    def _():
        strip = outs[0].shape[1]
        first = place[0] % 2 == 0
        for total, here, there in ((gate_sum, *outs[:2]), (up_sum, *outs[2:])):
            left, right = total[:, :strip], total[:, strip:]
            here[...] = jnp.where(first, left, right)
            there[...] = jnp.where(first, right, left)


def inner(place, own, left, right, gate, up, depth, streams):
    part, width = own.shape
    rows, units = 4 * part, gate.shape[2]
    steps = width // depth
    weights = [
        pl.BlockSpec((1, depth // streams, units), functools.partial(lambda s, i: (0, i * streams + s, 0), s))
        for s in range(streams)
    ]
    lefts = [pl.BlockSpec((n * part, depth), lambda i: (0, jnp.minimum(i, steps // 2 - 1))) for n in (1, 2)]
    rights = [pl.BlockSpec((n * part, depth), lambda i: (0, jnp.maximum(i - steps // 2, 0))) for n in (1, 2)]
    strip = jax.ShapeDtypeStruct((rows, units // 2), jnp.float32)
    gate, up = in_hbm(gate), in_hbm(up)
    return pl.pallas_call(
        functools.partial(inner_kernel, streams),
        grid=(steps,),
        out_shape=[strip] * 4,
        in_specs=[SMEM, pl.BlockSpec((part, depth), lambda i: (0, i)), *lefts, *rights, *weights, *weights],
        out_specs=[pl.BlockSpec(strip.shape, lambda i: (0, 0))] * 4,
        scratch_shapes=[pltpu.VMEM((rows, depth), own.dtype)]
        + [pltpu.VMEM((rows, units), jnp.float32)] * 2,
        cost_estimate=cost(2 * rows * (gate.size + up.size), 2 * (gate.size + up.size)),
        compiler_params=pltpu.CompilerParams(vmem_limit_bytes=20 << 20),
    )(place, own, *left, *right, *[gate] * streams, *[up] * streams)


def hidden_kernel(
    place, folded, row_owner, column_owner, scale, expand, gate, gate_in, up, up_in, hidden
):
    rows, columns = row_owner.shape[0], column_owner.shape[1]
    keep = jnp.where(row_owner[...] == column_owner[...], scale[...], 0.0)
    order = own_order(place[0], rows, 0)
    sums = []
    for k in range(2):
        shrunk = jnp.concatenate([folded[k]] * (columns // FOLD), axis=1) * keep
        shrunk = jnp.dot(
            order, shrunk.astype(jnp.bfloat16), preferred_element_type=jnp.float32
        ).astype(jnp.bfloat16)
        factors = expand[:, k].reshape(columns, expand.shape[3])
        sums.append(jnp.dot(shrunk, factors, preferred_element_type=jnp.float32))
    gate_sum = gate[...] + gate_in[...] + sums[0]
    up_sum = up[...] + up_in[...] + sums[1]
    hidden[...] = (gate_sum / (1.0 + jnp.exp(-gate_sum)) * up_sum).astype(hidden.dtype)


def hidden_strip(*operands):
    expand, gate = operands[5], operands[6]
    return pl.pallas_call(
        hidden_kernel,
        out_shape=jax.ShapeDtypeStruct(gate.shape, jnp.bfloat16),
        in_specs=[SMEM] + [VMEM] * 9,
        out_specs=VMEM,
        cost_estimate=cost(2 * gate.shape[0] * expand.size, 2 * expand.size),
        compiler_params=pltpu.CompilerParams(vmem_limit_bytes=12 << 20),
    )(*operands)


def down_kernel(tile, place, mine, other, weights, *outs):
    first = place[0] % 2 == 0
    hidden = jnp.concatenate(
        [jnp.where(first, mine[...], other[...]), jnp.where(first, other[...], mine[...])], axis=1
    )
    part = hidden.shape[0] // 4
    start = 0
    for x_first, stays, sends in ((True, *outs[:2]), (False, *outs[2:])):
        for at in range(0, stays.shape[1], tile):
            terms = jnp.dot(
                hidden, weights[0, :, start + at : start + at + tile], preferred_element_type=jnp.float32
            )
            low_y, high_y, far_low, far_high = [terms[i * part : (i + 1) * part] for i in range(4)]
            if x_first:
                stay, send = (low_y, high_y), (far_low, far_high)
            else:
                stay, send = (low_y, far_low), (high_y, far_high)
            stays[:, at : at + tile] = jnp.concatenate(stay, axis=0)
            sends[:, at : at + tile] = jnp.concatenate(send, axis=0).astype(sends.dtype)
        start += stays.shape[1]


def down(place, mine, other, weights, widths, tile):
    rows = mine.shape[0]
    return pl.pallas_call(
        functools.partial(down_kernel, tile),
        out_shape=[
            jax.ShapeDtypeStruct((rows // 2, width), dtype)
            for width in widths
            for dtype in (jnp.float32, jnp.bfloat16)
        ],
        in_specs=[SMEM] + [VMEM] * 3,
        out_specs=[VMEM] * 4,
        cost_estimate=cost(2 * rows * weights.size, 2 * weights.size),
        compiler_params=pltpu.CompilerParams(vmem_limit_bytes=8 << 20),
    )(place, mine, other, weights)


def halved(terms, apart):
    half = terms.shape[0] // 2
    return terms[:half] + to_chip(terms[half:].astype(jnp.bfloat16), apart)


def shards(tokens, w_gate, w_up, w_down, shrink_factors, expand_factors, rank_blocks, row_counts):
    count = lax.axis_size("tensor")
    units = w_gate.shape[2]
    if count != 32 or units % 256:
        return general_shards(
            tokens, w_gate, w_up, w_down, shrink_factors, expand_factors, rank_blocks, row_counts
        )
    device = lax.axis_index("tensor")
    place = device.reshape(1)
    x, y, z = device // 2 % 2, device // 4 % 2, device // 8
    block_rows, width = tokens.shape[1], tokens.shape[2]
    rows = 16 * block_rows
    slab, half = width // 16, width // 2
    columns = shrink_factors.shape[2]
    blocks = blocks_of(expand_factors, count)

    own = tokens[0]
    for apart in (Z2, Z1):
        other = to_chip(own, apart)
        if apart == Z2:
            blocks, other = lax.optimization_barrier((blocks, other))
        own = jnp.concatenate([own, other], 0)

    near = lax.dynamic_slice_in_dim(own, z * 4 * slab, 4 * slab, 1)
    for apart, bit, size in ((Y, y, 2 * slab), (X, x, slab)):
        other = to_chip(lax.dynamic_slice_in_dim(near, (1 - bit) * size, size, 1), apart)
        near = lax.dynamic_slice_in_dim(near, bit * size, size, 1)
        if apart == Y:
            near = jnp.concatenate([near, other], 0)
    blocks, near, other = lax.optimization_barrier((blocks, near, other))
    expand = lax.all_to_all(blocks, "tensor", split_axis=0, concat_axis=0, tiled=True)

    column_owner, row_owner, scale = owners(rank_blocks, row_counts, columns, rows)
    folded = shrink_sums(place, near, other, shrink_factors, row_owner, column_owner)
    for apart in (Y, X):
        folded = folded + to_chip(folded, apart)
    folded = folded + swapped(folded, "tensor", 0)
    sent = folded.astype(jnp.bfloat16)
    received = [to_chip(sent, apart) for apart in (Z1, Z2, Z1 | Z2)]
    folded = (folded + received[0]) + (received[1].astype(jnp.float32) + received[2])

    left, right = own[:, :half], own[:, half:]
    left_y, right_x = to_chip(left, Y), to_chip(right, X)
    kept = fetch(w_down, own, 4)
    left_y, right_x, kept = lax.optimization_barrier((left_y, right_x, kept))
    left_x = to_chip(jnp.concatenate([left, left_y], 0), X)
    right_y = to_chip(jnp.concatenate([right, right_x], 0), Y)
    gate, gate_out, up, up_out = inner(
        place, own, (left_y, left_x), (right_x, right_y), w_gate, w_up, 512, 2
    )
    gate_in = swapped(gate_out, "tensor", 0)
    up_in = swapped(up_out, "tensor", 0)
    hidden = hidden_strip(
        place, folded, row_owner, column_owner, scale, expand, gate, gate_in, up, up_in
    )
    other = swapped(hidden, "tensor", 0)
    split = width // 2
    outs = down(place, hidden, other, kept, (split, width - split), 256)
    sums = []
    for (stays, sends), (first, second) in zip((outs[:2], outs[2:]), ((X, Y), (Y, X))):
        sums.append((stays + to_chip(sends, first), second))
    terms = jnp.concatenate([halved(*pair) for pair in sums], 1)
    for apart in (Z1, Z2):
        terms = halved(terms, apart)
    return terms.astype(jnp.bfloat16)[None]


def solution(mesh):
    placed = (
        P(("groups", "tensor"), None, None),
        P("tensor", None, None),
        P("tensor", None, None),
        P("tensor", None, None),
        P("groups", "tensor", None),
        P("groups", "tensor", None),
        P("groups"),
        P("groups"),
    )
    return jax.shard_map(
        shards,
        mesh=mesh,
        in_specs=placed,
        out_specs=P(("groups", "tensor"), None, None),
        check_vma=False,
    )
```

```python
import functools

import jax
import jax.numpy as jnp
from jax import lax
from jax.experimental import pallas as pl
from jax.experimental.pallas import tpu as pltpu
from jax.sharding import PartitionSpec as P

HIDDEN_BITS = 4
FOLD = 128


def swapped(block, axis, apart):
    count = lax.axis_size(axis)
    return lax.ppermute(block, axis, [(i, i ^ (1 << apart)) for i in range(count)])


def by_target(expand, count):
    kinds, depth, width = expand.shape
    return expand.reshape(kinds, depth, count, width // count).transpose(2, 0, 1, 3)


def owner_of(ends, ids):
    return jnp.sum((ends[None, :] <= ids[:, None]).astype(jnp.int32), axis=1)


def keep_mask(rank_blocks, row_counts, columns, rows):
    adapters = rank_blocks.shape[0]
    earlier = jnp.arange(adapters)[:, None] >= jnp.arange(adapters)[None, :]
    block_end = jnp.sum(jnp.where(earlier, rank_blocks[None, :], 0), axis=1)
    row_end = jnp.sum(jnp.where(earlier, row_counts[None, :], 0), axis=1)
    column_owner = owner_of(block_end, jnp.arange(columns, dtype=jnp.int32) // 16)
    row_owner = owner_of(row_end, jnp.arange(rows, dtype=jnp.int32))
    ids = jnp.arange(adapters, dtype=jnp.int32)
    row_blocks = jnp.sum(
        jnp.where(row_owner[:, None] == ids[None, :], rank_blocks[None, :], 0), axis=1
    )
    same = (row_owner[:, None] == column_owner[None, :]).astype(jnp.float32)
    return same, 1.0 / row_blocks.astype(jnp.float32)


def general_shards(tokens, w_gate, w_up, w_down, shrink_factors, expand_factors, rank_blocks, row_counts):
    count = lax.axis_size("tensor")
    low_bits = count.bit_length() - 1 - HIDDEN_BITS
    fgroups = 1 << low_bits
    place = lax.axis_index("tensor")
    feature_group = place % fgroups
    hidden_group = place // fgroups
    block_rows = tokens.shape[1]
    rows = block_rows << HIDDEN_BITS
    units = w_gate.shape[2]
    strip = units // fgroups

    expand = lax.all_to_all(
        by_target(expand_factors, count), "tensor", split_axis=0, concat_axis=0, tiled=True
    )

    gathered = tokens[0]
    for bit in reversed(range(HIDDEN_BITS)):
        other = swapped(gathered, "tensor", low_bits + bit)
        gathered = jnp.concatenate([gathered, other], 0)
    spots = jnp.arange(1 << HIDDEN_BITS, dtype=jnp.int32)
    moved = sum(((spots >> i) & 1) << (HIDDEN_BITS - 1 - i) for i in range(HIDDEN_BITS))
    natural = (
        (moved ^ hidden_group)[:, None] * block_rows + jnp.arange(block_rows, dtype=jnp.int32)[None, :]
    ).reshape(rows)
    to_own = (natural[:, None] == jnp.arange(rows, dtype=jnp.int32)[None, :]).astype(jnp.bfloat16)

    columns = shrink_factors.shape[2]
    same, scale = keep_mask(rank_blocks, row_counts, columns, rows)
    slab = shrink_factors.shape[1]
    features = lax.dynamic_slice_in_dim(gathered, hidden_group * slab, slab, 1)
    features = jnp.dot(to_own.T, features, preferred_element_type=jnp.float32).astype(jnp.bfloat16)
    partial_value = jnp.einsum(
        "rd,kdc->krc", features, shrink_factors, preferred_element_type=jnp.float32
    )
    folded = jnp.sum((partial_value * same).reshape(2, rows, columns // FOLD, FOLD), axis=2)
    for bit in range(low_bits + HIDDEN_BITS):
        folded = folded + swapped(folded, "tensor", bit)
    shrunk = jnp.tile(folded, (1, 1, columns // FOLD)) * (same * scale[:, None])[None]
    shrunk = shrunk.astype(jnp.bfloat16)
    shrunk = jnp.einsum("or,krc->koc", to_own, shrunk, preferred_element_type=jnp.float32)
    shrunk = shrunk.astype(jnp.bfloat16)

    gate_part = jnp.dot(gathered, w_gate[0], preferred_element_type=jnp.float32)
    up_part = jnp.dot(gathered, w_up[0], preferred_element_type=jnp.float32)
    partials = jnp.stack([gate_part, up_part])
    for step in range(low_bits):
        bit = low_bits - 1 - step
        half = partials.shape[2] // 2
        high = feature_group // (1 << bit) % 2
        outgoing = lax.dynamic_slice_in_dim(partials, (1 - high) * half, half, 2)
        staying = lax.dynamic_slice_in_dim(partials, high * half, half, 2)
        partials = staying + swapped(outgoing, "tensor", bit)
    depth = expand.shape[2]
    low_rank = jnp.einsum(
        "krsd,skdc->krc",
        shrunk.reshape(2, rows, count, depth),
        expand,
        preferred_element_type=jnp.float32,
    )
    partials = partials + low_rank
    hidden = (jax.nn.silu(partials[0]) * partials[1]).astype(jnp.bfloat16)
    for step in range(low_bits):
        other = swapped(hidden, "tensor", step)
        high = feature_group // (1 << step) % 2 == 1
        hidden = jnp.where(
            high, jnp.concatenate([other, hidden], 1), jnp.concatenate([hidden, other], 1)
        )
    terms = jnp.dot(hidden, w_down[0], preferred_element_type=jnp.float32)
    for bit in range(HIDDEN_BITS):
        half = terms.shape[0] // 2
        outgoing = terms[half:].astype(jnp.bfloat16)
        terms = terms[:half] + swapped(outgoing, "tensor", low_bits + bit).astype(jnp.float32)
    return terms.astype(jnp.bfloat16)[None]


def owners(rank_blocks, row_counts, columns, rows):
    adapters = rank_blocks.shape[0]
    ids = jnp.arange(adapters, dtype=jnp.int32)
    earlier = ids[:, None] >= ids[None, :]
    block_end = jnp.sum(jnp.where(earlier, rank_blocks[None, :], 0), axis=1)
    row_end = jnp.sum(jnp.where(earlier, row_counts[None, :], 0), axis=1)
    column_owner = owner_of(block_end, jnp.arange(columns, dtype=jnp.int32) // 16)
    row_owner = owner_of(row_end, jnp.arange(rows, dtype=jnp.int32))
    row_blocks = jnp.sum(
        jnp.where(row_owner[:, None] == ids[None, :], rank_blocks[None, :], 0), axis=1
    )
    scale = 1.0 / row_blocks.astype(jnp.float32)
    return column_owner[None, :], row_owner[:, None], scale[:, None]


VMEM = pl.BlockSpec(memory_space=pltpu.VMEM)
SMEM = pl.BlockSpec(memory_space=pltpu.SMEM)
ANY = pl.BlockSpec(memory_space=pl.ANY)
X, Y, Z1, Z2 = 1, 2, 4, 8


def to_chip(block, apart):
    count = lax.axis_size("tensor")
    return lax.ppermute(block, "tensor", [(i, i ^ (apart << 1)) for i in range(count)])


def cost(flops, read):
    return pl.CostEstimate(flops=flops, bytes_accessed=read, transcendentals=0)


def in_hbm(array):
    return pltpu.with_memory_space_constraint(array, pltpu.HBM)


def blocks_kernel(count, strip, source, target):
    for j in range(count):
        target[j] = source[:, :, j * strip : (j + 1) * strip]


def blocks_of(expand, count):
    kinds, depth, width = expand.shape
    strip = width // count
    return pl.pallas_call(
        functools.partial(blocks_kernel, count, strip),
        out_shape=jax.ShapeDtypeStruct((count, kinds, depth, strip), expand.dtype),
        in_specs=[VMEM],
        out_specs=VMEM,
        cost_estimate=cost(0, 4 * expand.size),
        compiler_params=pltpu.CompilerParams(vmem_limit_bytes=10 << 20),
    )(expand)


def own_order(place, rows, own_axis):
    block = rows // 16
    own, natural = [lax.broadcasted_iota(jnp.int32, (rows, rows), axis) for axis in (own_axis, 1 - own_axis)]
    spot = own // block
    far = spot // 8 + spot // 4 % 2 * 2 + spot // 2 % 2 * 4 + spot % 2 * 8
    return ((far ^ (place // 2)) * block + (own - spot * block) == natural).astype(jnp.bfloat16)


def shrink_kernel(place, near, far, factors, row_owner, column_owner, folded):
    same = row_owner[...] == column_owner[...]
    rows = row_owner.shape[0]
    features = jnp.concatenate([near[...], far[...]], axis=0)
    features = jnp.dot(
        own_order(place[0], rows, 1), features, preferred_element_type=jnp.float32
    ).astype(jnp.bfloat16)
    for k in range(2):
        value = jnp.dot(features, factors[k], preferred_element_type=jnp.float32)
        value = jnp.where(same, value, 0.0)
        total = value[:, :FOLD]
        for start in range(FOLD, value.shape[1], FOLD):
            total = total + value[:, start : start + FOLD]
        folded[k] = total


def shrink_sums(place, near, far, factors, row_owner, column_owner):
    rows = row_owner.shape[0]
    return pl.pallas_call(
        shrink_kernel,
        out_shape=jax.ShapeDtypeStruct((2, rows, FOLD), jnp.float32),
        in_specs=[SMEM] + [VMEM] * 5,
        out_specs=VMEM,
        cost_estimate=cost(2 * rows * factors.size, 2 * factors.size),
        compiler_params=pltpu.CompilerParams(vmem_limit_bytes=10 << 20),
    )(place, near, far, factors, row_owner, column_owner)


def joined_kernel(place, near, far, rows, *slabs):
    wide = [part[...].astype(jnp.float32) for part in (near, far)]
    rows[...] = jnp.concatenate(wide, axis=0).astype(rows.dtype)
    if slabs:
        keep, send = slabs
        size = keep.shape[1]
        at = place[0] // 8 * 2 * size
        low, high = [rows[:, pl.ds(pl.multiple_of(at + i * size, size), size)] for i in range(2)]
        first = place[0] // 4 % 2 == 0
        keep[...] = jnp.where(first, low, high)
        send[...] = jnp.where(first, high, low)


def joined(place, near, far, slabs=0):
    part, width = near.shape
    shapes = [(2 * part, width)] + [(2 * part, slabs)] * (2 if slabs else 0)
    return pl.pallas_call(
        joined_kernel,
        out_shape=[jax.ShapeDtypeStruct(shape, near.dtype) for shape in shapes],
        in_specs=[SMEM, VMEM, VMEM],
        out_specs=[VMEM] * len(shapes),
        cost_estimate=cost(0, 8 * near.size),
        compiler_params=pltpu.CompilerParams(vmem_limit_bytes=8 << 20),
    )(place, near, far)


def tiles(sources, targets, sems, tile):
    copies = []
    for i in range(targets[0].shape[1] // tile):
        columns = pl.ds(i * tile, tile)
        copies.append(
            [
                pltpu.make_async_copy(source.at[0, :, columns], target.at[:, columns], sems.at[k, i])
                for k, (source, target) in enumerate(zip(sources, targets))
            ]
        )
        for copy in copies[-1]:
            copy.start()
    return copies


def inner_kernel(tile, place, own, left_y, left_x, right_x, right_y, *refs):
    sources, outs, targets, totals, (rows, sems) = refs[:2], refs[2:6], refs[6:8], refs[8:10], refs[10:]
    copies = tiles(sources, targets, sems, tile)
    part, half = left_y.shape
    wide = [piece[...].astype(jnp.float32) for piece in (own, left_y, left_x, right_x, right_y)]
    own_wide, left_y_wide, left_x_wide, right_x_wide, right_y_wide = wide
    left = jnp.concatenate([own_wide[:, :half], left_y_wide, left_x_wide], axis=0)
    right = jnp.concatenate(
        [own_wide[:, half:], right_y_wide[:part], right_x_wide, right_y_wide[part:]], axis=0
    )
    rows[:, :half] = left.astype(rows.dtype)
    rows[:, half:] = right.astype(rows.dtype)
    for i, pair in enumerate(copies):
        columns = pl.ds(i * tile, tile)
        for copy, target, total in zip(pair, targets, totals):
            copy.wait()
            total[:, columns] = jnp.dot(
                rows[...], target[:, columns], preferred_element_type=jnp.float32
            )
    strip = outs[0].shape[1]
    first = place[0] % 2 == 0
    for total, here, there in zip(totals, outs[::2], outs[1::2]):
        low, high = total[:, :strip], total[:, strip:]
        here[...] = jnp.where(first, low, high)
        there[...] = jnp.where(first, high, low)


def inner(place, own, left, right, gate, up, tile):
    part, width = own.shape
    rows, units = 4 * part, gate.shape[2]
    strip = jax.ShapeDtypeStruct((rows, units // 2), jnp.float32)
    return pl.pallas_call(
        functools.partial(inner_kernel, tile),
        out_shape=[strip] * 4,
        in_specs=[SMEM] + [VMEM] * 5 + [ANY] * 2,
        out_specs=[VMEM] * 4,
        scratch_shapes=[pltpu.VMEM((width, units), gate.dtype)] * 2
        + [pltpu.VMEM((rows, units), jnp.float32)] * 2
        + [pltpu.VMEM((rows, width), own.dtype), pltpu.SemaphoreType.DMA((2, units // tile))],
        cost_estimate=cost(2 * rows * (gate.size + up.size), 2 * (gate.size + up.size)),
        compiler_params=pltpu.CompilerParams(vmem_limit_bytes=44 << 20),
    )(place, own, *left, *right, in_hbm(gate), in_hbm(up))


def hidden_kernel(
    place, folded, row_owner, column_owner, scale, expand, gate, gate_in, up, up_in, hidden
):
    rows, columns = row_owner.shape[0], column_owner.shape[1]
    keep = jnp.where(row_owner[...] == column_owner[...], scale[...], 0.0)
    order = own_order(place[0], rows, 0)
    sums = []
    for k in range(2):
        shrunk = jnp.concatenate([folded[k]] * (columns // FOLD), axis=1) * keep
        shrunk = jnp.dot(
            order, shrunk.astype(jnp.bfloat16), preferred_element_type=jnp.float32
        ).astype(jnp.bfloat16)
        factors = expand[:, k].reshape(columns, expand.shape[3])
        sums.append(jnp.dot(shrunk, factors, preferred_element_type=jnp.float32))
    gate_sum = gate[...] + gate_in[...] + sums[0]
    up_sum = up[...] + up_in[...] + sums[1]
    hidden[...] = (gate_sum / (1.0 + jnp.exp(-gate_sum)) * up_sum).astype(hidden.dtype)


def hidden_strip(*operands):
    expand, gate = operands[5], operands[6]
    return pl.pallas_call(
        hidden_kernel,
        out_shape=jax.ShapeDtypeStruct(gate.shape, jnp.bfloat16),
        in_specs=[SMEM] + [VMEM] * 9,
        out_specs=VMEM,
        cost_estimate=cost(2 * gate.shape[0] * expand.size, 2 * expand.size),
        compiler_params=pltpu.CompilerParams(vmem_limit_bytes=12 << 20),
    )(*operands)


def down_kernel(tile, place, mine, other, weights, *refs):
    outs, (target, sems) = refs[:4], refs[4:]
    copies = tiles([weights], [target], sems, tile)
    first = place[0] % 2 == 0
    hidden = jnp.concatenate(
        [jnp.where(first, mine[...], other[...]), jnp.where(first, other[...], mine[...])], axis=1
    )
    part = hidden.shape[0] // 4
    per_half = len(copies) // 2
    for i, (copy,) in enumerate(copies):
        copy.wait()
        terms = jnp.dot(
            hidden, target[:, i * tile : (i + 1) * tile], preferred_element_type=jnp.float32
        )
        low_y, high_y, far_low, far_high = [terms[k * part : (k + 1) * part] for k in range(4)]
        if i < per_half:
            stays, sends = outs[:2]
            stay, send = (low_y, high_y), (far_low, far_high)
        else:
            stays, sends = outs[2:]
            stay, send = (low_y, far_low), (high_y, far_high)
        columns = pl.ds(i % per_half * tile, tile)
        stays[:, columns] = jnp.concatenate(stay, axis=0)
        sends[:, columns] = jnp.concatenate(send, axis=0).astype(sends.dtype)


def down(place, mine, other, weights, tile):
    rows = mine.shape[0]
    units, width = weights.shape[1:]
    return pl.pallas_call(
        functools.partial(down_kernel, tile),
        out_shape=[
            jax.ShapeDtypeStruct((rows // 2, width // 2), dtype)
            for dtype in (jnp.float32, jnp.bfloat16) * 2
        ],
        in_specs=[SMEM] + [VMEM] * 2 + [ANY],
        out_specs=[VMEM] * 4,
        scratch_shapes=[
            pltpu.VMEM((units, width), weights.dtype),
            pltpu.SemaphoreType.DMA((1, width // tile)),
        ],
        cost_estimate=cost(2 * rows * weights.size, 2 * weights.size),
        compiler_params=pltpu.CompilerParams(vmem_limit_bytes=24 << 20),
    )(place, mine, other, in_hbm(weights))


def halved(terms, apart):
    half = terms.shape[0] // 2
    return terms[:half] + to_chip(terms[half:].astype(jnp.bfloat16), apart)


def shards(tokens, w_gate, w_up, w_down, shrink_factors, expand_factors, rank_blocks, row_counts):
    count = lax.axis_size("tensor")
    units = w_gate.shape[2]
    if count != 32 or units % 256:
        return general_shards(
            tokens, w_gate, w_up, w_down, shrink_factors, expand_factors, rank_blocks, row_counts
        )
    device = lax.axis_index("tensor")
    place = device.reshape(1)
    x = device // 2 % 2
    block_rows, width = tokens.shape[1], tokens.shape[2]
    rows = 16 * block_rows
    slab, half = width // 16, width // 2
    columns = shrink_factors.shape[2]
    blocks = blocks_of(expand_factors, count)

    own = tokens[0]
    (own,) = joined(place, own, to_chip(own, Z2))
    other = to_chip(own, Z1)
    blocks, other = lax.optimization_barrier((blocks, other))

    own, near, other = joined(place, own, other, 2 * slab)
    near = jnp.concatenate([near, to_chip(other, Y)], 0)
    other = to_chip(lax.dynamic_slice_in_dim(near, (1 - x) * slab, slab, 1), X)
    near = lax.dynamic_slice_in_dim(near, x * slab, slab, 1)
    blocks, near, other = lax.optimization_barrier((blocks, near, other))
    expand = lax.all_to_all(blocks, "tensor", split_axis=0, concat_axis=0, tiled=True)

    column_owner, row_owner, scale = owners(rank_blocks, row_counts, columns, rows)
    folded = shrink_sums(place, near, other, shrink_factors, row_owner, column_owner)
    for apart in (Y, X):
        folded = folded + to_chip(folded, apart)
    folded = folded + swapped(folded, "tensor", 0)
    sent = folded.astype(jnp.bfloat16)
    received = [to_chip(sent, apart) for apart in (Z1, Z2, Z1 | Z2)]
    folded = (folded + received[0]) + (received[1].astype(jnp.float32) + received[2])

    left, right = own[:, :half], own[:, half:]
    left_y, right_x = to_chip(left, Y), to_chip(right, X)
    left_x = to_chip(jnp.concatenate([left, left_y], 0), X)
    right_y = to_chip(jnp.concatenate([right, right_x], 0), Y)
    gate, gate_out, up, up_out = inner(
        place, own, (left_y, left_x), (right_x, right_y), w_gate, w_up, 256
    )
    gate_in = swapped(gate_out, "tensor", 0)
    up_in = swapped(up_out, "tensor", 0)
    hidden = hidden_strip(
        place, folded, row_owner, column_owner, scale, expand, gate, gate_in, up, up_in
    )
    other = swapped(hidden, "tensor", 0)
    outs = down(place, hidden, other, w_down, 256)
    sums = []
    for (stays, sends), (first, second) in zip((outs[:2], outs[2:]), ((X, Y), (Y, X))):
        sums.append((stays + to_chip(sends, first), second))
    terms = jnp.concatenate([halved(*pair) for pair in sums], 1)
    for apart in (Z1, Z2):
        terms = halved(terms, apart)
    return terms.astype(jnp.bfloat16)[None]


def solution(mesh):
    placed = (
        P(("groups", "tensor"), None, None),
        P("tensor", None, None),
        P("tensor", None, None),
        P("tensor", None, None),
        P("groups", "tensor", None),
        P("groups", "tensor", None),
        P("groups"),
        P("groups"),
    )
    return jax.shard_map(
        shards,
        mesh=mesh,
        in_specs=placed,
        out_specs=P(("groups", "tensor"), None, None),
        check_vma=False,
    )
```

```python
import functools

import jax
import jax.numpy as jnp
from jax import lax
from jax.experimental import pallas as pl
from jax.experimental.pallas import tpu as pltpu
from jax.sharding import PartitionSpec as P

HIDDEN_BITS = 4
FOLD = 128


def swapped(block, axis, apart):
    count = lax.axis_size(axis)
    return lax.ppermute(block, axis, [(i, i ^ (1 << apart)) for i in range(count)])


def by_target(expand, count):
    kinds, depth, width = expand.shape
    return expand.reshape(kinds, depth, count, width // count).transpose(2, 0, 1, 3)


def owner_of(ends, ids):
    return jnp.sum((ends[None, :] <= ids[:, None]).astype(jnp.int32), axis=1)


def keep_mask(rank_blocks, row_counts, columns, rows):
    adapters = rank_blocks.shape[0]
    earlier = jnp.arange(adapters)[:, None] >= jnp.arange(adapters)[None, :]
    block_end = jnp.sum(jnp.where(earlier, rank_blocks[None, :], 0), axis=1)
    row_end = jnp.sum(jnp.where(earlier, row_counts[None, :], 0), axis=1)
    column_owner = owner_of(block_end, jnp.arange(columns, dtype=jnp.int32) // 16)
    row_owner = owner_of(row_end, jnp.arange(rows, dtype=jnp.int32))
    ids = jnp.arange(adapters, dtype=jnp.int32)
    row_blocks = jnp.sum(
        jnp.where(row_owner[:, None] == ids[None, :], rank_blocks[None, :], 0), axis=1
    )
    same = (row_owner[:, None] == column_owner[None, :]).astype(jnp.float32)
    return same, 1.0 / row_blocks.astype(jnp.float32)


def general_shards(tokens, w_gate, w_up, w_down, shrink_factors, expand_factors, rank_blocks, row_counts):
    count = lax.axis_size("tensor")
    low_bits = count.bit_length() - 1 - HIDDEN_BITS
    fgroups = 1 << low_bits
    place = lax.axis_index("tensor")
    feature_group = place % fgroups
    hidden_group = place // fgroups
    block_rows = tokens.shape[1]
    rows = block_rows << HIDDEN_BITS
    units = w_gate.shape[2]
    strip = units // fgroups

    expand = lax.all_to_all(
        by_target(expand_factors, count), "tensor", split_axis=0, concat_axis=0, tiled=True
    )

    gathered = tokens[0]
    for bit in reversed(range(HIDDEN_BITS)):
        other = swapped(gathered, "tensor", low_bits + bit)
        gathered = jnp.concatenate([gathered, other], 0)
    spots = jnp.arange(1 << HIDDEN_BITS, dtype=jnp.int32)
    moved = sum(((spots >> i) & 1) << (HIDDEN_BITS - 1 - i) for i in range(HIDDEN_BITS))
    natural = (
        (moved ^ hidden_group)[:, None] * block_rows + jnp.arange(block_rows, dtype=jnp.int32)[None, :]
    ).reshape(rows)
    to_own = (natural[:, None] == jnp.arange(rows, dtype=jnp.int32)[None, :]).astype(jnp.bfloat16)

    columns = shrink_factors.shape[2]
    same, scale = keep_mask(rank_blocks, row_counts, columns, rows)
    slab = shrink_factors.shape[1]
    features = lax.dynamic_slice_in_dim(gathered, hidden_group * slab, slab, 1)
    features = jnp.dot(to_own.T, features, preferred_element_type=jnp.float32).astype(jnp.bfloat16)
    partial_value = jnp.einsum(
        "rd,kdc->krc", features, shrink_factors, preferred_element_type=jnp.float32
    )
    folded = jnp.sum((partial_value * same).reshape(2, rows, columns // FOLD, FOLD), axis=2)
    for bit in range(low_bits + HIDDEN_BITS):
        folded = folded + swapped(folded, "tensor", bit)
    shrunk = jnp.tile(folded, (1, 1, columns // FOLD)) * (same * scale[:, None])[None]
    shrunk = shrunk.astype(jnp.bfloat16)
    shrunk = jnp.einsum("or,krc->koc", to_own, shrunk, preferred_element_type=jnp.float32)
    shrunk = shrunk.astype(jnp.bfloat16)

    gate_part = jnp.dot(gathered, w_gate[0], preferred_element_type=jnp.float32)
    up_part = jnp.dot(gathered, w_up[0], preferred_element_type=jnp.float32)
    partials = jnp.stack([gate_part, up_part])
    for step in range(low_bits):
        bit = low_bits - 1 - step
        half = partials.shape[2] // 2
        high = feature_group // (1 << bit) % 2
        outgoing = lax.dynamic_slice_in_dim(partials, (1 - high) * half, half, 2)
        staying = lax.dynamic_slice_in_dim(partials, high * half, half, 2)
        partials = staying + swapped(outgoing, "tensor", bit)
    depth = expand.shape[2]
    low_rank = jnp.einsum(
        "krsd,skdc->krc",
        shrunk.reshape(2, rows, count, depth),
        expand,
        preferred_element_type=jnp.float32,
    )
    partials = partials + low_rank
    hidden = (jax.nn.silu(partials[0]) * partials[1]).astype(jnp.bfloat16)
    for step in range(low_bits):
        other = swapped(hidden, "tensor", step)
        high = feature_group // (1 << step) % 2 == 1
        hidden = jnp.where(
            high, jnp.concatenate([other, hidden], 1), jnp.concatenate([hidden, other], 1)
        )
    terms = jnp.dot(hidden, w_down[0], preferred_element_type=jnp.float32)
    for bit in range(HIDDEN_BITS):
        half = terms.shape[0] // 2
        outgoing = terms[half:].astype(jnp.bfloat16)
        terms = terms[:half] + swapped(outgoing, "tensor", low_bits + bit).astype(jnp.float32)
    return terms.astype(jnp.bfloat16)[None]


def owners(rank_blocks, row_counts, columns, rows):
    adapters = rank_blocks.shape[0]
    ids = jnp.arange(adapters, dtype=jnp.int32)
    earlier = ids[:, None] >= ids[None, :]
    block_end = jnp.sum(jnp.where(earlier, rank_blocks[None, :], 0), axis=1)
    row_end = jnp.sum(jnp.where(earlier, row_counts[None, :], 0), axis=1)
    column_owner = owner_of(block_end, jnp.arange(columns, dtype=jnp.int32) // 16)
    row_owner = owner_of(row_end, jnp.arange(rows, dtype=jnp.int32))
    row_blocks = jnp.sum(
        jnp.where(row_owner[:, None] == ids[None, :], rank_blocks[None, :], 0), axis=1
    )
    scale = 1.0 / row_blocks.astype(jnp.float32)
    return column_owner[None, :], row_owner[:, None], scale[:, None]


VMEM = pl.BlockSpec(memory_space=pltpu.VMEM)
SMEM = pl.BlockSpec(memory_space=pltpu.SMEM)
ANY = pl.BlockSpec(memory_space=pl.ANY)
X, Y, Z1, Z2 = 1, 2, 4, 8


def to_chip(block, apart):
    count = lax.axis_size("tensor")
    return lax.ppermute(block, "tensor", [(i, i ^ (apart << 1)) for i in range(count)])


def cost(flops, read):
    return pl.CostEstimate(flops=flops, bytes_accessed=read, transcendentals=0)


def in_hbm(array):
    return pltpu.with_memory_space_constraint(array, pltpu.HBM)


def blocks_kernel(count, strip, source, target):
    for j in range(count):
        target[j] = source[:, :, j * strip : (j + 1) * strip]


def blocks_of(expand, count):
    kinds, depth, width = expand.shape
    strip = width // count
    return pl.pallas_call(
        functools.partial(blocks_kernel, count, strip),
        out_shape=jax.ShapeDtypeStruct((count, kinds, depth, strip), expand.dtype),
        in_specs=[VMEM],
        out_specs=VMEM,
        cost_estimate=cost(0, 4 * expand.size),
        compiler_params=pltpu.CompilerParams(vmem_limit_bytes=10 << 20),
    )(expand)


def own_order(place, rows, own_axis):
    block = rows // 16
    own, natural = [lax.broadcasted_iota(jnp.int32, (rows, rows), axis) for axis in (own_axis, 1 - own_axis)]
    spot = own // block
    far = spot // 8 + spot // 4 % 2 * 2 + spot // 2 % 2 * 4 + spot % 2 * 8
    return ((far ^ (place // 2)) * block + (own - spot * block) == natural).astype(jnp.bfloat16)


def shrink_kernel(place, near, far, factors, row_owner, column_owner, folded):
    same = row_owner[...] == column_owner[...]
    rows = row_owner.shape[0]
    features = jnp.concatenate([near[...], far[...]], axis=0)
    features = jnp.dot(
        own_order(place[0], rows, 1), features, preferred_element_type=jnp.float32
    ).astype(jnp.bfloat16)
    for k in range(2):
        value = jnp.dot(features, factors[k], preferred_element_type=jnp.float32)
        value = jnp.where(same, value, 0.0)
        total = value[:, :FOLD]
        for start in range(FOLD, value.shape[1], FOLD):
            total = total + value[:, start : start + FOLD]
        folded[k] = total


def shrink_sums(place, near, far, factors, row_owner, column_owner):
    rows = row_owner.shape[0]
    return pl.pallas_call(
        shrink_kernel,
        out_shape=jax.ShapeDtypeStruct((2, rows, FOLD), jnp.float32),
        in_specs=[SMEM] + [VMEM] * 5,
        out_specs=VMEM,
        cost_estimate=cost(2 * rows * factors.size, 2 * factors.size),
        compiler_params=pltpu.CompilerParams(vmem_limit_bytes=10 << 20),
    )(place, near, far, factors, row_owner, column_owner)


def joined_kernel(place, near, far, rows, *slabs):
    wide = [part[...].astype(jnp.float32) for part in (near, far)]
    rows[...] = jnp.concatenate(wide, axis=0).astype(rows.dtype)
    if slabs:
        keep, send = slabs
        size = keep.shape[1]
        at = place[0] // 8 * 2 * size
        low, high = [rows[:, pl.ds(pl.multiple_of(at + i * size, size), size)] for i in range(2)]
        first = place[0] // 4 % 2 == 0
        keep[...] = jnp.where(first, low, high)
        send[...] = jnp.where(first, high, low)


def joined(place, near, far, slabs=0):
    part, width = near.shape
    shapes = [(2 * part, width)] + [(2 * part, slabs)] * (2 if slabs else 0)
    return pl.pallas_call(
        joined_kernel,
        out_shape=[jax.ShapeDtypeStruct(shape, near.dtype) for shape in shapes],
        in_specs=[SMEM, VMEM, VMEM],
        out_specs=[VMEM] * len(shapes),
        cost_estimate=cost(0, 8 * near.size),
        compiler_params=pltpu.CompilerParams(vmem_limit_bytes=8 << 20),
    )(place, near, far)


def chunks(width, most):
    return [(at, min(most, width - at)) for at in range(0, width, most)]


def started(sources, targets, sems, most, start=0):
    copies = []
    for i, (at, size) in enumerate(chunks(targets[0].shape[1], most)):
        copies.append(
            [
                pltpu.make_async_copy(
                    source.at[0, :, pl.ds(start + at, size)], target.at[:, pl.ds(at, size)], sems.at[k, i]
                )
                for k, (source, target) in enumerate(zip(sources, targets))
            ]
        )
        for copy in copies[-1]:
            copy.start()
    return copies


def inner_kernel(most, tile, place, own, left_y, left_x, right_x, right_y, *refs):
    sources, outs, targets, totals, (rows, sems) = refs[:2], refs[2:6], refs[6:8], refs[8:10], refs[10:]
    copies = started(sources, targets, sems, most)
    part, half = left_y.shape
    wide = [piece[...].astype(jnp.float32) for piece in (own, left_y, left_x, right_x, right_y)]
    own_wide, left_y_wide, left_x_wide, right_x_wide, right_y_wide = wide
    left = jnp.concatenate([own_wide[:, :half], left_y_wide, left_x_wide], axis=0)
    right = jnp.concatenate(
        [own_wide[:, half:], right_y_wide[:part], right_x_wide, right_y_wide[part:]], axis=0
    )
    rows[:, :half] = left.astype(rows.dtype)
    rows[:, half:] = right.astype(rows.dtype)
    for (at, size), pair in zip(chunks(targets[0].shape[1], most), copies):
        for copy, target, total in zip(pair, targets, totals):
            copy.wait()
            for inside, wide in chunks(size, tile):
                columns = pl.ds(at + inside, wide)
                total[:, columns] = jnp.dot(
                    rows[...], target[:, columns], preferred_element_type=jnp.float32
                )
    strip = outs[0].shape[1]
    first = place[0] % 2 == 0
    for total, here, there in zip(totals, outs[::2], outs[1::2]):
        low, high = total[:, :strip], total[:, strip:]
        here[...] = jnp.where(first, low, high)
        there[...] = jnp.where(first, high, low)


def inner(place, own, left, right, gate, up, most, tile):
    part, width = own.shape
    rows, units = 4 * part, gate.shape[2]
    strip = jax.ShapeDtypeStruct((rows, units // 2), jnp.float32)
    return pl.pallas_call(
        functools.partial(inner_kernel, most, tile),
        out_shape=[strip] * 4,
        in_specs=[SMEM] + [VMEM] * 5 + [ANY] * 2,
        out_specs=[VMEM] * 4,
        scratch_shapes=[pltpu.VMEM((width, units), gate.dtype)] * 2
        + [pltpu.VMEM((rows, units), jnp.float32)] * 2
        + [pltpu.VMEM((rows, width), own.dtype), pltpu.SemaphoreType.DMA((2, len(chunks(units, most))))],
        cost_estimate=cost(2 * rows * (gate.size + up.size), 2 * (gate.size + up.size)),
        compiler_params=pltpu.CompilerParams(vmem_limit_bytes=44 << 20),
    )(place, own, *left, *right, in_hbm(gate), in_hbm(up))


def hidden_kernel(
    place, folded, row_owner, column_owner, scale, expand, gate, gate_in, up, up_in, hidden
):
    rows, columns = row_owner.shape[0], column_owner.shape[1]
    keep = jnp.where(row_owner[...] == column_owner[...], scale[...], 0.0)
    order = own_order(place[0], rows, 0)
    sums = []
    for k in range(2):
        shrunk = jnp.concatenate([folded[k]] * (columns // FOLD), axis=1) * keep
        shrunk = jnp.dot(
            order, shrunk.astype(jnp.bfloat16), preferred_element_type=jnp.float32
        ).astype(jnp.bfloat16)
        factors = expand[:, k].reshape(columns, expand.shape[3])
        sums.append(jnp.dot(shrunk, factors, preferred_element_type=jnp.float32))
    gate_sum = gate[...] + gate_in[...] + sums[0]
    up_sum = up[...] + up_in[...] + sums[1]
    hidden[...] = (gate_sum / (1.0 + jnp.exp(-gate_sum)) * up_sum).astype(hidden.dtype)


def hidden_strip(*operands):
    expand, gate = operands[5], operands[6]
    return pl.pallas_call(
        hidden_kernel,
        out_shape=jax.ShapeDtypeStruct(gate.shape, jnp.bfloat16),
        in_specs=[SMEM] + [VMEM] * 9,
        out_specs=VMEM,
        cost_estimate=cost(2 * gate.shape[0] * expand.size, 2 * expand.size),
        compiler_params=pltpu.CompilerParams(vmem_limit_bytes=12 << 20),
    )(*operands)


def down_kernel(x_first, start, most, tile, place, mine, other, weights, stays, sends, target, sems):
    copies = started([weights], [target], sems, most, start)
    first = place[0] % 2 == 0
    hidden = jnp.concatenate(
        [jnp.where(first, mine[...], other[...]), jnp.where(first, other[...], mine[...])], axis=1
    )
    part = hidden.shape[0] // 4
    for (at, size), (copy,) in zip(chunks(target.shape[1], most), copies):
        copy.wait()
        for inside, wide in chunks(size, tile):
            columns = pl.ds(at + inside, wide)
            terms = jnp.dot(hidden, target[:, columns], preferred_element_type=jnp.float32)
            low_y, high_y, far_low, far_high = [terms[k * part : (k + 1) * part] for k in range(4)]
            if x_first:
                stay, send = (low_y, high_y), (far_low, far_high)
            else:
                stay, send = (low_y, far_low), (high_y, far_high)
            stays[:, columns] = jnp.concatenate(stay, axis=0)
            sends[:, columns] = jnp.concatenate(send, axis=0).astype(sends.dtype)


def down(x_first, place, mine, other, weights, start, width, most, tile):
    rows, units = mine.shape[0], weights.shape[1]
    return pl.pallas_call(
        functools.partial(down_kernel, x_first, start, most, tile),
        out_shape=[
            jax.ShapeDtypeStruct((rows // 2, width), dtype) for dtype in (jnp.float32, jnp.bfloat16)
        ],
        in_specs=[SMEM] + [VMEM] * 2 + [ANY],
        out_specs=[VMEM] * 2,
        scratch_shapes=[
            pltpu.VMEM((units, width), weights.dtype),
            pltpu.SemaphoreType.DMA((1, len(chunks(width, most)))),
        ],
        cost_estimate=cost(2 * rows * units * width, 2 * units * width),
        compiler_params=pltpu.CompilerParams(vmem_limit_bytes=16 << 20),
    )(place, mine, other, in_hbm(weights))


def halved(terms, apart):
    half = terms.shape[0] // 2
    return terms[:half] + to_chip(terms[half:].astype(jnp.bfloat16), apart)


def shards(tokens, w_gate, w_up, w_down, shrink_factors, expand_factors, rank_blocks, row_counts):
    count = lax.axis_size("tensor")
    units = w_gate.shape[2]
    if count != 32 or units % 256:
        return general_shards(
            tokens, w_gate, w_up, w_down, shrink_factors, expand_factors, rank_blocks, row_counts
        )
    device = lax.axis_index("tensor")
    place = device.reshape(1)
    x = device // 2 % 2
    block_rows, width = tokens.shape[1], tokens.shape[2]
    rows = 16 * block_rows
    slab, half = width // 16, width // 2
    columns = shrink_factors.shape[2]
    blocks = blocks_of(expand_factors, count)

    own = tokens[0]
    (own,) = joined(place, own, to_chip(own, Z2))
    other = to_chip(own, Z1)
    blocks, other = lax.optimization_barrier((blocks, other))

    own, near, other = joined(place, own, other, 2 * slab)
    blocks, own, near, other = lax.optimization_barrier((blocks, own, near, other))
    expand = lax.all_to_all(blocks, "tensor", split_axis=0, concat_axis=0, tiled=True)

    near = jnp.concatenate([near, to_chip(other, Y)], 0)
    other = to_chip(lax.dynamic_slice_in_dim(near, (1 - x) * slab, slab, 1), X)
    near = lax.dynamic_slice_in_dim(near, x * slab, slab, 1)
    column_owner, row_owner, scale = owners(rank_blocks, row_counts, columns, rows)
    folded = shrink_sums(place, near, other, shrink_factors, row_owner, column_owner)
    folded = folded + swapped(folded, "tensor", 0)
    for apart in (Y, X):
        folded = folded + to_chip(folded, apart)
    sent = folded.astype(jnp.bfloat16)
    received = [to_chip(sent, apart) for apart in (Z1, Z2, Z1 | Z2)]
    folded = (folded + received[0]) + (received[1].astype(jnp.float32) + received[2])

    left, right = own[:, :half], own[:, half:]
    left_y, right_x = to_chip(left, Y), to_chip(right, X)
    left_x = to_chip(jnp.concatenate([left, left_y], 0), X)
    right_y = to_chip(jnp.concatenate([right, right_x], 0), Y)
    gate, gate_out, up, up_out = inner(
        place, own, (left_y, left_x), (right_x, right_y), w_gate, w_up, 512, 256
    )
    gate_in = swapped(gate_out, "tensor", 0)
    up_in = swapped(up_out, "tensor", 0)
    hidden = hidden_strip(
        place, folded, row_owner, column_owner, scale, expand, gate, gate_in, up, up_in
    )
    other = swapped(hidden, "tensor", 0)
    sums = []
    for x_first, first, second in ((True, X, Y), (False, Y, X)):
        start = 0 if x_first else half
        stays, sends = down(x_first, place, hidden, other, w_down, start, half, 512, 256)
        sums.append((stays + to_chip(sends, first), second))
    terms = jnp.concatenate([halved(*pair) for pair in sums], 1)
    for apart in (Z1, Z2):
        terms = halved(terms, apart)
    return terms.astype(jnp.bfloat16)[None]


def solution(mesh):
    placed = (
        P(("groups", "tensor"), None, None),
        P("tensor", None, None),
        P("tensor", None, None),
        P("tensor", None, None),
        P("groups", "tensor", None),
        P("groups", "tensor", None),
        P("groups"),
        P("groups"),
    )
    return jax.shard_map(
        shards,
        mesh=mesh,
        in_specs=placed,
        out_specs=P(("groups", "tensor"), None, None),
        check_vma=False,
    )
```

```python
import functools

import jax
import jax.numpy as jnp
from jax import lax
from jax.experimental import pallas as pl
from jax.experimental.pallas import tpu as pltpu
from jax.sharding import PartitionSpec as P

HIDDEN_BITS = 4
FOLD = 128


def swapped(block, axis, apart):
    count = lax.axis_size(axis)
    return lax.ppermute(block, axis, [(i, i ^ (1 << apart)) for i in range(count)])


def by_target(expand, count):
    kinds, depth, width = expand.shape
    return expand.reshape(kinds, depth, count, width // count).transpose(2, 0, 1, 3)


def owner_of(ends, ids):
    return jnp.sum((ends[None, :] <= ids[:, None]).astype(jnp.int32), axis=1)


def keep_mask(rank_blocks, row_counts, columns, rows):
    adapters = rank_blocks.shape[0]
    earlier = jnp.arange(adapters)[:, None] >= jnp.arange(adapters)[None, :]
    block_end = jnp.sum(jnp.where(earlier, rank_blocks[None, :], 0), axis=1)
    row_end = jnp.sum(jnp.where(earlier, row_counts[None, :], 0), axis=1)
    column_owner = owner_of(block_end, jnp.arange(columns, dtype=jnp.int32) // 16)
    row_owner = owner_of(row_end, jnp.arange(rows, dtype=jnp.int32))
    ids = jnp.arange(adapters, dtype=jnp.int32)
    row_blocks = jnp.sum(
        jnp.where(row_owner[:, None] == ids[None, :], rank_blocks[None, :], 0), axis=1
    )
    same = (row_owner[:, None] == column_owner[None, :]).astype(jnp.float32)
    return same, 1.0 / row_blocks.astype(jnp.float32)


def general_shards(tokens, w_gate, w_up, w_down, shrink_factors, expand_factors, rank_blocks, row_counts):
    count = lax.axis_size("tensor")
    low_bits = count.bit_length() - 1 - HIDDEN_BITS
    fgroups = 1 << low_bits
    place = lax.axis_index("tensor")
    feature_group = place % fgroups
    hidden_group = place // fgroups
    block_rows = tokens.shape[1]
    rows = block_rows << HIDDEN_BITS
    units = w_gate.shape[2]
    strip = units // fgroups

    expand = lax.all_to_all(
        by_target(expand_factors, count), "tensor", split_axis=0, concat_axis=0, tiled=True
    )

    gathered = tokens[0]
    for bit in reversed(range(HIDDEN_BITS)):
        other = swapped(gathered, "tensor", low_bits + bit)
        gathered = jnp.concatenate([gathered, other], 0)
    spots = jnp.arange(1 << HIDDEN_BITS, dtype=jnp.int32)
    moved = sum(((spots >> i) & 1) << (HIDDEN_BITS - 1 - i) for i in range(HIDDEN_BITS))
    natural = (
        (moved ^ hidden_group)[:, None] * block_rows + jnp.arange(block_rows, dtype=jnp.int32)[None, :]
    ).reshape(rows)
    to_own = (natural[:, None] == jnp.arange(rows, dtype=jnp.int32)[None, :]).astype(jnp.bfloat16)

    columns = shrink_factors.shape[2]
    same, scale = keep_mask(rank_blocks, row_counts, columns, rows)
    slab = shrink_factors.shape[1]
    features = lax.dynamic_slice_in_dim(gathered, hidden_group * slab, slab, 1)
    features = jnp.dot(to_own.T, features, preferred_element_type=jnp.float32).astype(jnp.bfloat16)
    partial_value = jnp.einsum(
        "rd,kdc->krc", features, shrink_factors, preferred_element_type=jnp.float32
    )
    folded = jnp.sum((partial_value * same).reshape(2, rows, columns // FOLD, FOLD), axis=2)
    for bit in range(low_bits + HIDDEN_BITS):
        folded = folded + swapped(folded, "tensor", bit)
    shrunk = jnp.tile(folded, (1, 1, columns // FOLD)) * (same * scale[:, None])[None]
    shrunk = shrunk.astype(jnp.bfloat16)
    shrunk = jnp.einsum("or,krc->koc", to_own, shrunk, preferred_element_type=jnp.float32)
    shrunk = shrunk.astype(jnp.bfloat16)

    gate_part = jnp.dot(gathered, w_gate[0], preferred_element_type=jnp.float32)
    up_part = jnp.dot(gathered, w_up[0], preferred_element_type=jnp.float32)
    partials = jnp.stack([gate_part, up_part])
    for step in range(low_bits):
        bit = low_bits - 1 - step
        half = partials.shape[2] // 2
        high = feature_group // (1 << bit) % 2
        outgoing = lax.dynamic_slice_in_dim(partials, (1 - high) * half, half, 2)
        staying = lax.dynamic_slice_in_dim(partials, high * half, half, 2)
        partials = staying + swapped(outgoing, "tensor", bit)
    depth = expand.shape[2]
    low_rank = jnp.einsum(
        "krsd,skdc->krc",
        shrunk.reshape(2, rows, count, depth),
        expand,
        preferred_element_type=jnp.float32,
    )
    partials = partials + low_rank
    hidden = (jax.nn.silu(partials[0]) * partials[1]).astype(jnp.bfloat16)
    for step in range(low_bits):
        other = swapped(hidden, "tensor", step)
        high = feature_group // (1 << step) % 2 == 1
        hidden = jnp.where(
            high, jnp.concatenate([other, hidden], 1), jnp.concatenate([hidden, other], 1)
        )
    terms = jnp.dot(hidden, w_down[0], preferred_element_type=jnp.float32)
    for bit in range(HIDDEN_BITS):
        half = terms.shape[0] // 2
        outgoing = terms[half:].astype(jnp.bfloat16)
        terms = terms[:half] + swapped(outgoing, "tensor", low_bits + bit).astype(jnp.float32)
    return terms.astype(jnp.bfloat16)[None]


def owners(rank_blocks, row_counts, columns, rows):
    adapters = rank_blocks.shape[0]
    ids = jnp.arange(adapters, dtype=jnp.int32)
    earlier = ids[:, None] >= ids[None, :]
    block_end = jnp.sum(jnp.where(earlier, rank_blocks[None, :], 0), axis=1)
    row_end = jnp.sum(jnp.where(earlier, row_counts[None, :], 0), axis=1)
    column_owner = owner_of(block_end, jnp.arange(columns, dtype=jnp.int32) // 16)
    row_owner = owner_of(row_end, jnp.arange(rows, dtype=jnp.int32))
    row_blocks = jnp.sum(
        jnp.where(row_owner[:, None] == ids[None, :], rank_blocks[None, :], 0), axis=1
    )
    scale = 1.0 / row_blocks.astype(jnp.float32)
    return column_owner[None, :], row_owner[:, None], scale[:, None]


VMEM = pl.BlockSpec(memory_space=pltpu.VMEM)
SMEM = pl.BlockSpec(memory_space=pltpu.SMEM)
ANY = pl.BlockSpec(memory_space=pl.ANY)
X, Y, Z1, Z2 = 1, 2, 4, 8


def to_chip(block, apart):
    count = lax.axis_size("tensor")
    return lax.ppermute(block, "tensor", [(i, i ^ (apart << 1)) for i in range(count)])


def cost(flops, read):
    return pl.CostEstimate(flops=flops, bytes_accessed=read, transcendentals=0)


def in_hbm(array):
    return pltpu.with_memory_space_constraint(array, pltpu.HBM)


def blocks_kernel(count, strip, source, target):
    for j in range(count):
        target[j] = source[:, :, j * strip : (j + 1) * strip]


def blocks_of(expand, count):
    kinds, depth, width = expand.shape
    strip = width // count
    return pl.pallas_call(
        functools.partial(blocks_kernel, count, strip),
        out_shape=jax.ShapeDtypeStruct((count, kinds, depth, strip), expand.dtype),
        in_specs=[VMEM],
        out_specs=VMEM,
        cost_estimate=cost(0, 4 * expand.size),
        compiler_params=pltpu.CompilerParams(vmem_limit_bytes=10 << 20),
    )(expand)


def own_order(place, rows, own_axis):
    block = rows // 16
    own, natural = [lax.broadcasted_iota(jnp.int32, (rows, rows), axis) for axis in (own_axis, 1 - own_axis)]
    spot = own // block
    far = spot // 8 + spot // 4 % 2 * 2 + spot // 2 % 2 * 4 + spot % 2 * 8
    return ((far ^ (place // 2)) * block + (own - spot * block) == natural).astype(jnp.bfloat16)


def shrink_kernel(place, near, far, factors, row_owner, column_owner, folded):
    same = row_owner[...] == column_owner[...]
    rows = row_owner.shape[0]
    features = jnp.concatenate([near[...], far[...]], axis=0)
    features = jnp.dot(
        own_order(place[0], rows, 1), features, preferred_element_type=jnp.float32
    ).astype(jnp.bfloat16)
    for k in range(2):
        value = jnp.dot(features, factors[k], preferred_element_type=jnp.float32)
        value = jnp.where(same, value, 0.0)
        total = value[:, :FOLD]
        for start in range(FOLD, value.shape[1], FOLD):
            total = total + value[:, start : start + FOLD]
        folded[k] = total


def shrink_sums(place, near, far, factors, row_owner, column_owner):
    rows = row_owner.shape[0]
    return pl.pallas_call(
        shrink_kernel,
        out_shape=jax.ShapeDtypeStruct((2, rows, FOLD), jnp.float32),
        in_specs=[SMEM] + [VMEM] * 5,
        out_specs=VMEM,
        cost_estimate=cost(2 * rows * factors.size, 2 * factors.size),
        compiler_params=pltpu.CompilerParams(vmem_limit_bytes=10 << 20),
    )(place, near, far, factors, row_owner, column_owner)


def joined_kernel(place, near, far, rows, *slabs):
    wide = [part[...].astype(jnp.float32) for part in (near, far)]
    rows[...] = jnp.concatenate(wide, axis=0).astype(rows.dtype)
    if slabs:
        keep, send = slabs
        size = keep.shape[1]
        at = place[0] // 8 * 2 * size
        low, high = [rows[:, pl.ds(pl.multiple_of(at + i * size, size), size)] for i in range(2)]
        first = place[0] // 4 % 2 == 0
        keep[...] = jnp.where(first, low, high)
        send[...] = jnp.where(first, high, low)


def joined(place, near, far, slabs=0):
    part, width = near.shape
    shapes = [(2 * part, width)] + [(2 * part, slabs)] * (2 if slabs else 0)
    return pl.pallas_call(
        joined_kernel,
        out_shape=[jax.ShapeDtypeStruct(shape, near.dtype) for shape in shapes],
        in_specs=[SMEM, VMEM, VMEM],
        out_specs=[VMEM] * len(shapes),
        cost_estimate=cost(0, 8 * near.size),
        compiler_params=pltpu.CompilerParams(vmem_limit_bytes=8 << 20),
    )(place, near, far)


def chunks(width, most):
    return [(at, min(most, width - at)) for at in range(0, width, most)]


def started(sources, targets, sems, most, start=0):
    copies = []
    for i, (at, size) in enumerate(chunks(targets[0].shape[1], most)):
        copies.append(
            [
                pltpu.make_async_copy(
                    source.at[0, :, pl.ds(start + at, size)], target.at[:, pl.ds(at, size)], sems.at[k, i]
                )
                for k, (source, target) in enumerate(zip(sources, targets))
            ]
        )
        for copy in copies[-1]:
            copy.start()
    return copies


def inner_kernel(most, tile, place, own, left_y, left_x, right_x, right_y, *refs):
    sources, outs, targets, totals, (rows, sems) = refs[:2], refs[2:6], refs[6:8], refs[8:10], refs[10:]
    copies = started(sources, targets, sems, most)
    part, half = left_y.shape
    wide = [piece[...].astype(jnp.float32) for piece in (own, left_y, left_x, right_x, right_y)]
    own_wide, left_y_wide, left_x_wide, right_x_wide, right_y_wide = wide
    left = jnp.concatenate([own_wide[:, :half], left_y_wide, left_x_wide], axis=0)
    right = jnp.concatenate(
        [own_wide[:, half:], right_y_wide[:part], right_x_wide, right_y_wide[part:]], axis=0
    )
    rows[:, :half] = left.astype(rows.dtype)
    rows[:, half:] = right.astype(rows.dtype)
    for (at, size), pair in zip(chunks(targets[0].shape[1], most), copies):
        for copy, target, total in zip(pair, targets, totals):
            copy.wait()
            for inside, wide in chunks(size, tile):
                columns = pl.ds(at + inside, wide)
                total[:, columns] = jnp.dot(
                    rows[...], target[:, columns], preferred_element_type=jnp.float32
                )
    strip = outs[0].shape[1]
    first = place[0] % 2 == 0
    for total, here, there in zip(totals, outs[::2], outs[1::2]):
        low, high = total[:, :strip], total[:, strip:]
        here[...] = jnp.where(first, low, high)
        there[...] = jnp.where(first, high, low)


def inner(place, own, left, right, gate, up, most, tile):
    part, width = own.shape
    rows, units = 4 * part, gate.shape[2]
    strip = jax.ShapeDtypeStruct((rows, units // 2), jnp.float32)
    return pl.pallas_call(
        functools.partial(inner_kernel, most, tile),
        out_shape=[strip] * 4,
        in_specs=[SMEM] + [VMEM] * 5 + [ANY] * 2,
        out_specs=[VMEM] * 4,
        scratch_shapes=[pltpu.VMEM((width, units), gate.dtype)] * 2
        + [pltpu.VMEM((rows, units), jnp.float32)] * 2
        + [pltpu.VMEM((rows, width), own.dtype), pltpu.SemaphoreType.DMA((2, len(chunks(units, most))))],
        cost_estimate=cost(2 * rows * (gate.size + up.size), 2 * (gate.size + up.size)),
        compiler_params=pltpu.CompilerParams(vmem_limit_bytes=44 << 20),
    )(place, own, *left, *right, in_hbm(gate), in_hbm(up))


def hidden_kernel(
    place, folded, near, far, both, row_owner, column_owner, scale, expand, gate, gate_in, up, up_in, hidden
):
    rows, columns = row_owner.shape[0], column_owner.shape[1]
    keep = jnp.where(row_owner[...] == column_owner[...], scale[...], 0.0)
    order = own_order(place[0], rows, 0)
    sums = []
    for k in range(2):
        planes = [part[k].astype(jnp.float32) for part in (near, far, both)]
        total = (folded[k] + planes[0]) + (planes[1] + planes[2])
        shrunk = jnp.concatenate([total] * (columns // FOLD), axis=1) * keep
        shrunk = jnp.dot(
            order, shrunk.astype(jnp.bfloat16), preferred_element_type=jnp.float32
        ).astype(jnp.bfloat16)
        factors = expand[:, k].reshape(columns, expand.shape[3])
        sums.append(jnp.dot(shrunk, factors, preferred_element_type=jnp.float32))
    gate_sum = gate[...] + gate_in[...] + sums[0]
    up_sum = up[...] + up_in[...] + sums[1]
    hidden[...] = (gate_sum / (1.0 + jnp.exp(-gate_sum)) * up_sum).astype(hidden.dtype)


def hidden_strip(*operands):
    expand, gate = operands[8], operands[9]
    return pl.pallas_call(
        hidden_kernel,
        out_shape=jax.ShapeDtypeStruct(gate.shape, jnp.bfloat16),
        in_specs=[SMEM] + [VMEM] * 12,
        out_specs=VMEM,
        cost_estimate=cost(2 * gate.shape[0] * expand.size, 2 * expand.size),
        compiler_params=pltpu.CompilerParams(vmem_limit_bytes=12 << 20),
    )(*operands)


def down_kernel(x_first, start, most, tile, place, mine, other, weights, stays, sends, target, sems):
    copies = started([weights], [target], sems, most, start)
    first = place[0] % 2 == 0
    hidden = jnp.concatenate(
        [jnp.where(first, mine[...], other[...]), jnp.where(first, other[...], mine[...])], axis=1
    )
    part = hidden.shape[0] // 4
    for (at, size), (copy,) in zip(chunks(target.shape[1], most), copies):
        copy.wait()
        for inside, wide in chunks(size, tile):
            columns = pl.ds(at + inside, wide)
            terms = jnp.dot(hidden, target[:, columns], preferred_element_type=jnp.float32)
            low_y, high_y, far_low, far_high = [terms[k * part : (k + 1) * part] for k in range(4)]
            if x_first:
                stay, send = (low_y, high_y), (far_low, far_high)
            else:
                stay, send = (low_y, far_low), (high_y, far_high)
            stays[:, columns] = jnp.concatenate(stay, axis=0)
            sends[:, columns] = jnp.concatenate(send, axis=0).astype(sends.dtype)


def down(x_first, place, mine, other, weights, start, width, most, tile):
    rows, units = mine.shape[0], weights.shape[1]
    return pl.pallas_call(
        functools.partial(down_kernel, x_first, start, most, tile),
        out_shape=[
            jax.ShapeDtypeStruct((rows // 2, width), dtype) for dtype in (jnp.float32, jnp.bfloat16)
        ],
        in_specs=[SMEM] + [VMEM] * 2 + [ANY],
        out_specs=[VMEM] * 2,
        scratch_shapes=[
            pltpu.VMEM((units, width), weights.dtype),
            pltpu.SemaphoreType.DMA((1, len(chunks(width, most)))),
        ],
        cost_estimate=cost(2 * rows * units * width, 2 * units * width),
        compiler_params=pltpu.CompilerParams(vmem_limit_bytes=16 << 20),
    )(place, mine, other, in_hbm(weights))


def split_kernel(left, left_in, right, right_in, left_stay, right_stay, send):
    totals = [
        part[...] + received[...].astype(jnp.float32)
        for part, received in ((left, left_in), (right, right_in))
    ]
    half = left_stay.shape[0]
    left_stay[...], right_stay[...] = [total[:half] for total in totals]
    send[...] = jnp.concatenate([total[half:] for total in totals], axis=0).astype(send.dtype)


def split_kernel_last(left, right, received, stay, send):
    rows, width = left.shape
    half, piece = rows // 2, width // 2
    wide = received[...].astype(jnp.float32)
    totals = [left[...] + wide[:rows], right[...] + wide[rows:]]
    stay[...] = jnp.concatenate([total[:half] for total in totals], axis=1)
    send[...] = jnp.concatenate(
        [total[half:, at : at + piece] for total in totals for at in (0, piece)], axis=0
    ).astype(send.dtype)


def last_kernel(stay, received, out):
    rows = stay.shape[0]
    wide = received[...].astype(jnp.float32)
    pieces = [wide[i * rows : (i + 1) * rows] for i in range(4)]
    out[0] = (stay[...] + jnp.concatenate(pieces, axis=1)).astype(out.dtype)


def small(kernel, shapes, *operands):
    return pl.pallas_call(
        kernel,
        out_shape=[jax.ShapeDtypeStruct(shape, dtype) for shape, dtype in shapes],
        in_specs=[VMEM] * len(operands),
        out_specs=[VMEM] * len(shapes),
        cost_estimate=cost(0, 1 << 20),
        compiler_params=pltpu.CompilerParams(vmem_limit_bytes=8 << 20),
    )(*operands)


def shards(tokens, w_gate, w_up, w_down, shrink_factors, expand_factors, rank_blocks, row_counts):
    count = lax.axis_size("tensor")
    units = w_gate.shape[2]
    if count != 32 or units % 256:
        return general_shards(
            tokens, w_gate, w_up, w_down, shrink_factors, expand_factors, rank_blocks, row_counts
        )
    device = lax.axis_index("tensor")
    place = device.reshape(1)
    x = device // 2 % 2
    block_rows, width = tokens.shape[1], tokens.shape[2]
    rows = 16 * block_rows
    slab, half = width // 16, width // 2
    columns = shrink_factors.shape[2]
    blocks = blocks_of(expand_factors, count)

    own = tokens[0]
    (own,) = joined(place, own, to_chip(own, Z2))
    other = to_chip(own, Z1)
    blocks, other = lax.optimization_barrier((blocks, other))

    own, near, other = joined(place, own, other, 2 * slab)
    blocks, own, near, other = lax.optimization_barrier((blocks, own, near, other))
    expand = lax.all_to_all(blocks, "tensor", split_axis=0, concat_axis=0, tiled=True)

    near = jnp.concatenate([near, to_chip(other, Y)], 0)
    other = to_chip(lax.dynamic_slice_in_dim(near, (1 - x) * slab, slab, 1), X)
    near = lax.dynamic_slice_in_dim(near, x * slab, slab, 1)
    column_owner, row_owner, scale = owners(rank_blocks, row_counts, columns, rows)
    folded = shrink_sums(place, near, other, shrink_factors, row_owner, column_owner)
    folded = folded + swapped(folded, "tensor", 0)
    for apart in (Y, X):
        folded = folded + to_chip(folded, apart)
    left, right = own[:, :half], own[:, half:]
    left_y, right_x = to_chip(left, Y), to_chip(right, X)
    left_y, right_x, folded = lax.optimization_barrier((left_y, right_x, folded))
    sent = folded.astype(jnp.bfloat16)
    received = [to_chip(sent, apart) for apart in (Z1, Z2, Z1 | Z2)]
    left_x = to_chip(jnp.concatenate([left, left_y], 0), X)
    right_y = to_chip(jnp.concatenate([right, right_x], 0), Y)
    gate, gate_out, up, up_out = inner(
        place, own, (left_y, left_x), (right_x, right_y), w_gate, w_up, 512, 256
    )
    gate_in = swapped(gate_out, "tensor", 0)
    up_in = swapped(up_out, "tensor", 0)
    hidden = hidden_strip(
        place, folded, *received, row_owner, column_owner, scale, expand, gate, gate_in, up, up_in
    )
    other = swapped(hidden, "tensor", 0)
    sums = []
    for x_first, first, second in ((True, X, Y), (False, Y, X)):
        start = 0 if x_first else half
        stays, sends = down(x_first, place, hidden, other, w_down, start, half, 512, 256)
        stays = stays + to_chip(sends, first)
        part = 4 * block_rows
        sums += [stays[:part], to_chip(stays[part:].astype(jnp.bfloat16), second)]
    wide, narrow = jnp.float32, jnp.bfloat16
    part = 2 * block_rows
    left, right, send = small(
        split_kernel, [((part, half), wide)] * 2 + [((2 * part, half), narrow)], *sums
    )
    stay, send = small(
        split_kernel_last,
        [((block_rows, width), wide), ((4 * block_rows, width // 4), narrow)],
        left,
        right,
        to_chip(send, Z1),
    )
    (out,) = small(last_kernel, [((1, block_rows, width), narrow)], stay, to_chip(send, Z2))
    return out


def solution(mesh):
    placed = (
        P(("groups", "tensor"), None, None),
        P("tensor", None, None),
        P("tensor", None, None),
        P("tensor", None, None),
        P("groups", "tensor", None),
        P("groups", "tensor", None),
        P("groups"),
        P("groups"),
    )
    return jax.shard_map(
        shards,
        mesh=mesh,
        in_specs=placed,
        out_specs=P(("groups", "tensor"), None, None),
        check_vma=False,
    )
```

```python
import functools

import jax
import jax.numpy as jnp
from jax import lax
from jax.experimental import pallas as pl
from jax.experimental.pallas import tpu as pltpu
from jax.sharding import PartitionSpec as P

HIDDEN_BITS = 4
FOLD = 128


def swapped(block, axis, apart):
    count = lax.axis_size(axis)
    return lax.ppermute(block, axis, [(i, i ^ (1 << apart)) for i in range(count)])


def by_target(expand, count):
    kinds, depth, width = expand.shape
    return expand.reshape(kinds, depth, count, width // count).transpose(2, 0, 1, 3)


def owner_of(ends, ids):
    return jnp.sum((ends[None, :] <= ids[:, None]).astype(jnp.int32), axis=1)


def keep_mask(rank_blocks, row_counts, columns, rows):
    adapters = rank_blocks.shape[0]
    earlier = jnp.arange(adapters)[:, None] >= jnp.arange(adapters)[None, :]
    block_end = jnp.sum(jnp.where(earlier, rank_blocks[None, :], 0), axis=1)
    row_end = jnp.sum(jnp.where(earlier, row_counts[None, :], 0), axis=1)
    column_owner = owner_of(block_end, jnp.arange(columns, dtype=jnp.int32) // 16)
    row_owner = owner_of(row_end, jnp.arange(rows, dtype=jnp.int32))
    ids = jnp.arange(adapters, dtype=jnp.int32)
    row_blocks = jnp.sum(
        jnp.where(row_owner[:, None] == ids[None, :], rank_blocks[None, :], 0), axis=1
    )
    same = (row_owner[:, None] == column_owner[None, :]).astype(jnp.float32)
    return same, 1.0 / row_blocks.astype(jnp.float32)


def general_shards(tokens, w_gate, w_up, w_down, shrink_factors, expand_factors, rank_blocks, row_counts):
    count = lax.axis_size("tensor")
    low_bits = count.bit_length() - 1 - HIDDEN_BITS
    fgroups = 1 << low_bits
    place = lax.axis_index("tensor")
    feature_group = place % fgroups
    hidden_group = place // fgroups
    block_rows = tokens.shape[1]
    rows = block_rows << HIDDEN_BITS
    units = w_gate.shape[2]
    strip = units // fgroups

    expand = lax.all_to_all(
        by_target(expand_factors, count), "tensor", split_axis=0, concat_axis=0, tiled=True
    )

    gathered = tokens[0]
    for bit in reversed(range(HIDDEN_BITS)):
        other = swapped(gathered, "tensor", low_bits + bit)
        gathered = jnp.concatenate([gathered, other], 0)
    spots = jnp.arange(1 << HIDDEN_BITS, dtype=jnp.int32)
    moved = sum(((spots >> i) & 1) << (HIDDEN_BITS - 1 - i) for i in range(HIDDEN_BITS))
    natural = (
        (moved ^ hidden_group)[:, None] * block_rows + jnp.arange(block_rows, dtype=jnp.int32)[None, :]
    ).reshape(rows)
    to_own = (natural[:, None] == jnp.arange(rows, dtype=jnp.int32)[None, :]).astype(jnp.bfloat16)

    columns = shrink_factors.shape[2]
    same, scale = keep_mask(rank_blocks, row_counts, columns, rows)
    slab = shrink_factors.shape[1]
    features = lax.dynamic_slice_in_dim(gathered, hidden_group * slab, slab, 1)
    features = jnp.dot(to_own.T, features, preferred_element_type=jnp.float32).astype(jnp.bfloat16)
    partial_value = jnp.einsum(
        "rd,kdc->krc", features, shrink_factors, preferred_element_type=jnp.float32
    )
    folded = jnp.sum((partial_value * same).reshape(2, rows, columns // FOLD, FOLD), axis=2)
    for bit in range(low_bits + HIDDEN_BITS):
        folded = folded + swapped(folded, "tensor", bit)
    shrunk = jnp.tile(folded, (1, 1, columns // FOLD)) * (same * scale[:, None])[None]
    shrunk = shrunk.astype(jnp.bfloat16)
    shrunk = jnp.einsum("or,krc->koc", to_own, shrunk, preferred_element_type=jnp.float32)
    shrunk = shrunk.astype(jnp.bfloat16)

    gate_part = jnp.dot(gathered, w_gate[0], preferred_element_type=jnp.float32)
    up_part = jnp.dot(gathered, w_up[0], preferred_element_type=jnp.float32)
    partials = jnp.stack([gate_part, up_part])
    for step in range(low_bits):
        bit = low_bits - 1 - step
        half = partials.shape[2] // 2
        high = feature_group // (1 << bit) % 2
        outgoing = lax.dynamic_slice_in_dim(partials, (1 - high) * half, half, 2)
        staying = lax.dynamic_slice_in_dim(partials, high * half, half, 2)
        partials = staying + swapped(outgoing, "tensor", bit)
    depth = expand.shape[2]
    low_rank = jnp.einsum(
        "krsd,skdc->krc",
        shrunk.reshape(2, rows, count, depth),
        expand,
        preferred_element_type=jnp.float32,
    )
    partials = partials + low_rank
    hidden = (jax.nn.silu(partials[0]) * partials[1]).astype(jnp.bfloat16)
    for step in range(low_bits):
        other = swapped(hidden, "tensor", step)
        high = feature_group // (1 << step) % 2 == 1
        hidden = jnp.where(
            high, jnp.concatenate([other, hidden], 1), jnp.concatenate([hidden, other], 1)
        )
    terms = jnp.dot(hidden, w_down[0], preferred_element_type=jnp.float32)
    for bit in range(HIDDEN_BITS):
        half = terms.shape[0] // 2
        outgoing = terms[half:].astype(jnp.bfloat16)
        terms = terms[:half] + swapped(outgoing, "tensor", low_bits + bit).astype(jnp.float32)
    return terms.astype(jnp.bfloat16)[None]


def keeping(ranks, counts, rows, columns):
    row = lax.broadcasted_iota(jnp.int32, (rows, 1), 0)
    block = lax.broadcasted_iota(jnp.int32, (1, columns), 1) // 16
    row_owner, column_owner = jnp.zeros_like(row), jnp.zeros_like(block)
    row_end = block_end = 0
    for adapter in range(ranks.shape[0]):
        row_end, block_end = row_end + counts[adapter], block_end + ranks[adapter]
        row_owner += (row >= row_end).astype(jnp.int32)
        column_owner += (block >= block_end).astype(jnp.int32)
    blocks = jnp.zeros_like(row)
    for adapter in range(ranks.shape[0]):
        blocks = jnp.where(row_owner == adapter, ranks[adapter], blocks)
    return row_owner == column_owner, 1.0 / blocks.astype(jnp.float32)


VMEM = pl.BlockSpec(memory_space=pltpu.VMEM)
SMEM = pl.BlockSpec(memory_space=pltpu.SMEM)
ANY = pl.BlockSpec(memory_space=pl.ANY)
X, Y, Z1, Z2 = 1, 2, 4, 8


def to_chip(block, apart):
    count = lax.axis_size("tensor")
    return lax.ppermute(block, "tensor", [(i, i ^ (apart << 1)) for i in range(count)])


def cost(flops, read):
    return pl.CostEstimate(flops=flops, bytes_accessed=read, transcendentals=0)


def in_hbm(array):
    return pltpu.with_memory_space_constraint(array, pltpu.HBM)


def blocks_kernel(count, strip, source, target):
    for j in range(count):
        target[j] = source[:, :, j * strip : (j + 1) * strip]


def blocks_of(expand, count):
    kinds, depth, width = expand.shape
    strip = width // count
    return pl.pallas_call(
        functools.partial(blocks_kernel, count, strip),
        out_shape=jax.ShapeDtypeStruct((count, kinds, depth, strip), expand.dtype),
        in_specs=[VMEM],
        out_specs=VMEM,
        cost_estimate=cost(0, 4 * expand.size),
        compiler_params=pltpu.CompilerParams(vmem_limit_bytes=10 << 20),
    )(expand)


def own_order(place, rows, own_axis):
    block = rows // 16
    own, natural = [lax.broadcasted_iota(jnp.int32, (rows, rows), axis) for axis in (own_axis, 1 - own_axis)]
    spot = own // block
    far = spot // 8 + spot // 4 % 2 * 2 + spot // 2 % 2 * 4 + spot % 2 * 8
    return ((far ^ (place // 2)) * block + (own - spot * block) == natural).astype(jnp.bfloat16)


def shrink_kernel(place, ranks, counts, near, far, factors, folded):
    rows, columns = folded.shape[1], factors.shape[2]
    same, _ = keeping(ranks, counts, rows, columns)
    features = jnp.concatenate([near[...], far[...]], axis=0)
    features = jnp.dot(
        own_order(place[0], rows, 1), features, preferred_element_type=jnp.float32
    ).astype(jnp.bfloat16)
    for k in range(2):
        value = jnp.dot(features, factors[k], preferred_element_type=jnp.float32)
        value = jnp.where(same, value, 0.0)
        total = value[:, :FOLD]
        for start in range(FOLD, columns, FOLD):
            total = total + value[:, start : start + FOLD]
        folded[k] = total


def small(kernel, shapes, *operands, scalars=0, limit=8):
    return pl.pallas_call(
        kernel,
        out_shape=[jax.ShapeDtypeStruct(shape, dtype) for shape, dtype in shapes],
        in_specs=[SMEM] * scalars + [VMEM] * (len(operands) - scalars),
        out_specs=[VMEM] * len(shapes),
        cost_estimate=cost(0, 1 << 20),
        compiler_params=pltpu.CompilerParams(vmem_limit_bytes=limit << 20),
    )(*operands)


def same_kernel(source, target):
    target[...] = source[0]


def rows_joined(*parts):
    wide = [part.astype(jnp.float32) for part in parts]
    return jnp.concatenate(wide, axis=0).astype(parts[0].dtype)


def joined_kernel(near, far, rows):
    rows[...] = rows_joined(near[...], far[...])


def parted_kernel(place, near, far, left, right, keep, send, rows):
    rows[...] = rows_joined(near[...], far[...])
    half, size = left.shape[1], keep.shape[1]
    left[...], right[...] = rows[:, :half], rows[:, half:]
    at = place[0] // 8 * 2 * size
    low, high = [rows[:, pl.ds(pl.multiple_of(at + i * size, size), size)] for i in range(2)]
    first = place[0] // 4 % 2 == 0
    keep[...] = jnp.where(first, low, high)
    send[...] = jnp.where(first, high, low)


def parted(place, near, far, slabs):
    part, width = near.shape
    shapes = [(2 * part, width // 2)] * 2 + [(2 * part, slabs)] * 2
    return pl.pallas_call(
        parted_kernel,
        out_shape=[jax.ShapeDtypeStruct(shape, near.dtype) for shape in shapes],
        in_specs=[SMEM, VMEM, VMEM],
        out_specs=[VMEM] * 4,
        scratch_shapes=[pltpu.VMEM((2 * part, width), near.dtype)],
        cost_estimate=cost(0, 8 * near.size),
        compiler_params=pltpu.CompilerParams(vmem_limit_bytes=8 << 20),
    )(place, near, far)


def middle_kernel(place, left, left_y, right, right_x, slab, slab_y, lefts, rights, keep, send):
    lefts[...] = rows_joined(left[...], left_y[...])
    rights[...] = rows_joined(right[...], right_x[...])
    slabs = rows_joined(slab[...], slab_y[...])
    size = keep.shape[1]
    first = place[0] // 2 % 2 == 0
    keep[...] = jnp.where(first, slabs[:, :size], slabs[:, size:])
    send[...] = jnp.where(first, slabs[:, size:], slabs[:, :size])


def fetch_kernel(pieces, *refs):
    count = (len(refs) - 2) // 2
    sources, targets, sems = refs[:count], refs[count + 1 : -1], refs[-1]
    copies = []
    for k, (source, target) in enumerate(zip(sources, targets)):
        size = source.shape[1] // pieces
        for i in range(pieces):
            rows = pl.ds(i * size, size)
            copies.append(
                pltpu.make_async_copy(source.at[:, rows], target.at[:, rows], sems.at[k, i])
            )
    for copy in copies:
        copy.start()
    for copy in copies:
        copy.wait()


def fetch(sources, after, pieces):
    return pl.pallas_call(
        functools.partial(fetch_kernel, pieces),
        out_shape=[pltpu.VMEM(source.shape, source.dtype) for source in sources],
        in_specs=[ANY] * (len(sources) + 1),
        out_specs=[VMEM] * len(sources),
        scratch_shapes=[pltpu.SemaphoreType.DMA((len(sources), pieces))],
        cost_estimate=cost(0, 2 * sum(source.size for source in sources)),
        compiler_params=pltpu.CompilerParams(vmem_limit_bytes=1 << 20),
    )(*[in_hbm(source) for source in sources], after)


def chunks(width, most):
    return [(at, min(most, width - at)) for at in range(0, width, most)]


def started(source, target, sems, most, row, start=0):
    depth, width = target.shape
    copies = [
        pltpu.make_async_copy(
            source.at[0, pl.ds(row, depth), pl.ds(start + at, size)],
            target.at[:, pl.ds(at, size)],
            sems.at[i],
        )
        for i, (at, size) in enumerate(chunks(width, most))
    ]
    for copy in copies:
        copy.start()
    return copies


def inner_kernel(tile, place, lefts, left_x, rights, right_y, gate, up, *refs):
    outs, (gate_sum, up_sum, rows) = refs[:4], refs[4:]
    half = lefts.shape[1]
    part = lefts.shape[0] // 2
    rows[:, :half] = rows_joined(lefts[...], left_x[...])
    wide, corner = rights[...].astype(jnp.float32), right_y[...].astype(jnp.float32)
    rows[:, half:] = jnp.concatenate(
        [wide[:part], corner[:part], wide[part:], corner[part:]], axis=0
    ).astype(rows.dtype)
    strip = outs[0].shape[1]
    first = place[0] % 2 == 0
    for weights, total, here, there in ((gate, gate_sum, *outs[:2]), (up, up_sum, *outs[2:])):
        for at, size in chunks(total.shape[1], tile):
            total[:, at : at + size] = jnp.dot(
                rows[...], weights[0, :, at : at + size], preferred_element_type=jnp.float32
            )
        low, high = total[:, :strip], total[:, strip:]
        here[...] = jnp.where(first, low, high)
        there[...] = jnp.where(first, high, low)


def inner(place, lefts, left_x, rights, right_y, gate, up, tile):
    half, width = lefts.shape
    rows, units = 2 * half, gate.shape[2]
    strip = jax.ShapeDtypeStruct((rows, units // 2), jnp.float32)
    return pl.pallas_call(
        functools.partial(inner_kernel, tile),
        out_shape=[strip] * 4,
        in_specs=[SMEM] + [VMEM] * 6,
        out_specs=[VMEM] * 4,
        scratch_shapes=[pltpu.VMEM((rows, units), jnp.float32)] * 2
        + [pltpu.VMEM((rows, 2 * width), lefts.dtype)],
        cost_estimate=cost(2 * rows * (gate.size + up.size), 2 * (gate.size + up.size)),
        compiler_params=pltpu.CompilerParams(vmem_limit_bytes=12 << 20),
    )(place, lefts, left_x, rights, right_y, gate, up)


def hidden_kernel(
    place, ranks, counts, folded, near, far, both, expand, gate, gate_in, up, up_in, hidden
):
    rows, columns = gate.shape[0], expand.shape[0] * expand.shape[2]
    same, scale = keeping(ranks, counts, rows, columns)
    keep = jnp.where(same, scale, 0.0)
    order = own_order(place[0], rows, 0)
    sums = []
    for k in range(2):
        planes = [part[k].astype(jnp.float32) for part in (near, far, both)]
        total = (folded[k] + planes[0]) + (planes[1] + planes[2])
        shrunk = jnp.concatenate([total] * (columns // FOLD), axis=1) * keep
        shrunk = jnp.dot(
            order, shrunk.astype(jnp.bfloat16), preferred_element_type=jnp.float32
        ).astype(jnp.bfloat16)
        factors = expand[:, k].reshape(columns, expand.shape[3])
        sums.append(jnp.dot(shrunk, factors, preferred_element_type=jnp.float32))
    gate_sum = gate[...] + gate_in[...] + sums[0]
    up_sum = up[...] + up_in[...] + sums[1]
    hidden[...] = (gate_sum / (1.0 + jnp.exp(-gate_sum)) * up_sum).astype(hidden.dtype)


def hidden_strip(*operands):
    expand, gate = operands[7], operands[8]
    return pl.pallas_call(
        hidden_kernel,
        out_shape=jax.ShapeDtypeStruct(gate.shape, jnp.bfloat16),
        in_specs=[SMEM] * 3 + [VMEM] * 9,
        out_specs=VMEM,
        cost_estimate=cost(2 * gate.shape[0] * expand.size, 2 * expand.size),
        compiler_params=pltpu.CompilerParams(vmem_limit_bytes=12 << 20),
    )(*operands)


def down_first_kernel(most, tile, place, mine, weights, terms, target, sems):
    strip = mine.shape[1]
    row = pl.multiple_of(place[0] % 2 * strip, 128)
    copies = started(weights, target, sems, most, row)
    for (at, size), copy in zip(chunks(target.shape[1], most), copies):
        copy.wait()
        for inside, wide in chunks(size, tile):
            columns = pl.ds(at + inside, wide)
            terms[:, columns] = jnp.dot(
                mine[...], target[:, columns], preferred_element_type=jnp.float32
            )


def down_first(place, mine, weights, most, tile):
    rows, strip = mine.shape
    width = weights.shape[2]
    return pl.pallas_call(
        functools.partial(down_first_kernel, most, tile),
        out_shape=jax.ShapeDtypeStruct((rows, width), jnp.float32),
        in_specs=[SMEM, VMEM, ANY],
        out_specs=VMEM,
        scratch_shapes=[
            pltpu.VMEM((strip, width), weights.dtype),
            pltpu.SemaphoreType.DMA((len(chunks(width, most)),)),
        ],
        cost_estimate=cost(2 * rows * strip * width, 2 * strip * width),
        compiler_params=pltpu.CompilerParams(vmem_limit_bytes=14 << 20),
    )(place, mine, in_hbm(weights))


def down_kernel(x_first, start, most, tile, place, other, before, weights, stays, sends, target, sems):
    strip = other.shape[1]
    row = pl.multiple_of((1 - place[0] % 2) * strip, 128)
    copies = started(weights, target, sems, most, row, start)
    part = other.shape[0] // 4
    for (at, size), copy in zip(chunks(target.shape[1], most), copies):
        copy.wait()
        for inside, wide in chunks(size, tile):
            columns = pl.ds(at + inside, wide)
            terms = before[:, pl.ds(start + at + inside, wide)] + jnp.dot(
                other[...], target[:, columns], preferred_element_type=jnp.float32
            )
            low_y, high_y, far_low, far_high = [terms[k * part : (k + 1) * part] for k in range(4)]
            if x_first:
                stay, send = (low_y, high_y), (far_low, far_high)
            else:
                stay, send = (low_y, far_low), (high_y, far_high)
            stays[:, columns] = jnp.concatenate(stay, axis=0)
            sends[:, columns] = jnp.concatenate(send, axis=0).astype(sends.dtype)


def down(x_first, place, other, before, weights, start, width, most, tile):
    rows, strip = other.shape
    return pl.pallas_call(
        functools.partial(down_kernel, x_first, start, most, tile),
        out_shape=[
            jax.ShapeDtypeStruct((rows // 2, width), dtype) for dtype in (jnp.float32, jnp.bfloat16)
        ],
        in_specs=[SMEM] + [VMEM] * 2 + [ANY],
        out_specs=[VMEM] * 2,
        scratch_shapes=[
            pltpu.VMEM((strip, width), weights.dtype),
            pltpu.SemaphoreType.DMA((len(chunks(width, most)),)),
        ],
        cost_estimate=cost(2 * rows * strip * width, 2 * strip * width),
        compiler_params=pltpu.CompilerParams(vmem_limit_bytes=12 << 20),
    )(place, other, before, in_hbm(weights))


def split_kernel(left, left_in, right, right_in, left_stay, right_stay, send):
    totals = [
        part[...] + received[...].astype(jnp.float32)
        for part, received in ((left, left_in), (right, right_in))
    ]
    half = left_stay.shape[0]
    left_stay[...], right_stay[...] = [total[:half] for total in totals]
    send[...] = jnp.concatenate([total[half:] for total in totals], axis=0).astype(send.dtype)


def split_kernel_last(left, right, received, stay, send):
    rows, width = left.shape
    half, piece = rows // 2, width // 2
    wide = received[...].astype(jnp.float32)
    totals = [left[...] + wide[:rows], right[...] + wide[rows:]]
    stay[...] = jnp.concatenate([total[:half] for total in totals], axis=1)
    send[...] = jnp.concatenate(
        [total[half:, at : at + piece] for total in totals for at in (0, piece)], axis=0
    ).astype(send.dtype)


def last_kernel(stay, received, out):
    rows = stay.shape[0]
    wide = received[...].astype(jnp.float32)
    pieces = [wide[i * rows : (i + 1) * rows] for i in range(4)]
    out[0] = (stay[...] + jnp.concatenate(pieces, axis=1)).astype(out.dtype)


def shards(tokens, w_gate, w_up, w_down, shrink_factors, expand_factors, rank_blocks, row_counts):
    count = lax.axis_size("tensor")
    units = w_gate.shape[2]
    if count != 32 or units % 256:
        return general_shards(
            tokens, w_gate, w_up, w_down, shrink_factors, expand_factors, rank_blocks, row_counts
        )
    place = lax.axis_index("tensor").reshape(1)
    block_rows, width = tokens.shape[1], tokens.shape[2]
    rows = 16 * block_rows
    slab, half = width // 16, width // 2
    wide, narrow = jnp.float32, jnp.bfloat16
    blocks = blocks_of(expand_factors, count)

    (own,) = small(same_kernel, [((block_rows, width), narrow)], tokens)
    own, other = lax.optimization_barrier((own, to_chip(tokens[0], Z2)))
    (own,) = small(joined_kernel, [((2 * block_rows, width), narrow)], own, other)
    blocks, other = lax.optimization_barrier((blocks, to_chip(own, Z1)))
    left, right, near, other = parted(place, own, other, 2 * slab)
    blocks, left, right, near, other = lax.optimization_barrier((blocks, left, right, near, other))
    expand = lax.all_to_all(blocks, "tensor", split_axis=0, concat_axis=0, tiled=True)

    hops = to_chip(other, Y), to_chip(left, Y), to_chip(right, X)
    fetched = fetch((w_gate, w_up, shrink_factors), near, 4)
    hops, fetched = lax.optimization_barrier((hops, fetched))
    other, left_y, right_x = hops
    gate_weights, up_weights, factors = fetched
    lefts, rights, near, other = small(
        middle_kernel,
        [((8 * block_rows, half), narrow)] * 2 + [((8 * block_rows, slab), narrow)] * 2,
        place,
        left,
        left_y,
        right,
        right_x,
        near,
        other,
        scalars=1,
    )
    other, left_x, right_y = to_chip(other, X), to_chip(lefts, X), to_chip(rights, Y)
    adapters = (place, rank_blocks, row_counts)
    (folded,) = small(
        shrink_kernel, [((2, rows, FOLD), wide)], *adapters, near, other, factors, scalars=3
    )
    folded = folded + swapped(folded, "tensor", 0)
    for apart in (Y, X):
        folded = folded + to_chip(folded, apart)
    sent = folded.astype(narrow)
    received = [to_chip(sent, apart) for apart in (Z1, Z2, Z1 | Z2)]

    gate, gate_out, up, up_out = inner(
        place, lefts, left_x, rights, right_y, gate_weights, up_weights, 256
    )
    gate_in = swapped(gate_out, "tensor", 0)
    up_in = swapped(up_out, "tensor", 0)
    hidden = hidden_strip(*adapters, folded, *received, expand, gate, gate_in, up, up_in)
    other = swapped(hidden, "tensor", 0)
    before = down_first(place, hidden, w_down, 1024, 256)
    sums = []
    for x_first, first, second in ((True, X, Y), (False, Y, X)):
        start = 0 if x_first else half
        stays, sends = down(x_first, place, other, before, w_down, start, half, 1024, 256)
        stays = stays + to_chip(sends, first)
        part = 4 * block_rows
        sums += [stays[:part], to_chip(stays[part:].astype(jnp.bfloat16), second)]
    part = 2 * block_rows
    left, right, send = small(
        split_kernel, [((part, half), wide)] * 2 + [((2 * part, half), narrow)], *sums
    )
    stay, send = small(
        split_kernel_last,
        [((block_rows, width), wide), ((4 * block_rows, width // 4), narrow)],
        left,
        right,
        to_chip(send, Z1),
    )
    (out,) = small(last_kernel, [((1, block_rows, width), narrow)], stay, to_chip(send, Z2))
    return out


def solution(mesh):
    placed = (
        P(("groups", "tensor"), None, None),
        P("tensor", None, None),
        P("tensor", None, None),
        P("tensor", None, None),
        P("groups", "tensor", None),
        P("groups", "tensor", None),
        P("groups"),
        P("groups"),
    )
    return jax.shard_map(
        shards,
        mesh=mesh,
        in_specs=placed,
        out_specs=P(("groups", "tensor"), None, None),
        check_vma=False,
    )
```

```python
import functools

import jax
import jax.numpy as jnp
from jax import lax
from jax.experimental import pallas as pl
from jax.experimental.pallas import tpu as pltpu
from jax.sharding import PartitionSpec as P

HIDDEN_BITS = 4
FOLD = 128


def swapped(block, axis, apart):
    count = lax.axis_size(axis)
    return lax.ppermute(block, axis, [(i, i ^ (1 << apart)) for i in range(count)])


def by_target(expand, count):
    kinds, depth, width = expand.shape
    return expand.reshape(kinds, depth, count, width // count).transpose(2, 0, 1, 3)


def owner_of(ends, ids):
    return jnp.sum((ends[None, :] <= ids[:, None]).astype(jnp.int32), axis=1)


def keep_mask(rank_blocks, row_counts, columns, rows):
    adapters = rank_blocks.shape[0]
    earlier = jnp.arange(adapters)[:, None] >= jnp.arange(adapters)[None, :]
    block_end = jnp.sum(jnp.where(earlier, rank_blocks[None, :], 0), axis=1)
    row_end = jnp.sum(jnp.where(earlier, row_counts[None, :], 0), axis=1)
    column_owner = owner_of(block_end, jnp.arange(columns, dtype=jnp.int32) // 16)
    row_owner = owner_of(row_end, jnp.arange(rows, dtype=jnp.int32))
    ids = jnp.arange(adapters, dtype=jnp.int32)
    row_blocks = jnp.sum(
        jnp.where(row_owner[:, None] == ids[None, :], rank_blocks[None, :], 0), axis=1
    )
    same = (row_owner[:, None] == column_owner[None, :]).astype(jnp.float32)
    return same, 1.0 / row_blocks.astype(jnp.float32)


def general_shards(tokens, w_gate, w_up, w_down, shrink_factors, expand_factors, rank_blocks, row_counts):
    count = lax.axis_size("tensor")
    low_bits = count.bit_length() - 1 - HIDDEN_BITS
    fgroups = 1 << low_bits
    place = lax.axis_index("tensor")
    feature_group = place % fgroups
    hidden_group = place // fgroups
    block_rows = tokens.shape[1]
    rows = block_rows << HIDDEN_BITS
    units = w_gate.shape[2]
    strip = units // fgroups

    expand = lax.all_to_all(
        by_target(expand_factors, count), "tensor", split_axis=0, concat_axis=0, tiled=True
    )

    gathered = tokens[0]
    for bit in reversed(range(HIDDEN_BITS)):
        other = swapped(gathered, "tensor", low_bits + bit)
        gathered = jnp.concatenate([gathered, other], 0)
    spots = jnp.arange(1 << HIDDEN_BITS, dtype=jnp.int32)
    moved = sum(((spots >> i) & 1) << (HIDDEN_BITS - 1 - i) for i in range(HIDDEN_BITS))
    natural = (
        (moved ^ hidden_group)[:, None] * block_rows + jnp.arange(block_rows, dtype=jnp.int32)[None, :]
    ).reshape(rows)
    to_own = (natural[:, None] == jnp.arange(rows, dtype=jnp.int32)[None, :]).astype(jnp.bfloat16)

    columns = shrink_factors.shape[2]
    same, scale = keep_mask(rank_blocks, row_counts, columns, rows)
    slab = shrink_factors.shape[1]
    features = lax.dynamic_slice_in_dim(gathered, hidden_group * slab, slab, 1)
    features = jnp.dot(to_own.T, features, preferred_element_type=jnp.float32).astype(jnp.bfloat16)
    partial_value = jnp.einsum(
        "rd,kdc->krc", features, shrink_factors, preferred_element_type=jnp.float32
    )
    folded = jnp.sum((partial_value * same).reshape(2, rows, columns // FOLD, FOLD), axis=2)
    for bit in range(low_bits + HIDDEN_BITS):
        folded = folded + swapped(folded, "tensor", bit)
    shrunk = jnp.tile(folded, (1, 1, columns // FOLD)) * (same * scale[:, None])[None]
    shrunk = shrunk.astype(jnp.bfloat16)
    shrunk = jnp.einsum("or,krc->koc", to_own, shrunk, preferred_element_type=jnp.float32)
    shrunk = shrunk.astype(jnp.bfloat16)

    gate_part = jnp.dot(gathered, w_gate[0], preferred_element_type=jnp.float32)
    up_part = jnp.dot(gathered, w_up[0], preferred_element_type=jnp.float32)
    partials = jnp.stack([gate_part, up_part])
    for step in range(low_bits):
        bit = low_bits - 1 - step
        half = partials.shape[2] // 2
        high = feature_group // (1 << bit) % 2
        outgoing = lax.dynamic_slice_in_dim(partials, (1 - high) * half, half, 2)
        staying = lax.dynamic_slice_in_dim(partials, high * half, half, 2)
        partials = staying + swapped(outgoing, "tensor", bit)
    depth = expand.shape[2]
    low_rank = jnp.einsum(
        "krsd,skdc->krc",
        shrunk.reshape(2, rows, count, depth),
        expand,
        preferred_element_type=jnp.float32,
    )
    partials = partials + low_rank
    hidden = (jax.nn.silu(partials[0]) * partials[1]).astype(jnp.bfloat16)
    for step in range(low_bits):
        other = swapped(hidden, "tensor", step)
        high = feature_group // (1 << step) % 2 == 1
        hidden = jnp.where(
            high, jnp.concatenate([other, hidden], 1), jnp.concatenate([hidden, other], 1)
        )
    terms = jnp.dot(hidden, w_down[0], preferred_element_type=jnp.float32)
    for bit in range(HIDDEN_BITS):
        half = terms.shape[0] // 2
        outgoing = terms[half:].astype(jnp.bfloat16)
        terms = terms[:half] + swapped(outgoing, "tensor", low_bits + bit).astype(jnp.float32)
    return terms.astype(jnp.bfloat16)[None]


def keeping(ranks, counts, rows, columns):
    row = lax.broadcasted_iota(jnp.int32, (rows, 1), 0)
    block = lax.broadcasted_iota(jnp.int32, (1, columns), 1) // 16
    row_owner, column_owner = jnp.zeros_like(row), jnp.zeros_like(block)
    row_end = block_end = 0
    for adapter in range(ranks.shape[0]):
        row_end, block_end = row_end + counts[adapter], block_end + ranks[adapter]
        row_owner += (row >= row_end).astype(jnp.int32)
        column_owner += (block >= block_end).astype(jnp.int32)
    blocks = jnp.zeros_like(row)
    for adapter in range(ranks.shape[0]):
        blocks = jnp.where(row_owner == adapter, ranks[adapter], blocks)
    return row_owner == column_owner, 1.0 / blocks.astype(jnp.float32)


VMEM = pl.BlockSpec(memory_space=pltpu.VMEM)
SMEM = pl.BlockSpec(memory_space=pltpu.SMEM)
ANY = pl.BlockSpec(memory_space=pl.ANY)
X, Y, Z1, Z2 = 1, 2, 4, 8


def to_chip(block, apart):
    count = lax.axis_size("tensor")
    return lax.ppermute(block, "tensor", [(i, i ^ (apart << 1)) for i in range(count)])


def cost(flops, read):
    return pl.CostEstimate(flops=flops, bytes_accessed=read, transcendentals=0)


def in_hbm(array):
    return pltpu.with_memory_space_constraint(array, pltpu.HBM)


def blocks_kernel(count, strip, source, target):
    for j in range(count):
        target[j] = source[:, :, j * strip : (j + 1) * strip]


def blocks_of(expand, count):
    kinds, depth, width = expand.shape
    strip = width // count
    return pl.pallas_call(
        functools.partial(blocks_kernel, count, strip),
        out_shape=jax.ShapeDtypeStruct((count, kinds, depth, strip), expand.dtype),
        in_specs=[VMEM],
        out_specs=VMEM,
        cost_estimate=cost(0, 4 * expand.size),
        compiler_params=pltpu.CompilerParams(vmem_limit_bytes=10 << 20),
    )(expand)


def own_order(place, rows, own_axis):
    block = rows // 16
    own, natural = [lax.broadcasted_iota(jnp.int32, (rows, rows), axis) for axis in (own_axis, 1 - own_axis)]
    spot = own // block
    far = spot // 8 + spot // 4 % 2 * 2 + spot // 2 % 2 * 4 + spot % 2 * 8
    return ((far ^ (place // 2)) * block + (own - spot * block) == natural).astype(jnp.bfloat16)


def gathered_right(rights, right_y):
    part = rights.shape[0] // 2
    wide, corner = rights.astype(jnp.float32), right_y.astype(jnp.float32)
    pieces = [wide[:part], corner[:part], wide[part:], corner[part:]]
    return jnp.concatenate(pieces, axis=0).astype(rights.dtype)


def shrink_kernel(
    place, ranks, counts, lefts, left_x, rights, right_y, factors, folded, keep, order
):
    rows, columns = folded.shape[1], factors.shape[2]
    same, scale = keeping(ranks, counts, rows, columns)
    keep[...] = jnp.where(same, scale, 0.0)
    order[...] = own_order(place[0], rows, 0)
    slab = factors.shape[1]
    chip, chips = place[0] // 2, lefts.shape[1] // slab
    columns_here = pl.ds(pl.multiple_of(chip % chips * slab, slab), slab)
    left = rows_joined(lefts[:, columns_here], left_x[:, columns_here])
    right = gathered_right(rights[:, columns_here], right_y[:, columns_here])
    features = jnp.where(chip < chips, left, right)
    features = jnp.dot(
        own_order(place[0], rows, 1), features, preferred_element_type=jnp.float32
    ).astype(jnp.bfloat16)
    for k in range(2):
        value = jnp.dot(features, factors[k], preferred_element_type=jnp.float32)
        value = jnp.where(same, value, 0.0)
        total = value[:, :FOLD]
        for start in range(FOLD, columns, FOLD):
            total = total + value[:, start : start + FOLD]
        folded[k] = total


def small(kernel, shapes, *operands, scalars=0, limit=8):
    return pl.pallas_call(
        kernel,
        out_shape=[jax.ShapeDtypeStruct(shape, dtype) for shape, dtype in shapes],
        in_specs=[SMEM] * scalars + [VMEM] * (len(operands) - scalars),
        out_specs=[VMEM] * len(shapes),
        cost_estimate=cost(0, 1 << 20),
        compiler_params=pltpu.CompilerParams(vmem_limit_bytes=limit << 20),
    )(*operands)


def same_kernel(source, target):
    target[...] = source[0]


def rows_joined(*parts):
    wide = [part.astype(jnp.float32) for part in parts]
    return jnp.concatenate(wide, axis=0).astype(parts[0].dtype)


def joined_kernel(near, far, rows):
    rows[...] = rows_joined(near[...], far[...])


def parted_kernel(near, far, left, right):
    rows = rows_joined(near[...], far[...])
    half = left.shape[1]
    left[...], right[...] = rows[:, :half], rows[:, half:]


def middle_kernel(left, left_y, right, right_x, lefts, rights):
    lefts[...] = rows_joined(left[...], left_y[...])
    rights[...] = rows_joined(right[...], right_x[...])


def fetch_kernel(pieces, *refs):
    count = (len(refs) - 2) // 2
    sources, targets, sems = refs[:count], refs[count + 1 : -1], refs[-1]
    copies = []
    for k, (source, target) in enumerate(zip(sources, targets)):
        size = source.shape[1] // pieces
        for i in range(pieces):
            rows = pl.ds(i * size, size)
            copies.append(
                pltpu.make_async_copy(source.at[:, rows], target.at[:, rows], sems.at[k, i])
            )
    for copy in copies:
        copy.start()
    for copy in copies:
        copy.wait()


def fetch(sources, after, pieces):
    return pl.pallas_call(
        functools.partial(fetch_kernel, pieces),
        out_shape=[pltpu.VMEM(source.shape, source.dtype) for source in sources],
        in_specs=[ANY] * (len(sources) + 1),
        out_specs=[VMEM] * len(sources),
        scratch_shapes=[pltpu.SemaphoreType.DMA((len(sources), pieces))],
        cost_estimate=cost(0, 2 * sum(source.size for source in sources)),
        compiler_params=pltpu.CompilerParams(vmem_limit_bytes=1 << 20),
    )(*[in_hbm(source) for source in sources], after)


def chunks(width, most):
    return [(at, min(most, width - at)) for at in range(0, width, most)]


def started(source, target, sems, most, row, start=0):
    depth, width = target.shape
    copies = [
        pltpu.make_async_copy(
            source.at[0, pl.ds(row, depth), pl.ds(start + at, size)],
            target.at[:, pl.ds(at, size)],
            sems.at[i],
        )
        for i, (at, size) in enumerate(chunks(width, most))
    ]
    for copy in copies:
        copy.start()
    return copies


def inner_kernel(tile, place, lefts, left_x, rights, right_y, gate, up, *refs):
    outs, (gate_sum, up_sum, rows) = refs[:4], refs[4:]
    half = lefts.shape[1]
    rows[:, :half] = rows_joined(lefts[...], left_x[...])
    rows[:, half:] = gathered_right(rights[...], right_y[...])
    strip = outs[0].shape[1]
    first = place[0] % 2 == 0
    for weights, total, here, there in ((gate, gate_sum, *outs[:2]), (up, up_sum, *outs[2:])):
        for at, size in chunks(total.shape[1], tile):
            total[:, at : at + size] = jnp.dot(
                rows[...], weights[0, :, at : at + size], preferred_element_type=jnp.float32
            )
        low, high = total[:, :strip], total[:, strip:]
        here[...] = jnp.where(first, low, high)
        there[...] = jnp.where(first, high, low)


def inner(place, lefts, left_x, rights, right_y, gate, up, tile):
    half, width = lefts.shape
    rows, units = 2 * half, gate.shape[2]
    strip = jax.ShapeDtypeStruct((rows, units // 2), jnp.float32)
    return pl.pallas_call(
        functools.partial(inner_kernel, tile),
        out_shape=[strip] * 4,
        in_specs=[SMEM] + [VMEM] * 6,
        out_specs=[VMEM] * 4,
        scratch_shapes=[pltpu.VMEM((rows, units), jnp.float32)] * 2
        + [pltpu.VMEM((rows, 2 * width), lefts.dtype)],
        cost_estimate=cost(2 * rows * (gate.size + up.size), 2 * (gate.size + up.size)),
        compiler_params=pltpu.CompilerParams(vmem_limit_bytes=12 << 20),
    )(place, lefts, left_x, rights, right_y, gate, up)


def hidden_kernel(
    keep, order, folded, near, far, both, expand, gate, gate_in, up, up_in, hidden
):
    columns = keep.shape[1]
    sums = []
    for k in range(2):
        planes = [part[k].astype(jnp.float32) for part in (near, far, both)]
        total = (folded[k] + planes[0]) + (planes[1] + planes[2])
        shrunk = jnp.concatenate([total] * (columns // FOLD), axis=1) * keep[...]
        shrunk = jnp.dot(
            order[...], shrunk.astype(jnp.bfloat16), preferred_element_type=jnp.float32
        ).astype(jnp.bfloat16)
        factors = expand[:, k].reshape(columns, expand.shape[3])
        sums.append(jnp.dot(shrunk, factors, preferred_element_type=jnp.float32))
    gate_sum = gate[...] + gate_in[...] + sums[0]
    up_sum = up[...] + up_in[...] + sums[1]
    hidden[...] = (gate_sum / (1.0 + jnp.exp(-gate_sum)) * up_sum).astype(hidden.dtype)


def hidden_strip(*operands):
    expand, gate = operands[6], operands[7]
    return pl.pallas_call(
        hidden_kernel,
        out_shape=jax.ShapeDtypeStruct(gate.shape, jnp.bfloat16),
        in_specs=[VMEM] * 11,
        out_specs=VMEM,
        cost_estimate=cost(2 * gate.shape[0] * expand.size, 2 * expand.size),
        compiler_params=pltpu.CompilerParams(vmem_limit_bytes=12 << 20),
    )(*operands)


def down_first_kernel(most, tile, place, mine, weights, terms, target, sems):
    strip = mine.shape[1]
    row = pl.multiple_of(place[0] % 2 * strip, 128)
    copies = started(weights, target, sems, most, row)
    for (at, size), copy in zip(chunks(target.shape[1], most), copies):
        copy.wait()
        for inside, wide in chunks(size, tile):
            columns = pl.ds(at + inside, wide)
            terms[:, columns] = jnp.dot(
                mine[...], target[:, columns], preferred_element_type=jnp.float32
            )


def down_first(place, mine, weights, most, tile):
    rows, strip = mine.shape
    width = weights.shape[2]
    return pl.pallas_call(
        functools.partial(down_first_kernel, most, tile),
        out_shape=jax.ShapeDtypeStruct((rows, width), jnp.float32),
        in_specs=[SMEM, VMEM, ANY],
        out_specs=VMEM,
        scratch_shapes=[
            pltpu.VMEM((strip, width), weights.dtype),
            pltpu.SemaphoreType.DMA((len(chunks(width, most)),)),
        ],
        cost_estimate=cost(2 * rows * strip * width, 2 * strip * width),
        compiler_params=pltpu.CompilerParams(vmem_limit_bytes=14 << 20),
    )(place, mine, in_hbm(weights))


def down_kernel(x_first, start, most, tile, place, other, before, weights, stays, sends, target, sems):
    strip = other.shape[1]
    row = pl.multiple_of((1 - place[0] % 2) * strip, 128)
    copies = started(weights, target, sems, most, row, start)
    part = other.shape[0] // 4
    for (at, size), copy in zip(chunks(target.shape[1], most), copies):
        copy.wait()
        for inside, wide in chunks(size, tile):
            columns = pl.ds(at + inside, wide)
            terms = before[:, pl.ds(start + at + inside, wide)] + jnp.dot(
                other[...], target[:, columns], preferred_element_type=jnp.float32
            )
            low_y, high_y, far_low, far_high = [terms[k * part : (k + 1) * part] for k in range(4)]
            if x_first:
                stay, send = (low_y, high_y), (far_low, far_high)
            else:
                stay, send = (low_y, far_low), (high_y, far_high)
            stays[:, columns] = jnp.concatenate(stay, axis=0)
            sends[:, columns] = jnp.concatenate(send, axis=0).astype(sends.dtype)


def down(x_first, place, other, before, weights, start, width, most, tile):
    rows, strip = other.shape
    return pl.pallas_call(
        functools.partial(down_kernel, x_first, start, most, tile),
        out_shape=[
            jax.ShapeDtypeStruct((rows // 2, width), dtype) for dtype in (jnp.float32, jnp.bfloat16)
        ],
        in_specs=[SMEM] + [VMEM] * 2 + [ANY],
        out_specs=[VMEM] * 2,
        scratch_shapes=[
            pltpu.VMEM((strip, width), weights.dtype),
            pltpu.SemaphoreType.DMA((len(chunks(width, most)),)),
        ],
        cost_estimate=cost(2 * rows * strip * width, 2 * strip * width),
        compiler_params=pltpu.CompilerParams(vmem_limit_bytes=12 << 20),
    )(place, other, before, in_hbm(weights))


def packed(total, pieces):
    size = total.shape[1] // pieces
    return jnp.concatenate([total[:, i * size : (i + 1) * size] for i in range(pieces)], axis=0)


def unpacked(packed_rows, pieces):
    wide = packed_rows.astype(jnp.float32)
    rows = wide.shape[0] // pieces
    return jnp.concatenate([wide[i * rows : (i + 1) * rows] for i in range(pieces)], axis=1)


def split_kernel(left, left_in, right, right_in, stay, send):
    totals = [
        part[...] + received[...].astype(jnp.float32)
        for part, received in ((left, left_in), (right, right_in))
    ]
    total = jnp.concatenate(totals, axis=1)
    half = stay.shape[0]
    stay[...], send[...] = total[:half], packed(total[half:], 2).astype(send.dtype)


def split_kernel_last(before, received, stay, send):
    total = before[...] + unpacked(received[...], 2)
    half = stay.shape[0]
    stay[...], send[...] = total[:half], packed(total[half:], 4).astype(send.dtype)


def last_kernel(stay, received, out):
    out[0] = (stay[...] + unpacked(received[...], 4)).astype(out.dtype)


def shards(tokens, w_gate, w_up, w_down, shrink_factors, expand_factors, rank_blocks, row_counts):
    count = lax.axis_size("tensor")
    units = w_gate.shape[2]
    if count != 32 or units % 256:
        return general_shards(
            tokens, w_gate, w_up, w_down, shrink_factors, expand_factors, rank_blocks, row_counts
        )
    place = lax.axis_index("tensor").reshape(1)
    block_rows, width = tokens.shape[1], tokens.shape[2]
    rows = 16 * block_rows
    half, columns = width // 2, shrink_factors.shape[2]
    wide, narrow = jnp.float32, jnp.bfloat16
    blocks = blocks_of(expand_factors, count)

    (own,) = small(same_kernel, [((block_rows, width), narrow)], tokens)
    own, other = lax.optimization_barrier((own, to_chip(tokens[0], Z2)))
    (own,) = small(joined_kernel, [((2 * block_rows, width), narrow)], own, other)
    blocks, other = lax.optimization_barrier((blocks, to_chip(own, Z1)))
    left, right = small(parted_kernel, [((4 * block_rows, half), narrow)] * 2, own, other)
    blocks, left, right = lax.optimization_barrier((blocks, left, right))
    expand = lax.all_to_all(blocks, "tensor", split_axis=0, concat_axis=0, tiled=True)

    hops = to_chip(left, Y), to_chip(right, X)
    fetched = fetch((w_gate, w_up, shrink_factors), left, 4)
    hops, fetched = lax.optimization_barrier((hops, fetched))
    gate_weights, up_weights, factors = fetched
    lefts, rights = small(
        middle_kernel, [((8 * block_rows, half), narrow)] * 2, left, hops[0], right, hops[1]
    )
    gathered = lefts, to_chip(lefts, X), rights, to_chip(rights, Y)

    folded, keep, order = small(
        shrink_kernel,
        [((2, rows, FOLD), wide), ((rows, columns), wide), ((rows, rows), narrow)],
        place,
        rank_blocks,
        row_counts,
        *gathered,
        factors,
        scalars=3,
    )
    folded = folded + swapped(folded, "tensor", 0)
    for apart in (Y, X):
        folded = folded + to_chip(folded, apart)
    sent = folded.astype(narrow)
    received = [to_chip(sent, apart) for apart in (Z1, Z2, Z1 | Z2)]

    gate, gate_out, up, up_out = inner(place, *gathered, gate_weights, up_weights, 256)
    gate_in = swapped(gate_out, "tensor", 0)
    up_in = swapped(up_out, "tensor", 0)
    hidden = hidden_strip(keep, order, folded, *received, expand, gate, gate_in, up, up_in)
    other = swapped(hidden, "tensor", 0)
    before = down_first(place, hidden, w_down, 1024, 256)
    split = width * 5 // 8 // 256 * 256
    sums = []
    for x_first, first, second in ((True, X, Y), (False, Y, X)):
        start, size = (0, split) if x_first else (split, width - split)
        stays, sends = down(x_first, place, other, before, w_down, start, size, 1024, 256)
        stays = stays + to_chip(sends, first)
        part = 4 * block_rows
        sums += [stays[:part], to_chip(stays[part:].astype(narrow), second)]
    stay, send = small(
        split_kernel, [((part // 2, width), wide), ((part, half), narrow)], *sums
    )
    stay, send = small(
        split_kernel_last,
        [((block_rows, width), wide), ((part, width // 4), narrow)],
        stay,
        to_chip(send, Z1),
    )
    (out,) = small(last_kernel, [((1, block_rows, width), narrow)], stay, to_chip(send, Z2))
    return out


def solution(mesh):
    placed = (
        P(("groups", "tensor"), None, None),
        P("tensor", None, None),
        P("tensor", None, None),
        P("tensor", None, None),
        P("groups", "tensor", None),
        P("groups", "tensor", None),
        P("groups"),
        P("groups"),
    )
    return jax.shard_map(
        shards,
        mesh=mesh,
        in_specs=placed,
        out_specs=P(("groups", "tensor"), None, None),
        check_vma=False,
    )
```

```python
import functools

import jax
import jax.numpy as jnp
from jax import lax
from jax.experimental import pallas as pl
from jax.experimental.pallas import tpu as pltpu
from jax.sharding import PartitionSpec as P

HIDDEN_BITS = 4
FOLD = 128


def swapped(block, axis, apart):
    count = lax.axis_size(axis)
    return lax.ppermute(block, axis, [(i, i ^ (1 << apart)) for i in range(count)])


def by_target(expand, count):
    kinds, depth, width = expand.shape
    return expand.reshape(kinds, depth, count, width // count).transpose(2, 0, 1, 3)


def owner_of(ends, ids):
    return jnp.sum((ends[None, :] <= ids[:, None]).astype(jnp.int32), axis=1)


def keep_mask(rank_blocks, row_counts, columns, rows):
    adapters = rank_blocks.shape[0]
    earlier = jnp.arange(adapters)[:, None] >= jnp.arange(adapters)[None, :]
    block_end = jnp.sum(jnp.where(earlier, rank_blocks[None, :], 0), axis=1)
    row_end = jnp.sum(jnp.where(earlier, row_counts[None, :], 0), axis=1)
    column_owner = owner_of(block_end, jnp.arange(columns, dtype=jnp.int32) // 16)
    row_owner = owner_of(row_end, jnp.arange(rows, dtype=jnp.int32))
    ids = jnp.arange(adapters, dtype=jnp.int32)
    row_blocks = jnp.sum(
        jnp.where(row_owner[:, None] == ids[None, :], rank_blocks[None, :], 0), axis=1
    )
    same = (row_owner[:, None] == column_owner[None, :]).astype(jnp.float32)
    return same, 1.0 / row_blocks.astype(jnp.float32)


def general_shards(tokens, w_gate, w_up, w_down, shrink_factors, expand_factors, rank_blocks, row_counts):
    count = lax.axis_size("tensor")
    low_bits = count.bit_length() - 1 - HIDDEN_BITS
    fgroups = 1 << low_bits
    place = lax.axis_index("tensor")
    feature_group = place % fgroups
    hidden_group = place // fgroups
    block_rows = tokens.shape[1]
    rows = block_rows << HIDDEN_BITS
    units = w_gate.shape[2]
    strip = units // fgroups

    expand = lax.all_to_all(
        by_target(expand_factors, count), "tensor", split_axis=0, concat_axis=0, tiled=True
    )

    gathered = tokens[0]
    for bit in reversed(range(HIDDEN_BITS)):
        other = swapped(gathered, "tensor", low_bits + bit)
        gathered = jnp.concatenate([gathered, other], 0)
    spots = jnp.arange(1 << HIDDEN_BITS, dtype=jnp.int32)
    moved = sum(((spots >> i) & 1) << (HIDDEN_BITS - 1 - i) for i in range(HIDDEN_BITS))
    natural = (
        (moved ^ hidden_group)[:, None] * block_rows + jnp.arange(block_rows, dtype=jnp.int32)[None, :]
    ).reshape(rows)
    to_own = (natural[:, None] == jnp.arange(rows, dtype=jnp.int32)[None, :]).astype(jnp.bfloat16)

    columns = shrink_factors.shape[2]
    same, scale = keep_mask(rank_blocks, row_counts, columns, rows)
    slab = shrink_factors.shape[1]
    features = lax.dynamic_slice_in_dim(gathered, hidden_group * slab, slab, 1)
    features = jnp.dot(to_own.T, features, preferred_element_type=jnp.float32).astype(jnp.bfloat16)
    partial_value = jnp.einsum(
        "rd,kdc->krc", features, shrink_factors, preferred_element_type=jnp.float32
    )
    folded = jnp.sum((partial_value * same).reshape(2, rows, columns // FOLD, FOLD), axis=2)
    for bit in range(low_bits + HIDDEN_BITS):
        folded = folded + swapped(folded, "tensor", bit)
    shrunk = jnp.tile(folded, (1, 1, columns // FOLD)) * (same * scale[:, None])[None]
    shrunk = shrunk.astype(jnp.bfloat16)
    shrunk = jnp.einsum("or,krc->koc", to_own, shrunk, preferred_element_type=jnp.float32)
    shrunk = shrunk.astype(jnp.bfloat16)

    gate_part = jnp.dot(gathered, w_gate[0], preferred_element_type=jnp.float32)
    up_part = jnp.dot(gathered, w_up[0], preferred_element_type=jnp.float32)
    partials = jnp.stack([gate_part, up_part])
    for step in range(low_bits):
        bit = low_bits - 1 - step
        half = partials.shape[2] // 2
        high = feature_group // (1 << bit) % 2
        outgoing = lax.dynamic_slice_in_dim(partials, (1 - high) * half, half, 2)
        staying = lax.dynamic_slice_in_dim(partials, high * half, half, 2)
        partials = staying + swapped(outgoing, "tensor", bit)
    depth = expand.shape[2]
    low_rank = jnp.einsum(
        "krsd,skdc->krc",
        shrunk.reshape(2, rows, count, depth),
        expand,
        preferred_element_type=jnp.float32,
    )
    partials = partials + low_rank
    hidden = (jax.nn.silu(partials[0]) * partials[1]).astype(jnp.bfloat16)
    for step in range(low_bits):
        other = swapped(hidden, "tensor", step)
        high = feature_group // (1 << step) % 2 == 1
        hidden = jnp.where(
            high, jnp.concatenate([other, hidden], 1), jnp.concatenate([hidden, other], 1)
        )
    terms = jnp.dot(hidden, w_down[0], preferred_element_type=jnp.float32)
    for bit in range(HIDDEN_BITS):
        half = terms.shape[0] // 2
        outgoing = terms[half:].astype(jnp.bfloat16)
        terms = terms[:half] + swapped(outgoing, "tensor", low_bits + bit).astype(jnp.float32)
    return terms.astype(jnp.bfloat16)[None]


def keeping(ranks, counts, rows, columns):
    row = lax.broadcasted_iota(jnp.int32, (rows, 1), 0)
    block = lax.broadcasted_iota(jnp.int32, (1, columns), 1) // 16
    row_owner, column_owner = jnp.zeros_like(row), jnp.zeros_like(block)
    row_end = block_end = 0
    for adapter in range(ranks.shape[0]):
        row_end, block_end = row_end + counts[adapter], block_end + ranks[adapter]
        row_owner += (row >= row_end).astype(jnp.int32)
        column_owner += (block >= block_end).astype(jnp.int32)
    blocks = jnp.zeros_like(row)
    for adapter in range(ranks.shape[0]):
        blocks = jnp.where(row_owner == adapter, ranks[adapter], blocks)
    return row_owner == column_owner, 1.0 / blocks.astype(jnp.float32)


VMEM = pl.BlockSpec(memory_space=pltpu.VMEM)
SMEM = pl.BlockSpec(memory_space=pltpu.SMEM)
ANY = pl.BlockSpec(memory_space=pl.ANY)
X, Y, Z1, Z2 = 1, 2, 4, 8


def to_chip(block, apart):
    count = lax.axis_size("tensor")
    return lax.ppermute(block, "tensor", [(i, i ^ (apart << 1)) for i in range(count)])


def cost(flops, read):
    return pl.CostEstimate(flops=flops, bytes_accessed=read, transcendentals=0)


def in_hbm(array):
    return pltpu.with_memory_space_constraint(array, pltpu.HBM)


def blocks_kernel(count, strip, source, target):
    for j in range(count):
        target[j] = source[:, :, j * strip : (j + 1) * strip]


def blocks_of(expand, count):
    kinds, depth, width = expand.shape
    strip = width // count
    return pl.pallas_call(
        functools.partial(blocks_kernel, count, strip),
        out_shape=jax.ShapeDtypeStruct((count, kinds, depth, strip), expand.dtype),
        in_specs=[VMEM],
        out_specs=VMEM,
        cost_estimate=cost(0, 4 * expand.size),
        compiler_params=pltpu.CompilerParams(vmem_limit_bytes=10 << 20),
    )(expand)


def own_order(place, rows, own_axis):
    block = rows // 16
    own, natural = [lax.broadcasted_iota(jnp.int32, (rows, rows), axis) for axis in (own_axis, 1 - own_axis)]
    spot = own // block
    far = spot // 8 + spot // 4 % 2 * 2 + spot // 2 % 2 * 4 + spot % 2 * 8
    return ((far ^ (place // 2)) * block + (own - spot * block) == natural).astype(jnp.bfloat16)


def gathered_right(rights, right_y):
    part = rights.shape[0] // 2
    wide, corner = rights.astype(jnp.float32), right_y.astype(jnp.float32)
    pieces = [wide[:part], corner[:part], wide[part:], corner[part:]]
    return jnp.concatenate(pieces, axis=0).astype(rights.dtype)


def shrink_kernel(
    place, ranks, counts, lefts, left_x, rights, right_y, factors, folded, keep, order
):
    rows, columns = folded.shape[1], factors.shape[2]
    same, scale = keeping(ranks, counts, rows, columns)
    keep[...] = jnp.where(same, scale, 0.0)
    order[...] = own_order(place[0], rows, 0)
    slab = factors.shape[1]
    chip, chips = place[0] // 2, lefts.shape[1] // slab
    columns_here = pl.ds(pl.multiple_of(chip % chips * slab, slab), slab)
    left = rows_joined(lefts[:, columns_here], left_x[:, columns_here])
    right = gathered_right(rights[:, columns_here], right_y[:, columns_here])
    features = jnp.where(chip < chips, left, right)
    features = jnp.dot(
        own_order(place[0], rows, 1), features, preferred_element_type=jnp.float32
    ).astype(jnp.bfloat16)
    for k in range(2):
        value = jnp.dot(features, factors[k], preferred_element_type=jnp.float32)
        value = jnp.where(same, value, 0.0)
        total = value[:, :FOLD]
        for start in range(FOLD, columns, FOLD):
            total = total + value[:, start : start + FOLD]
        folded[k] = total


def small(kernel, shapes, *operands, scalars=0, limit=8):
    return pl.pallas_call(
        kernel,
        out_shape=[jax.ShapeDtypeStruct(shape, dtype) for shape, dtype in shapes],
        in_specs=[SMEM] * scalars + [VMEM] * (len(operands) - scalars),
        out_specs=[VMEM] * len(shapes),
        cost_estimate=cost(0, 1 << 20),
        compiler_params=pltpu.CompilerParams(vmem_limit_bytes=limit << 20),
    )(*operands)


def same_kernel(source, target):
    target[...] = source[0]


def rows_joined(*parts):
    wide = [part.astype(jnp.float32) for part in parts]
    return jnp.concatenate(wide, axis=0).astype(parts[0].dtype)


def joined_kernel(near, far, rows):
    rows[...] = rows_joined(near[...], far[...])


def parted_kernel(near, far, left, right):
    rows = rows_joined(near[...], far[...])
    half = left.shape[1]
    left[...], right[...] = rows[:, :half], rows[:, half:]


def middle_kernel(left, left_y, right, right_x, lefts, rights):
    lefts[...] = rows_joined(left[...], left_y[...])
    rights[...] = rows_joined(right[...], right_x[...])


def fetch_kernel(pieces, *refs):
    count = (len(refs) - 2) // 2
    sources, targets, sems = refs[:count], refs[count + 1 : -1], refs[-1]
    copies = []
    for k, (source, target) in enumerate(zip(sources, targets)):
        size = source.shape[1] // pieces
        for i in range(pieces):
            rows = pl.ds(i * size, size)
            copies.append(
                pltpu.make_async_copy(source.at[:, rows], target.at[:, rows], sems.at[k, i])
            )
    for copy in copies:
        copy.start()
    for copy in copies:
        copy.wait()


def fetch(sources, after, pieces):
    return pl.pallas_call(
        functools.partial(fetch_kernel, pieces),
        out_shape=[pltpu.VMEM(source.shape, source.dtype) for source in sources],
        in_specs=[ANY] * (len(sources) + 1),
        out_specs=[VMEM] * len(sources),
        scratch_shapes=[pltpu.SemaphoreType.DMA((len(sources), pieces))],
        cost_estimate=cost(0, 2 * sum(source.size for source in sources)),
        compiler_params=pltpu.CompilerParams(vmem_limit_bytes=1 << 20),
    )(*[in_hbm(source) for source in sources], after)


def chunks(width, most):
    return [(at, min(most, width - at)) for at in range(0, width, most)]


def started(source, target, sems, most, row, start=0):
    depth, width = target.shape
    copies = [
        pltpu.make_async_copy(
            source.at[0, pl.ds(row, depth), pl.ds(start + at, size)],
            target.at[:, pl.ds(at, size)],
            sems.at[i],
        )
        for i, (at, size) in enumerate(chunks(width, most))
    ]
    for copy in copies:
        copy.start()
    return copies


def inner_kernel(tile, place, lefts, left_x, rights, right_y, gate, up, *refs):
    outs, (gate_sum, up_sum, rows) = refs[:4], refs[4:]
    half = lefts.shape[1]
    rows[:, :half] = rows_joined(lefts[...], left_x[...])
    rows[:, half:] = gathered_right(rights[...], right_y[...])
    strip = outs[0].shape[1]
    first = place[0] % 2 == 0
    for weights, total, here, there in ((gate, gate_sum, *outs[:2]), (up, up_sum, *outs[2:])):
        for at, size in chunks(total.shape[1], tile):
            total[:, at : at + size] = jnp.dot(
                rows[...], weights[0, :, at : at + size], preferred_element_type=jnp.float32
            )
        low, high = total[:, :strip], total[:, strip:]
        here[...] = jnp.where(first, low, high)
        there[...] = jnp.where(first, high, low)


def inner(place, lefts, left_x, rights, right_y, gate, up, tile):
    half, width = lefts.shape
    rows, units = 2 * half, gate.shape[2]
    strip = jax.ShapeDtypeStruct((rows, units // 2), jnp.float32)
    return pl.pallas_call(
        functools.partial(inner_kernel, tile),
        out_shape=[strip] * 4,
        in_specs=[SMEM] + [VMEM] * 6,
        out_specs=[VMEM] * 4,
        scratch_shapes=[pltpu.VMEM((rows, units), jnp.float32)] * 2
        + [pltpu.VMEM((rows, 2 * width), lefts.dtype)],
        cost_estimate=cost(2 * rows * (gate.size + up.size), 2 * (gate.size + up.size)),
        compiler_params=pltpu.CompilerParams(vmem_limit_bytes=12 << 20),
    )(place, lefts, left_x, rights, right_y, gate, up)


def ready_kernel(
    keep, order, folded, near, far, both, gate, gate_in, up, up_in, shrunk, gate_sum, up_sum
):
    for k in range(2):
        planes = [part[k].astype(jnp.float32) for part in (near, far, both)]
        total = (folded[k] + planes[0]) + (planes[1] + planes[2])
        value = jnp.concatenate([total] * (keep.shape[1] // FOLD), axis=1) * keep[...]
        shrunk[k] = jnp.dot(
            order[...], value.astype(shrunk.dtype), preferred_element_type=jnp.float32
        ).astype(shrunk.dtype)
    gate_sum[...] = gate[...] + gate_in[...]
    up_sum[...] = up[...] + up_in[...]


def hidden_kernel(shrunk, gate, up, expand, hidden):
    columns = shrunk.shape[2]
    gate_sum, up_sum = [
        part[...]
        + jnp.dot(
            shrunk[k],
            expand[:, k].reshape(columns, expand.shape[3]),
            preferred_element_type=jnp.float32,
        )
        for k, part in enumerate((gate, up))
    ]
    hidden[...] = (gate_sum / (1.0 + jnp.exp(-gate_sum)) * up_sum).astype(hidden.dtype)


def down_first_kernel(most, tile, place, mine, weights, terms, target, sems):
    strip = mine.shape[1]
    row = pl.multiple_of(place[0] % 2 * strip, 128)
    copies = started(weights, target, sems, most, row)
    for (at, size), copy in zip(chunks(target.shape[1], most), copies):
        copy.wait()
        for inside, wide in chunks(size, tile):
            columns = pl.ds(at + inside, wide)
            terms[:, columns] = jnp.dot(
                mine[...], target[:, columns], preferred_element_type=jnp.float32
            )


def down_first(place, mine, weights, most, tile):
    rows, strip = mine.shape
    width = weights.shape[2]
    return pl.pallas_call(
        functools.partial(down_first_kernel, most, tile),
        out_shape=jax.ShapeDtypeStruct((rows, width), jnp.float32),
        in_specs=[SMEM, VMEM, ANY],
        out_specs=VMEM,
        scratch_shapes=[
            pltpu.VMEM((strip, width), weights.dtype),
            pltpu.SemaphoreType.DMA((len(chunks(width, most)),)),
        ],
        cost_estimate=cost(2 * rows * strip * width, 2 * strip * width),
        compiler_params=pltpu.CompilerParams(vmem_limit_bytes=14 << 20),
    )(place, mine, in_hbm(weights))


def down_kernel(x_first, start, most, tile, place, other, before, weights, stays, sends, target, sems):
    strip = other.shape[1]
    row = pl.multiple_of((1 - place[0] % 2) * strip, 128)
    copies = started(weights, target, sems, most, row, start)
    part = other.shape[0] // 4
    for (at, size), copy in zip(chunks(target.shape[1], most), copies):
        copy.wait()
        for inside, wide in chunks(size, tile):
            columns = pl.ds(at + inside, wide)
            terms = before[:, pl.ds(start + at + inside, wide)] + jnp.dot(
                other[...], target[:, columns], preferred_element_type=jnp.float32
            )
            low_y, high_y, far_low, far_high = [terms[k * part : (k + 1) * part] for k in range(4)]
            if x_first:
                stay, send = (low_y, high_y), (far_low, far_high)
            else:
                stay, send = (low_y, far_low), (high_y, far_high)
            stays[:, columns] = jnp.concatenate(stay, axis=0)
            sends[:, columns] = jnp.concatenate(send, axis=0).astype(sends.dtype)


def down(x_first, place, other, before, weights, start, width, most, tile):
    rows, strip = other.shape
    return pl.pallas_call(
        functools.partial(down_kernel, x_first, start, most, tile),
        out_shape=[
            jax.ShapeDtypeStruct((rows // 2, width), dtype) for dtype in (jnp.float32, jnp.bfloat16)
        ],
        in_specs=[SMEM] + [VMEM] * 2 + [ANY],
        out_specs=[VMEM] * 2,
        scratch_shapes=[
            pltpu.VMEM((strip, width), weights.dtype),
            pltpu.SemaphoreType.DMA((len(chunks(width, most)),)),
        ],
        cost_estimate=cost(2 * rows * strip * width, 2 * strip * width),
        compiler_params=pltpu.CompilerParams(vmem_limit_bytes=12 << 20),
    )(place, other, before, in_hbm(weights))


def packed(total, pieces):
    size = total.shape[1] // pieces
    return jnp.concatenate([total[:, i * size : (i + 1) * size] for i in range(pieces)], axis=0)


def unpacked(packed_rows, pieces):
    wide = packed_rows.astype(jnp.float32)
    rows = wide.shape[0] // pieces
    return jnp.concatenate([wide[i * rows : (i + 1) * rows] for i in range(pieces)], axis=1)


def split_kernel(left, left_in, right, right_in, stay, send):
    totals = [
        part[...] + received[...].astype(jnp.float32)
        for part, received in ((left, left_in), (right, right_in))
    ]
    total = jnp.concatenate(totals, axis=1)
    half = stay.shape[0]
    stay[...], send[...] = total[:half], packed(total[half:], 2).astype(send.dtype)


def split_kernel_last(before, received, stay, send):
    total = before[...] + unpacked(received[...], 2)
    half = stay.shape[0]
    stay[...], send[...] = total[:half], packed(total[half:], 4).astype(send.dtype)


def last_kernel(stay, received, out):
    out[0] = (stay[...] + unpacked(received[...], 4)).astype(out.dtype)


def shards(tokens, w_gate, w_up, w_down, shrink_factors, expand_factors, rank_blocks, row_counts):
    count = lax.axis_size("tensor")
    units = w_gate.shape[2]
    if count != 32 or units % 256:
        return general_shards(
            tokens, w_gate, w_up, w_down, shrink_factors, expand_factors, rank_blocks, row_counts
        )
    place = lax.axis_index("tensor").reshape(1)
    block_rows, width = tokens.shape[1], tokens.shape[2]
    rows = 16 * block_rows
    half, columns = width // 2, shrink_factors.shape[2]
    wide, narrow = jnp.float32, jnp.bfloat16
    blocks = blocks_of(expand_factors, count)

    (own,) = small(same_kernel, [((block_rows, width), narrow)], tokens)
    own, other = lax.optimization_barrier((own, to_chip(tokens[0], Z2)))
    (own,) = small(joined_kernel, [((2 * block_rows, width), narrow)], own, other)
    blocks, other = lax.optimization_barrier((blocks, to_chip(own, Z1)))
    left, right = small(parted_kernel, [((4 * block_rows, half), narrow)] * 2, own, other)
    place, blocks, left, right = lax.optimization_barrier((place, blocks, left, right))
    expand = lax.all_to_all(blocks, "tensor", split_axis=0, concat_axis=0, tiled=True)

    hops = to_chip(left, Y), to_chip(right, X)
    fetched = fetch((w_gate, w_up, shrink_factors), left, 4)
    hops, fetched = lax.optimization_barrier((hops, fetched))
    gate_weights, up_weights, factors = fetched
    lefts, rights = small(
        middle_kernel, [((8 * block_rows, half), narrow)] * 2, left, hops[0], right, hops[1]
    )
    gathered = lefts, to_chip(lefts, X), rights, to_chip(rights, Y)

    folded, keep, order = small(
        shrink_kernel,
        [((2, rows, FOLD), wide), ((rows, columns), wide), ((rows, rows), narrow)],
        place,
        rank_blocks,
        row_counts,
        *gathered,
        factors,
        scalars=3,
    )
    folded = folded + swapped(folded, "tensor", 0)
    for apart in (Y, X):
        folded = folded + to_chip(folded, apart)
    sent = folded.astype(narrow)
    received = [to_chip(sent, apart) for apart in (Z1, Z2, Z1 | Z2)]

    gate, gate_out, up, up_out = inner(place, *gathered, gate_weights, up_weights, 256)
    gate_in = swapped(gate_out, "tensor", 0)
    up_in = swapped(up_out, "tensor", 0)
    strip = gate.shape
    sums = small(
        ready_kernel,
        [((2, rows, columns), narrow), (strip, wide), (strip, wide)],
        *(keep, order, folded, *received, gate, gate_in, up, up_in),
    )
    (hidden,) = small(hidden_kernel, [(strip, narrow)], *sums, expand)
    other = swapped(hidden, "tensor", 0)
    before = down_first(place, hidden, w_down, 1024, 256)
    split = width * 5 // 8 // 256 * 256
    sums = []
    for x_first, first, second in ((True, X, Y), (False, Y, X)):
        start, size = (0, split) if x_first else (split, width - split)
        stays, sends = down(x_first, place, other, before, w_down, start, size, 1024, 256)
        stays = stays + to_chip(sends, first)
        part = 4 * block_rows
        sums += [stays[:part], to_chip(stays[part:].astype(narrow), second)]
    stay, send = small(
        split_kernel, [((part // 2, width), wide), ((part, half), narrow)], *sums
    )
    stay, send = small(
        split_kernel_last,
        [((block_rows, width), wide), ((part, width // 4), narrow)],
        stay,
        to_chip(send, Z1),
    )
    (out,) = small(last_kernel, [((1, block_rows, width), narrow)], stay, to_chip(send, Z2))
    return out


def solution(mesh):
    placed = (
        P(("groups", "tensor"), None, None),
        P("tensor", None, None),
        P("tensor", None, None),
        P("tensor", None, None),
        P("groups", "tensor", None),
        P("groups", "tensor", None),
        P("groups"),
        P("groups"),
    )
    return jax.shard_map(
        shards,
        mesh=mesh,
        in_specs=placed,
        out_specs=P(("groups", "tensor"), None, None),
        check_vma=False,
    )
```

```python
import functools

import jax
import jax.numpy as jnp
from jax import lax
from jax.experimental import pallas as pl
from jax.experimental.pallas import tpu as pltpu
from jax.sharding import PartitionSpec as P

HIDDEN_BITS = 4
FOLD = 128


def swapped(block, axis, apart):
    count = lax.axis_size(axis)
    return lax.ppermute(block, axis, [(i, i ^ (1 << apart)) for i in range(count)])


def by_target(expand, count):
    kinds, depth, width = expand.shape
    return expand.reshape(kinds, depth, count, width // count).transpose(2, 0, 1, 3)


def owner_of(ends, ids):
    return jnp.sum((ends[None, :] <= ids[:, None]).astype(jnp.int32), axis=1)


def keep_mask(rank_blocks, row_counts, columns, rows):
    adapters = rank_blocks.shape[0]
    earlier = jnp.arange(adapters)[:, None] >= jnp.arange(adapters)[None, :]
    block_end = jnp.sum(jnp.where(earlier, rank_blocks[None, :], 0), axis=1)
    row_end = jnp.sum(jnp.where(earlier, row_counts[None, :], 0), axis=1)
    column_owner = owner_of(block_end, jnp.arange(columns, dtype=jnp.int32) // 16)
    row_owner = owner_of(row_end, jnp.arange(rows, dtype=jnp.int32))
    ids = jnp.arange(adapters, dtype=jnp.int32)
    row_blocks = jnp.sum(
        jnp.where(row_owner[:, None] == ids[None, :], rank_blocks[None, :], 0), axis=1
    )
    same = (row_owner[:, None] == column_owner[None, :]).astype(jnp.float32)
    return same, 1.0 / row_blocks.astype(jnp.float32)


def general_shards(tokens, w_gate, w_up, w_down, shrink_factors, expand_factors, rank_blocks, row_counts):
    count = lax.axis_size("tensor")
    low_bits = count.bit_length() - 1 - HIDDEN_BITS
    fgroups = 1 << low_bits
    place = lax.axis_index("tensor")
    feature_group = place % fgroups
    hidden_group = place // fgroups
    block_rows = tokens.shape[1]
    rows = block_rows << HIDDEN_BITS
    units = w_gate.shape[2]
    strip = units // fgroups

    expand = lax.all_to_all(
        by_target(expand_factors, count), "tensor", split_axis=0, concat_axis=0, tiled=True
    )

    gathered = tokens[0]
    for bit in reversed(range(HIDDEN_BITS)):
        other = swapped(gathered, "tensor", low_bits + bit)
        gathered = jnp.concatenate([gathered, other], 0)
    spots = jnp.arange(1 << HIDDEN_BITS, dtype=jnp.int32)
    moved = sum(((spots >> i) & 1) << (HIDDEN_BITS - 1 - i) for i in range(HIDDEN_BITS))
    natural = (
        (moved ^ hidden_group)[:, None] * block_rows + jnp.arange(block_rows, dtype=jnp.int32)[None, :]
    ).reshape(rows)
    to_own = (natural[:, None] == jnp.arange(rows, dtype=jnp.int32)[None, :]).astype(jnp.bfloat16)

    columns = shrink_factors.shape[2]
    same, scale = keep_mask(rank_blocks, row_counts, columns, rows)
    slab = shrink_factors.shape[1]
    features = lax.dynamic_slice_in_dim(gathered, hidden_group * slab, slab, 1)
    features = jnp.dot(to_own.T, features, preferred_element_type=jnp.float32).astype(jnp.bfloat16)
    partial_value = jnp.einsum(
        "rd,kdc->krc", features, shrink_factors, preferred_element_type=jnp.float32
    )
    folded = jnp.sum((partial_value * same).reshape(2, rows, columns // FOLD, FOLD), axis=2)
    for bit in range(low_bits + HIDDEN_BITS):
        folded = folded + swapped(folded, "tensor", bit)
    shrunk = jnp.tile(folded, (1, 1, columns // FOLD)) * (same * scale[:, None])[None]
    shrunk = shrunk.astype(jnp.bfloat16)
    shrunk = jnp.einsum("or,krc->koc", to_own, shrunk, preferred_element_type=jnp.float32)
    shrunk = shrunk.astype(jnp.bfloat16)

    gate_part = jnp.dot(gathered, w_gate[0], preferred_element_type=jnp.float32)
    up_part = jnp.dot(gathered, w_up[0], preferred_element_type=jnp.float32)
    partials = jnp.stack([gate_part, up_part])
    for step in range(low_bits):
        bit = low_bits - 1 - step
        half = partials.shape[2] // 2
        high = feature_group // (1 << bit) % 2
        outgoing = lax.dynamic_slice_in_dim(partials, (1 - high) * half, half, 2)
        staying = lax.dynamic_slice_in_dim(partials, high * half, half, 2)
        partials = staying + swapped(outgoing, "tensor", bit)
    depth = expand.shape[2]
    low_rank = jnp.einsum(
        "krsd,skdc->krc",
        shrunk.reshape(2, rows, count, depth),
        expand,
        preferred_element_type=jnp.float32,
    )
    partials = partials + low_rank
    hidden = (jax.nn.silu(partials[0]) * partials[1]).astype(jnp.bfloat16)
    for step in range(low_bits):
        other = swapped(hidden, "tensor", step)
        high = feature_group // (1 << step) % 2 == 1
        hidden = jnp.where(
            high, jnp.concatenate([other, hidden], 1), jnp.concatenate([hidden, other], 1)
        )
    terms = jnp.dot(hidden, w_down[0], preferred_element_type=jnp.float32)
    for bit in range(HIDDEN_BITS):
        half = terms.shape[0] // 2
        outgoing = terms[half:].astype(jnp.bfloat16)
        terms = terms[:half] + swapped(outgoing, "tensor", low_bits + bit).astype(jnp.float32)
    return terms.astype(jnp.bfloat16)[None]


def keeping(ranks, counts, rows, columns):
    row = lax.broadcasted_iota(jnp.int32, (rows, 1), 0)
    block = lax.broadcasted_iota(jnp.int32, (1, columns), 1) // 16
    row_owner, column_owner = jnp.zeros_like(row), jnp.zeros_like(block)
    row_end = block_end = 0
    for adapter in range(ranks.shape[0]):
        row_end, block_end = row_end + counts[adapter], block_end + ranks[adapter]
        row_owner += (row >= row_end).astype(jnp.int32)
        column_owner += (block >= block_end).astype(jnp.int32)
    blocks = jnp.zeros_like(row)
    for adapter in range(ranks.shape[0]):
        blocks = jnp.where(row_owner == adapter, ranks[adapter], blocks)
    return row_owner == column_owner, 1.0 / blocks.astype(jnp.float32)


VMEM = pl.BlockSpec(memory_space=pltpu.VMEM)
SMEM = pl.BlockSpec(memory_space=pltpu.SMEM)
ANY = pl.BlockSpec(memory_space=pl.ANY)
X, Y, Z1, Z2 = 1, 2, 4, 8


def to_chip(block, apart):
    count = lax.axis_size("tensor")
    return lax.ppermute(block, "tensor", [(i, i ^ (apart << 1)) for i in range(count)])


def cost(flops, read):
    return pl.CostEstimate(flops=flops, bytes_accessed=read, transcendentals=0)


def in_hbm(array):
    return pltpu.with_memory_space_constraint(array, pltpu.HBM)


def blocks_kernel(count, strip, source, target):
    for j in range(count):
        target[j] = source[:, :, j * strip : (j + 1) * strip]


def blocks_of(expand, count):
    kinds, depth, width = expand.shape
    strip = width // count
    return pl.pallas_call(
        functools.partial(blocks_kernel, count, strip),
        out_shape=jax.ShapeDtypeStruct((count, kinds, depth, strip), expand.dtype),
        in_specs=[VMEM],
        out_specs=VMEM,
        cost_estimate=cost(0, 4 * expand.size),
        compiler_params=pltpu.CompilerParams(vmem_limit_bytes=10 << 20),
    )(expand)


def own_order(place, rows, own_axis):
    block = rows // 16
    own, natural = [lax.broadcasted_iota(jnp.int32, (rows, rows), axis) for axis in (own_axis, 1 - own_axis)]
    spot = own // block
    far = spot // 8 + spot // 4 % 2 * 2 + spot // 2 % 2 * 4 + spot % 2 * 8
    return ((far ^ (place // 2)) * block + (own - spot * block) == natural).astype(jnp.bfloat16)


def gathered_right(rights, right_y):
    part = rights.shape[0] // 2
    wide, corner = rights.astype(jnp.float32), right_y.astype(jnp.float32)
    pieces = [wide[:part], corner[:part], wide[part:], corner[part:]]
    return jnp.concatenate(pieces, axis=0).astype(rights.dtype)


def shrink_kernel(
    place, ranks, counts, lefts, left_x, rights, right_y, factors, folded, keep, order
):
    rows, columns = folded.shape[1], factors.shape[2]
    same, scale = keeping(ranks, counts, rows, columns)
    keep[...] = jnp.where(same, scale, 0.0)
    order[...] = own_order(place[0], rows, 0)
    slab = factors.shape[1]
    chip, chips = place[0] // 2, lefts.shape[1] // slab
    columns_here = pl.ds(pl.multiple_of(chip % chips * slab, slab), slab)
    left = rows_joined(lefts[:, columns_here], left_x[:, columns_here])
    right = gathered_right(rights[:, columns_here], right_y[:, columns_here])
    features = jnp.where(chip < chips, left, right)
    features = jnp.dot(
        own_order(place[0], rows, 1), features, preferred_element_type=jnp.float32
    ).astype(jnp.bfloat16)
    for k in range(2):
        value = jnp.dot(features, factors[k], preferred_element_type=jnp.float32)
        value = jnp.where(same, value, 0.0)
        total = value[:, :FOLD]
        for start in range(FOLD, columns, FOLD):
            total = total + value[:, start : start + FOLD]
        folded[k] = total


def small(kernel, shapes, *operands, scalars=0, limit=8):
    return pl.pallas_call(
        kernel,
        out_shape=[jax.ShapeDtypeStruct(shape, dtype) for shape, dtype in shapes],
        in_specs=[SMEM] * scalars + [VMEM] * (len(operands) - scalars),
        out_specs=[VMEM] * len(shapes),
        cost_estimate=cost(0, 1 << 20),
        compiler_params=pltpu.CompilerParams(vmem_limit_bytes=limit << 20),
    )(*operands)


def same_kernel(source, target):
    target[...] = source[0]


def rows_joined(*parts):
    wide = [part.astype(jnp.float32) for part in parts]
    return jnp.concatenate(wide, axis=0).astype(parts[0].dtype)


def joined_kernel(near, far, rows):
    rows[...] = rows_joined(near[...], far[...])


def parted_kernel(near, far, left, right):
    rows = rows_joined(near[...], far[...])
    half = left.shape[1]
    left[...], right[...] = rows[:, :half], rows[:, half:]


def middle_kernel(left, left_y, right, right_x, lefts, rights):
    lefts[...] = rows_joined(left[...], left_y[...])
    rights[...] = rows_joined(right[...], right_x[...])


def fetch_kernel(pieces, *refs):
    count = (len(refs) - 2) // 2
    sources, targets, sems = refs[:count], refs[count + 1 : -1], refs[-1]
    copies = []
    for k, (source, target) in enumerate(zip(sources, targets)):
        size = source.shape[1] // pieces
        for i in range(pieces):
            rows = pl.ds(i * size, size)
            copies.append(
                pltpu.make_async_copy(source.at[:, rows], target.at[:, rows], sems.at[k, i])
            )
    for copy in copies:
        copy.start()
    for copy in copies:
        copy.wait()


def fetch(sources, after, pieces):
    return pl.pallas_call(
        functools.partial(fetch_kernel, pieces),
        out_shape=[pltpu.VMEM(source.shape, source.dtype) for source in sources],
        in_specs=[ANY] * (len(sources) + 1),
        out_specs=[VMEM] * len(sources),
        scratch_shapes=[pltpu.SemaphoreType.DMA((len(sources), pieces))],
        cost_estimate=cost(0, 2 * sum(source.size for source in sources)),
        compiler_params=pltpu.CompilerParams(vmem_limit_bytes=1 << 20),
    )(*[in_hbm(source) for source in sources], after)


def chunks(width, most):
    return [(at, min(most, width - at)) for at in range(0, width, most)]


def inner_kernel(tile, place, lefts, left_x, rights, right_y, gate, up, *refs):
    outs, (gate_sum, up_sum, rows) = refs[:4], refs[4:]
    half = lefts.shape[1]
    rows[:, :half] = rows_joined(lefts[...], left_x[...])
    rows[:, half:] = gathered_right(rights[...], right_y[...])
    strip = outs[0].shape[1]
    first = place[0] % 2 == 0
    for weights, total, here, there in ((gate, gate_sum, *outs[:2]), (up, up_sum, *outs[2:])):
        for at, size in chunks(total.shape[1], tile):
            total[:, at : at + size] = jnp.dot(
                rows[...], weights[0, :, at : at + size], preferred_element_type=jnp.float32
            )
        low, high = total[:, :strip], total[:, strip:]
        here[...] = jnp.where(first, low, high)
        there[...] = jnp.where(first, high, low)


def inner(place, lefts, left_x, rights, right_y, gate, up, tile):
    half, width = lefts.shape
    rows, units = 2 * half, gate.shape[2]
    strip = jax.ShapeDtypeStruct((rows, units // 2), jnp.float32)
    return pl.pallas_call(
        functools.partial(inner_kernel, tile),
        out_shape=[strip] * 4,
        in_specs=[SMEM] + [VMEM] * 6,
        out_specs=[VMEM] * 4,
        scratch_shapes=[pltpu.VMEM((rows, units), jnp.float32)] * 2
        + [pltpu.VMEM((rows, 2 * width), lefts.dtype)],
        cost_estimate=cost(2 * rows * (gate.size + up.size), 2 * (gate.size + up.size)),
        compiler_params=pltpu.CompilerParams(vmem_limit_bytes=12 << 20),
    )(place, lefts, left_x, rights, right_y, gate, up)


def ready_kernel(
    keep, order, folded, near, far, both, gate, gate_in, up, up_in, shrunk, gate_sum, up_sum
):
    for k in range(2):
        planes = [part[k].astype(jnp.float32) for part in (near, far, both)]
        total = (folded[k] + planes[0]) + (planes[1] + planes[2])
        value = jnp.concatenate([total] * (keep.shape[1] // FOLD), axis=1) * keep[...]
        shrunk[k] = jnp.dot(
            order[...], value.astype(shrunk.dtype), preferred_element_type=jnp.float32
        ).astype(shrunk.dtype)
    gate_sum[...] = gate[...] + gate_in[...]
    up_sum[...] = up[...] + up_in[...]


def hidden_kernel(shrunk, gate, up, expand, hidden):
    columns = shrunk.shape[2]
    gate_sum, up_sum = [
        part[...]
        + jnp.dot(
            shrunk[k],
            expand[:, k].reshape(columns, expand.shape[3]),
            preferred_element_type=jnp.float32,
        )
        for k, part in enumerate((gate, up))
    ]
    hidden[...] = (gate_sum / (1.0 + jnp.exp(-gate_sum)) * up_sum).astype(hidden.dtype)


def down_first_kernel(tile, place, mine, weights, terms):
    strip = mine.shape[1]
    rows = pl.ds(pl.multiple_of(place[0] % 2 * strip, 128), strip)
    for at, size in chunks(terms.shape[1], tile):
        terms[:, at : at + size] = jnp.dot(
            mine[...], weights[0, rows, at : at + size], preferred_element_type=jnp.float32
        )


def down_kernel(x_first, start, tile, place, other, before, weights, stays, sends):
    strip = other.shape[1]
    rows = pl.ds(pl.multiple_of((1 - place[0] % 2) * strip, 128), strip)
    part = other.shape[0] // 4
    for at, size in chunks(stays.shape[1], tile):
        source, columns = pl.ds(start + at, size), pl.ds(at, size)
        terms = before[:, source] + jnp.dot(
            other[...], weights[0, rows, source], preferred_element_type=jnp.float32
        )
        low_y, high_y, far_low, far_high = [terms[k * part : (k + 1) * part] for k in range(4)]
        if x_first:
            stay, send = (low_y, high_y), (far_low, far_high)
        else:
            stay, send = (low_y, far_low), (high_y, far_high)
        stays[:, columns] = jnp.concatenate(stay, axis=0)
        sends[:, columns] = jnp.concatenate(send, axis=0).astype(sends.dtype)


def packed(total, pieces):
    size = total.shape[1] // pieces
    return jnp.concatenate([total[:, i * size : (i + 1) * size] for i in range(pieces)], axis=0)


def unpacked(packed_rows, pieces):
    wide = packed_rows.astype(jnp.float32)
    rows = wide.shape[0] // pieces
    return jnp.concatenate([wide[i * rows : (i + 1) * rows] for i in range(pieces)], axis=1)


def split_kernel(left, left_in, right, right_in, stay, send):
    totals = [
        part[...] + received[...].astype(jnp.float32)
        for part, received in ((left, left_in), (right, right_in))
    ]
    total = jnp.concatenate(totals, axis=1)
    half = stay.shape[0]
    stay[...], send[...] = total[:half], packed(total[half:], 2).astype(send.dtype)


def split_kernel_last(before, received, stay, send):
    total = before[...] + unpacked(received[...], 2)
    half = stay.shape[0]
    stay[...], send[...] = total[:half], packed(total[half:], 4).astype(send.dtype)


def last_kernel(stay, received, out):
    out[0] = (stay[...] + unpacked(received[...], 4)).astype(out.dtype)


def shards(tokens, w_gate, w_up, w_down, shrink_factors, expand_factors, rank_blocks, row_counts):
    count = lax.axis_size("tensor")
    units = w_gate.shape[2]
    if count != 32 or units % 256:
        return general_shards(
            tokens, w_gate, w_up, w_down, shrink_factors, expand_factors, rank_blocks, row_counts
        )
    place = lax.axis_index("tensor").reshape(1)
    block_rows, width = tokens.shape[1], tokens.shape[2]
    rows = 16 * block_rows
    half, columns = width // 2, shrink_factors.shape[2]
    wide, narrow = jnp.float32, jnp.bfloat16
    blocks = blocks_of(expand_factors, count)

    (own,) = small(same_kernel, [((block_rows, width), narrow)], tokens)
    own, other = lax.optimization_barrier((own, to_chip(tokens[0], Z2)))
    (own,) = small(joined_kernel, [((2 * block_rows, width), narrow)], own, other)
    blocks, other = lax.optimization_barrier((blocks, to_chip(own, Z1)))
    left, right = small(parted_kernel, [((4 * block_rows, half), narrow)] * 2, own, other)
    place, blocks, left, right = lax.optimization_barrier((place, blocks, left, right))
    expand = lax.all_to_all(blocks, "tensor", split_axis=0, concat_axis=0, tiled=True)

    hops = to_chip(left, Y), to_chip(right, X)
    fetched = fetch((w_gate, w_up, shrink_factors), left, 4)
    hops, fetched = lax.optimization_barrier((hops, fetched))
    gate_weights, up_weights, factors = fetched
    lefts, rights = small(
        middle_kernel, [((8 * block_rows, half), narrow)] * 2, left, hops[0], right, hops[1]
    )
    gathered = lefts, to_chip(lefts, X), rights, to_chip(rights, Y)

    folded, keep, order = small(
        shrink_kernel,
        [((2, rows, FOLD), wide), ((rows, columns), wide), ((rows, rows), narrow)],
        place,
        rank_blocks,
        row_counts,
        *gathered,
        factors,
        scalars=3,
    )
    folded = folded + swapped(folded, "tensor", 0)
    for apart in (Y, X):
        folded = folded + to_chip(folded, apart)
    sent = folded.astype(narrow)
    received = [to_chip(sent, apart) for apart in (Z1, Z2, Z1 | Z2)]

    gate, gate_out, up, up_out = inner(place, *gathered, gate_weights, up_weights, 256)
    gate_in = swapped(gate_out, "tensor", 0)
    up_in = swapped(up_out, "tensor", 0)
    strip = gate.shape
    received, (down_weights,) = lax.optimization_barrier((received, fetch((w_down,), expand, 4)))
    sums = small(
        ready_kernel,
        [((2, rows, columns), narrow), (strip, wide), (strip, wide)],
        *(keep, order, folded, *received, gate, gate_in, up, up_in),
    )
    (hidden,) = small(hidden_kernel, [(strip, narrow)], *sums, expand)
    other = swapped(hidden, "tensor", 0)
    (before,) = small(
        functools.partial(down_first_kernel, 256),
        [((rows, width), wide)],
        place,
        hidden,
        down_weights,
        scalars=1,
    )
    split = width * 5 // 8 // 256 * 256
    sums = []
    for x_first, first, second in ((True, X, Y), (False, Y, X)):
        start, size = (0, split) if x_first else (split, width - split)
        stays, sends = small(
            functools.partial(down_kernel, x_first, start, 256),
            [((rows // 2, size), wide), ((rows // 2, size), narrow)],
            place,
            other,
            before,
            down_weights,
            scalars=1,
        )
        stays = stays + to_chip(sends, first)
        part = 4 * block_rows
        sums += [stays[:part], to_chip(stays[part:].astype(narrow), second)]
    stay, send = small(
        split_kernel, [((part // 2, width), wide), ((part, half), narrow)], *sums
    )
    stay, send = small(
        split_kernel_last,
        [((block_rows, width), wide), ((part, width // 4), narrow)],
        stay,
        to_chip(send, Z1),
    )
    (out,) = small(last_kernel, [((1, block_rows, width), narrow)], stay, to_chip(send, Z2))
    return out


def solution(mesh):
    placed = (
        P(("groups", "tensor"), None, None),
        P("tensor", None, None),
        P("tensor", None, None),
        P("tensor", None, None),
        P("groups", "tensor", None),
        P("groups", "tensor", None),
        P("groups"),
        P("groups"),
    )
    return jax.shard_map(
        shards,
        mesh=mesh,
        in_specs=placed,
        out_specs=P(("groups", "tensor"), None, None),
        check_vma=False,
    )
```

```python
import functools

import jax
import jax.numpy as jnp
from jax import lax
from jax.experimental import pallas as pl
from jax.experimental.pallas import tpu as pltpu
from jax.sharding import PartitionSpec as P

HIDDEN_BITS = 4
FOLD = 128


def swapped(block, axis, apart):
    count = lax.axis_size(axis)
    return lax.ppermute(block, axis, [(i, i ^ (1 << apart)) for i in range(count)])


def by_target(expand, count):
    kinds, depth, width = expand.shape
    return expand.reshape(kinds, depth, count, width // count).transpose(2, 0, 1, 3)


def owner_of(ends, ids):
    return jnp.sum((ends[None, :] <= ids[:, None]).astype(jnp.int32), axis=1)


def keep_mask(rank_blocks, row_counts, columns, rows):
    adapters = rank_blocks.shape[0]
    earlier = jnp.arange(adapters)[:, None] >= jnp.arange(adapters)[None, :]
    block_end = jnp.sum(jnp.where(earlier, rank_blocks[None, :], 0), axis=1)
    row_end = jnp.sum(jnp.where(earlier, row_counts[None, :], 0), axis=1)
    column_owner = owner_of(block_end, jnp.arange(columns, dtype=jnp.int32) // 16)
    row_owner = owner_of(row_end, jnp.arange(rows, dtype=jnp.int32))
    ids = jnp.arange(adapters, dtype=jnp.int32)
    row_blocks = jnp.sum(
        jnp.where(row_owner[:, None] == ids[None, :], rank_blocks[None, :], 0), axis=1
    )
    same = (row_owner[:, None] == column_owner[None, :]).astype(jnp.float32)
    return same, 1.0 / row_blocks.astype(jnp.float32)


def general_shards(tokens, w_gate, w_up, w_down, shrink_factors, expand_factors, rank_blocks, row_counts):
    count = lax.axis_size("tensor")
    low_bits = count.bit_length() - 1 - HIDDEN_BITS
    fgroups = 1 << low_bits
    place = lax.axis_index("tensor")
    feature_group = place % fgroups
    hidden_group = place // fgroups
    block_rows = tokens.shape[1]
    rows = block_rows << HIDDEN_BITS
    units = w_gate.shape[2]
    strip = units // fgroups

    expand = lax.all_to_all(
        by_target(expand_factors, count), "tensor", split_axis=0, concat_axis=0, tiled=True
    )

    gathered = tokens[0]
    for bit in reversed(range(HIDDEN_BITS)):
        other = swapped(gathered, "tensor", low_bits + bit)
        gathered = jnp.concatenate([gathered, other], 0)
    spots = jnp.arange(1 << HIDDEN_BITS, dtype=jnp.int32)
    moved = sum(((spots >> i) & 1) << (HIDDEN_BITS - 1 - i) for i in range(HIDDEN_BITS))
    natural = (
        (moved ^ hidden_group)[:, None] * block_rows + jnp.arange(block_rows, dtype=jnp.int32)[None, :]
    ).reshape(rows)
    to_own = (natural[:, None] == jnp.arange(rows, dtype=jnp.int32)[None, :]).astype(jnp.bfloat16)

    columns = shrink_factors.shape[2]
    same, scale = keep_mask(rank_blocks, row_counts, columns, rows)
    slab = shrink_factors.shape[1]
    features = lax.dynamic_slice_in_dim(gathered, hidden_group * slab, slab, 1)
    features = jnp.dot(to_own.T, features, preferred_element_type=jnp.float32).astype(jnp.bfloat16)
    partial_value = jnp.einsum(
        "rd,kdc->krc", features, shrink_factors, preferred_element_type=jnp.float32
    )
    folded = jnp.sum((partial_value * same).reshape(2, rows, columns // FOLD, FOLD), axis=2)
    for bit in range(low_bits + HIDDEN_BITS):
        folded = folded + swapped(folded, "tensor", bit)
    shrunk = jnp.tile(folded, (1, 1, columns // FOLD)) * (same * scale[:, None])[None]
    shrunk = shrunk.astype(jnp.bfloat16)
    shrunk = jnp.einsum("or,krc->koc", to_own, shrunk, preferred_element_type=jnp.float32)
    shrunk = shrunk.astype(jnp.bfloat16)

    gate_part = jnp.dot(gathered, w_gate[0], preferred_element_type=jnp.float32)
    up_part = jnp.dot(gathered, w_up[0], preferred_element_type=jnp.float32)
    partials = jnp.stack([gate_part, up_part])
    for step in range(low_bits):
        bit = low_bits - 1 - step
        half = partials.shape[2] // 2
        high = feature_group // (1 << bit) % 2
        outgoing = lax.dynamic_slice_in_dim(partials, (1 - high) * half, half, 2)
        staying = lax.dynamic_slice_in_dim(partials, high * half, half, 2)
        partials = staying + swapped(outgoing, "tensor", bit)
    depth = expand.shape[2]
    low_rank = jnp.einsum(
        "krsd,skdc->krc",
        shrunk.reshape(2, rows, count, depth),
        expand,
        preferred_element_type=jnp.float32,
    )
    partials = partials + low_rank
    hidden = (jax.nn.silu(partials[0]) * partials[1]).astype(jnp.bfloat16)
    for step in range(low_bits):
        other = swapped(hidden, "tensor", step)
        high = feature_group // (1 << step) % 2 == 1
        hidden = jnp.where(
            high, jnp.concatenate([other, hidden], 1), jnp.concatenate([hidden, other], 1)
        )
    terms = jnp.dot(hidden, w_down[0], preferred_element_type=jnp.float32)
    for bit in range(HIDDEN_BITS):
        half = terms.shape[0] // 2
        outgoing = terms[half:].astype(jnp.bfloat16)
        terms = terms[:half] + swapped(outgoing, "tensor", low_bits + bit).astype(jnp.float32)
    return terms.astype(jnp.bfloat16)[None]


def keeping(ranks, counts, rows, columns):
    row = lax.broadcasted_iota(jnp.int32, (rows, 1), 0)
    block = lax.broadcasted_iota(jnp.int32, (1, columns), 1) // 16
    row_owner, column_owner = jnp.zeros_like(row), jnp.zeros_like(block)
    row_end = block_end = 0
    for adapter in range(ranks.shape[0]):
        row_end, block_end = row_end + counts[adapter], block_end + ranks[adapter]
        row_owner += (row >= row_end).astype(jnp.int32)
        column_owner += (block >= block_end).astype(jnp.int32)
    blocks = jnp.zeros_like(row)
    for adapter in range(ranks.shape[0]):
        blocks = jnp.where(row_owner == adapter, ranks[adapter], blocks)
    return row_owner == column_owner, 1.0 / blocks.astype(jnp.float32)


VMEM = pl.BlockSpec(memory_space=pltpu.VMEM)
SMEM = pl.BlockSpec(memory_space=pltpu.SMEM)
ANY = pl.BlockSpec(memory_space=pl.ANY)
X, Y, Z1, Z2 = 1, 2, 4, 8


def to_chip(block, apart):
    count = lax.axis_size("tensor")
    return lax.ppermute(block, "tensor", [(i, i ^ (apart << 1)) for i in range(count)])


def cost(flops, read):
    return pl.CostEstimate(flops=flops, bytes_accessed=read, transcendentals=0)


def in_hbm(array):
    return pltpu.with_memory_space_constraint(array, pltpu.HBM)


def blocks_kernel(count, strip, source, target):
    for j in range(count):
        target[j] = source[:, :, j * strip : (j + 1) * strip]


def blocks_of(expand, count):
    kinds, depth, width = expand.shape
    strip = width // count
    return pl.pallas_call(
        functools.partial(blocks_kernel, count, strip),
        out_shape=jax.ShapeDtypeStruct((count, kinds, depth, strip), expand.dtype),
        in_specs=[VMEM],
        out_specs=VMEM,
        cost_estimate=cost(0, 4 * expand.size),
        compiler_params=pltpu.CompilerParams(vmem_limit_bytes=10 << 20),
    )(expand)


def own_order(place, rows, own_axis):
    block = rows // 16
    own, natural = [lax.broadcasted_iota(jnp.int32, (rows, rows), axis) for axis in (own_axis, 1 - own_axis)]
    spot = own // block
    far = spot // 8 + spot // 4 % 2 * 2 + spot // 2 % 2 * 4 + spot % 2 * 8
    return ((far ^ (place // 2)) * block + (own - spot * block) == natural).astype(jnp.bfloat16)


def gathered_right(rights, right_y):
    part = rights.shape[0] // 2
    wide, corner = rights.astype(jnp.float32), right_y.astype(jnp.float32)
    pieces = [wide[:part], corner[:part], wide[part:], corner[part:]]
    return jnp.concatenate(pieces, axis=0).astype(rights.dtype)


def shrink_kernel(
    place, ranks, counts, lefts, left_x, rights, right_y, factors, folded, keep, order
):
    rows, columns = folded.shape[1], factors.shape[2]
    same, scale = keeping(ranks, counts, rows, columns)
    keep[...] = jnp.where(same, scale, 0.0)
    order[...] = own_order(place[0], rows, 0)
    slab = factors.shape[1]
    chip, chips = place[0] // 2, lefts.shape[1] // slab
    columns_here = pl.ds(pl.multiple_of(chip % chips * slab, slab), slab)
    left = rows_joined(lefts[:, columns_here], left_x[:, columns_here])
    right = gathered_right(rights[:, columns_here], right_y[:, columns_here])
    features = jnp.where(chip < chips, left, right)
    features = jnp.dot(
        own_order(place[0], rows, 1), features, preferred_element_type=jnp.float32
    ).astype(jnp.bfloat16)
    for k in range(2):
        value = jnp.dot(features, factors[k], preferred_element_type=jnp.float32)
        value = jnp.where(same, value, 0.0)
        total = value[:, :FOLD]
        for start in range(FOLD, columns, FOLD):
            total = total + value[:, start : start + FOLD]
        folded[k] = total


def small(kernel, shapes, *operands, scalars=0, limit=8):
    return pl.pallas_call(
        kernel,
        out_shape=[jax.ShapeDtypeStruct(shape, dtype) for shape, dtype in shapes],
        in_specs=[SMEM] * scalars + [VMEM] * (len(operands) - scalars),
        out_specs=[VMEM] * len(shapes),
        cost_estimate=cost(0, 1 << 20),
        compiler_params=pltpu.CompilerParams(vmem_limit_bytes=limit << 20),
    )(*operands)


def same_kernel(source, target):
    target[...] = source[0]


def rows_joined(*parts):
    wide = [part.astype(jnp.float32) for part in parts]
    return jnp.concatenate(wide, axis=0).astype(parts[0].dtype)


def joined_kernel(near, far, rows):
    rows[...] = rows_joined(near[...], far[...])


def parted_kernel(near, far, left, right):
    rows = rows_joined(near[...], far[...])
    half = left.shape[1]
    left[...], right[...] = rows[:, :half], rows[:, half:]


def middle_kernel(left, left_y, right, right_x, lefts, rights):
    lefts[...] = rows_joined(left[...], left_y[...])
    rights[...] = rows_joined(right[...], right_x[...])


def fetch_kernel(count, pieces, *refs):
    sources, targets, sems = refs[:count], refs[-1 - count : -1], refs[-1]
    copies = []
    for k, (source, target) in enumerate(zip(sources, targets)):
        size = source.shape[1] // pieces
        for i in range(pieces):
            rows = pl.ds(i * size, size)
            copies.append(
                pltpu.make_async_copy(source.at[:, rows], target.at[:, rows], sems.at[k, i])
            )
    for copy in copies:
        copy.start()
    for copy in copies:
        copy.wait()


def fetch(sources, after, pieces):
    return pl.pallas_call(
        functools.partial(fetch_kernel, len(sources), pieces),
        out_shape=[pltpu.VMEM(source.shape, source.dtype) for source in sources],
        in_specs=[ANY] * (len(sources) + len(after)),
        out_specs=[VMEM] * len(sources),
        scratch_shapes=[pltpu.SemaphoreType.DMA((len(sources), pieces))],
        cost_estimate=cost(0, 2 * sum(source.size for source in sources)),
        compiler_params=pltpu.CompilerParams(vmem_limit_bytes=1 << 20),
    )(*[in_hbm(source) for source in sources], *after)


def chunks(width, most):
    return [(at, min(most, width - at)) for at in range(0, width, most)]


def inner_kernel(tile, place, lefts, left_x, rights, right_y, gate, up, *refs):
    outs, (gate_sum, up_sum, rows) = refs[:4], refs[4:]
    half = lefts.shape[1]
    rows[:, :half] = rows_joined(lefts[...], left_x[...])
    rows[:, half:] = gathered_right(rights[...], right_y[...])
    strip = outs[0].shape[1]
    first = place[0] % 2 == 0
    for weights, total, here, there in ((gate, gate_sum, *outs[:2]), (up, up_sum, *outs[2:])):
        for at, size in chunks(total.shape[1], tile):
            total[:, at : at + size] = jnp.dot(
                rows[...], weights[0, :, at : at + size], preferred_element_type=jnp.float32
            )
        low, high = total[:, :strip], total[:, strip:]
        here[...] = jnp.where(first, low, high)
        there[...] = jnp.where(first, high, low)


def inner(place, lefts, left_x, rights, right_y, gate, up, tile):
    half, width = lefts.shape
    rows, units = 2 * half, gate.shape[2]
    strip = jax.ShapeDtypeStruct((rows, units // 2), jnp.float32)
    return pl.pallas_call(
        functools.partial(inner_kernel, tile),
        out_shape=[strip] * 4,
        in_specs=[SMEM] + [VMEM] * 6,
        out_specs=[VMEM] * 4,
        scratch_shapes=[pltpu.VMEM((rows, units), jnp.float32)] * 2
        + [pltpu.VMEM((rows, 2 * width), lefts.dtype)],
        cost_estimate=cost(2 * rows * (gate.size + up.size), 2 * (gate.size + up.size)),
        compiler_params=pltpu.CompilerParams(vmem_limit_bytes=12 << 20),
    )(place, lefts, left_x, rights, right_y, gate, up)


def sums_kernel(gate, gate_in, up, up_in, gate_sum, up_sum):
    gate_sum[...] = gate[...] + gate_in[...]
    up_sum[...] = up[...] + up_in[...]


def ready_kernel(keep, order, folded, near, far, both, shrunk):
    for k in range(2):
        planes = [part[k].astype(jnp.float32) for part in (near, far, both)]
        total = (folded[k] + planes[0]) + (planes[1] + planes[2])
        value = jnp.concatenate([total] * (keep.shape[1] // FOLD), axis=1) * keep[...]
        shrunk[k] = jnp.dot(
            order[...], value.astype(shrunk.dtype), preferred_element_type=jnp.float32
        ).astype(shrunk.dtype)


def hidden_kernel(shrunk, gate, up, expand, hidden):
    columns = shrunk.shape[2]
    gate_sum, up_sum = [
        part[...]
        + jnp.dot(
            shrunk[k],
            expand[:, k].reshape(columns, expand.shape[3]),
            preferred_element_type=jnp.float32,
        )
        for k, part in enumerate((gate, up))
    ]
    hidden[...] = (gate_sum / (1.0 + jnp.exp(-gate_sum)) * up_sum).astype(hidden.dtype)


def down_first_kernel(tile, place, mine, weights, terms):
    strip = mine.shape[1]
    rows = pl.ds(pl.multiple_of(place[0] % 2 * strip, 128), strip)
    for at, size in chunks(terms.shape[1], tile):
        terms[:, at : at + size] = jnp.dot(
            mine[...], weights[0, rows, at : at + size], preferred_element_type=jnp.float32
        )


def down_kernel(x_first, start, tile, place, other, before, weights, stays, sends):
    strip = other.shape[1]
    rows = pl.ds(pl.multiple_of((1 - place[0] % 2) * strip, 128), strip)
    part = other.shape[0] // 4
    for at, size in chunks(stays.shape[1], tile):
        source, columns = pl.ds(start + at, size), pl.ds(at, size)
        terms = before[:, source] + jnp.dot(
            other[...], weights[0, rows, source], preferred_element_type=jnp.float32
        )
        low_y, high_y, far_low, far_high = [terms[k * part : (k + 1) * part] for k in range(4)]
        if x_first:
            stay, send = (low_y, high_y), (far_low, far_high)
        else:
            stay, send = (low_y, far_low), (high_y, far_high)
        stays[:, columns] = jnp.concatenate(stay, axis=0)
        sends[:, columns] = jnp.concatenate(send, axis=0).astype(sends.dtype)


def packed(total, pieces):
    size = total.shape[1] // pieces
    return jnp.concatenate([total[:, i * size : (i + 1) * size] for i in range(pieces)], axis=0)


def unpacked(packed_rows, pieces):
    wide = packed_rows.astype(jnp.float32)
    rows = wide.shape[0] // pieces
    return jnp.concatenate([wide[i * rows : (i + 1) * rows] for i in range(pieces)], axis=1)


def split_kernel(left, left_in, right, right_in, stay, send):
    totals = [
        part[...] + received[...].astype(jnp.float32)
        for part, received in ((left, left_in), (right, right_in))
    ]
    total = jnp.concatenate(totals, axis=1)
    half = stay.shape[0]
    stay[...], send[...] = total[:half], packed(total[half:], 2).astype(send.dtype)


def split_kernel_last(before, received, stay, send):
    total = before[...] + unpacked(received[...], 2)
    half = stay.shape[0]
    stay[...], send[...] = total[:half], packed(total[half:], 4).astype(send.dtype)


def last_kernel(stay, received, out):
    out[0] = (stay[...] + unpacked(received[...], 4)).astype(out.dtype)


def shards(tokens, w_gate, w_up, w_down, shrink_factors, expand_factors, rank_blocks, row_counts):
    count = lax.axis_size("tensor")
    units = w_gate.shape[2]
    if count != 32 or units % 256:
        return general_shards(
            tokens, w_gate, w_up, w_down, shrink_factors, expand_factors, rank_blocks, row_counts
        )
    place = lax.axis_index("tensor").reshape(1)
    block_rows, width = tokens.shape[1], tokens.shape[2]
    rows = 16 * block_rows
    half, columns = width // 2, shrink_factors.shape[2]
    wide, narrow = jnp.float32, jnp.bfloat16
    blocks = blocks_of(expand_factors, count)

    (own,) = small(same_kernel, [((block_rows, width), narrow)], tokens)
    own, other = lax.optimization_barrier((own, to_chip(tokens[0], Z2)))
    (own,) = small(joined_kernel, [((2 * block_rows, width), narrow)], own, other)
    blocks, other = lax.optimization_barrier((blocks, to_chip(own, Z1)))
    left, right = small(parted_kernel, [((4 * block_rows, half), narrow)] * 2, own, other)
    place, blocks, left, right = lax.optimization_barrier((place, blocks, left, right))
    expand = lax.all_to_all(blocks, "tensor", split_axis=0, concat_axis=0, tiled=True)

    hops = to_chip(left, Y), to_chip(right, X)
    fetched = fetch((w_gate, w_up, shrink_factors), (left,), 4)
    hops, fetched = lax.optimization_barrier((hops, fetched))
    gate_weights, up_weights, factors = fetched
    lefts, rights = small(
        middle_kernel, [((8 * block_rows, half), narrow)] * 2, left, hops[0], right, hops[1]
    )
    gathered = lefts, to_chip(lefts, X), rights, to_chip(rights, Y)

    folded, keep, order = small(
        shrink_kernel,
        [((2, rows, FOLD), wide), ((rows, columns), wide), ((rows, rows), narrow)],
        place,
        rank_blocks,
        row_counts,
        *gathered,
        factors,
        scalars=3,
    )
    folded = folded + swapped(folded, "tensor", 0)
    folded = folded + to_chip(folded, Y)
    strips = inner(place, *gathered, gate_weights, up_weights, 256)
    folded, strips = lax.optimization_barrier((folded, strips))
    folded = folded + to_chip(folded, X)
    sent = folded.astype(narrow)
    received = [to_chip(sent, apart) for apart in (Z1, Z2, Z1 | Z2)]

    gate, gate_out, up, up_out = strips
    strip = (gate.shape, wide)
    sums = small(
        sums_kernel, [strip] * 2, gate, swapped(gate_out, "tensor", 0), up, swapped(up_out, "tensor", 0)
    )
    received, (down_weights,) = lax.optimization_barrier(
        (received, fetch((w_down,), (expand, *sums), 4))
    )
    (shrunk,) = small(ready_kernel, [((2, rows, columns), narrow)], keep, order, folded, *received)
    hidden_shape = (strip[0], narrow)
    (hidden,) = small(hidden_kernel, [hidden_shape], shrunk, *sums, expand)
    other = swapped(hidden, "tensor", 0)
    (before,) = small(
        functools.partial(down_first_kernel, 256),
        [((rows, width), wide)],
        place,
        hidden,
        down_weights,
        scalars=1,
    )
    split = half
    sums = []
    for x_first, first, second in ((True, X, Y), (False, Y, X)):
        start, size = (0, split) if x_first else (split, width - split)
        stays, sends = small(
            functools.partial(down_kernel, x_first, start, 256),
            [((rows // 2, size), wide), ((rows // 2, size), narrow)],
            place,
            other,
            before,
            down_weights,
            scalars=1,
        )
        stays = stays + to_chip(sends, first)
        part = 4 * block_rows
        sums += [stays[:part], to_chip(stays[part:].astype(narrow), second)]
    stay, send = small(
        split_kernel, [((part // 2, width), wide), ((part, half), narrow)], *sums
    )
    stay, send = small(
        split_kernel_last,
        [((block_rows, width), wide), ((part, width // 4), narrow)],
        stay,
        to_chip(send, Z1),
    )
    (out,) = small(last_kernel, [((1, block_rows, width), narrow)], stay, to_chip(send, Z2))
    return out


def solution(mesh):
    placed = (
        P(("groups", "tensor"), None, None),
        P("tensor", None, None),
        P("tensor", None, None),
        P("tensor", None, None),
        P("groups", "tensor", None),
        P("groups", "tensor", None),
        P("groups"),
        P("groups"),
    )
    return jax.shard_map(
        shards,
        mesh=mesh,
        in_specs=placed,
        out_specs=P(("groups", "tensor"), None, None),
        check_vma=False,
    )
```

```python
import functools

import jax
import jax.numpy as jnp
from jax import lax
from jax.experimental import pallas as pl
from jax.experimental.pallas import tpu as pltpu
from jax.sharding import PartitionSpec as P

HIDDEN_BITS = 4
FOLD = 128


def swapped(block, axis, apart):
    count = lax.axis_size(axis)
    return lax.ppermute(block, axis, [(i, i ^ (1 << apart)) for i in range(count)])


def by_target(expand, count):
    kinds, depth, width = expand.shape
    return expand.reshape(kinds, depth, count, width // count).transpose(2, 0, 1, 3)


def owner_of(ends, ids):
    return jnp.sum((ends[None, :] <= ids[:, None]).astype(jnp.int32), axis=1)


def keep_mask(rank_blocks, row_counts, columns, rows):
    adapters = rank_blocks.shape[0]
    earlier = jnp.arange(adapters)[:, None] >= jnp.arange(adapters)[None, :]
    block_end = jnp.sum(jnp.where(earlier, rank_blocks[None, :], 0), axis=1)
    row_end = jnp.sum(jnp.where(earlier, row_counts[None, :], 0), axis=1)
    column_owner = owner_of(block_end, jnp.arange(columns, dtype=jnp.int32) // 16)
    row_owner = owner_of(row_end, jnp.arange(rows, dtype=jnp.int32))
    ids = jnp.arange(adapters, dtype=jnp.int32)
    row_blocks = jnp.sum(
        jnp.where(row_owner[:, None] == ids[None, :], rank_blocks[None, :], 0), axis=1
    )
    same = (row_owner[:, None] == column_owner[None, :]).astype(jnp.float32)
    return same, 1.0 / row_blocks.astype(jnp.float32)


def general_shards(tokens, w_gate, w_up, w_down, shrink_factors, expand_factors, rank_blocks, row_counts):
    count = lax.axis_size("tensor")
    low_bits = count.bit_length() - 1 - HIDDEN_BITS
    fgroups = 1 << low_bits
    place = lax.axis_index("tensor")
    feature_group = place % fgroups
    hidden_group = place // fgroups
    block_rows = tokens.shape[1]
    rows = block_rows << HIDDEN_BITS
    units = w_gate.shape[2]
    strip = units // fgroups

    expand = lax.all_to_all(
        by_target(expand_factors, count), "tensor", split_axis=0, concat_axis=0, tiled=True
    )

    gathered = tokens[0]
    for bit in reversed(range(HIDDEN_BITS)):
        other = swapped(gathered, "tensor", low_bits + bit)
        gathered = jnp.concatenate([gathered, other], 0)
    spots = jnp.arange(1 << HIDDEN_BITS, dtype=jnp.int32)
    moved = sum(((spots >> i) & 1) << (HIDDEN_BITS - 1 - i) for i in range(HIDDEN_BITS))
    natural = (
        (moved ^ hidden_group)[:, None] * block_rows + jnp.arange(block_rows, dtype=jnp.int32)[None, :]
    ).reshape(rows)
    to_own = (natural[:, None] == jnp.arange(rows, dtype=jnp.int32)[None, :]).astype(jnp.bfloat16)

    columns = shrink_factors.shape[2]
    same, scale = keep_mask(rank_blocks, row_counts, columns, rows)
    slab = shrink_factors.shape[1]
    features = lax.dynamic_slice_in_dim(gathered, hidden_group * slab, slab, 1)
    features = jnp.dot(to_own.T, features, preferred_element_type=jnp.float32).astype(jnp.bfloat16)
    partial_value = jnp.einsum(
        "rd,kdc->krc", features, shrink_factors, preferred_element_type=jnp.float32
    )
    folded = jnp.sum((partial_value * same).reshape(2, rows, columns // FOLD, FOLD), axis=2)
    for bit in range(low_bits + HIDDEN_BITS):
        folded = folded + swapped(folded, "tensor", bit)
    shrunk = jnp.tile(folded, (1, 1, columns // FOLD)) * (same * scale[:, None])[None]
    shrunk = shrunk.astype(jnp.bfloat16)
    shrunk = jnp.einsum("or,krc->koc", to_own, shrunk, preferred_element_type=jnp.float32)
    shrunk = shrunk.astype(jnp.bfloat16)

    gate_part = jnp.dot(gathered, w_gate[0], preferred_element_type=jnp.float32)
    up_part = jnp.dot(gathered, w_up[0], preferred_element_type=jnp.float32)
    partials = jnp.stack([gate_part, up_part])
    for step in range(low_bits):
        bit = low_bits - 1 - step
        half = partials.shape[2] // 2
        high = feature_group // (1 << bit) % 2
        outgoing = lax.dynamic_slice_in_dim(partials, (1 - high) * half, half, 2)
        staying = lax.dynamic_slice_in_dim(partials, high * half, half, 2)
        partials = staying + swapped(outgoing, "tensor", bit)
    depth = expand.shape[2]
    low_rank = jnp.einsum(
        "krsd,skdc->krc",
        shrunk.reshape(2, rows, count, depth),
        expand,
        preferred_element_type=jnp.float32,
    )
    partials = partials + low_rank
    hidden = (jax.nn.silu(partials[0]) * partials[1]).astype(jnp.bfloat16)
    for step in range(low_bits):
        other = swapped(hidden, "tensor", step)
        high = feature_group // (1 << step) % 2 == 1
        hidden = jnp.where(
            high, jnp.concatenate([other, hidden], 1), jnp.concatenate([hidden, other], 1)
        )
    terms = jnp.dot(hidden, w_down[0], preferred_element_type=jnp.float32)
    for bit in range(HIDDEN_BITS):
        half = terms.shape[0] // 2
        outgoing = terms[half:].astype(jnp.bfloat16)
        terms = terms[:half] + swapped(outgoing, "tensor", low_bits + bit).astype(jnp.float32)
    return terms.astype(jnp.bfloat16)[None]


def keeping(ranks, counts, rows, columns):
    row = lax.broadcasted_iota(jnp.int32, (rows, 1), 0)
    block = lax.broadcasted_iota(jnp.int32, (1, columns), 1) // 16
    row_owner, column_owner = jnp.zeros_like(row), jnp.zeros_like(block)
    row_end = block_end = 0
    for adapter in range(ranks.shape[0]):
        row_end, block_end = row_end + counts[adapter], block_end + ranks[adapter]
        row_owner += (row >= row_end).astype(jnp.int32)
        column_owner += (block >= block_end).astype(jnp.int32)
    blocks = jnp.zeros_like(row)
    for adapter in range(ranks.shape[0]):
        blocks = jnp.where(row_owner == adapter, ranks[adapter], blocks)
    return row_owner == column_owner, 1.0 / blocks.astype(jnp.float32)


VMEM = pl.BlockSpec(memory_space=pltpu.VMEM)
SMEM = pl.BlockSpec(memory_space=pltpu.SMEM)
ANY = pl.BlockSpec(memory_space=pl.ANY)
X, Y, Z1, Z2 = 1, 2, 4, 8


def to_chip(block, apart):
    count = lax.axis_size("tensor")
    return lax.ppermute(block, "tensor", [(i, i ^ (apart << 1)) for i in range(count)])


def cost(flops, read):
    return pl.CostEstimate(flops=flops, bytes_accessed=read, transcendentals=0)


def in_hbm(array):
    return pltpu.with_memory_space_constraint(array, pltpu.HBM)


def blocks_kernel(count, strip, source, target):
    for j in range(count):
        target[j] = source[:, :, j * strip : (j + 1) * strip]


def blocks_of(expand, count):
    kinds, depth, width = expand.shape
    strip = width // count
    return pl.pallas_call(
        functools.partial(blocks_kernel, count, strip),
        out_shape=jax.ShapeDtypeStruct((count, kinds, depth, strip), expand.dtype),
        in_specs=[VMEM],
        out_specs=VMEM,
        cost_estimate=cost(0, 4 * expand.size),
        compiler_params=pltpu.CompilerParams(vmem_limit_bytes=10 << 20),
    )(expand)


def own_order(place, rows, own_axis):
    block = rows // 16
    own, natural = [lax.broadcasted_iota(jnp.int32, (rows, rows), axis) for axis in (own_axis, 1 - own_axis)]
    spot = own // block
    far = spot // 8 + spot // 4 % 2 * 2 + spot // 2 % 2 * 4 + spot % 2 * 8
    return ((far ^ (place // 2)) * block + (own - spot * block) == natural).astype(jnp.bfloat16)


def gathered_right(rights, right_y):
    part = rights.shape[0] // 2
    wide, corner = rights.astype(jnp.float32), right_y.astype(jnp.float32)
    pieces = [wide[:part], corner[:part], wide[part:], corner[part:]]
    return jnp.concatenate(pieces, axis=0).astype(rights.dtype)


def shrink_kernel(
    place, ranks, counts, lefts, left_x, rights, right_y, factors, mine, send, keep, order
):
    rows, columns = mine.shape[0], factors.shape[2]
    same, scale = keeping(ranks, counts, rows, columns)
    keep[...] = jnp.where(same, scale, 0.0)
    order[...] = own_order(place[0], rows, 0)
    slab = factors.shape[1]
    chip, chips = place[0] // 2, lefts.shape[1] // slab
    columns_here = pl.ds(pl.multiple_of(chip % chips * slab, slab), slab)
    left = rows_joined(lefts[:, columns_here], left_x[:, columns_here])
    right = gathered_right(rights[:, columns_here], right_y[:, columns_here])
    features = jnp.where(chip < chips, left, right)
    features = jnp.dot(
        own_order(place[0], rows, 1), features, preferred_element_type=jnp.float32
    ).astype(jnp.bfloat16)
    kinds = []
    for k in range(2):
        value = jnp.dot(features, factors[k], preferred_element_type=jnp.float32)
        value = jnp.where(same, value, 0.0)
        total = value[:, :FOLD]
        for start in range(FOLD, columns, FOLD):
            total = total + value[:, start : start + FOLD]
        kinds.append(total)
    first = place[0] % 2 == 0
    mine[...] = jnp.where(first, kinds[0], kinds[1])
    send[...] = jnp.where(first, kinds[1], kinds[0])


def small(kernel, shapes, *operands, scalars=0, limit=8):
    return pl.pallas_call(
        kernel,
        out_shape=[jax.ShapeDtypeStruct(shape, dtype) for shape, dtype in shapes],
        in_specs=[SMEM] * scalars + [VMEM] * (len(operands) - scalars),
        out_specs=[VMEM] * len(shapes),
        cost_estimate=cost(0, 1 << 20),
        compiler_params=pltpu.CompilerParams(vmem_limit_bytes=limit << 20),
    )(*operands)


def same_kernel(source, target):
    target[...] = source[0]


def rows_joined(*parts):
    wide = [part.astype(jnp.float32) for part in parts]
    return jnp.concatenate(wide, axis=0).astype(parts[0].dtype)


def joined_kernel(near, far, rows):
    rows[...] = rows_joined(near[...], far[...])


def parted_kernel(near, far, left, right):
    rows = rows_joined(near[...], far[...])
    half = left.shape[1]
    left[...], right[...] = rows[:, :half], rows[:, half:]


def middle_kernel(left, left_y, right, right_x, lefts, rights):
    lefts[...] = rows_joined(left[...], left_y[...])
    rights[...] = rows_joined(right[...], right_x[...])


def fetch_kernel(count, pieces, *refs):
    sources, targets, sems = refs[:count], refs[-1 - count : -1], refs[-1]
    copies = []
    for k, (source, target) in enumerate(zip(sources, targets)):
        size = source.shape[1] // pieces
        for i in range(pieces):
            rows = pl.ds(i * size, size)
            copies.append(
                pltpu.make_async_copy(source.at[:, rows], target.at[:, rows], sems.at[k, i])
            )
    for copy in copies:
        copy.start()
    for copy in copies:
        copy.wait()


def fetch(sources, after, pieces):
    return pl.pallas_call(
        functools.partial(fetch_kernel, len(sources), pieces),
        out_shape=[pltpu.VMEM(source.shape, source.dtype) for source in sources],
        in_specs=[ANY] * (len(sources) + len(after)),
        out_specs=[VMEM] * len(sources),
        scratch_shapes=[pltpu.SemaphoreType.DMA((len(sources), pieces))],
        cost_estimate=cost(0, 2 * sum(source.size for source in sources)),
        compiler_params=pltpu.CompilerParams(vmem_limit_bytes=1 << 20),
    )(*[in_hbm(source) for source in sources], *after)


def chunks(width, most):
    return [(at, min(most, width - at)) for at in range(0, width, most)]


def inner_kernel(tile, place, lefts, left_x, rights, right_y, gate, up, *refs):
    outs, (gate_sum, up_sum, rows) = refs[:4], refs[4:]
    half = lefts.shape[1]
    rows[:, :half] = rows_joined(lefts[...], left_x[...])
    rows[:, half:] = gathered_right(rights[...], right_y[...])
    strip = outs[0].shape[1]
    first = place[0] % 2 == 0
    for weights, total, here, there in ((gate, gate_sum, *outs[:2]), (up, up_sum, *outs[2:])):
        for at, size in chunks(total.shape[1], tile):
            total[:, at : at + size] = jnp.dot(
                rows[...], weights[0, :, at : at + size], preferred_element_type=jnp.float32
            )
        low, high = total[:, :strip], total[:, strip:]
        here[...] = jnp.where(first, low, high)
        there[...] = jnp.where(first, high, low)


def inner(place, lefts, left_x, rights, right_y, gate, up, tile):
    half, width = lefts.shape
    rows, units = 2 * half, gate.shape[2]
    strip = jax.ShapeDtypeStruct((rows, units // 2), jnp.float32)
    return pl.pallas_call(
        functools.partial(inner_kernel, tile),
        out_shape=[strip] * 4,
        in_specs=[SMEM] + [VMEM] * 6,
        out_specs=[VMEM] * 4,
        scratch_shapes=[pltpu.VMEM((rows, units), jnp.float32)] * 2
        + [pltpu.VMEM((rows, 2 * width), lefts.dtype)],
        cost_estimate=cost(2 * rows * (gate.size + up.size), 2 * (gate.size + up.size)),
        compiler_params=pltpu.CompilerParams(vmem_limit_bytes=12 << 20),
    )(place, lefts, left_x, rights, right_y, gate, up)


def sums_kernel(gate, gate_in, up, up_in, gate_sum, up_sum):
    gate_sum[...] = gate[...] + gate_in[...]
    up_sum[...] = up[...] + up_in[...]


def ready_kernel(place, keep, order, mine, other, shrunk):
    first = place[0] % 2 == 0
    kinds = jnp.where(first, mine[...], other[...]), jnp.where(first, other[...], mine[...])
    for k, total in enumerate(kinds):
        value = jnp.concatenate([total] * (keep.shape[1] // FOLD), axis=1) * keep[...]
        shrunk[k] = jnp.dot(
            order[...], value.astype(shrunk.dtype), preferred_element_type=jnp.float32
        ).astype(shrunk.dtype)


def fetch_strip_kernel(other, pieces, place, source, *refs):
    target, sems = refs[-2:]
    strip = target.shape[1]
    core = place[0] % 2
    row = pl.multiple_of((1 - core if other else core) * strip, 128)
    size = strip // pieces
    copies = [
        pltpu.make_async_copy(
            source.at[:, pl.ds(row + i * size, size)], target.at[:, pl.ds(i * size, size)], sems.at[i]
        )
        for i in range(pieces)
    ]
    for copy in copies:
        copy.start()
    for copy in copies:
        copy.wait()


def fetch_strip(other, place, weights, after, pieces):
    shape = (1, weights.shape[1] // 2, weights.shape[2])
    return pl.pallas_call(
        functools.partial(fetch_strip_kernel, other, pieces),
        out_shape=pltpu.VMEM(shape, weights.dtype),
        in_specs=[SMEM] + [ANY] * (1 + len(after)),
        out_specs=VMEM,
        scratch_shapes=[pltpu.SemaphoreType.DMA((pieces,))],
        cost_estimate=cost(0, weights.size),
        compiler_params=pltpu.CompilerParams(vmem_limit_bytes=1 << 20),
    )(place, in_hbm(weights), *after)


def hidden_kernel(shrunk, gate, up, expand, hidden):
    columns = shrunk.shape[2]
    gate_sum, up_sum = [
        part[...]
        + jnp.dot(
            shrunk[k],
            expand[:, k].reshape(columns, expand.shape[3]),
            preferred_element_type=jnp.float32,
        )
        for k, part in enumerate((gate, up))
    ]
    hidden[...] = (gate_sum / (1.0 + jnp.exp(-gate_sum)) * up_sum).astype(hidden.dtype)


def down_first_kernel(tile, mine, weights, terms):
    for at, size in chunks(terms.shape[1], tile):
        terms[:, at : at + size] = jnp.dot(
            mine[...], weights[0, :, at : at + size], preferred_element_type=jnp.float32
        )


def down_kernel(x_first, start, tile, other, before, weights, stays, sends):
    part = other.shape[0] // 4
    for at, size in chunks(stays.shape[1], tile):
        source, columns = pl.ds(start + at, size), pl.ds(at, size)
        terms = before[:, source] + jnp.dot(
            other[...], weights[0, :, source], preferred_element_type=jnp.float32
        )
        low_y, high_y, far_low, far_high = [terms[k * part : (k + 1) * part] for k in range(4)]
        if x_first:
            stay, send = (low_y, high_y), (far_low, far_high)
        else:
            stay, send = (low_y, far_low), (high_y, far_high)
        stays[:, columns] = jnp.concatenate(stay, axis=0)
        sends[:, columns] = jnp.concatenate(send, axis=0).astype(sends.dtype)


def packed(total, pieces):
    size = total.shape[1] // pieces
    return jnp.concatenate([total[:, i * size : (i + 1) * size] for i in range(pieces)], axis=0)


def unpacked(packed_rows, pieces):
    wide = packed_rows.astype(jnp.float32)
    rows = wide.shape[0] // pieces
    return jnp.concatenate([wide[i * rows : (i + 1) * rows] for i in range(pieces)], axis=1)


def split_kernel(left, left_in, right, right_in, stay, send):
    totals = [
        part[...] + received[...].astype(jnp.float32)
        for part, received in ((left, left_in), (right, right_in))
    ]
    total = jnp.concatenate(totals, axis=1)
    half = stay.shape[0]
    stay[...], send[...] = total[:half], packed(total[half:], 2).astype(send.dtype)


def split_kernel_last(before, received, stay, send):
    total = before[...] + unpacked(received[...], 2)
    half = stay.shape[0]
    stay[...], send[...] = total[:half], packed(total[half:], 4).astype(send.dtype)


def last_kernel(stay, received, out):
    out[0] = (stay[...] + unpacked(received[...], 4)).astype(out.dtype)


def shards(tokens, w_gate, w_up, w_down, shrink_factors, expand_factors, rank_blocks, row_counts):
    count = lax.axis_size("tensor")
    units = w_gate.shape[2]
    if count != 32 or units % 256:
        return general_shards(
            tokens, w_gate, w_up, w_down, shrink_factors, expand_factors, rank_blocks, row_counts
        )
    place = lax.axis_index("tensor").reshape(1)
    block_rows, width = tokens.shape[1], tokens.shape[2]
    rows = 16 * block_rows
    half, columns = width // 2, shrink_factors.shape[2]
    wide, narrow = jnp.float32, jnp.bfloat16
    blocks = blocks_of(expand_factors, count)

    (own,) = small(same_kernel, [((block_rows, width), narrow)], tokens)
    own, other = lax.optimization_barrier((own, to_chip(tokens[0], Z2)))
    (own,) = small(joined_kernel, [((2 * block_rows, width), narrow)], own, other)
    blocks, other = lax.optimization_barrier((blocks, to_chip(own, Z1)))
    left, right = small(parted_kernel, [((4 * block_rows, half), narrow)] * 2, own, other)
    place, blocks, left, right = lax.optimization_barrier((place, blocks, left, right))
    expand = lax.all_to_all(blocks, "tensor", split_axis=0, concat_axis=0, tiled=True)

    hops = to_chip(left, Y), to_chip(right, X)
    fetched = fetch((w_gate, w_up, shrink_factors), (left,), 4)
    hops, fetched = lax.optimization_barrier((hops, fetched))
    gate_weights, up_weights, factors = fetched
    lefts, rights = small(
        middle_kernel, [((8 * block_rows, half), narrow)] * 2, left, hops[0], right, hops[1]
    )
    gathered = lefts, to_chip(lefts, X), rights, to_chip(rights, Y)

    folded, other, keep, order = small(
        shrink_kernel,
        [((rows, FOLD), wide)] * 2 + [((rows, columns), wide), ((rows, rows), narrow)],
        place,
        rank_blocks,
        row_counts,
        *gathered,
        factors,
        scalars=3,
    )
    folded = folded + swapped(other, "tensor", 0)
    folded = folded + to_chip(folded, Y)
    strips = inner(place, *gathered, gate_weights, up_weights, 256)
    folded, strips = lax.optimization_barrier((folded, strips))
    folded = folded + to_chip(folded, X)
    gate, gate_out, up, up_out = strips
    strip = (gate.shape, wide)
    sums = small(
        sums_kernel, [strip] * 2, gate, swapped(gate_out, "tensor", 0), up, swapped(up_out, "tensor", 0)
    )
    own_weights = fetch_strip(False, place, w_down, (expand, *sums), 4)
    received, own_weights = lax.optimization_barrier((to_chip(folded, Z1), own_weights))
    folded = folded + received
    other_weights = fetch_strip(True, place, w_down, (folded, own_weights), 4)
    received, other_weights = lax.optimization_barrier((to_chip(folded, Z2), other_weights))
    folded = folded + received
    (shrunk,) = small(
        ready_kernel,
        [((2, rows, columns), narrow)],
        place,
        keep,
        order,
        folded,
        swapped(folded, "tensor", 0),
        scalars=1,
    )
    hidden_shape = (strip[0], narrow)
    (hidden,) = small(hidden_kernel, [hidden_shape], shrunk, *sums, expand)
    other = swapped(hidden, "tensor", 0)
    (before,) = small(
        functools.partial(down_first_kernel, 256),
        [((rows, width), wide)],
        hidden,
        own_weights,
    )
    split = half
    sums = []
    for x_first, first, second in ((True, X, Y), (False, Y, X)):
        start, size = (0, split) if x_first else (split, width - split)
        stays, sends = small(
            functools.partial(down_kernel, x_first, start, 256),
            [((rows // 2, size), wide), ((rows // 2, size), narrow)],
            other,
            before,
            other_weights,
        )
        stays = stays + to_chip(sends, first)
        part = 4 * block_rows
        sums += [stays[:part], to_chip(stays[part:].astype(narrow), second)]
    stay, send = small(
        split_kernel, [((part // 2, width), wide), ((part, half), narrow)], *sums
    )
    stay, send = small(
        split_kernel_last,
        [((block_rows, width), wide), ((part, width // 4), narrow)],
        stay,
        to_chip(send, Z1),
    )
    (out,) = small(last_kernel, [((1, block_rows, width), narrow)], stay, to_chip(send, Z2))
    return out


def solution(mesh):
    placed = (
        P(("groups", "tensor"), None, None),
        P("tensor", None, None),
        P("tensor", None, None),
        P("tensor", None, None),
        P("groups", "tensor", None),
        P("groups", "tensor", None),
        P("groups"),
        P("groups"),
    )
    return jax.shard_map(
        shards,
        mesh=mesh,
        in_specs=placed,
        out_specs=P(("groups", "tensor"), None, None),
        check_vma=False,
    )
```

```python
import functools

import jax
import jax.numpy as jnp
from jax import lax
from jax.experimental import pallas as pl
from jax.experimental.pallas import tpu as pltpu
from jax.sharding import PartitionSpec as P

HIDDEN_BITS = 4
FOLD = 128


def swapped(block, axis, apart):
    count = lax.axis_size(axis)
    return lax.ppermute(block, axis, [(i, i ^ (1 << apart)) for i in range(count)])


def by_target(expand, count):
    kinds, depth, width = expand.shape
    return expand.reshape(kinds, depth, count, width // count).transpose(2, 0, 1, 3)


def owner_of(ends, ids):
    return jnp.sum((ends[None, :] <= ids[:, None]).astype(jnp.int32), axis=1)


def keep_mask(rank_blocks, row_counts, columns, rows):
    adapters = rank_blocks.shape[0]
    earlier = jnp.arange(adapters)[:, None] >= jnp.arange(adapters)[None, :]
    block_end = jnp.sum(jnp.where(earlier, rank_blocks[None, :], 0), axis=1)
    row_end = jnp.sum(jnp.where(earlier, row_counts[None, :], 0), axis=1)
    column_owner = owner_of(block_end, jnp.arange(columns, dtype=jnp.int32) // 16)
    row_owner = owner_of(row_end, jnp.arange(rows, dtype=jnp.int32))
    ids = jnp.arange(adapters, dtype=jnp.int32)
    row_blocks = jnp.sum(
        jnp.where(row_owner[:, None] == ids[None, :], rank_blocks[None, :], 0), axis=1
    )
    same = (row_owner[:, None] == column_owner[None, :]).astype(jnp.float32)
    return same, 1.0 / row_blocks.astype(jnp.float32)


def general_shards(tokens, w_gate, w_up, w_down, shrink_factors, expand_factors, rank_blocks, row_counts):
    count = lax.axis_size("tensor")
    low_bits = count.bit_length() - 1 - HIDDEN_BITS
    fgroups = 1 << low_bits
    place = lax.axis_index("tensor")
    feature_group = place % fgroups
    hidden_group = place // fgroups
    block_rows = tokens.shape[1]
    rows = block_rows << HIDDEN_BITS
    units = w_gate.shape[2]
    strip = units // fgroups

    expand = lax.all_to_all(
        by_target(expand_factors, count), "tensor", split_axis=0, concat_axis=0, tiled=True
    )

    gathered = tokens[0]
    for bit in reversed(range(HIDDEN_BITS)):
        other = swapped(gathered, "tensor", low_bits + bit)
        gathered = jnp.concatenate([gathered, other], 0)
    spots = jnp.arange(1 << HIDDEN_BITS, dtype=jnp.int32)
    moved = sum(((spots >> i) & 1) << (HIDDEN_BITS - 1 - i) for i in range(HIDDEN_BITS))
    natural = (
        (moved ^ hidden_group)[:, None] * block_rows + jnp.arange(block_rows, dtype=jnp.int32)[None, :]
    ).reshape(rows)
    to_own = (natural[:, None] == jnp.arange(rows, dtype=jnp.int32)[None, :]).astype(jnp.bfloat16)

    columns = shrink_factors.shape[2]
    same, scale = keep_mask(rank_blocks, row_counts, columns, rows)
    slab = shrink_factors.shape[1]
    features = lax.dynamic_slice_in_dim(gathered, hidden_group * slab, slab, 1)
    features = jnp.dot(to_own.T, features, preferred_element_type=jnp.float32).astype(jnp.bfloat16)
    partial_value = jnp.einsum(
        "rd,kdc->krc", features, shrink_factors, preferred_element_type=jnp.float32
    )
    folded = jnp.sum((partial_value * same).reshape(2, rows, columns // FOLD, FOLD), axis=2)
    for bit in range(low_bits + HIDDEN_BITS):
        folded = folded + swapped(folded, "tensor", bit)
    shrunk = jnp.tile(folded, (1, 1, columns // FOLD)) * (same * scale[:, None])[None]
    shrunk = shrunk.astype(jnp.bfloat16)
    shrunk = jnp.einsum("or,krc->koc", to_own, shrunk, preferred_element_type=jnp.float32)
    shrunk = shrunk.astype(jnp.bfloat16)

    gate_part = jnp.dot(gathered, w_gate[0], preferred_element_type=jnp.float32)
    up_part = jnp.dot(gathered, w_up[0], preferred_element_type=jnp.float32)
    partials = jnp.stack([gate_part, up_part])
    for step in range(low_bits):
        bit = low_bits - 1 - step
        half = partials.shape[2] // 2
        high = feature_group // (1 << bit) % 2
        outgoing = lax.dynamic_slice_in_dim(partials, (1 - high) * half, half, 2)
        staying = lax.dynamic_slice_in_dim(partials, high * half, half, 2)
        partials = staying + swapped(outgoing, "tensor", bit)
    depth = expand.shape[2]
    low_rank = jnp.einsum(
        "krsd,skdc->krc",
        shrunk.reshape(2, rows, count, depth),
        expand,
        preferred_element_type=jnp.float32,
    )
    partials = partials + low_rank
    hidden = (jax.nn.silu(partials[0]) * partials[1]).astype(jnp.bfloat16)
    for step in range(low_bits):
        other = swapped(hidden, "tensor", step)
        high = feature_group // (1 << step) % 2 == 1
        hidden = jnp.where(
            high, jnp.concatenate([other, hidden], 1), jnp.concatenate([hidden, other], 1)
        )
    terms = jnp.dot(hidden, w_down[0], preferred_element_type=jnp.float32)
    for bit in range(HIDDEN_BITS):
        half = terms.shape[0] // 2
        outgoing = terms[half:].astype(jnp.bfloat16)
        terms = terms[:half] + swapped(outgoing, "tensor", low_bits + bit).astype(jnp.float32)
    return terms.astype(jnp.bfloat16)[None]


def keeping(ranks, counts, rows, columns):
    row = lax.broadcasted_iota(jnp.int32, (rows, 1), 0)
    block = lax.broadcasted_iota(jnp.int32, (1, columns), 1) // 16
    row_owner, column_owner = jnp.zeros_like(row), jnp.zeros_like(block)
    row_end = block_end = 0
    for adapter in range(ranks.shape[0]):
        row_end, block_end = row_end + counts[adapter], block_end + ranks[adapter]
        row_owner += (row >= row_end).astype(jnp.int32)
        column_owner += (block >= block_end).astype(jnp.int32)
    blocks = jnp.zeros_like(row)
    for adapter in range(ranks.shape[0]):
        blocks = jnp.where(row_owner == adapter, ranks[adapter], blocks)
    return row_owner == column_owner, 1.0 / blocks.astype(jnp.float32)


VMEM = pl.BlockSpec(memory_space=pltpu.VMEM)
SMEM = pl.BlockSpec(memory_space=pltpu.SMEM)
ANY = pl.BlockSpec(memory_space=pl.ANY)
X, Y, Z1, Z2 = 1, 2, 4, 8


def to_chip(block, apart):
    count = lax.axis_size("tensor")
    return lax.ppermute(block, "tensor", [(i, i ^ (apart << 1)) for i in range(count)])


def cost(flops, read):
    return pl.CostEstimate(flops=flops, bytes_accessed=read, transcendentals=0)


def in_hbm(array):
    return pltpu.with_memory_space_constraint(array, pltpu.HBM)


def blocks_kernel(count, strip, source, target):
    for j in range(count):
        target[j] = source[:, :, j * strip : (j + 1) * strip]


def blocks_of(expand, count):
    kinds, depth, width = expand.shape
    strip = width // count
    return pl.pallas_call(
        functools.partial(blocks_kernel, count, strip),
        out_shape=jax.ShapeDtypeStruct((count, kinds, depth, strip), expand.dtype),
        in_specs=[VMEM],
        out_specs=VMEM,
        cost_estimate=cost(0, 4 * expand.size),
        compiler_params=pltpu.CompilerParams(vmem_limit_bytes=10 << 20),
    )(expand)


def own_order(place, rows, own_axis):
    block = rows // 16
    own, natural = [lax.broadcasted_iota(jnp.int32, (rows, rows), axis) for axis in (own_axis, 1 - own_axis)]
    spot = own // block
    far = spot // 8 + spot // 4 % 2 * 2 + spot // 2 % 2 * 4 + spot % 2 * 8
    return ((far ^ (place // 2)) * block + (own - spot * block) == natural).astype(jnp.bfloat16)


def gathered_right(rights, right_y):
    part = rights.shape[0] // 2
    wide, corner = rights.astype(jnp.float32), right_y.astype(jnp.float32)
    pieces = [wide[:part], corner[:part], wide[part:], corner[part:]]
    return jnp.concatenate(pieces, axis=0).astype(rights.dtype)


def shrink_kernel(place, ranks, counts, near, far, factors, folded, keep, order):
    rows, columns = folded.shape[1], factors.shape[2]
    same, scale = keeping(ranks, counts, rows, columns)
    keep[...] = jnp.where(same, scale, 0.0)
    order[...] = own_order(place[0], rows, 0)
    features = jnp.concatenate([near[...], far[...]], axis=0)
    features = jnp.dot(
        own_order(place[0], rows, 1), features, preferred_element_type=jnp.float32
    ).astype(jnp.bfloat16)
    for k in range(2):
        value = jnp.dot(features, factors[k], preferred_element_type=jnp.float32)
        value = jnp.where(same, value, 0.0)
        total = value[:, :FOLD]
        for start in range(FOLD, columns, FOLD):
            total = total + value[:, start : start + FOLD]
        folded[k] = total


def small(kernel, shapes, *operands, scalars=0, limit=8):
    return pl.pallas_call(
        kernel,
        out_shape=[jax.ShapeDtypeStruct(shape, dtype) for shape, dtype in shapes],
        in_specs=[SMEM] * scalars + [VMEM] * (len(operands) - scalars),
        out_specs=[VMEM] * len(shapes),
        cost_estimate=cost(0, 1 << 20),
        compiler_params=pltpu.CompilerParams(vmem_limit_bytes=limit << 20),
    )(*operands)


def same_kernel(source, target):
    target[...] = source[0]


def rows_joined(*parts):
    wide = [part.astype(jnp.float32) for part in parts]
    return jnp.concatenate(wide, axis=0).astype(parts[0].dtype)


def joined_kernel(near, far, rows):
    rows[...] = rows_joined(near[...], far[...])


def parted_kernel(place, near, far, left, right, keep, send, rows):
    rows[...] = rows_joined(near[...], far[...])
    half, size = left.shape[1], keep.shape[1]
    left[...], right[...] = rows[:, :half], rows[:, half:]
    at = place[0] // 8 * 2 * size
    low, high = [rows[:, pl.ds(pl.multiple_of(at + i * size, size), size)] for i in range(2)]
    first = place[0] // 4 % 2 == 0
    keep[...] = jnp.where(first, low, high)
    send[...] = jnp.where(first, high, low)


def parted(place, near, far, slabs):
    part, width = near.shape
    shapes = [(2 * part, width // 2)] * 2 + [(2 * part, slabs)] * 2
    return pl.pallas_call(
        parted_kernel,
        out_shape=[jax.ShapeDtypeStruct(shape, near.dtype) for shape in shapes],
        in_specs=[SMEM, VMEM, VMEM],
        out_specs=[VMEM] * 4,
        scratch_shapes=[pltpu.VMEM((2 * part, width), near.dtype)],
        cost_estimate=cost(0, 8 * near.size),
        compiler_params=pltpu.CompilerParams(vmem_limit_bytes=8 << 20),
    )(place, near, far)


def slab_kernel(place, slab, slab_y, keep, send):
    rows, size = rows_joined(slab[...], slab_y[...]), keep.shape[1]
    first = place[0] // 2 % 2 == 0
    keep[...] = jnp.where(first, rows[:, :size], rows[:, size:])
    send[...] = jnp.where(first, rows[:, size:], rows[:, :size])


def middle_kernel(left, left_y, right, right_x, lefts, rights):
    lefts[...] = rows_joined(left[...], left_y[...])
    rights[...] = rows_joined(right[...], right_x[...])


def fetch_kernel(count, pieces, *refs):
    sources, targets, sems = refs[:count], refs[-1 - count : -1], refs[-1]
    copies = []
    for k, (source, target) in enumerate(zip(sources, targets)):
        size = source.shape[1] // pieces
        for i in range(pieces):
            rows = pl.ds(i * size, size)
            copies.append(
                pltpu.make_async_copy(source.at[:, rows], target.at[:, rows], sems.at[k, i])
            )
    for copy in copies:
        copy.start()
    for copy in copies:
        copy.wait()


def fetch(sources, after, pieces):
    return pl.pallas_call(
        functools.partial(fetch_kernel, len(sources), pieces),
        out_shape=[pltpu.VMEM(source.shape, source.dtype) for source in sources],
        in_specs=[ANY] * (len(sources) + len(after)),
        out_specs=[VMEM] * len(sources),
        scratch_shapes=[pltpu.SemaphoreType.DMA((len(sources), pieces))],
        cost_estimate=cost(0, 2 * sum(source.size for source in sources)),
        compiler_params=pltpu.CompilerParams(vmem_limit_bytes=1 << 20),
    )(*[in_hbm(source) for source in sources], *after)


def chunks(width, most):
    return [(at, min(most, width - at)) for at in range(0, width, most)]


def inner_kernel(tile, place, lefts, left_x, rights, right_y, gate, up, *refs):
    outs, (gate_sum, up_sum, rows) = refs[:4], refs[4:]
    half = lefts.shape[1]
    rows[:, :half] = rows_joined(lefts[...], left_x[...])
    rows[:, half:] = gathered_right(rights[...], right_y[...])
    strip = outs[0].shape[1]
    first = place[0] % 2 == 0
    for weights, total, here, there in ((gate, gate_sum, *outs[:2]), (up, up_sum, *outs[2:])):
        for at, size in chunks(total.shape[1], tile):
            total[:, at : at + size] = jnp.dot(
                rows[...], weights[0, :, at : at + size], preferred_element_type=jnp.float32
            )
        low, high = total[:, :strip], total[:, strip:]
        here[...] = jnp.where(first, low, high)
        there[...] = jnp.where(first, high, low)


def inner(place, lefts, left_x, rights, right_y, gate, up, tile):
    half, width = lefts.shape
    rows, units = 2 * half, gate.shape[2]
    strip = jax.ShapeDtypeStruct((rows, units // 2), jnp.float32)
    return pl.pallas_call(
        functools.partial(inner_kernel, tile),
        out_shape=[strip] * 4,
        in_specs=[SMEM] + [VMEM] * 6,
        out_specs=[VMEM] * 4,
        scratch_shapes=[pltpu.VMEM((rows, units), jnp.float32)] * 2
        + [pltpu.VMEM((rows, 2 * width), lefts.dtype)],
        cost_estimate=cost(2 * rows * (gate.size + up.size), 2 * (gate.size + up.size)),
        compiler_params=pltpu.CompilerParams(vmem_limit_bytes=12 << 20),
    )(place, lefts, left_x, rights, right_y, gate, up)


def sums_kernel(gate, gate_in, up, up_in, gate_sum, up_sum):
    gate_sum[...] = gate[...] + gate_in[...]
    up_sum[...] = up[...] + up_in[...]


def ready_kernel(keep, order, folded, near, far, both, shrunk):
    for k in range(2):
        planes = [part[k].astype(jnp.float32) for part in (near, far, both)]
        total = (folded[k] + planes[0]) + (planes[1] + planes[2])
        value = jnp.concatenate([total] * (keep.shape[1] // FOLD), axis=1) * keep[...]
        shrunk[k] = jnp.dot(
            order[...], value.astype(shrunk.dtype), preferred_element_type=jnp.float32
        ).astype(shrunk.dtype)


def hidden_kernel(shrunk, gate, up, expand, hidden):
    columns = shrunk.shape[2]
    gate_sum, up_sum = [
        part[...]
        + jnp.dot(
            shrunk[k],
            expand[:, k].reshape(columns, expand.shape[3]),
            preferred_element_type=jnp.float32,
        )
        for k, part in enumerate((gate, up))
    ]
    hidden[...] = (gate_sum / (1.0 + jnp.exp(-gate_sum)) * up_sum).astype(hidden.dtype)


def down_first_kernel(tile, place, mine, weights, terms):
    strip = mine.shape[1]
    rows = pl.ds(pl.multiple_of(place[0] % 2 * strip, 128), strip)
    for at, size in chunks(terms.shape[1], tile):
        terms[:, at : at + size] = jnp.dot(
            mine[...], weights[0, rows, at : at + size], preferred_element_type=jnp.float32
        )


def down_kernel(x_first, start, tile, place, other, before, weights, stays, sends):
    strip = other.shape[1]
    rows = pl.ds(pl.multiple_of((1 - place[0] % 2) * strip, 128), strip)
    part = other.shape[0] // 4
    for at, size in chunks(stays.shape[1], tile):
        source, columns = pl.ds(start + at, size), pl.ds(at, size)
        terms = before[:, source] + jnp.dot(
            other[...], weights[0, rows, source], preferred_element_type=jnp.float32
        )
        low_y, high_y, far_low, far_high = [terms[k * part : (k + 1) * part] for k in range(4)]
        if x_first:
            stay, send = (low_y, high_y), (far_low, far_high)
        else:
            stay, send = (low_y, far_low), (high_y, far_high)
        stays[:, columns] = jnp.concatenate(stay, axis=0)
        sends[:, columns] = jnp.concatenate(send, axis=0).astype(sends.dtype)


def packed(total, pieces):
    size = total.shape[1] // pieces
    return jnp.concatenate([total[:, i * size : (i + 1) * size] for i in range(pieces)], axis=0)


def unpacked(packed_rows, pieces):
    wide = packed_rows.astype(jnp.float32)
    rows = wide.shape[0] // pieces
    return jnp.concatenate([wide[i * rows : (i + 1) * rows] for i in range(pieces)], axis=1)


def split_kernel(left, left_in, right, right_in, stay, send):
    totals = [
        part[...] + received[...].astype(jnp.float32)
        for part, received in ((left, left_in), (right, right_in))
    ]
    total = jnp.concatenate(totals, axis=1)
    half = stay.shape[0]
    stay[...], send[...] = total[:half], packed(total[half:], 2).astype(send.dtype)


def split_kernel_last(before, received, stay, send):
    total = before[...] + unpacked(received[...], 2)
    half = stay.shape[0]
    stay[...], send[...] = total[:half], packed(total[half:], 4).astype(send.dtype)


def last_kernel(stay, received, out):
    out[0] = (stay[...] + unpacked(received[...], 4)).astype(out.dtype)


def shards(tokens, w_gate, w_up, w_down, shrink_factors, expand_factors, rank_blocks, row_counts):
    count = lax.axis_size("tensor")
    units = w_gate.shape[2]
    if count != 32 or units % 256:
        return general_shards(
            tokens, w_gate, w_up, w_down, shrink_factors, expand_factors, rank_blocks, row_counts
        )
    place = lax.axis_index("tensor").reshape(1)
    block_rows, width = tokens.shape[1], tokens.shape[2]
    rows = 16 * block_rows
    half, columns = width // 2, shrink_factors.shape[2]
    wide, narrow = jnp.float32, jnp.bfloat16
    blocks = blocks_of(expand_factors, count)

    (own,) = small(same_kernel, [((block_rows, width), narrow)], tokens)
    own, other = lax.optimization_barrier((own, to_chip(tokens[0], Z2)))
    (own,) = small(joined_kernel, [((2 * block_rows, width), narrow)], own, other)
    blocks, other = lax.optimization_barrier((blocks, to_chip(own, Z1)))
    slab = shrink_factors.shape[1]
    left, right, near, far = parted(place, own, other, 2 * slab)
    place, blocks, left, right, near, far = lax.optimization_barrier(
        (place, blocks, left, right, near, far)
    )
    expand = lax.all_to_all(blocks, "tensor", split_axis=0, concat_axis=0, tiled=True)

    hops = to_chip(far, Y), to_chip(left, Y), to_chip(right, X)
    hops, (gate_weights,) = lax.optimization_barrier((hops, fetch((w_gate,), (left,), 4)))
    near, far = small(
        slab_kernel, [((8 * block_rows, slab), narrow)] * 2, place, near, hops[0], scalars=1
    )
    lefts, rights = small(
        middle_kernel, [((8 * block_rows, half), narrow)] * 2, left, hops[1], right, hops[2]
    )
    far, (up_weights, factors) = lax.optimization_barrier(
        (to_chip(far, X), fetch((w_up, shrink_factors), (far, lefts), 4))
    )
    gathered = lefts, to_chip(lefts, X), rights, to_chip(rights, Y)

    folded, keep, order = small(
        shrink_kernel,
        [((2, rows, FOLD), wide), ((rows, columns), wide), ((rows, rows), narrow)],
        place,
        rank_blocks,
        row_counts,
        near,
        far,
        factors,
        scalars=3,
    )
    folded = folded + swapped(folded, "tensor", 0)
    folded = folded + to_chip(folded, Y)
    strips = inner(place, *gathered, gate_weights, up_weights, 256)
    folded, strips = lax.optimization_barrier((folded, strips))
    folded = folded + to_chip(folded, X)
    sent = folded.astype(narrow)
    received = [to_chip(sent, apart) for apart in (Z1, Z2, Z1 | Z2)]

    gate, gate_out, up, up_out = strips
    strip = (gate.shape, wide)
    sums = small(
        sums_kernel, [strip] * 2, gate, swapped(gate_out, "tensor", 0), up, swapped(up_out, "tensor", 0)
    )
    received, (down_weights,) = lax.optimization_barrier(
        (received, fetch((w_down,), (expand, *sums), 4))
    )
    (shrunk,) = small(ready_kernel, [((2, rows, columns), narrow)], keep, order, folded, *received)
    hidden_shape = (strip[0], narrow)
    (hidden,) = small(hidden_kernel, [hidden_shape], shrunk, *sums, expand)
    other = swapped(hidden, "tensor", 0)
    (before,) = small(
        functools.partial(down_first_kernel, 256),
        [((rows, width), wide)],
        place,
        hidden,
        down_weights,
        scalars=1,
    )
    split = half
    sums = []
    for x_first, first, second in ((True, X, Y), (False, Y, X)):
        start, size = (0, split) if x_first else (split, width - split)
        stays, sends = small(
            functools.partial(down_kernel, x_first, start, 256),
            [((rows // 2, size), wide), ((rows // 2, size), narrow)],
            place,
            other,
            before,
            down_weights,
            scalars=1,
        )
        stays = stays + to_chip(sends, first)
        part = 4 * block_rows
        sums += [stays[:part], to_chip(stays[part:].astype(narrow), second)]
    stay, send = small(
        split_kernel, [((part // 2, width), wide), ((part, half), narrow)], *sums
    )
    stay, send = small(
        split_kernel_last,
        [((block_rows, width), wide), ((part, width // 4), narrow)],
        stay,
        to_chip(send, Z1),
    )
    (out,) = small(last_kernel, [((1, block_rows, width), narrow)], stay, to_chip(send, Z2))
    return out


def solution(mesh):
    placed = (
        P(("groups", "tensor"), None, None),
        P("tensor", None, None),
        P("tensor", None, None),
        P("tensor", None, None),
        P("groups", "tensor", None),
        P("groups", "tensor", None),
        P("groups"),
        P("groups"),
    )
    return jax.shard_map(
        shards,
        mesh=mesh,
        in_specs=placed,
        out_specs=P(("groups", "tensor"), None, None),
        check_vma=False,
    )
```

```python
import functools

import jax
import jax.numpy as jnp
from jax import lax
from jax.experimental import pallas as pl
from jax.experimental.pallas import tpu as pltpu
from jax.sharding import PartitionSpec as P

HIDDEN_BITS = 4
FOLD = 128


def swapped(block, axis, apart):
    count = lax.axis_size(axis)
    return lax.ppermute(block, axis, [(i, i ^ (1 << apart)) for i in range(count)])


def by_target(expand, count):
    kinds, depth, width = expand.shape
    return expand.reshape(kinds, depth, count, width // count).transpose(2, 0, 1, 3)


def owner_of(ends, ids):
    return jnp.sum((ends[None, :] <= ids[:, None]).astype(jnp.int32), axis=1)


def keep_mask(rank_blocks, row_counts, columns, rows):
    adapters = rank_blocks.shape[0]
    earlier = jnp.arange(adapters)[:, None] >= jnp.arange(adapters)[None, :]
    block_end = jnp.sum(jnp.where(earlier, rank_blocks[None, :], 0), axis=1)
    row_end = jnp.sum(jnp.where(earlier, row_counts[None, :], 0), axis=1)
    column_owner = owner_of(block_end, jnp.arange(columns, dtype=jnp.int32) // 16)
    row_owner = owner_of(row_end, jnp.arange(rows, dtype=jnp.int32))
    ids = jnp.arange(adapters, dtype=jnp.int32)
    row_blocks = jnp.sum(
        jnp.where(row_owner[:, None] == ids[None, :], rank_blocks[None, :], 0), axis=1
    )
    same = (row_owner[:, None] == column_owner[None, :]).astype(jnp.float32)
    return same, 1.0 / row_blocks.astype(jnp.float32)


def general_shards(tokens, w_gate, w_up, w_down, shrink_factors, expand_factors, rank_blocks, row_counts):
    count = lax.axis_size("tensor")
    low_bits = count.bit_length() - 1 - HIDDEN_BITS
    fgroups = 1 << low_bits
    place = lax.axis_index("tensor")
    feature_group = place % fgroups
    hidden_group = place // fgroups
    block_rows = tokens.shape[1]
    rows = block_rows << HIDDEN_BITS
    units = w_gate.shape[2]
    strip = units // fgroups

    expand = lax.all_to_all(
        by_target(expand_factors, count), "tensor", split_axis=0, concat_axis=0, tiled=True
    )

    gathered = tokens[0]
    for bit in reversed(range(HIDDEN_BITS)):
        other = swapped(gathered, "tensor", low_bits + bit)
        gathered = jnp.concatenate([gathered, other], 0)
    spots = jnp.arange(1 << HIDDEN_BITS, dtype=jnp.int32)
    moved = sum(((spots >> i) & 1) << (HIDDEN_BITS - 1 - i) for i in range(HIDDEN_BITS))
    natural = (
        (moved ^ hidden_group)[:, None] * block_rows + jnp.arange(block_rows, dtype=jnp.int32)[None, :]
    ).reshape(rows)
    to_own = (natural[:, None] == jnp.arange(rows, dtype=jnp.int32)[None, :]).astype(jnp.bfloat16)

    columns = shrink_factors.shape[2]
    same, scale = keep_mask(rank_blocks, row_counts, columns, rows)
    slab = shrink_factors.shape[1]
    features = lax.dynamic_slice_in_dim(gathered, hidden_group * slab, slab, 1)
    features = jnp.dot(to_own.T, features, preferred_element_type=jnp.float32).astype(jnp.bfloat16)
    partial_value = jnp.einsum(
        "rd,kdc->krc", features, shrink_factors, preferred_element_type=jnp.float32
    )
    folded = jnp.sum((partial_value * same).reshape(2, rows, columns // FOLD, FOLD), axis=2)
    for bit in range(low_bits + HIDDEN_BITS):
        folded = folded + swapped(folded, "tensor", bit)
    shrunk = jnp.tile(folded, (1, 1, columns // FOLD)) * (same * scale[:, None])[None]
    shrunk = shrunk.astype(jnp.bfloat16)
    shrunk = jnp.einsum("or,krc->koc", to_own, shrunk, preferred_element_type=jnp.float32)
    shrunk = shrunk.astype(jnp.bfloat16)

    gate_part = jnp.dot(gathered, w_gate[0], preferred_element_type=jnp.float32)
    up_part = jnp.dot(gathered, w_up[0], preferred_element_type=jnp.float32)
    partials = jnp.stack([gate_part, up_part])
    for step in range(low_bits):
        bit = low_bits - 1 - step
        half = partials.shape[2] // 2
        high = feature_group // (1 << bit) % 2
        outgoing = lax.dynamic_slice_in_dim(partials, (1 - high) * half, half, 2)
        staying = lax.dynamic_slice_in_dim(partials, high * half, half, 2)
        partials = staying + swapped(outgoing, "tensor", bit)
    depth = expand.shape[2]
    low_rank = jnp.einsum(
        "krsd,skdc->krc",
        shrunk.reshape(2, rows, count, depth),
        expand,
        preferred_element_type=jnp.float32,
    )
    partials = partials + low_rank
    hidden = (jax.nn.silu(partials[0]) * partials[1]).astype(jnp.bfloat16)
    for step in range(low_bits):
        other = swapped(hidden, "tensor", step)
        high = feature_group // (1 << step) % 2 == 1
        hidden = jnp.where(
            high, jnp.concatenate([other, hidden], 1), jnp.concatenate([hidden, other], 1)
        )
    terms = jnp.dot(hidden, w_down[0], preferred_element_type=jnp.float32)
    for bit in range(HIDDEN_BITS):
        half = terms.shape[0] // 2
        outgoing = terms[half:].astype(jnp.bfloat16)
        terms = terms[:half] + swapped(outgoing, "tensor", low_bits + bit).astype(jnp.float32)
    return terms.astype(jnp.bfloat16)[None]


def keeping(ranks, counts, rows, columns):
    row = lax.broadcasted_iota(jnp.int32, (rows, 1), 0)
    block = lax.broadcasted_iota(jnp.int32, (1, columns), 1) // 16
    row_owner, column_owner = jnp.zeros_like(row), jnp.zeros_like(block)
    row_end = block_end = 0
    for adapter in range(ranks.shape[0]):
        row_end, block_end = row_end + counts[adapter], block_end + ranks[adapter]
        row_owner += (row >= row_end).astype(jnp.int32)
        column_owner += (block >= block_end).astype(jnp.int32)
    blocks = jnp.zeros_like(row)
    for adapter in range(ranks.shape[0]):
        blocks = jnp.where(row_owner == adapter, ranks[adapter], blocks)
    return row_owner == column_owner, 1.0 / blocks.astype(jnp.float32)


VMEM = pl.BlockSpec(memory_space=pltpu.VMEM)
SMEM = pl.BlockSpec(memory_space=pltpu.SMEM)
ANY = pl.BlockSpec(memory_space=pl.ANY)
X, Y, Z1, Z2 = 1, 2, 4, 8


def to_chip(block, apart):
    count = lax.axis_size("tensor")
    return lax.ppermute(block, "tensor", [(i, i ^ (apart << 1)) for i in range(count)])


def cost(flops, read):
    return pl.CostEstimate(flops=flops, bytes_accessed=read, transcendentals=0)


def in_hbm(array):
    return pltpu.with_memory_space_constraint(array, pltpu.HBM)


def blocks_kernel(count, strip, source, target):
    for j in range(count):
        target[j] = source[:, :, j * strip : (j + 1) * strip]


def blocks_of(expand, count):
    kinds, depth, width = expand.shape
    strip = width // count
    return pl.pallas_call(
        functools.partial(blocks_kernel, count, strip),
        out_shape=jax.ShapeDtypeStruct((count, kinds, depth, strip), expand.dtype),
        in_specs=[VMEM],
        out_specs=VMEM,
        cost_estimate=cost(0, 4 * expand.size),
        compiler_params=pltpu.CompilerParams(vmem_limit_bytes=10 << 20),
    )(expand)


def own_order(place, rows, own_axis):
    block = rows // 16
    own, natural = [lax.broadcasted_iota(jnp.int32, (rows, rows), axis) for axis in (own_axis, 1 - own_axis)]
    spot = own // block
    far = spot // 8 + spot // 4 % 2 * 2 + spot // 2 % 2 * 4 + spot % 2 * 8
    return ((far ^ (place // 2)) * block + (own - spot * block) == natural).astype(jnp.bfloat16)


def gathered_right(rights, right_y):
    part = rights.shape[0] // 2
    wide, corner = rights.astype(jnp.float32), right_y.astype(jnp.float32)
    pieces = [wide[:part], corner[:part], wide[part:], corner[part:]]
    return jnp.concatenate(pieces, axis=0).astype(rights.dtype)


def shrink_kernel(place, ranks, counts, near, far, factors, folded, keep, order):
    rows, columns = folded.shape[1], factors.shape[2]
    same, scale = keeping(ranks, counts, rows, columns)
    keep[...] = jnp.where(same, scale, 0.0)
    order[...] = own_order(place[0], rows, 0)
    features = jnp.concatenate([near[...], far[...]], axis=0)
    features = jnp.dot(
        own_order(place[0], rows, 1), features, preferred_element_type=jnp.float32
    ).astype(jnp.bfloat16)
    for k in range(2):
        value = jnp.dot(features, factors[k], preferred_element_type=jnp.float32)
        value = jnp.where(same, value, 0.0)
        total = value[:, :FOLD]
        for start in range(FOLD, columns, FOLD):
            total = total + value[:, start : start + FOLD]
        folded[k] = total


def small(kernel, shapes, *operands, scalars=0, limit=8):
    return pl.pallas_call(
        kernel,
        out_shape=[jax.ShapeDtypeStruct(shape, dtype) for shape, dtype in shapes],
        in_specs=[SMEM] * scalars + [VMEM] * (len(operands) - scalars),
        out_specs=[VMEM] * len(shapes),
        cost_estimate=cost(0, 1 << 20),
        compiler_params=pltpu.CompilerParams(vmem_limit_bytes=limit << 20),
    )(*operands)


def same_kernel(source, target):
    target[...] = source[0]


def rows_joined(*parts):
    wide = [part.astype(jnp.float32) for part in parts]
    return jnp.concatenate(wide, axis=0).astype(parts[0].dtype)


def joined_kernel(near, far, rows):
    rows[...] = rows_joined(near[...], far[...])


def parted_kernel(place, near, far, left, right, keep, send, rows):
    rows[...] = rows_joined(near[...], far[...])
    half, size = left.shape[1], keep.shape[1]
    left[...], right[...] = rows[:, :half], rows[:, half:]
    at = place[0] // 8 * 2 * size
    low, high = [rows[:, pl.ds(pl.multiple_of(at + i * size, size), size)] for i in range(2)]
    first = place[0] // 4 % 2 == 0
    keep[...] = jnp.where(first, low, high)
    send[...] = jnp.where(first, high, low)


def parted(place, near, far, slabs):
    part, width = near.shape
    shapes = [(2 * part, width // 2)] * 2 + [(2 * part, slabs)] * 2
    return pl.pallas_call(
        parted_kernel,
        out_shape=[jax.ShapeDtypeStruct(shape, near.dtype) for shape in shapes],
        in_specs=[SMEM, VMEM, VMEM],
        out_specs=[VMEM] * 4,
        scratch_shapes=[pltpu.VMEM((2 * part, width), near.dtype)],
        cost_estimate=cost(0, 8 * near.size),
        compiler_params=pltpu.CompilerParams(vmem_limit_bytes=8 << 20),
    )(place, near, far)


def slab_kernel(place, slab, slab_y, keep, send):
    rows, size = rows_joined(slab[...], slab_y[...]), keep.shape[1]
    first = place[0] // 2 % 2 == 0
    keep[...] = jnp.where(first, rows[:, :size], rows[:, size:])
    send[...] = jnp.where(first, rows[:, size:], rows[:, :size])


def middle_kernel(left, left_y, right, right_x, lefts, rights):
    lefts[...] = rows_joined(left[...], left_y[...])
    rights[...] = rows_joined(right[...], right_x[...])


def fetch_kernel(count, pieces, *refs):
    sources, targets, sems = refs[:count], refs[-1 - count : -1], refs[-1]
    copies = []
    for k, (source, target) in enumerate(zip(sources, targets)):
        size = source.shape[1] // pieces
        for i in range(pieces):
            rows = pl.ds(i * size, size)
            copies.append(
                pltpu.make_async_copy(source.at[:, rows], target.at[:, rows], sems.at[k, i])
            )
    for copy in copies:
        copy.start()
    for copy in copies:
        copy.wait()


def fetch(sources, after, pieces):
    return pl.pallas_call(
        functools.partial(fetch_kernel, len(sources), pieces),
        out_shape=[pltpu.VMEM(source.shape, source.dtype) for source in sources],
        in_specs=[ANY] * (len(sources) + len(after)),
        out_specs=[VMEM] * len(sources),
        scratch_shapes=[pltpu.SemaphoreType.DMA((len(sources), pieces))],
        cost_estimate=cost(0, 2 * sum(source.size for source in sources)),
        compiler_params=pltpu.CompilerParams(vmem_limit_bytes=1 << 20),
    )(*[in_hbm(source) for source in sources], *after)


def chunks(width, most):
    return [(at, min(most, width - at)) for at in range(0, width, most)]


def inner_kernel(tile, place, lefts, left_x, rights, right_y, gate, up, *refs):
    outs, (gate_sum, up_sum, rows) = refs[:4], refs[4:]
    half = lefts.shape[1]
    rows[:, :half] = rows_joined(lefts[...], left_x[...])
    rows[:, half:] = gathered_right(rights[...], right_y[...])
    strip = outs[0].shape[1]
    first = place[0] % 2 == 0
    for weights, total, here, there in ((gate, gate_sum, *outs[:2]), (up, up_sum, *outs[2:])):
        for at, size in chunks(total.shape[1], tile):
            total[:, at : at + size] = jnp.dot(
                rows[...], weights[0, :, at : at + size], preferred_element_type=jnp.float32
            )
        low, high = total[:, :strip], total[:, strip:]
        here[...] = jnp.where(first, low, high)
        there[...] = jnp.where(first, high, low)


def inner(place, lefts, left_x, rights, right_y, gate, up, tile):
    half, width = lefts.shape
    rows, units = 2 * half, gate.shape[2]
    strip = jax.ShapeDtypeStruct((rows, units // 2), jnp.float32)
    return pl.pallas_call(
        functools.partial(inner_kernel, tile),
        out_shape=[strip] * 4,
        in_specs=[SMEM] + [VMEM] * 6,
        out_specs=[VMEM] * 4,
        scratch_shapes=[pltpu.VMEM((rows, units), jnp.float32)] * 2
        + [pltpu.VMEM((rows, 2 * width), lefts.dtype)],
        cost_estimate=cost(2 * rows * (gate.size + up.size), 2 * (gate.size + up.size)),
        compiler_params=pltpu.CompilerParams(vmem_limit_bytes=12 << 20),
    )(place, lefts, left_x, rights, right_y, gate, up)


def sums_kernel(gate, gate_in, up, up_in, gate_sum, up_sum):
    gate_sum[...] = gate[...] + gate_in[...]
    up_sum[...] = up[...] + up_in[...]


def ready_kernel(keep, order, folded, near, far, both, shrunk):
    for k in range(2):
        planes = [part[k].astype(jnp.float32) for part in (near, far, both)]
        total = (folded[k] + planes[0]) + (planes[1] + planes[2])
        value = jnp.concatenate([total] * (keep.shape[1] // FOLD), axis=1) * keep[...]
        shrunk[k] = jnp.dot(
            order[...], value.astype(shrunk.dtype), preferred_element_type=jnp.float32
        ).astype(shrunk.dtype)


def hidden_kernel(shrunk, gate, up, expand, hidden):
    columns = shrunk.shape[2]
    gate_sum, up_sum = [
        part[...]
        + jnp.dot(
            shrunk[k],
            expand[:, k].reshape(columns, expand.shape[3]),
            preferred_element_type=jnp.float32,
        )
        for k, part in enumerate((gate, up))
    ]
    hidden[...] = (gate_sum / (1.0 + jnp.exp(-gate_sum)) * up_sum).astype(hidden.dtype)


def down_first_kernel(tile, place, mine, weights, terms):
    strip = mine.shape[1]
    rows = pl.ds(pl.multiple_of(place[0] % 2 * strip, 128), strip)
    for at, size in chunks(terms.shape[1], tile):
        terms[:, at : at + size] = jnp.dot(
            mine[...], weights[0, rows, at : at + size], preferred_element_type=jnp.float32
        )


def down_kernel(x_first, start, tile, place, other, before, weights, stays, sends):
    strip = other.shape[1]
    rows = pl.ds(pl.multiple_of((1 - place[0] % 2) * strip, 128), strip)
    part = other.shape[0] // 4
    for at, size in chunks(stays.shape[1], tile):
        source, columns = pl.ds(start + at, size), pl.ds(at, size)
        terms = before[:, source] + jnp.dot(
            other[...], weights[0, rows, source], preferred_element_type=jnp.float32
        )
        low_y, high_y, far_low, far_high = [terms[k * part : (k + 1) * part] for k in range(4)]
        if x_first:
            stay, send = (low_y, high_y), (far_low, far_high)
        else:
            stay, send = (low_y, far_low), (high_y, far_high)
        stays[:, columns] = jnp.concatenate(stay, axis=0)
        sends[:, columns] = jnp.concatenate(send, axis=0).astype(sends.dtype)


def packed(total, pieces):
    size = total.shape[1] // pieces
    return jnp.concatenate([total[:, i * size : (i + 1) * size] for i in range(pieces)], axis=0)


def unpacked(packed_rows, pieces):
    wide = packed_rows.astype(jnp.float32)
    rows = wide.shape[0] // pieces
    return jnp.concatenate([wide[i * rows : (i + 1) * rows] for i in range(pieces)], axis=1)


def split_kernel(left, left_in, right, right_in, stay, send):
    totals = [
        part[...] + received[...].astype(jnp.float32)
        for part, received in ((left, left_in), (right, right_in))
    ]
    total = jnp.concatenate(totals, axis=1)
    half = stay.shape[0]
    stay[...], send[...] = total[:half], packed(total[half:], 2).astype(send.dtype)


def split_kernel_last(before, received, stay, send):
    total = before[...] + unpacked(received[...], 2)
    half = stay.shape[0]
    stay[...], send[...] = total[:half], packed(total[half:], 4).astype(send.dtype)


def last_kernel(stay, received, out):
    out[0] = (stay[...] + unpacked(received[...], 4)).astype(out.dtype)


def shards(tokens, w_gate, w_up, w_down, shrink_factors, expand_factors, rank_blocks, row_counts):
    count = lax.axis_size("tensor")
    units = w_gate.shape[2]
    if count != 32 or units % 256:
        return general_shards(
            tokens, w_gate, w_up, w_down, shrink_factors, expand_factors, rank_blocks, row_counts
        )
    place = lax.axis_index("tensor").reshape(1)
    block_rows, width = tokens.shape[1], tokens.shape[2]
    rows = 16 * block_rows
    half, columns = width // 2, shrink_factors.shape[2]
    wide, narrow = jnp.float32, jnp.bfloat16
    blocks = blocks_of(expand_factors, count)

    (own,) = small(same_kernel, [((block_rows, width), narrow)], tokens)
    own, other = lax.optimization_barrier((own, to_chip(tokens[0], Z2)))
    (own,) = small(joined_kernel, [((2 * block_rows, width), narrow)], own, other)
    blocks, other = lax.optimization_barrier((blocks, to_chip(own, Z1)))
    slab = shrink_factors.shape[1]
    left, right, near, far = parted(place, own, other, 2 * slab)
    place, blocks, left, right, near, far = lax.optimization_barrier(
        (place, blocks, left, right, near, far)
    )
    expand = lax.all_to_all(blocks, "tensor", split_axis=0, concat_axis=0, tiled=True)

    hops = to_chip(far, Y), to_chip(left, Y), to_chip(right, X)
    hops, (gate_weights,) = lax.optimization_barrier((hops, fetch((w_gate,), (left,), 4)))
    near, far = small(
        slab_kernel, [((8 * block_rows, slab), narrow)] * 2, place, near, hops[0], scalars=1
    )
    lefts, rights = small(
        middle_kernel, [((8 * block_rows, half), narrow)] * 2, left, hops[1], right, hops[2]
    )
    far, (up_weights, factors), lefts, rights = lax.optimization_barrier(
        (to_chip(far, X), fetch((w_up, shrink_factors), (far,), 4), lefts, rights)
    )
    gathered = lefts, to_chip(lefts, X), rights, to_chip(rights, Y)

    folded, keep, order = small(
        shrink_kernel,
        [((2, rows, FOLD), wide), ((rows, columns), wide), ((rows, rows), narrow)],
        place,
        rank_blocks,
        row_counts,
        near,
        far,
        factors,
        scalars=3,
    )
    folded = folded + swapped(folded, "tensor", 0)
    folded = folded + to_chip(folded, Y)
    strips = inner(place, *gathered, gate_weights, up_weights, 256)
    folded = folded + to_chip(folded, X)
    sent = folded.astype(narrow)
    received = [to_chip(sent, apart) for apart in (Z1, Z2, Z1 | Z2)]

    gate, gate_out, up, up_out = strips
    strip = (gate.shape, wide)
    sums = small(
        sums_kernel, [strip] * 2, gate, swapped(gate_out, "tensor", 0), up, swapped(up_out, "tensor", 0)
    )
    received, (down_weights,) = lax.optimization_barrier(
        (received, fetch((w_down,), (expand, *sums), 4))
    )
    (shrunk,) = small(ready_kernel, [((2, rows, columns), narrow)], keep, order, folded, *received)
    hidden_shape = (strip[0], narrow)
    (hidden,) = small(hidden_kernel, [hidden_shape], shrunk, *sums, expand)
    other = swapped(hidden, "tensor", 0)
    (before,) = small(
        functools.partial(down_first_kernel, 256),
        [((rows, width), wide)],
        place,
        hidden,
        down_weights,
        scalars=1,
    )
    split = half
    sums = []
    for x_first, first, second in ((True, X, Y), (False, Y, X)):
        start, size = (0, split) if x_first else (split, width - split)
        stays, sends = small(
            functools.partial(down_kernel, x_first, start, 256),
            [((rows // 2, size), wide), ((rows // 2, size), narrow)],
            place,
            other,
            before,
            down_weights,
            scalars=1,
        )
        stays = stays + to_chip(sends, first)
        part = 4 * block_rows
        sums += [stays[:part], to_chip(stays[part:].astype(narrow), second)]
    stay, send = small(
        split_kernel, [((part // 2, width), wide), ((part, half), narrow)], *sums
    )
    stay, send = small(
        split_kernel_last,
        [((block_rows, width), wide), ((part, width // 4), narrow)],
        stay,
        to_chip(send, Z1),
    )
    (out,) = small(last_kernel, [((1, block_rows, width), narrow)], stay, to_chip(send, Z2))
    return out


def solution(mesh):
    placed = (
        P(("groups", "tensor"), None, None),
        P("tensor", None, None),
        P("tensor", None, None),
        P("tensor", None, None),
        P("groups", "tensor", None),
        P("groups", "tensor", None),
        P("groups"),
        P("groups"),
    )
    return jax.shard_map(
        shards,
        mesh=mesh,
        in_specs=placed,
        out_specs=P(("groups", "tensor"), None, None),
        check_vma=False,
    )
```

```python
import functools

import jax
import jax.numpy as jnp
from jax import lax
from jax.experimental import pallas as pl
from jax.experimental.pallas import tpu as pltpu
from jax.sharding import PartitionSpec as P

HIDDEN_BITS = 4
FOLD = 128


def swapped(block, axis, apart):
    count = lax.axis_size(axis)
    return lax.ppermute(block, axis, [(i, i ^ (1 << apart)) for i in range(count)])


def by_target(expand, count):
    kinds, depth, width = expand.shape
    return expand.reshape(kinds, depth, count, width // count).transpose(2, 0, 1, 3)


def owner_of(ends, ids):
    return jnp.sum((ends[None, :] <= ids[:, None]).astype(jnp.int32), axis=1)


def keep_mask(rank_blocks, row_counts, columns, rows):
    adapters = rank_blocks.shape[0]
    earlier = jnp.arange(adapters)[:, None] >= jnp.arange(adapters)[None, :]
    block_end = jnp.sum(jnp.where(earlier, rank_blocks[None, :], 0), axis=1)
    row_end = jnp.sum(jnp.where(earlier, row_counts[None, :], 0), axis=1)
    column_owner = owner_of(block_end, jnp.arange(columns, dtype=jnp.int32) // 16)
    row_owner = owner_of(row_end, jnp.arange(rows, dtype=jnp.int32))
    ids = jnp.arange(adapters, dtype=jnp.int32)
    row_blocks = jnp.sum(
        jnp.where(row_owner[:, None] == ids[None, :], rank_blocks[None, :], 0), axis=1
    )
    same = (row_owner[:, None] == column_owner[None, :]).astype(jnp.float32)
    return same, 1.0 / row_blocks.astype(jnp.float32)


def general_shards(tokens, w_gate, w_up, w_down, shrink_factors, expand_factors, rank_blocks, row_counts):
    count = lax.axis_size("tensor")
    low_bits = count.bit_length() - 1 - HIDDEN_BITS
    fgroups = 1 << low_bits
    place = lax.axis_index("tensor")
    feature_group = place % fgroups
    hidden_group = place // fgroups
    block_rows = tokens.shape[1]
    rows = block_rows << HIDDEN_BITS
    units = w_gate.shape[2]
    strip = units // fgroups

    expand = lax.all_to_all(
        by_target(expand_factors, count), "tensor", split_axis=0, concat_axis=0, tiled=True
    )

    gathered = tokens[0]
    for bit in reversed(range(HIDDEN_BITS)):
        other = swapped(gathered, "tensor", low_bits + bit)
        gathered = jnp.concatenate([gathered, other], 0)
    spots = jnp.arange(1 << HIDDEN_BITS, dtype=jnp.int32)
    moved = sum(((spots >> i) & 1) << (HIDDEN_BITS - 1 - i) for i in range(HIDDEN_BITS))
    natural = (
        (moved ^ hidden_group)[:, None] * block_rows + jnp.arange(block_rows, dtype=jnp.int32)[None, :]
    ).reshape(rows)
    to_own = (natural[:, None] == jnp.arange(rows, dtype=jnp.int32)[None, :]).astype(jnp.bfloat16)

    columns = shrink_factors.shape[2]
    same, scale = keep_mask(rank_blocks, row_counts, columns, rows)
    slab = shrink_factors.shape[1]
    features = lax.dynamic_slice_in_dim(gathered, hidden_group * slab, slab, 1)
    features = jnp.dot(to_own.T, features, preferred_element_type=jnp.float32).astype(jnp.bfloat16)
    partial_value = jnp.einsum(
        "rd,kdc->krc", features, shrink_factors, preferred_element_type=jnp.float32
    )
    folded = jnp.sum((partial_value * same).reshape(2, rows, columns // FOLD, FOLD), axis=2)
    for bit in range(low_bits + HIDDEN_BITS):
        folded = folded + swapped(folded, "tensor", bit)
    shrunk = jnp.tile(folded, (1, 1, columns // FOLD)) * (same * scale[:, None])[None]
    shrunk = shrunk.astype(jnp.bfloat16)
    shrunk = jnp.einsum("or,krc->koc", to_own, shrunk, preferred_element_type=jnp.float32)
    shrunk = shrunk.astype(jnp.bfloat16)

    gate_part = jnp.dot(gathered, w_gate[0], preferred_element_type=jnp.float32)
    up_part = jnp.dot(gathered, w_up[0], preferred_element_type=jnp.float32)
    partials = jnp.stack([gate_part, up_part])
    for step in range(low_bits):
        bit = low_bits - 1 - step
        half = partials.shape[2] // 2
        high = feature_group // (1 << bit) % 2
        outgoing = lax.dynamic_slice_in_dim(partials, (1 - high) * half, half, 2)
        staying = lax.dynamic_slice_in_dim(partials, high * half, half, 2)
        partials = staying + swapped(outgoing, "tensor", bit)
    depth = expand.shape[2]
    low_rank = jnp.einsum(
        "krsd,skdc->krc",
        shrunk.reshape(2, rows, count, depth),
        expand,
        preferred_element_type=jnp.float32,
    )
    partials = partials + low_rank
    hidden = (jax.nn.silu(partials[0]) * partials[1]).astype(jnp.bfloat16)
    for step in range(low_bits):
        other = swapped(hidden, "tensor", step)
        high = feature_group // (1 << step) % 2 == 1
        hidden = jnp.where(
            high, jnp.concatenate([other, hidden], 1), jnp.concatenate([hidden, other], 1)
        )
    terms = jnp.dot(hidden, w_down[0], preferred_element_type=jnp.float32)
    for bit in range(HIDDEN_BITS):
        half = terms.shape[0] // 2
        outgoing = terms[half:].astype(jnp.bfloat16)
        terms = terms[:half] + swapped(outgoing, "tensor", low_bits + bit).astype(jnp.float32)
    return terms.astype(jnp.bfloat16)[None]


def keeping(ranks, counts, rows, columns):
    row = lax.broadcasted_iota(jnp.int32, (rows, 1), 0)
    block = lax.broadcasted_iota(jnp.int32, (1, columns), 1) // 16
    row_owner, column_owner = jnp.zeros_like(row), jnp.zeros_like(block)
    row_end = block_end = 0
    for adapter in range(ranks.shape[0]):
        row_end, block_end = row_end + counts[adapter], block_end + ranks[adapter]
        row_owner += (row >= row_end).astype(jnp.int32)
        column_owner += (block >= block_end).astype(jnp.int32)
    blocks = jnp.zeros_like(row)
    for adapter in range(ranks.shape[0]):
        blocks = jnp.where(row_owner == adapter, ranks[adapter], blocks)
    return row_owner == column_owner, 1.0 / blocks.astype(jnp.float32)


VMEM = pl.BlockSpec(memory_space=pltpu.VMEM)
SMEM = pl.BlockSpec(memory_space=pltpu.SMEM)
ANY = pl.BlockSpec(memory_space=pl.ANY)
X, Y, Z1, Z2 = 1, 2, 4, 8


def to_chip(block, apart):
    count = lax.axis_size("tensor")
    return lax.ppermute(block, "tensor", [(i, i ^ (apart << 1)) for i in range(count)])


def cost(flops, read):
    return pl.CostEstimate(flops=flops, bytes_accessed=read, transcendentals=0)


def in_hbm(array):
    return pltpu.with_memory_space_constraint(array, pltpu.HBM)


def blocks_kernel(count, strip, source, target):
    for j in range(count):
        target[j] = source[:, :, j * strip : (j + 1) * strip]


def blocks_of(expand, count):
    kinds, depth, width = expand.shape
    strip = width // count
    return pl.pallas_call(
        functools.partial(blocks_kernel, count, strip),
        out_shape=jax.ShapeDtypeStruct((count, kinds, depth, strip), expand.dtype),
        in_specs=[VMEM],
        out_specs=VMEM,
        cost_estimate=cost(0, 4 * expand.size),
        compiler_params=pltpu.CompilerParams(vmem_limit_bytes=10 << 20),
    )(expand)


def own_order(place, rows, own_axis):
    block = rows // 16
    own, natural = [lax.broadcasted_iota(jnp.int32, (rows, rows), axis) for axis in (own_axis, 1 - own_axis)]
    spot = own // block
    far = spot // 8 + spot // 4 % 2 * 2 + spot // 2 % 2 * 4 + spot % 2 * 8
    return ((far ^ (place // 2)) * block + (own - spot * block) == natural).astype(jnp.bfloat16)


def gathered_right(rights, right_y):
    part = rights.shape[0] // 2
    wide, corner = rights.astype(jnp.float32), right_y.astype(jnp.float32)
    pieces = [wide[:part], corner[:part], wide[part:], corner[part:]]
    return jnp.concatenate(pieces, axis=0).astype(rights.dtype)


def shrink_kernel(
    place, ranks, counts, lefts, left_x, rights, right_y, factors, folded, keep, order
):
    rows, columns = folded.shape[1], factors.shape[2]
    same, scale = keeping(ranks, counts, rows, columns)
    keep[...] = jnp.where(same, scale, 0.0)
    order[...] = own_order(place[0], rows, 0)
    slab = factors.shape[1]
    chip, chips = place[0] // 2, lefts.shape[1] // slab
    columns_here = pl.ds(pl.multiple_of(chip % chips * slab, slab), slab)
    left = rows_joined(lefts[:, columns_here], left_x[:, columns_here])
    right = gathered_right(rights[:, columns_here], right_y[:, columns_here])
    features = jnp.where(chip < chips, left, right)
    features = jnp.dot(
        own_order(place[0], rows, 1), features, preferred_element_type=jnp.float32
    ).astype(jnp.bfloat16)
    for k in range(2):
        value = jnp.dot(features, factors[k], preferred_element_type=jnp.float32)
        value = jnp.where(same, value, 0.0)
        total = value[:, :FOLD]
        for start in range(FOLD, columns, FOLD):
            total = total + value[:, start : start + FOLD]
        folded[k] = total


def small(kernel, shapes, *operands, scalars=0, limit=8):
    return pl.pallas_call(
        kernel,
        out_shape=[jax.ShapeDtypeStruct(shape, dtype) for shape, dtype in shapes],
        in_specs=[SMEM] * scalars + [VMEM] * (len(operands) - scalars),
        out_specs=[VMEM] * len(shapes),
        cost_estimate=cost(0, 1 << 20),
        compiler_params=pltpu.CompilerParams(vmem_limit_bytes=limit << 20),
    )(*operands)


def same_kernel(source, target):
    target[...] = source[0]


def rows_joined(*parts):
    wide = [part.astype(jnp.float32) for part in parts]
    return jnp.concatenate(wide, axis=0).astype(parts[0].dtype)


def joined_kernel(near, far, rows):
    rows[...] = rows_joined(near[...], far[...])


def parted_kernel(near, far, left, right):
    rows = rows_joined(near[...], far[...])
    half = left.shape[1]
    left[...], right[...] = rows[:, :half], rows[:, half:]


def middle_kernel(left, left_y, right, right_x, lefts, rights):
    lefts[...] = rows_joined(left[...], left_y[...])
    rights[...] = rows_joined(right[...], right_x[...])


def fetch_kernel(count, pieces, *refs):
    sources, targets, sems = refs[:count], refs[-1 - count : -1], refs[-1]
    copies = []
    for k, (source, target) in enumerate(zip(sources, targets)):
        size = source.shape[1] // pieces
        for i in range(pieces):
            rows = pl.ds(i * size, size)
            copies.append(
                pltpu.make_async_copy(source.at[:, rows], target.at[:, rows], sems.at[k, i])
            )
    for copy in copies:
        copy.start()
    for copy in copies:
        copy.wait()


def fetch(sources, after, pieces):
    return pl.pallas_call(
        functools.partial(fetch_kernel, len(sources), pieces),
        out_shape=[pltpu.VMEM(source.shape, source.dtype) for source in sources],
        in_specs=[ANY] * (len(sources) + len(after)),
        out_specs=[VMEM] * len(sources),
        scratch_shapes=[pltpu.SemaphoreType.DMA((len(sources), pieces))],
        cost_estimate=cost(0, 2 * sum(source.size for source in sources)),
        compiler_params=pltpu.CompilerParams(vmem_limit_bytes=1 << 20),
    )(*[in_hbm(source) for source in sources], *after)


def chunks(width, most):
    return [(at, min(most, width - at)) for at in range(0, width, most)]


def inner_kernel(tile, place, lefts, left_x, rights, right_y, gate, up, *refs):
    outs, (gate_sum, up_sum, rows) = refs[:4], refs[4:]
    half = lefts.shape[1]
    rows[:, :half] = rows_joined(lefts[...], left_x[...])
    rows[:, half:] = gathered_right(rights[...], right_y[...])
    strip = outs[0].shape[1]
    first = place[0] % 2 == 0
    for weights, total, here, there in ((gate, gate_sum, *outs[:2]), (up, up_sum, *outs[2:])):
        for at, size in chunks(total.shape[1], tile):
            total[:, at : at + size] = jnp.dot(
                rows[...], weights[0, :, at : at + size], preferred_element_type=jnp.float32
            )
        low, high = total[:, :strip], total[:, strip:]
        here[...] = jnp.where(first, low, high)
        there[...] = jnp.where(first, high, low)


def inner(place, lefts, left_x, rights, right_y, gate, up, tile):
    half, width = lefts.shape
    rows, units = 2 * half, gate.shape[2]
    strip = jax.ShapeDtypeStruct((rows, units // 2), jnp.float32)
    return pl.pallas_call(
        functools.partial(inner_kernel, tile),
        out_shape=[strip] * 4,
        in_specs=[SMEM] + [VMEM] * 6,
        out_specs=[VMEM] * 4,
        scratch_shapes=[pltpu.VMEM((rows, units), jnp.float32)] * 2
        + [pltpu.VMEM((rows, 2 * width), lefts.dtype)],
        cost_estimate=cost(2 * rows * (gate.size + up.size), 2 * (gate.size + up.size)),
        compiler_params=pltpu.CompilerParams(vmem_limit_bytes=12 << 20),
    )(place, lefts, left_x, rights, right_y, gate, up)


def sums_kernel(gate, gate_in, up, up_in, gate_sum, up_sum):
    gate_sum[...] = gate[...] + gate_in[...]
    up_sum[...] = up[...] + up_in[...]


def ready_kernel(keep, order, folded, near, far, both, shrunk):
    for k in range(2):
        planes = [part[k].astype(jnp.float32) for part in (near, far, both)]
        total = (folded[k] + planes[0]) + (planes[1] + planes[2])
        value = jnp.concatenate([total] * (keep.shape[1] // FOLD), axis=1) * keep[...]
        shrunk[k] = jnp.dot(
            order[...], value.astype(shrunk.dtype), preferred_element_type=jnp.float32
        ).astype(shrunk.dtype)


def fetch_strip_kernel(other, pieces, place, source, *refs):
    target, sems = refs[-2:]
    strip = target.shape[1]
    core = place[0] % 2
    row = pl.multiple_of((1 - core if other else core) * strip, 128)
    size = strip // pieces
    copies = [
        pltpu.make_async_copy(
            source.at[:, pl.ds(row + i * size, size)], target.at[:, pl.ds(i * size, size)], sems.at[i]
        )
        for i in range(pieces)
    ]
    for copy in copies:
        copy.start()
    for copy in copies:
        copy.wait()


def fetch_strip(other, place, weights, after, pieces):
    shape = (1, weights.shape[1] // 2, weights.shape[2])
    return pl.pallas_call(
        functools.partial(fetch_strip_kernel, other, pieces),
        out_shape=pltpu.VMEM(shape, weights.dtype),
        in_specs=[SMEM] + [ANY] * (1 + len(after)),
        out_specs=VMEM,
        scratch_shapes=[pltpu.SemaphoreType.DMA((pieces,))],
        cost_estimate=cost(0, weights.size),
        compiler_params=pltpu.CompilerParams(vmem_limit_bytes=1 << 20),
    )(place, in_hbm(weights), *after)


def hidden_kernel(shrunk, gate, up, expand, hidden):
    columns = shrunk.shape[2]
    gate_sum, up_sum = [
        part[...]
        + jnp.dot(
            shrunk[k],
            expand[:, k].reshape(columns, expand.shape[3]),
            preferred_element_type=jnp.float32,
        )
        for k, part in enumerate((gate, up))
    ]
    hidden[...] = (gate_sum / (1.0 + jnp.exp(-gate_sum)) * up_sum).astype(hidden.dtype)


def down_first_kernel(tile, mine, weights, terms):
    for at, size in chunks(terms.shape[1], tile):
        terms[:, at : at + size] = jnp.dot(
            mine[...], weights[0, :, at : at + size], preferred_element_type=jnp.float32
        )


def down_kernel(x_first, start, tile, other, before, weights, stays, sends):
    part = other.shape[0] // 4
    for at, size in chunks(stays.shape[1], tile):
        source, columns = pl.ds(start + at, size), pl.ds(at, size)
        terms = before[:, source] + jnp.dot(
            other[...], weights[0, :, source], preferred_element_type=jnp.float32
        )
        low_y, high_y, far_low, far_high = [terms[k * part : (k + 1) * part] for k in range(4)]
        if x_first:
            stay, send = (low_y, high_y), (far_low, far_high)
        else:
            stay, send = (low_y, far_low), (high_y, far_high)
        stays[:, columns] = jnp.concatenate(stay, axis=0)
        sends[:, columns] = jnp.concatenate(send, axis=0).astype(sends.dtype)


def packed(total, pieces):
    size = total.shape[1] // pieces
    return jnp.concatenate([total[:, i * size : (i + 1) * size] for i in range(pieces)], axis=0)


def unpacked(packed_rows, pieces):
    wide = packed_rows.astype(jnp.float32)
    rows = wide.shape[0] // pieces
    return jnp.concatenate([wide[i * rows : (i + 1) * rows] for i in range(pieces)], axis=1)


def split_kernel(left, left_in, right, right_in, stay, send):
    totals = [
        part[...] + received[...].astype(jnp.float32)
        for part, received in ((left, left_in), (right, right_in))
    ]
    total = jnp.concatenate(totals, axis=1)
    half = stay.shape[0]
    stay[...], send[...] = total[:half], packed(total[half:], 2).astype(send.dtype)


def split_kernel_last(before, received, stay, send):
    total = before[...] + unpacked(received[...], 2)
    half = stay.shape[0]
    stay[...], send[...] = total[:half], packed(total[half:], 4).astype(send.dtype)


def last_kernel(stay, received, out):
    out[0] = (stay[...] + unpacked(received[...], 4)).astype(out.dtype)


def shards(tokens, w_gate, w_up, w_down, shrink_factors, expand_factors, rank_blocks, row_counts):
    count = lax.axis_size("tensor")
    units = w_gate.shape[2]
    if count != 32 or units % 256:
        return general_shards(
            tokens, w_gate, w_up, w_down, shrink_factors, expand_factors, rank_blocks, row_counts
        )
    place = lax.axis_index("tensor").reshape(1)
    block_rows, width = tokens.shape[1], tokens.shape[2]
    rows = 16 * block_rows
    half, columns = width // 2, shrink_factors.shape[2]
    wide, narrow = jnp.float32, jnp.bfloat16
    blocks = blocks_of(expand_factors, count)

    (own,) = small(same_kernel, [((block_rows, width), narrow)], tokens)
    own, other = lax.optimization_barrier((own, to_chip(tokens[0], Z2)))
    (own,) = small(joined_kernel, [((2 * block_rows, width), narrow)], own, other)
    blocks, other = lax.optimization_barrier((blocks, to_chip(own, Z1)))
    left, right = small(parted_kernel, [((4 * block_rows, half), narrow)] * 2, own, other)
    place, blocks, left, right = lax.optimization_barrier((place, blocks, left, right))
    expand = lax.all_to_all(blocks, "tensor", split_axis=0, concat_axis=0, tiled=True)

    hops = to_chip(left, Y), to_chip(right, X)
    fetched = fetch((w_gate, w_up, shrink_factors), (left,), 4)
    hops, fetched = lax.optimization_barrier((hops, fetched))
    gate_weights, up_weights, factors = fetched
    lefts, rights = small(
        middle_kernel, [((8 * block_rows, half), narrow)] * 2, left, hops[0], right, hops[1]
    )
    gathered = lefts, to_chip(lefts, X), rights, to_chip(rights, Y)

    folded, keep, order = small(
        shrink_kernel,
        [((2, rows, FOLD), wide), ((rows, columns), wide), ((rows, rows), narrow)],
        place,
        rank_blocks,
        row_counts,
        *gathered,
        factors,
        scalars=3,
    )
    folded = folded + swapped(folded, "tensor", 0)
    folded = folded + to_chip(folded, Y)
    strips = inner(place, *gathered, gate_weights, up_weights, 256)
    folded, strips = lax.optimization_barrier((folded, strips))
    gate, gate_out, up, up_out = strips
    strip = (gate.shape, wide)
    sums = small(
        sums_kernel, [strip] * 2, gate, swapped(gate_out, "tensor", 0), up, swapped(up_out, "tensor", 0)
    )
    own_weights = fetch_strip(False, place, w_down, (expand, *sums), 4)
    received, own_weights = lax.optimization_barrier((to_chip(folded, X), own_weights))
    folded = folded + received
    sent = folded.astype(narrow)
    received = [to_chip(sent, apart) for apart in (Z1, Z2, Z1 | Z2)]
    received, other_weights = lax.optimization_barrier(
        (received, fetch_strip(True, place, w_down, (folded, own_weights), 4))
    )
    (shrunk,) = small(ready_kernel, [((2, rows, columns), narrow)], keep, order, folded, *received)
    hidden_shape = (strip[0], narrow)
    (hidden,) = small(hidden_kernel, [hidden_shape], shrunk, *sums, expand)
    other = swapped(hidden, "tensor", 0)
    (before,) = small(
        functools.partial(down_first_kernel, 256),
        [((rows, width), wide)],
        hidden,
        own_weights,
    )
    split = half
    sums = []
    for x_first, first, second in ((True, X, Y), (False, Y, X)):
        start, size = (0, split) if x_first else (split, width - split)
        stays, sends = small(
            functools.partial(down_kernel, x_first, start, 256),
            [((rows // 2, size), wide), ((rows // 2, size), narrow)],
            other,
            before,
            other_weights,
        )
        stays = stays + to_chip(sends, first)
        part = 4 * block_rows
        sums += [stays[:part], to_chip(stays[part:].astype(narrow), second)]
    stay, send = small(
        split_kernel, [((part // 2, width), wide), ((part, half), narrow)], *sums
    )
    stay, send = small(
        split_kernel_last,
        [((block_rows, width), wide), ((part, width // 4), narrow)],
        stay,
        to_chip(send, Z1),
    )
    (out,) = small(last_kernel, [((1, block_rows, width), narrow)], stay, to_chip(send, Z2))
    return out


def solution(mesh):
    placed = (
        P(("groups", "tensor"), None, None),
        P("tensor", None, None),
        P("tensor", None, None),
        P("tensor", None, None),
        P("groups", "tensor", None),
        P("groups", "tensor", None),
        P("groups"),
        P("groups"),
    )
    return jax.shard_map(
        shards,
        mesh=mesh,
        in_specs=placed,
        out_specs=P(("groups", "tensor"), None, None),
        check_vma=False,
    )
```

```python
import functools

import jax
import jax.numpy as jnp
from jax import lax
from jax.experimental import pallas as pl
from jax.experimental.pallas import tpu as pltpu
from jax.sharding import PartitionSpec as P

HIDDEN_BITS = 4
FOLD = 128


def swapped(block, axis, apart):
    count = lax.axis_size(axis)
    return lax.ppermute(block, axis, [(i, i ^ (1 << apart)) for i in range(count)])


def by_target(expand, count):
    kinds, depth, width = expand.shape
    return expand.reshape(kinds, depth, count, width // count).transpose(2, 0, 1, 3)


def owner_of(ends, ids):
    return jnp.sum((ends[None, :] <= ids[:, None]).astype(jnp.int32), axis=1)


def keep_mask(rank_blocks, row_counts, columns, rows):
    adapters = rank_blocks.shape[0]
    earlier = jnp.arange(adapters)[:, None] >= jnp.arange(adapters)[None, :]
    block_end = jnp.sum(jnp.where(earlier, rank_blocks[None, :], 0), axis=1)
    row_end = jnp.sum(jnp.where(earlier, row_counts[None, :], 0), axis=1)
    column_owner = owner_of(block_end, jnp.arange(columns, dtype=jnp.int32) // 16)
    row_owner = owner_of(row_end, jnp.arange(rows, dtype=jnp.int32))
    ids = jnp.arange(adapters, dtype=jnp.int32)
    row_blocks = jnp.sum(
        jnp.where(row_owner[:, None] == ids[None, :], rank_blocks[None, :], 0), axis=1
    )
    same = (row_owner[:, None] == column_owner[None, :]).astype(jnp.float32)
    return same, 1.0 / row_blocks.astype(jnp.float32)


def general_shards(tokens, w_gate, w_up, w_down, shrink_factors, expand_factors, rank_blocks, row_counts):
    count = lax.axis_size("tensor")
    low_bits = count.bit_length() - 1 - HIDDEN_BITS
    fgroups = 1 << low_bits
    place = lax.axis_index("tensor")
    feature_group = place % fgroups
    hidden_group = place // fgroups
    block_rows = tokens.shape[1]
    rows = block_rows << HIDDEN_BITS
    units = w_gate.shape[2]
    strip = units // fgroups

    expand = lax.all_to_all(
        by_target(expand_factors, count), "tensor", split_axis=0, concat_axis=0, tiled=True
    )

    gathered = tokens[0]
    for bit in reversed(range(HIDDEN_BITS)):
        other = swapped(gathered, "tensor", low_bits + bit)
        gathered = jnp.concatenate([gathered, other], 0)
    spots = jnp.arange(1 << HIDDEN_BITS, dtype=jnp.int32)
    moved = sum(((spots >> i) & 1) << (HIDDEN_BITS - 1 - i) for i in range(HIDDEN_BITS))
    natural = (
        (moved ^ hidden_group)[:, None] * block_rows + jnp.arange(block_rows, dtype=jnp.int32)[None, :]
    ).reshape(rows)
    to_own = (natural[:, None] == jnp.arange(rows, dtype=jnp.int32)[None, :]).astype(jnp.bfloat16)

    columns = shrink_factors.shape[2]
    same, scale = keep_mask(rank_blocks, row_counts, columns, rows)
    slab = shrink_factors.shape[1]
    features = lax.dynamic_slice_in_dim(gathered, hidden_group * slab, slab, 1)
    features = jnp.dot(to_own.T, features, preferred_element_type=jnp.float32).astype(jnp.bfloat16)
    partial_value = jnp.einsum(
        "rd,kdc->krc", features, shrink_factors, preferred_element_type=jnp.float32
    )
    folded = jnp.sum((partial_value * same).reshape(2, rows, columns // FOLD, FOLD), axis=2)
    for bit in range(low_bits + HIDDEN_BITS):
        folded = folded + swapped(folded, "tensor", bit)
    shrunk = jnp.tile(folded, (1, 1, columns // FOLD)) * (same * scale[:, None])[None]
    shrunk = shrunk.astype(jnp.bfloat16)
    shrunk = jnp.einsum("or,krc->koc", to_own, shrunk, preferred_element_type=jnp.float32)
    shrunk = shrunk.astype(jnp.bfloat16)

    gate_part = jnp.dot(gathered, w_gate[0], preferred_element_type=jnp.float32)
    up_part = jnp.dot(gathered, w_up[0], preferred_element_type=jnp.float32)
    partials = jnp.stack([gate_part, up_part])
    for step in range(low_bits):
        bit = low_bits - 1 - step
        half = partials.shape[2] // 2
        high = feature_group // (1 << bit) % 2
        outgoing = lax.dynamic_slice_in_dim(partials, (1 - high) * half, half, 2)
        staying = lax.dynamic_slice_in_dim(partials, high * half, half, 2)
        partials = staying + swapped(outgoing, "tensor", bit)
    depth = expand.shape[2]
    low_rank = jnp.einsum(
        "krsd,skdc->krc",
        shrunk.reshape(2, rows, count, depth),
        expand,
        preferred_element_type=jnp.float32,
    )
    partials = partials + low_rank
    hidden = (jax.nn.silu(partials[0]) * partials[1]).astype(jnp.bfloat16)
    for step in range(low_bits):
        other = swapped(hidden, "tensor", step)
        high = feature_group // (1 << step) % 2 == 1
        hidden = jnp.where(
            high, jnp.concatenate([other, hidden], 1), jnp.concatenate([hidden, other], 1)
        )
    terms = jnp.dot(hidden, w_down[0], preferred_element_type=jnp.float32)
    for bit in range(HIDDEN_BITS):
        half = terms.shape[0] // 2
        outgoing = terms[half:].astype(jnp.bfloat16)
        terms = terms[:half] + swapped(outgoing, "tensor", low_bits + bit).astype(jnp.float32)
    return terms.astype(jnp.bfloat16)[None]


def keeping(ranks, counts, rows, columns):
    row = lax.broadcasted_iota(jnp.int32, (rows, 1), 0)
    block = lax.broadcasted_iota(jnp.int32, (1, columns), 1) // 16
    row_owner, column_owner = jnp.zeros_like(row), jnp.zeros_like(block)
    row_end = block_end = 0
    for adapter in range(ranks.shape[0]):
        row_end, block_end = row_end + counts[adapter], block_end + ranks[adapter]
        row_owner += (row >= row_end).astype(jnp.int32)
        column_owner += (block >= block_end).astype(jnp.int32)
    blocks = jnp.zeros_like(row)
    for adapter in range(ranks.shape[0]):
        blocks = jnp.where(row_owner == adapter, ranks[adapter], blocks)
    return row_owner == column_owner, 1.0 / blocks.astype(jnp.float32)


VMEM = pl.BlockSpec(memory_space=pltpu.VMEM)
SMEM = pl.BlockSpec(memory_space=pltpu.SMEM)
ANY = pl.BlockSpec(memory_space=pl.ANY)
X, Y, Z1, Z2 = 1, 2, 4, 8


def to_chip(block, apart):
    count = lax.axis_size("tensor")
    return lax.ppermute(block, "tensor", [(i, i ^ (apart << 1)) for i in range(count)])


def cost(flops, read):
    return pl.CostEstimate(flops=flops, bytes_accessed=read, transcendentals=0)


def in_hbm(array):
    return pltpu.with_memory_space_constraint(array, pltpu.HBM)


def blocks_kernel(count, strip, source, target):
    for j in range(count):
        target[j] = source[:, :, j * strip : (j + 1) * strip]


def blocks_of(expand, count):
    kinds, depth, width = expand.shape
    strip = width // count
    return pl.pallas_call(
        functools.partial(blocks_kernel, count, strip),
        out_shape=jax.ShapeDtypeStruct((count, kinds, depth, strip), expand.dtype),
        in_specs=[VMEM],
        out_specs=VMEM,
        cost_estimate=cost(0, 4 * expand.size),
        compiler_params=pltpu.CompilerParams(vmem_limit_bytes=10 << 20),
    )(expand)


def own_order(place, rows, own_axis):
    block = rows // 16
    own, natural = [lax.broadcasted_iota(jnp.int32, (rows, rows), axis) for axis in (own_axis, 1 - own_axis)]
    spot = own // block
    far = spot // 8 + spot // 4 % 2 * 2 + spot // 2 % 2 * 4 + spot % 2 * 8
    return ((far ^ (place // 2)) * block + (own - spot * block) == natural).astype(jnp.bfloat16)


def gathered_right(rights, right_y):
    part = rights.shape[0] // 2
    wide, corner = rights.astype(jnp.float32), right_y.astype(jnp.float32)
    pieces = [wide[:part], corner[:part], wide[part:], corner[part:]]
    return jnp.concatenate(pieces, axis=0).astype(rights.dtype)


def shrink_kernel(
    place, ranks, counts, lefts, left_x, rights, right_y, factors, folded, keep, order
):
    rows, columns = folded.shape[1], factors.shape[2]
    same, scale = keeping(ranks, counts, rows, columns)
    keep[...] = jnp.where(same, scale, 0.0)
    order[...] = own_order(place[0], rows, 0)
    slab = factors.shape[1]
    chip, chips = place[0] // 2, lefts.shape[1] // slab
    columns_here = pl.ds(pl.multiple_of(chip % chips * slab, slab), slab)
    left = rows_joined(lefts[:, columns_here], left_x[:, columns_here])
    right = gathered_right(rights[:, columns_here], right_y[:, columns_here])
    features = jnp.where(chip < chips, left, right)
    features = jnp.dot(
        own_order(place[0], rows, 1), features, preferred_element_type=jnp.float32
    ).astype(jnp.bfloat16)
    for k in range(2):
        value = jnp.dot(features, factors[k], preferred_element_type=jnp.float32)
        value = jnp.where(same, value, 0.0)
        total = value[:, :FOLD]
        for start in range(FOLD, columns, FOLD):
            total = total + value[:, start : start + FOLD]
        folded[k] = total


def small(kernel, shapes, *operands, scalars=0, limit=8):
    return pl.pallas_call(
        kernel,
        out_shape=[jax.ShapeDtypeStruct(shape, dtype) for shape, dtype in shapes],
        in_specs=[SMEM] * scalars + [VMEM] * (len(operands) - scalars),
        out_specs=[VMEM] * len(shapes),
        cost_estimate=cost(0, 1 << 20),
        compiler_params=pltpu.CompilerParams(vmem_limit_bytes=limit << 20),
    )(*operands)


def same_kernel(source, target):
    target[...] = source[0]


def rows_joined(*parts):
    wide = [part.astype(jnp.float32) for part in parts]
    return jnp.concatenate(wide, axis=0).astype(parts[0].dtype)


def joined_kernel(near, far, rows, send):
    total = rows_joined(near[...], far[...]).astype(jnp.float32)
    rows[...], send[...] = total.astype(rows.dtype), packed(total, 2).astype(send.dtype)


def parted_kernel(near, far, left, right):
    part, half = near.shape[0], left.shape[1]
    rows, wide = near[...].astype(jnp.float32), far[...].astype(jnp.float32)
    left[...] = jnp.concatenate([rows[:, :half], wide[:part]], axis=0).astype(left.dtype)
    right[...] = jnp.concatenate([rows[:, half:], wide[part:]], axis=0).astype(right.dtype)


def middle_kernel(left, left_y, right, right_x, lefts, rights):
    lefts[...] = rows_joined(left[...], left_y[...])
    rights[...] = rows_joined(right[...], right_x[...])


def fetch_kernel(count, pieces, *refs):
    sources, targets, sems = refs[:count], refs[-1 - count : -1], refs[-1]
    copies = []
    for k, (source, target) in enumerate(zip(sources, targets)):
        size = source.shape[1] // pieces
        for i in range(pieces):
            rows = pl.ds(i * size, size)
            copies.append(
                pltpu.make_async_copy(source.at[:, rows], target.at[:, rows], sems.at[k, i])
            )
    for copy in copies:
        copy.start()
    for copy in copies:
        copy.wait()


def fetch(sources, after, pieces):
    return pl.pallas_call(
        functools.partial(fetch_kernel, len(sources), pieces),
        out_shape=[pltpu.VMEM(source.shape, source.dtype) for source in sources],
        in_specs=[ANY] * (len(sources) + len(after)),
        out_specs=[VMEM] * len(sources),
        scratch_shapes=[pltpu.SemaphoreType.DMA((len(sources), pieces))],
        cost_estimate=cost(0, 2 * sum(source.size for source in sources)),
        compiler_params=pltpu.CompilerParams(vmem_limit_bytes=1 << 20),
    )(*[in_hbm(source) for source in sources], *after)


def chunks(width, most):
    return [(at, min(most, width - at)) for at in range(0, width, most)]


def inner_kernel(tile, place, lefts, left_x, rights, right_y, gate, up, *refs):
    outs, (gate_sum, up_sum, rows) = refs[:4], refs[4:]
    half = lefts.shape[1]
    rows[:, :half] = rows_joined(lefts[...], left_x[...])
    rows[:, half:] = gathered_right(rights[...], right_y[...])
    strip = outs[0].shape[1]
    first = place[0] % 2 == 0
    for weights, total, here, there in ((gate, gate_sum, *outs[:2]), (up, up_sum, *outs[2:])):
        for at, size in chunks(total.shape[1], tile):
            total[:, at : at + size] = jnp.dot(
                rows[...], weights[0, :, at : at + size], preferred_element_type=jnp.float32
            )
        low, high = total[:, :strip], total[:, strip:]
        here[...] = jnp.where(first, low, high)
        there[...] = jnp.where(first, high, low)


def inner(place, lefts, left_x, rights, right_y, gate, up, tile):
    half, width = lefts.shape
    rows, units = 2 * half, gate.shape[2]
    strip = jax.ShapeDtypeStruct((rows, units // 2), jnp.float32)
    return pl.pallas_call(
        functools.partial(inner_kernel, tile),
        out_shape=[strip] * 4,
        in_specs=[SMEM] + [VMEM] * 6,
        out_specs=[VMEM] * 4,
        scratch_shapes=[pltpu.VMEM((rows, units), jnp.float32)] * 2
        + [pltpu.VMEM((rows, 2 * width), lefts.dtype)],
        cost_estimate=cost(2 * rows * (gate.size + up.size), 2 * (gate.size + up.size)),
        compiler_params=pltpu.CompilerParams(vmem_limit_bytes=12 << 20),
    )(place, lefts, left_x, rights, right_y, gate, up)


def sums_kernel(gate, gate_in, up, up_in, gate_sum, up_sum):
    gate_sum[...] = gate[...] + gate_in[...]
    up_sum[...] = up[...] + up_in[...]


def ready_kernel(keep, order, folded, near, far, both, shrunk):
    for k in range(2):
        planes = [part[k].astype(jnp.float32) for part in (near, far, both)]
        total = (folded[k] + planes[0]) + (planes[1] + planes[2])
        value = jnp.concatenate([total] * (keep.shape[1] // FOLD), axis=1) * keep[...]
        shrunk[k] = jnp.dot(
            order[...], value.astype(shrunk.dtype), preferred_element_type=jnp.float32
        ).astype(shrunk.dtype)


def hidden_kernel(shrunk, gate, up, expand, hidden):
    columns = shrunk.shape[2]
    gate_sum, up_sum = [
        part[...]
        + jnp.dot(
            shrunk[k],
            expand[:, k].reshape(columns, expand.shape[3]),
            preferred_element_type=jnp.float32,
        )
        for k, part in enumerate((gate, up))
    ]
    hidden[...] = (gate_sum / (1.0 + jnp.exp(-gate_sum)) * up_sum).astype(hidden.dtype)


def down_first_kernel(tile, place, mine, weights, terms):
    strip = mine.shape[1]
    rows = pl.ds(pl.multiple_of(place[0] % 2 * strip, 128), strip)
    for at, size in chunks(terms.shape[1], tile):
        terms[:, at : at + size] = jnp.dot(
            mine[...], weights[0, rows, at : at + size], preferred_element_type=jnp.float32
        )


def down_kernel(x_first, start, tile, place, other, before, weights, stays, sends):
    strip = other.shape[1]
    rows = pl.ds(pl.multiple_of((1 - place[0] % 2) * strip, 128), strip)
    part = other.shape[0] // 4
    for at, size in chunks(stays.shape[1], tile):
        source, columns = pl.ds(start + at, size), pl.ds(at, size)
        terms = before[:, source] + jnp.dot(
            other[...], weights[0, rows, source], preferred_element_type=jnp.float32
        )
        low_y, high_y, far_low, far_high = [terms[k * part : (k + 1) * part] for k in range(4)]
        if x_first:
            stay, send = (low_y, high_y), (far_low, far_high)
        else:
            stay, send = (low_y, far_low), (high_y, far_high)
        stays[:, columns] = jnp.concatenate(stay, axis=0)
        sends[:, columns] = jnp.concatenate(send, axis=0).astype(sends.dtype)


def packed(total, pieces):
    size = total.shape[1] // pieces
    return jnp.concatenate([total[:, i * size : (i + 1) * size] for i in range(pieces)], axis=0)


def unpacked(packed_rows, pieces):
    wide = packed_rows.astype(jnp.float32)
    rows = wide.shape[0] // pieces
    return jnp.concatenate([wide[i * rows : (i + 1) * rows] for i in range(pieces)], axis=1)


def split_kernel(left, left_in, right, right_in, stay, send):
    totals = [
        part[...] + received[...].astype(jnp.float32)
        for part, received in ((left, left_in), (right, right_in))
    ]
    total = jnp.concatenate(totals, axis=1)
    half = stay.shape[0]
    stay[...], send[...] = total[:half], packed(total[half:], 2).astype(send.dtype)


def split_kernel_last(before, received, stay, send):
    total = before[...] + unpacked(received[...], 2)
    half = stay.shape[0]
    stay[...], send[...] = total[:half], packed(total[half:], 4).astype(send.dtype)


def last_kernel(stay, received, out):
    out[0] = (stay[...] + unpacked(received[...], 4)).astype(out.dtype)


def shards(tokens, w_gate, w_up, w_down, shrink_factors, expand_factors, rank_blocks, row_counts):
    count = lax.axis_size("tensor")
    units = w_gate.shape[2]
    if count != 32 or units % 256:
        return general_shards(
            tokens, w_gate, w_up, w_down, shrink_factors, expand_factors, rank_blocks, row_counts
        )
    place = lax.axis_index("tensor").reshape(1)
    block_rows, width = tokens.shape[1], tokens.shape[2]
    rows = 16 * block_rows
    half, columns = width // 2, shrink_factors.shape[2]
    wide, narrow = jnp.float32, jnp.bfloat16
    blocks = blocks_of(expand_factors, count)

    (own,) = small(same_kernel, [((block_rows, width), narrow)], tokens)
    own, other = lax.optimization_barrier((own, to_chip(tokens[0], Z2)))
    own, send = small(
        joined_kernel,
        [((2 * block_rows, width), narrow), ((4 * block_rows, half), narrow)],
        own,
        other,
    )
    blocks, other = lax.optimization_barrier((blocks, to_chip(send, Z1)))
    left, right = small(parted_kernel, [((4 * block_rows, half), narrow)] * 2, own, other)
    place, blocks, left, right = lax.optimization_barrier((place, blocks, left, right))
    expand = lax.all_to_all(blocks, "tensor", split_axis=0, concat_axis=0, tiled=True)

    hops = to_chip(left, Y), to_chip(right, X)
    fetched = fetch((w_gate, w_up, shrink_factors), (left,), 4)
    hops, fetched = lax.optimization_barrier((hops, fetched))
    gate_weights, up_weights, factors = fetched
    lefts, rights = small(
        middle_kernel, [((8 * block_rows, half), narrow)] * 2, left, hops[0], right, hops[1]
    )
    gathered = lefts, to_chip(lefts, X), rights, to_chip(rights, Y)

    folded, keep, order = small(
        shrink_kernel,
        [((2, rows, FOLD), wide), ((rows, columns), wide), ((rows, rows), narrow)],
        place,
        rank_blocks,
        row_counts,
        *gathered,
        factors,
        scalars=3,
    )
    folded = folded + swapped(folded, "tensor", 0)
    folded = folded + to_chip(folded, Y)
    strips = inner(place, *gathered, gate_weights, up_weights, 256)
    folded, strips = lax.optimization_barrier((folded, strips))
    folded = folded + to_chip(folded, X)
    sent = folded.astype(narrow)
    received = [to_chip(sent, apart) for apart in (Z1, Z2, Z1 | Z2)]

    gate, gate_out, up, up_out = strips
    strip = (gate.shape, wide)
    sums = small(
        sums_kernel, [strip] * 2, gate, swapped(gate_out, "tensor", 0), up, swapped(up_out, "tensor", 0)
    )
    received, (down_weights,) = lax.optimization_barrier(
        (received, fetch((w_down,), (expand, *sums), 8))
    )
    (shrunk,) = small(ready_kernel, [((2, rows, columns), narrow)], keep, order, folded, *received)
    hidden_shape = (strip[0], narrow)
    (hidden,) = small(hidden_kernel, [hidden_shape], shrunk, *sums, expand)
    other = swapped(hidden, "tensor", 0)
    (before,) = small(
        functools.partial(down_first_kernel, 256),
        [((rows, width), wide)],
        place,
        hidden,
        down_weights,
        scalars=1,
    )
    split = half
    sums = []
    for x_first, first, second in ((True, X, Y), (False, Y, X)):
        start, size = (0, split) if x_first else (split, width - split)
        stays, sends = small(
            functools.partial(down_kernel, x_first, start, 256),
            [((rows // 2, size), wide), ((rows // 2, size), narrow)],
            place,
            other,
            before,
            down_weights,
            scalars=1,
        )
        stays = stays + to_chip(sends, first)
        part = 4 * block_rows
        sums += [stays[:part], to_chip(stays[part:].astype(narrow), second)]
    stay, send = small(
        split_kernel, [((part // 2, width), wide), ((part, half), narrow)], *sums
    )
    stay, send = small(
        split_kernel_last,
        [((block_rows, width), wide), ((part, width // 4), narrow)],
        stay,
        to_chip(send, Z1),
    )
    (out,) = small(last_kernel, [((1, block_rows, width), narrow)], stay, to_chip(send, Z2))
    return out


def solution(mesh):
    placed = (
        P(("groups", "tensor"), None, None),
        P("tensor", None, None),
        P("tensor", None, None),
        P("tensor", None, None),
        P("groups", "tensor", None),
        P("groups", "tensor", None),
        P("groups"),
        P("groups"),
    )
    return jax.shard_map(
        shards,
        mesh=mesh,
        in_specs=placed,
        out_specs=P(("groups", "tensor"), None, None),
        check_vma=False,
    )
```

```python
import functools

import jax
import jax.numpy as jnp
from jax import lax
from jax.experimental import pallas as pl
from jax.experimental.pallas import tpu as pltpu
from jax.sharding import PartitionSpec as P

HIDDEN_BITS = 4
FOLD = 128


def swapped(block, axis, apart):
    count = lax.axis_size(axis)
    return lax.ppermute(block, axis, [(i, i ^ (1 << apart)) for i in range(count)])


def by_target(expand, count):
    kinds, depth, width = expand.shape
    return expand.reshape(kinds, depth, count, width // count).transpose(2, 0, 1, 3)


def owner_of(ends, ids):
    return jnp.sum((ends[None, :] <= ids[:, None]).astype(jnp.int32), axis=1)


def keep_mask(rank_blocks, row_counts, columns, rows):
    adapters = rank_blocks.shape[0]
    earlier = jnp.arange(adapters)[:, None] >= jnp.arange(adapters)[None, :]
    block_end = jnp.sum(jnp.where(earlier, rank_blocks[None, :], 0), axis=1)
    row_end = jnp.sum(jnp.where(earlier, row_counts[None, :], 0), axis=1)
    column_owner = owner_of(block_end, jnp.arange(columns, dtype=jnp.int32) // 16)
    row_owner = owner_of(row_end, jnp.arange(rows, dtype=jnp.int32))
    ids = jnp.arange(adapters, dtype=jnp.int32)
    row_blocks = jnp.sum(
        jnp.where(row_owner[:, None] == ids[None, :], rank_blocks[None, :], 0), axis=1
    )
    same = (row_owner[:, None] == column_owner[None, :]).astype(jnp.float32)
    return same, 1.0 / row_blocks.astype(jnp.float32)


def general_shards(tokens, w_gate, w_up, w_down, shrink_factors, expand_factors, rank_blocks, row_counts):
    count = lax.axis_size("tensor")
    low_bits = count.bit_length() - 1 - HIDDEN_BITS
    fgroups = 1 << low_bits
    place = lax.axis_index("tensor")
    feature_group = place % fgroups
    hidden_group = place // fgroups
    block_rows = tokens.shape[1]
    rows = block_rows << HIDDEN_BITS
    units = w_gate.shape[2]
    strip = units // fgroups

    expand = lax.all_to_all(
        by_target(expand_factors, count), "tensor", split_axis=0, concat_axis=0, tiled=True
    )

    gathered = tokens[0]
    for bit in reversed(range(HIDDEN_BITS)):
        other = swapped(gathered, "tensor", low_bits + bit)
        gathered = jnp.concatenate([gathered, other], 0)
    spots = jnp.arange(1 << HIDDEN_BITS, dtype=jnp.int32)
    moved = sum(((spots >> i) & 1) << (HIDDEN_BITS - 1 - i) for i in range(HIDDEN_BITS))
    natural = (
        (moved ^ hidden_group)[:, None] * block_rows + jnp.arange(block_rows, dtype=jnp.int32)[None, :]
    ).reshape(rows)
    to_own = (natural[:, None] == jnp.arange(rows, dtype=jnp.int32)[None, :]).astype(jnp.bfloat16)

    columns = shrink_factors.shape[2]
    same, scale = keep_mask(rank_blocks, row_counts, columns, rows)
    slab = shrink_factors.shape[1]
    features = lax.dynamic_slice_in_dim(gathered, hidden_group * slab, slab, 1)
    features = jnp.dot(to_own.T, features, preferred_element_type=jnp.float32).astype(jnp.bfloat16)
    partial_value = jnp.einsum(
        "rd,kdc->krc", features, shrink_factors, preferred_element_type=jnp.float32
    )
    folded = jnp.sum((partial_value * same).reshape(2, rows, columns // FOLD, FOLD), axis=2)
    for bit in range(low_bits + HIDDEN_BITS):
        folded = folded + swapped(folded, "tensor", bit)
    shrunk = jnp.tile(folded, (1, 1, columns // FOLD)) * (same * scale[:, None])[None]
    shrunk = shrunk.astype(jnp.bfloat16)
    shrunk = jnp.einsum("or,krc->koc", to_own, shrunk, preferred_element_type=jnp.float32)
    shrunk = shrunk.astype(jnp.bfloat16)

    gate_part = jnp.dot(gathered, w_gate[0], preferred_element_type=jnp.float32)
    up_part = jnp.dot(gathered, w_up[0], preferred_element_type=jnp.float32)
    partials = jnp.stack([gate_part, up_part])
    for step in range(low_bits):
        bit = low_bits - 1 - step
        half = partials.shape[2] // 2
        high = feature_group // (1 << bit) % 2
        outgoing = lax.dynamic_slice_in_dim(partials, (1 - high) * half, half, 2)
        staying = lax.dynamic_slice_in_dim(partials, high * half, half, 2)
        partials = staying + swapped(outgoing, "tensor", bit)
    depth = expand.shape[2]
    low_rank = jnp.einsum(
        "krsd,skdc->krc",
        shrunk.reshape(2, rows, count, depth),
        expand,
        preferred_element_type=jnp.float32,
    )
    partials = partials + low_rank
    hidden = (jax.nn.silu(partials[0]) * partials[1]).astype(jnp.bfloat16)
    for step in range(low_bits):
        other = swapped(hidden, "tensor", step)
        high = feature_group // (1 << step) % 2 == 1
        hidden = jnp.where(
            high, jnp.concatenate([other, hidden], 1), jnp.concatenate([hidden, other], 1)
        )
    terms = jnp.dot(hidden, w_down[0], preferred_element_type=jnp.float32)
    for bit in range(HIDDEN_BITS):
        half = terms.shape[0] // 2
        outgoing = terms[half:].astype(jnp.bfloat16)
        terms = terms[:half] + swapped(outgoing, "tensor", low_bits + bit).astype(jnp.float32)
    return terms.astype(jnp.bfloat16)[None]


def keeping(ranks, counts, rows, columns):
    row = lax.broadcasted_iota(jnp.int32, (rows, 1), 0)
    block = lax.broadcasted_iota(jnp.int32, (1, columns), 1) // 16
    row_owner, column_owner = jnp.zeros_like(row), jnp.zeros_like(block)
    row_end = block_end = 0
    for adapter in range(ranks.shape[0]):
        row_end, block_end = row_end + counts[adapter], block_end + ranks[adapter]
        row_owner += (row >= row_end).astype(jnp.int32)
        column_owner += (block >= block_end).astype(jnp.int32)
    blocks = jnp.zeros_like(row)
    for adapter in range(ranks.shape[0]):
        blocks = jnp.where(row_owner == adapter, ranks[adapter], blocks)
    return row_owner == column_owner, 1.0 / blocks.astype(jnp.float32)


VMEM = pl.BlockSpec(memory_space=pltpu.VMEM)
SMEM = pl.BlockSpec(memory_space=pltpu.SMEM)
ANY = pl.BlockSpec(memory_space=pl.ANY)
X, Y, Z1, Z2 = 1, 2, 4, 8


def to_chip(block, apart):
    count = lax.axis_size("tensor")
    return lax.ppermute(block, "tensor", [(i, i ^ (apart << 1)) for i in range(count)])


def cost(flops, read):
    return pl.CostEstimate(flops=flops, bytes_accessed=read, transcendentals=0)


def in_hbm(array):
    return pltpu.with_memory_space_constraint(array, pltpu.HBM)


def blocks_kernel(count, strip, source, target):
    for j in range(count):
        target[j] = source[:, :, j * strip : (j + 1) * strip]


def blocks_of(expand, count):
    kinds, depth, width = expand.shape
    strip = width // count
    return pl.pallas_call(
        functools.partial(blocks_kernel, count, strip),
        out_shape=jax.ShapeDtypeStruct((count, kinds, depth, strip), expand.dtype),
        in_specs=[VMEM],
        out_specs=VMEM,
        cost_estimate=cost(0, 4 * expand.size),
        compiler_params=pltpu.CompilerParams(vmem_limit_bytes=10 << 20),
    )(expand)


def own_order(place, rows, own_axis):
    block = rows // 16
    own, natural = [lax.broadcasted_iota(jnp.int32, (rows, rows), axis) for axis in (own_axis, 1 - own_axis)]
    spot = own // block
    far = spot // 8 + spot // 4 % 2 * 2 + spot // 2 % 2 * 4 + spot % 2 * 8
    return ((far ^ (place // 2)) * block + (own - spot * block) == natural).astype(jnp.bfloat16)


def gathered_right(rights, right_y):
    part = rights.shape[0] // 2
    wide, corner = rights.astype(jnp.float32), right_y.astype(jnp.float32)
    pieces = [wide[:part], corner[:part], wide[part:], corner[part:]]
    return jnp.concatenate(pieces, axis=0).astype(rights.dtype)


def shrink_kernel(
    place, ranks, counts, lefts, left_x, rights, right_y, factors, folded, keep, order
):
    rows, columns = folded.shape[1], factors.shape[2]
    same, scale = keeping(ranks, counts, rows, columns)
    keep[...] = jnp.where(same, scale, 0.0)
    order[...] = own_order(place[0], rows, 0)
    slab = factors.shape[1]
    chip, chips = place[0] // 2, lefts.shape[1] // slab
    columns_here = pl.ds(pl.multiple_of(chip % chips * slab, slab), slab)
    left = rows_joined(lefts[:, columns_here], left_x[:, columns_here])
    right = gathered_right(rights[:, columns_here], right_y[:, columns_here])
    features = jnp.where(chip < chips, left, right)
    features = jnp.dot(
        own_order(place[0], rows, 1), features, preferred_element_type=jnp.float32
    ).astype(jnp.bfloat16)
    for k in range(2):
        value = jnp.dot(features, factors[k], preferred_element_type=jnp.float32)
        value = jnp.where(same, value, 0.0)
        total = value[:, :FOLD]
        for start in range(FOLD, columns, FOLD):
            total = total + value[:, start : start + FOLD]
        folded[k] = total


def small(kernel, shapes, *operands, scalars=0, limit=8):
    return pl.pallas_call(
        kernel,
        out_shape=[jax.ShapeDtypeStruct(shape, dtype) for shape, dtype in shapes],
        in_specs=[SMEM] * scalars + [VMEM] * (len(operands) - scalars),
        out_specs=[VMEM] * len(shapes),
        cost_estimate=cost(0, 1 << 20),
        compiler_params=pltpu.CompilerParams(vmem_limit_bytes=limit << 20),
    )(*operands)


def same_kernel(source, target):
    target[...] = source[0]


def rows_joined(*parts):
    wide = [part.astype(jnp.float32) for part in parts]
    return jnp.concatenate(wide, axis=0).astype(parts[0].dtype)


def joined_kernel(near, far, rows, send):
    total = rows_joined(near[...], far[...]).astype(jnp.float32)
    rows[...], send[...] = total.astype(rows.dtype), packed(total, 2).astype(send.dtype)


def parted_kernel(near, far, left, right):
    part, half = near.shape[0], left.shape[1]
    rows, wide = near[...].astype(jnp.float32), far[...].astype(jnp.float32)
    left[...] = jnp.concatenate([rows[:, :half], wide[:part]], axis=0).astype(left.dtype)
    right[...] = jnp.concatenate([rows[:, half:], wide[part:]], axis=0).astype(right.dtype)


def middle_kernel(left, left_y, right, right_x, lefts, rights):
    lefts[...] = rows_joined(left[...], left_y[...])
    rights[...] = rows_joined(right[...], right_x[...])


def fetch_kernel(count, pieces, *refs):
    sources, targets, sems = refs[:count], refs[-1 - count : -1], refs[-1]
    copies = []
    for k, (source, target) in enumerate(zip(sources, targets)):
        size = source.shape[1] // pieces
        for i in range(pieces):
            rows = pl.ds(i * size, size)
            copies.append(
                pltpu.make_async_copy(source.at[:, rows], target.at[:, rows], sems.at[k, i])
            )
    for copy in copies:
        copy.start()
    for copy in copies:
        copy.wait()


def fetch(sources, after, pieces):
    return pl.pallas_call(
        functools.partial(fetch_kernel, len(sources), pieces),
        out_shape=[pltpu.VMEM(source.shape, source.dtype) for source in sources],
        in_specs=[ANY] * (len(sources) + len(after)),
        out_specs=[VMEM] * len(sources),
        scratch_shapes=[pltpu.SemaphoreType.DMA((len(sources), pieces))],
        cost_estimate=cost(0, 2 * sum(source.size for source in sources)),
        compiler_params=pltpu.CompilerParams(vmem_limit_bytes=1 << 20),
    )(*[in_hbm(source) for source in sources], *after)


def chunks(width, most):
    return [(at, min(most, width - at)) for at in range(0, width, most)]


def inner_kernel(tile, place, lefts, left_x, rights, right_y, gate, up, *refs):
    outs, (gate_sum, up_sum, rows) = refs[:4], refs[4:]
    half = lefts.shape[1]
    rows[:, :half] = rows_joined(lefts[...], left_x[...])
    rows[:, half:] = gathered_right(rights[...], right_y[...])
    strip = outs[0].shape[1]
    first = place[0] % 2 == 0
    for weights, total, here, there in ((gate, gate_sum, *outs[:2]), (up, up_sum, *outs[2:])):
        for at, size in chunks(total.shape[1], tile):
            total[:, at : at + size] = jnp.dot(
                rows[...], weights[0, :, at : at + size], preferred_element_type=jnp.float32
            )
        low, high = total[:, :strip], total[:, strip:]
        here[...] = jnp.where(first, low, high)
        there[...] = jnp.where(first, high, low)


def inner(place, lefts, left_x, rights, right_y, gate, up, tile):
    half, width = lefts.shape
    rows, units = 2 * half, gate.shape[2]
    strip = jax.ShapeDtypeStruct((rows, units // 2), jnp.float32)
    return pl.pallas_call(
        functools.partial(inner_kernel, tile),
        out_shape=[strip] * 4,
        in_specs=[SMEM] + [VMEM] * 6,
        out_specs=[VMEM] * 4,
        scratch_shapes=[pltpu.VMEM((rows, units), jnp.float32)] * 2
        + [pltpu.VMEM((rows, 2 * width), lefts.dtype)],
        cost_estimate=cost(2 * rows * (gate.size + up.size), 2 * (gate.size + up.size)),
        compiler_params=pltpu.CompilerParams(vmem_limit_bytes=12 << 20),
    )(place, lefts, left_x, rights, right_y, gate, up)


def sums_kernel(gate, gate_in, up, up_in, gate_sum, up_sum):
    gate_sum[...] = gate[...] + gate_in[...]
    up_sum[...] = up[...] + up_in[...]


def ready_kernel(keep, order, folded, near, far, both, shrunk):
    for k in range(2):
        planes = [part[k].astype(jnp.float32) for part in (near, far, both)]
        total = (folded[k] + planes[0]) + (planes[1] + planes[2])
        value = jnp.concatenate([total] * (keep.shape[1] // FOLD), axis=1) * keep[...]
        shrunk[k] = jnp.dot(
            order[...], value.astype(shrunk.dtype), preferred_element_type=jnp.float32
        ).astype(shrunk.dtype)


def fetch_strip_kernel(other, pieces, place, source, *refs):
    target, sems = refs[-2:]
    strip = target.shape[1]
    core = place[0] % 2
    row = pl.multiple_of((1 - core if other else core) * strip, 128)
    size = strip // pieces
    copies = [
        pltpu.make_async_copy(
            source.at[:, pl.ds(row + i * size, size)], target.at[:, pl.ds(i * size, size)], sems.at[i]
        )
        for i in range(pieces)
    ]
    for copy in copies:
        copy.start()
    for copy in copies:
        copy.wait()


def fetch_strip(other, place, weights, after, pieces):
    shape = (1, weights.shape[1] // 2, weights.shape[2])
    return pl.pallas_call(
        functools.partial(fetch_strip_kernel, other, pieces),
        out_shape=pltpu.VMEM(shape, weights.dtype),
        in_specs=[SMEM] + [ANY] * (1 + len(after)),
        out_specs=VMEM,
        scratch_shapes=[pltpu.SemaphoreType.DMA((pieces,))],
        cost_estimate=cost(0, weights.size),
        compiler_params=pltpu.CompilerParams(vmem_limit_bytes=1 << 20),
    )(place, in_hbm(weights), *after)


def hidden_kernel(shrunk, gate, up, expand, hidden):
    columns = shrunk.shape[2]
    gate_sum, up_sum = [
        part[...]
        + jnp.dot(
            shrunk[k],
            expand[:, k].reshape(columns, expand.shape[3]),
            preferred_element_type=jnp.float32,
        )
        for k, part in enumerate((gate, up))
    ]
    hidden[...] = (gate_sum / (1.0 + jnp.exp(-gate_sum)) * up_sum).astype(hidden.dtype)


def other_strip(place, source, target, sems, start):
    depth, width = target.shape[1:]
    row, size = pl.multiple_of((1 - place[0] % 2) * depth, 128), depth // 4
    copies = [
        pltpu.make_async_copy(
            source.at[:, pl.ds(row + i * size, size), pl.ds(start, width)],
            target.at[:, pl.ds(i * size, size)],
            sems.at[i],
        )
        for i in range(4)
    ]
    for copy in copies:
        copy.start()
    return copies


def down_first_kernel(tile, place, mine, weights, source, terms, fetched, sems):
    copies = other_strip(place, source, fetched, sems, 0)
    for at, size in chunks(terms.shape[1], tile):
        terms[:, at : at + size] = jnp.dot(
            mine[...], weights[0, :, at : at + size], preferred_element_type=jnp.float32
        )
    for copy in copies:
        copy.wait()


def down_first(place, mine, own_weights, weights, half):
    rows, strip = mine.shape
    return pl.pallas_call(
        functools.partial(down_first_kernel, 256),
        out_shape=[
            jax.ShapeDtypeStruct((rows, weights.shape[2]), jnp.float32),
            pltpu.VMEM((1, strip, half), weights.dtype),
        ],
        in_specs=[SMEM, VMEM, VMEM, ANY],
        out_specs=[VMEM] * 2,
        scratch_shapes=[pltpu.SemaphoreType.DMA((4,))],
        cost_estimate=cost(2 * rows * own_weights.size, 3 * own_weights.size),
        compiler_params=pltpu.CompilerParams(vmem_limit_bytes=8 << 20),
    )(place, mine, own_weights, in_hbm(weights))


def down_last_kernel(start, tile, place, other, before, source, stays, sends, target, sems):
    for copy in other_strip(place, source, target, sems, start):
        copy.wait()
    down_kernel(False, start, tile, other, before, target, stays, sends)


def down_last(place, other, before, weights, start):
    rows, strip = other.shape
    width = weights.shape[2] - start
    return pl.pallas_call(
        functools.partial(down_last_kernel, start, 256),
        out_shape=[
            jax.ShapeDtypeStruct((rows // 2, width), dtype) for dtype in (jnp.float32, jnp.bfloat16)
        ],
        in_specs=[SMEM, VMEM, VMEM, ANY],
        out_specs=[VMEM] * 2,
        scratch_shapes=[pltpu.VMEM((1, strip, width), weights.dtype), pltpu.SemaphoreType.DMA((4,))],
        cost_estimate=cost(2 * rows * strip * width, 2 * strip * width),
        compiler_params=pltpu.CompilerParams(vmem_limit_bytes=12 << 20),
    )(place, other, before, in_hbm(weights))


def down_kernel(x_first, start, tile, other, before, weights, stays, sends):
    part = other.shape[0] // 4
    for at, size in chunks(stays.shape[1], tile):
        source, columns = pl.ds(start + at, size), pl.ds(at, size)
        terms = before[:, source] + jnp.dot(
            other[...], weights[0, :, columns], preferred_element_type=jnp.float32
        )
        low_y, high_y, far_low, far_high = [terms[k * part : (k + 1) * part] for k in range(4)]
        if x_first:
            stay, send = (low_y, high_y), (far_low, far_high)
        else:
            stay, send = (low_y, far_low), (high_y, far_high)
        stays[:, columns] = jnp.concatenate(stay, axis=0)
        sends[:, columns] = jnp.concatenate(send, axis=0).astype(sends.dtype)


def packed(total, pieces):
    size = total.shape[1] // pieces
    return jnp.concatenate([total[:, i * size : (i + 1) * size] for i in range(pieces)], axis=0)


def unpacked(packed_rows, pieces):
    wide = packed_rows.astype(jnp.float32)
    rows = wide.shape[0] // pieces
    return jnp.concatenate([wide[i * rows : (i + 1) * rows] for i in range(pieces)], axis=1)


def split_kernel(left, left_in, right, right_in, stay, send):
    totals = [
        part[...] + received[...].astype(jnp.float32)
        for part, received in ((left, left_in), (right, right_in))
    ]
    total = jnp.concatenate(totals, axis=1)
    half = stay.shape[0]
    stay[...], send[...] = total[:half], packed(total[half:], 2).astype(send.dtype)


def split_kernel_last(before, received, stay, send):
    total = before[...] + unpacked(received[...], 2)
    half = stay.shape[0]
    stay[...], send[...] = total[:half], packed(total[half:], 4).astype(send.dtype)


def last_kernel(stay, received, out):
    out[0] = (stay[...] + unpacked(received[...], 4)).astype(out.dtype)


def shards(tokens, w_gate, w_up, w_down, shrink_factors, expand_factors, rank_blocks, row_counts):
    count = lax.axis_size("tensor")
    units = w_gate.shape[2]
    if count != 32 or units % 256:
        return general_shards(
            tokens, w_gate, w_up, w_down, shrink_factors, expand_factors, rank_blocks, row_counts
        )
    place = lax.axis_index("tensor").reshape(1)
    block_rows, width = tokens.shape[1], tokens.shape[2]
    rows = 16 * block_rows
    half, columns = width // 2, shrink_factors.shape[2]
    wide, narrow = jnp.float32, jnp.bfloat16
    blocks = blocks_of(expand_factors, count)

    (own,) = small(same_kernel, [((block_rows, width), narrow)], tokens)
    own, other = lax.optimization_barrier((own, to_chip(tokens[0], Z2)))
    own, send = small(
        joined_kernel,
        [((2 * block_rows, width), narrow), ((4 * block_rows, half), narrow)],
        own,
        other,
    )
    blocks, other = lax.optimization_barrier((blocks, to_chip(send, Z1)))
    left, right = small(parted_kernel, [((4 * block_rows, half), narrow)] * 2, own, other)
    place, blocks, left, right = lax.optimization_barrier((place, blocks, left, right))
    expand = lax.all_to_all(blocks, "tensor", split_axis=0, concat_axis=0, tiled=True)

    hops = to_chip(left, Y), to_chip(right, X)
    fetched = fetch((w_gate, w_up, shrink_factors), (left,), 4)
    hops, fetched = lax.optimization_barrier((hops, fetched))
    gate_weights, up_weights, factors = fetched
    lefts, rights = small(
        middle_kernel, [((8 * block_rows, half), narrow)] * 2, left, hops[0], right, hops[1]
    )
    gathered = lefts, to_chip(lefts, X), rights, to_chip(rights, Y)

    folded, keep, order = small(
        shrink_kernel,
        [((2, rows, FOLD), wide), ((rows, columns), wide), ((rows, rows), narrow)],
        place,
        rank_blocks,
        row_counts,
        *gathered,
        factors,
        scalars=3,
    )
    folded = folded + swapped(folded, "tensor", 0)
    folded = folded + to_chip(folded, Y)
    strips = inner(place, *gathered, gate_weights, up_weights, 256)
    folded, strips = lax.optimization_barrier((folded, strips))
    folded = folded + to_chip(folded, X)
    sent = folded.astype(narrow)
    received = [to_chip(sent, apart) for apart in (Z1, Z2, Z1 | Z2)]

    gate, gate_out, up, up_out = strips
    strip = (gate.shape, wide)
    sums = small(
        sums_kernel, [strip] * 2, gate, swapped(gate_out, "tensor", 0), up, swapped(up_out, "tensor", 0)
    )
    received, own_weights = lax.optimization_barrier(
        (received, fetch_strip(False, place, w_down, (expand, *sums), 4))
    )
    (shrunk,) = small(ready_kernel, [((2, rows, columns), narrow)], keep, order, folded, *received)
    hidden_shape = (strip[0], narrow)
    (hidden,) = small(hidden_kernel, [hidden_shape], shrunk, *sums, expand)
    other = swapped(hidden, "tensor", 0)
    before, other_weights = down_first(place, hidden, own_weights, w_down, half)
    split = half
    sums = []
    for x_first, first, second in ((True, X, Y), (False, Y, X)):
        if x_first:
            stays, sends = small(
                functools.partial(down_kernel, True, 0, 256),
                [((rows // 2, split), wide), ((rows // 2, split), narrow)],
                other,
                before,
                other_weights,
            )
        else:
            stays, sends = down_last(place, other, before, w_down, split)
        stays = stays + to_chip(sends, first)
        part = 4 * block_rows
        sums += [stays[:part], to_chip(stays[part:].astype(narrow), second)]
    stay, send = small(
        split_kernel, [((part // 2, width), wide), ((part, half), narrow)], *sums
    )
    stay, send = small(
        split_kernel_last,
        [((block_rows, width), wide), ((part, width // 4), narrow)],
        stay,
        to_chip(send, Z1),
    )
    (out,) = small(last_kernel, [((1, block_rows, width), narrow)], stay, to_chip(send, Z2))
    return out


def solution(mesh):
    placed = (
        P(("groups", "tensor"), None, None),
        P("tensor", None, None),
        P("tensor", None, None),
        P("tensor", None, None),
        P("groups", "tensor", None),
        P("groups", "tensor", None),
        P("groups"),
        P("groups"),
    )
    return jax.shard_map(
        shards,
        mesh=mesh,
        in_specs=placed,
        out_specs=P(("groups", "tensor"), None, None),
        check_vma=False,
    )
```
